32 devices in a mesh: pipe: 2 (over core), dp: 8 (over z, x), tensor: 2 (over y).
Axes of the slice: x: 2, y: 2, z: 4, core: 2. Of those that a mesh axis runs over, the one named last changes fastest.
Arguments:
- block_input: bfloat16 [2, 1024, 2048], P(None, ('dp', 'tensor')), may hold values from -6 to 6
- cotangent: bfloat16 [2, 1024, 2048], P(None, ('dp', 'tensor')), may hold values from -6 to 6
- segments: int32 [2, 1024], replicated, may hold values from 0 to 3, never falling along the last dimension, each value on 1 to 512 neighbouring positions
- norm_gains: float32 [2, 2, 2048], P('pipe', None, ('dp', 'tensor')), may hold values from 0.5 to 1.5
- w_query: bfloat16 [2, 2048, 2048], P('pipe', 'dp', 'tensor'), may hold values from -0.125 to 0.125
- key_matrix: bfloat16 [2, 2048, 512], P('pipe', 'dp', 'tensor'), may hold values from -0.125 to 0.125
- value_matrix: bfloat16 [2, 2048, 512], P('pipe', 'dp', 'tensor'), may hold values from -0.125 to 0.125
- w_output: bfloat16 [2, 2048, 2048], P('pipe', 'tensor', 'dp'), may hold values from -1 to 1
- w_gate: bfloat16 [2, 2048, 8192], P('pipe', 'dp', 'tensor'), may hold values from -0.125 to 0.125
- w_up: bfloat16 [2, 2048, 8192], P('pipe', 'dp', 'tensor'), may hold values from -0.125 to 0.125
- w_down: bfloat16 [2, 8192, 2048], P('pipe', 'tensor', 'dp'), may hold values from -0.125 to 0.125
Outputs:
- layer_out: bfloat16 [2, 2, 1024, 2048], P('pipe', None, ('dp', 'tensor'))
- input_grad: bfloat16 [2, 2, 1024, 2048], P('pipe', None, ('dp', 'tensor'))
- grad_norm_gains: float32 [2, 2, 2048], P('pipe', None, ('dp', 'tensor'))
- grad_w_query: float32 [2, 2048, 2048], P('pipe', 'dp', 'tensor')
- grad_w_key: float32 [2, 2048, 512], P('pipe', 'dp', 'tensor')
- grad_w_value: float32 [2, 2048, 512], P('pipe', 'dp', 'tensor')
- grad_w_output: float32 [2, 2048, 2048], P('pipe', 'tensor', 'dp')
- grad_w_gate: float32 [2, 2048, 8192], P('pipe', 'dp', 'tensor')
- grad_w_up: float32 [2, 2048, 8192], P('pipe', 'dp', 'tensor')
- grad_w_down: float32 [2, 8192, 2048], P('pipe', 'tensor', 'dp')
The draws below stay inside these ranges and needn't reach their ends.
Inputs may be any that keep to these rules, and one draw needn't show every extreme that they name: `segments`: document numbers never fall along a sequence; each of the 4 documents holds 1 to 512 consecutive tokens, one exactly 512.
All inputs are finite; a program needn't handle non-finite values.
Results may differ from the reference program's by a relative error of at most 0.03.
Values may be sent and summed in bfloat16 or wider, within the bound.
No kernel may reach another device: no remote copies, remote signals or barrier semaphores. Data moves between devices by JAX's collectives and lax.ppermute only.
A program may use at most 256 MiB of HBM per device.

```python
import math
import jax
import jax.numpy as jnp
import numpy as np
from jax import lax

MODEL_WIDTH = 2048
QUERY_HEADS = 32
KEY_VALUE_HEADS = 8
HEAD_SIZE = 64
FF = 8192
MB = 2
LENGTH = 1024
DOCS = 4
DOC_MOST = 512


def levels(own_key, dims, split, smallest, high):
    def one(axis_at, parts):
        heights = jax.random.uniform(jax.random.fold_in(jax.random.fold_in(own_key, 6), axis_at), (parts,), jnp.float32, smallest / len(split), high / len(split))
        return jnp.repeat(jnp.exp(heights), dims[axis_at] // parts).reshape((-1,) + (1,) * (len(dims) - axis_at - 1))

    gain = one(*split[0])
    for cut in split[1:]:
        gain = gain * one(*cut)
    return gain


def length_profile(amount, total, most, slope):
    portions = [(1 << 20) // math.isqrt(grade ** slope) + 1 for grade in range(2, amount + 1)]
    spare, holding = total - most - (amount - 1), [1] * (amount - 1)
    while spare > 0:
        free = [i for i in range(amount - 1) if holding[i] < most]
        whole, budget = sum([portions[i] for i in free]), spare
        for i in free:
            extra = min(most - holding[i], max(1, budget * portions[i] // whole), spare)
            holding[i] = holding[i] + extra
            spare = spare - extra
    return np.array([most] + holding)


def uneven_parts(key, amount, total, bound, lean):
    if amount == 2:
        one = jax.random.randint(key, (), max(1, total - bound), min(bound, total - 1) + 1)
        return jnp.stack([one, total - one])
    lengths = jnp.asarray(length_profile(amount, total, bound, lean), jnp.int32)
    pairs = (amount - 1) // 2
    giver, taker = lengths[1:1 + 2 * pairs:2], lengths[2:2 + 2 * pairs:2]
    margin = jnp.minimum(giver - 1, bound - taker)
    moved = jax.random.randint(jax.random.fold_in(key, 1), (pairs,), 0, 1 << 20) % (margin + 1)
    lengths = lengths.at[1:1 + 2 * pairs:2].set(giver - moved).at[2:2 + 2 * pairs:2].set(taker + moved)
    return lengths[jax.random.permutation(jax.random.fold_in(key, 2), amount)]


def gaussian(rng, dims, spread, reach, pieces=(), kind=jnp.bfloat16):
    loudness = levels(rng, dims, pieces, -0.22, 0.18) if pieces else 1.0
    values = jax.random.normal(rng, dims, jnp.float32) * spread * loudness
    return jnp.minimum(jnp.maximum(values, -reach), reach).astype(kind)


def setup_inputs(seed: int = 0) -> dict:
    streams_of = jax.random.split(jax.random.key(seed), 12)
    return {
        "block_input": gaussian(streams_of[0], (MB, LENGTH, MODEL_WIDTH), 1.0, 6.0, ((1, 16),)),
        "cotangent": gaussian(streams_of[1], (MB, LENGTH, MODEL_WIDTH), 1.0, 6.0, ((1, 16),)),
        "segments": jax.vmap(lambda own: jnp.searchsorted(jnp.cumsum(uneven_parts(own, DOCS, LENGTH, DOC_MOST, 1)), jnp.arange(LENGTH), side="right"))(jax.random.split(streams_of[2], MB)).reshape((MB, LENGTH)).astype(jnp.int32),
        "norm_gains": jnp.clip(1.0 + 0.1 * jax.random.normal(streams_of[3], (2, 2, MODEL_WIDTH), jnp.float32), 0.5, 1.5),
        "w_query": gaussian(streams_of[4], (2, MODEL_WIDTH, QUERY_HEADS * HEAD_SIZE), MODEL_WIDTH ** -0.5, 0.125, ((0, 2), (1, 8), (2, 2))),
        "key_matrix": gaussian(streams_of[5], (2, MODEL_WIDTH, KEY_VALUE_HEADS * HEAD_SIZE), MODEL_WIDTH ** -0.5, 0.125, ((0, 2), (1, 8), (2, 2))),
        "value_matrix": gaussian(streams_of[6], (2, MODEL_WIDTH, KEY_VALUE_HEADS * HEAD_SIZE), MODEL_WIDTH ** -0.5, 0.125, ((0, 2), (1, 8), (2, 2))),
        "w_output": gaussian(streams_of[7], (2, QUERY_HEADS * HEAD_SIZE, MODEL_WIDTH), (max(4, QUERY_HEADS * HEAD_SIZE // 64)) ** -0.5, 1.0, ((0, 2), (1, 2), (2, 8))),
        "w_gate": gaussian(streams_of[8], (2, MODEL_WIDTH, FF), MODEL_WIDTH ** -0.5, 0.125, ((0, 2), (1, 8), (2, 2))),
        "w_up": gaussian(streams_of[9], (2, MODEL_WIDTH, FF), MODEL_WIDTH ** -0.5, 0.125, ((0, 2), (1, 8), (2, 2))),
        "w_down": gaussian(streams_of[10], (2, FF, MODEL_WIDTH), (FF // 4) ** -0.5, 0.125, ((0, 2), (1, 2), (2, 8))),
    }


EPS = 1e-05
ROPE_BASE = 500000.0
NEG_FILL = -1e+30
HIGH = lax.Precision.HIGHEST

@jax.custom_vjp
def lower_bound(v):
    return lax.optimization_barrier(v.astype(jnp.bfloat16)).astype(jnp.float32)

@jax.custom_vjp
def lower_bound_backward(v):
    return v

def low_keep(v):
    return (lower_bound(v), None)

def low_pass(kept, grad):
    return (grad,)

def back_keep(v):
    return (v, None)

def back_low(kept, grad):
    return (lower_bound(grad),)
lower_bound.defvjp(low_keep, low_pass)
lower_bound_backward.defvjp(back_keep, back_low)

def matmul(left_rows, right_rows):
    return jnp.dot(left_rows, right_rows, preferred_element_type=jnp.float32, precision=HIGH)

def rms_scale(row_values):
    return lax.rsqrt(lax.optimization_barrier(jnp.mean(row_values * row_values, axis=-1, keepdims=True)) + EPS)

def doc_positions(seg_row):
    places = jnp.arange(seg_row.shape[0], dtype=jnp.int32)
    before = jnp.concatenate([seg_row[:1] - 1, seg_row[:-1]])
    starts = lax.cummax(jnp.where(seg_row != before, places, 0), axis=0)
    return places - starts

def rope_tables(positions):
    half_dim = HEAD_SIZE // 2
    freqs = ROPE_BASE ** (-(jnp.arange(half_dim, dtype=jnp.float32) * 2.0 / HEAD_SIZE))
    angles = positions.astype(jnp.float32)[:, None] * freqs[None, :]
    return (jnp.cos(angles), jnp.sin(angles))

def rotary_apply(head_values, cosine_table, sine_values):
    half_dim = head_values.shape[-1] // 2
    first_half = head_values[..., :half_dim]
    second_half = head_values[..., half_dim:]
    cos_rows = cosine_table[:, None, :]
    sin_rows = sine_values[:, None, :]
    return jnp.concatenate([first_half * cos_rows - second_half * sin_rows, second_half * cos_rows + first_half * sin_rows], axis=-1)

def attention(query_rows, key_rows, value_rows, seg_row):
    sequence_length = query_rows.shape[0]
    rows_per_block = min(512, sequence_length)
    total_blocks = sequence_length // rows_per_block
    query_group_width = QUERY_HEADS // KEY_VALUE_HEADS
    blocks_of_query = query_rows.reshape(total_blocks, rows_per_block, KEY_VALUE_HEADS, query_group_width, HEAD_SIZE)
    seg_blocks = seg_row.reshape(total_blocks, rows_per_block)
    places = jnp.arange(sequence_length, dtype=jnp.int32)
    place_blocks = places.reshape(total_blocks, rows_per_block)

    @jax.checkpoint
    def one_block(block_items):
        query_blk, seg_blk, place_blk = block_items
        scores = lower_bound_backward(jnp.einsum('qhgd,khd->hgqk', query_blk, key_rows, precision=HIGH)) * HEAD_SIZE ** (-0.5)
        allowed = (places[None, :] <= place_blk[:, None]) & (seg_row[None, :] == seg_blk[:, None])
        masked = jnp.where(allowed, scores, NEG_FILL)
        row_max = lax.optimization_barrier(jnp.max(masked, axis=-1, keepdims=True))
        exps = jnp.where(allowed, jnp.exp(masked - row_max), 0.0)
        probs = lower_bound(exps / lax.optimization_barrier(jnp.sum(exps, axis=-1, keepdims=True)))
        return jnp.einsum('hgqk,khd->qhgd', probs, value_rows, precision=HIGH)
    context = lax.map(one_block, (blocks_of_query, seg_blocks, place_blocks))
    return context.reshape(sequence_length, QUERY_HEADS * HEAD_SIZE)

def layer_apply(x_rows, gain_pair, w_query, key_matrix, value_matrix, w_output, w_gate, w_up, w_down, seg_row):
    sequence_length = x_rows.shape[0]
    cosine_table, sine_values = rope_tables(doc_positions(seg_row))
    normed_a = lower_bound(x_rows * rms_scale(x_rows) * gain_pair[0])
    query_lin = lower_bound_backward(matmul(normed_a, w_query))
    key_linear = lower_bound_backward(matmul(normed_a, key_matrix))
    value_linear = matmul(normed_a, value_matrix)
    query_rows = lower_bound_backward(lower_bound(rotary_apply(query_lin.reshape(sequence_length, QUERY_HEADS, HEAD_SIZE), cosine_table, sine_values)))
    key_rows = lower_bound_backward(lower_bound(rotary_apply(key_linear.reshape(sequence_length, KEY_VALUE_HEADS, HEAD_SIZE), cosine_table, sine_values)))
    value_rows = lower_bound_backward(lower_bound(value_linear.reshape(sequence_length, KEY_VALUE_HEADS, HEAD_SIZE)))
    context = lower_bound_backward(lower_bound(attention(query_rows, key_rows, value_rows, seg_row)))
    mid_rows = x_rows + lower_bound_backward(matmul(context, w_output))
    normed_b = lower_bound(mid_rows * rms_scale(mid_rows) * gain_pair[1])
    gate_lin = lower_bound_backward(matmul(normed_b, w_gate))
    up_lin = lower_bound_backward(matmul(normed_b, w_up))
    hidden = lower_bound(jax.nn.silu(gate_lin) * up_lin)
    return mid_rows + lower_bound_backward(matmul(hidden, w_down))

def reference(block_input, cotangent, segments, norm_gains, w_query, key_matrix, value_matrix, w_output, w_gate, w_up, w_down):
    inputs_wide = block_input.astype(jnp.float32)
    probe = jnp.zeros_like(inputs_wide)
    params = (norm_gains.astype(jnp.float32), w_query.astype(jnp.float32), key_matrix.astype(jnp.float32), value_matrix.astype(jnp.float32), w_output.astype(jnp.float32), w_gate.astype(jnp.float32), w_up.astype(jnp.float32), w_down.astype(jnp.float32))

    def full_model(inputs, probe_in, gains, wq_all, wk_all, wv_all, wo_all, wg_all, wu_all, wd_all):

        def one_sequence(carry_value, items):
            x_seq, probe_seq, seg_row = items
            first_out = layer_apply(x_seq, gains[0], wq_all[0], wk_all[0], wv_all[0], wo_all[0], wg_all[0], wu_all[0], wd_all[0], seg_row)
            middle = lower_bound_backward(lower_bound(first_out)) + probe_seq
            last_out = layer_apply(middle, gains[1], wq_all[1], wk_all[1], wv_all[1], wo_all[1], wg_all[1], wu_all[1], wd_all[1], seg_row)
            return (carry_value, (middle, last_out))
        _, (middles, lasts) = lax.scan(one_sequence, jnp.zeros((), jnp.float32), (inputs, probe_in, segments))
        return (middles, lasts)
    (middles, lasts), pullback = jax.vjp(full_model, inputs_wide, probe, *params)
    grads = pullback((jnp.zeros_like(middles), cotangent.astype(jnp.float32)))
    grad_x, grad_probe, grad_gains, grad_q, grad_k, grad_v, grad_o, grad_g, grad_u, grad_d = grads
    layer_out = jnp.stack([middles, lasts]).astype(jnp.bfloat16)
    input_grad = jnp.stack([grad_x, grad_probe]).astype(jnp.bfloat16)
    return (layer_out, input_grad, grad_gains, grad_q, grad_k, grad_v, grad_o, grad_g, grad_u, grad_d)
```

```python
import functools

import jax
import jax.numpy as jnp
from jax import lax
from jax.experimental import pallas as pl
from jax.experimental.pallas import tpu as pltpu
from jax.sharding import Mesh, PartitionSpec as P

HEAD_SIZE = 64
KV_HEADS = 8
EPS = 1e-05
ROPE_BASE = 500000.0
NEG_FILL = -1e30
BF = jnp.bfloat16
F32 = jnp.float32
CUBE = ("wd", "tensor")


def rms_scale(row_values):
    return lax.rsqrt(jnp.mean(row_values * row_values, axis=-1, keepdims=True) + EPS)


def apply_norm(row_values, gain_vector):
    return row_values * rms_scale(row_values) * gain_vector


def norm_back(row_values, gain_vector, grad_normed):
    _, pullback = jax.vjp(apply_norm, row_values, gain_vector)
    return pullback(grad_normed)


def doc_starts(seg_row):
    places = jnp.arange(seg_row.shape[0], dtype=jnp.int32)
    before = jnp.concatenate([seg_row[:1] - 1, seg_row[:-1]])
    return lax.cummax(jnp.where(seg_row != before, places, 0), axis=0)


def rope_tables(positions):
    half_dim = HEAD_SIZE // 2
    freqs = ROPE_BASE ** (-(jnp.arange(half_dim, dtype=F32) * 2.0 / HEAD_SIZE))
    angles = positions.astype(F32)[:, None] * freqs[None, :]
    return (jnp.cos(angles), jnp.sin(angles))


def rotary_apply(head_values, cosine_table, sine_values):
    half_dim = head_values.shape[-1] // 2
    first_half = head_values[..., :half_dim]
    second_half = head_values[..., half_dim:]
    cos_rows = cosine_table[:, None, :]
    sin_rows = sine_values[:, None, :]
    return jnp.concatenate(
        [
            first_half * cos_rows - second_half * sin_rows,
            second_half * cos_rows + first_half * sin_rows,
        ],
        axis=-1,
    )


def mm(left, right):
    return jnp.dot(left, right, preferred_element_type=F32)


def mm_t(left, right):
    return lax.dot_general(left, right, (((1,), (1,)), ((), ())), preferred_element_type=F32)


def mm_tl(left, right):
    return lax.dot_general(left, right, (((0,), (0,)), ((), ())), preferred_element_type=F32)


def trade(blocks, axes):
    return lax.all_to_all(blocks, axes, 0, 0, tiled=True)


def gather_rows(rows):
    count = lax.axis_size(CUBE)
    spread = jnp.broadcast_to(rows[None], (count,) + rows.shape)
    return trade(spread, CUBE).reshape((count * rows.shape[0],) + rows.shape[1:])


def sum_rows(partial):
    count = lax.axis_size(CUBE)
    blocks = partial.astype(BF).reshape((count, -1) + partial.shape[1:])
    return jnp.sum(trade(blocks, CUBE).astype(F32), axis=0)


def hop(block, axis, step):
    size = lax.axis_size(axis)
    return lax.ppermute(block, axis, [(i, i ^ step) for i in range(size)])


def others(block, axis):
    return [block] + [hop(block, axis, k) for k in range(1, lax.axis_size(axis))]


def sum_others(blocks, axis):
    total = blocks[0].astype(F32)
    for k in range(1, lax.axis_size(axis)):
        total = total + hop(blocks[k].astype(BF), axis, k).astype(F32)
    return total


def relative(values, dim):
    count = lax.axis_size("grp")
    me = lax.axis_index("grp")
    step = 1
    while step < count:
        shape = values.shape
        cut = shape[:dim] + (count // (2 * step), 2, step * (shape[dim] // count)) + shape[dim + 1 :]
        view = values.reshape(cut)
        swapped = jnp.concatenate(
            [lax.slice_in_dim(view, 1, 2, axis=dim + 1), lax.slice_in_dim(view, 0, 1, axis=dim + 1)],
            axis=dim + 1,
        )
        values = jnp.where((me & step) != 0, swapped.reshape(shape), values)
        step *= 2
    return values


def masked_probs(q, k, q_place, q_start, k_place):
    scores = lax.dot_general(q, k, (((1,), (1,)), ((), ())), preferred_element_type=F32)
    scores = scores * HEAD_SIZE ** (-0.5)
    allowed = (k_place <= q_place) & (k_place >= q_start)
    masked = jnp.where(allowed, scores, NEG_FILL)
    exps = jnp.exp(masked - jnp.max(masked, axis=-1, keepdims=True))
    return exps / jnp.sum(exps, axis=-1, keepdims=True)


def attend_kernel(q_ref, k_ref, v_ref, qp_ref, qs_ref, kp_ref, o_ref):
    probs = masked_probs(q_ref[0], k_ref[...], qp_ref[...], qs_ref[...], kp_ref[...])
    o_ref[0] = jnp.dot(probs.astype(BF), v_ref[...], preferred_element_type=F32).astype(BF)


def attend_back_kernel(q_ref, do_ref, k_ref, v_ref, qp_ref, qs_ref, kp_ref, dq_ref, dk_ref, dv_ref):
    @pl.when((pl.program_id(0) == 0) & (pl.program_id(1) == 0))
    def _():
        dk_ref[...] = jnp.zeros_like(dk_ref)
        dv_ref[...] = jnp.zeros_like(dv_ref)

    q = q_ref[0]
    do = do_ref[0]
    k = k_ref[...]
    probs = masked_probs(q, k, qp_ref[...], qs_ref[...], kp_ref[...])
    grad_probs = lax.dot_general(do, v_ref[...], (((1,), (1,)), ((), ())), preferred_element_type=F32)
    delta = jnp.sum(probs * grad_probs, axis=-1, keepdims=True)
    grad_scores = (probs * (grad_probs - delta) * HEAD_SIZE ** (-0.5)).astype(BF)
    dq_ref[0] = jnp.dot(grad_scores, k, preferred_element_type=F32).astype(BF)
    dk_ref[...] += lax.dot_general(
        grad_scores, q, (((0,), (0,)), ((), ())), preferred_element_type=F32
    )
    dv_ref[...] += lax.dot_general(
        probs.astype(BF), do, (((0,), (0,)), ((), ())), preferred_element_type=F32
    )


def attention_specs(heads, rows, keys):
    rows_blk = max(16, min(rows, (512 * 1024) // keys))
    per_head = pl.BlockSpec((1, rows_blk, HEAD_SIZE), lambda b, h: (h, b, 0))
    full = pl.BlockSpec((keys, HEAD_SIZE), lambda b, h: (0, 0))
    row_info = pl.BlockSpec((rows_blk, 1), lambda b, h: (b, 0))
    key_info = pl.BlockSpec((1, keys), lambda b, h: (0, 0))
    return ((rows // rows_blk, heads), per_head, full, row_info, key_info)


PARAMS = dict(
    compiler_params=pltpu.CompilerParams(vmem_limit_bytes=50 * 1024 * 1024),
)


def attend(q, k, v, q_place, q_start, k_place):
    heads, rows, _ = q.shape
    keys = k.shape[0]
    grid, per_head, full, row_info, key_info = attention_specs(heads, rows, keys)
    return pl.pallas_call(
        attend_kernel,
        grid=grid,
        in_specs=[per_head, full, full, row_info, row_info, key_info],
        out_specs=per_head,
        out_shape=jax.ShapeDtypeStruct(q.shape, BF),
        cost_estimate=pl.CostEstimate(
            flops=4 * heads * rows * keys * HEAD_SIZE,
            bytes_accessed=4 * q.size + 4 * k.size,
            transcendentals=heads * rows * keys,
        ),
        **PARAMS,
    )(q, k, v, q_place, q_start, k_place)


def attend_back(q, do, k, v, q_place, q_start, k_place):
    heads, rows, _ = q.shape
    keys = k.shape[0]
    grid, per_head, full, row_info, key_info = attention_specs(heads, rows, keys)
    return pl.pallas_call(
        attend_back_kernel,
        grid=grid,
        in_specs=[per_head, per_head, full, full, row_info, row_info, key_info],
        out_specs=[per_head, full, full],
        out_shape=[
            jax.ShapeDtypeStruct(q.shape, BF),
            jax.ShapeDtypeStruct(k.shape, F32),
            jax.ShapeDtypeStruct(k.shape, F32),
        ],
        cost_estimate=pl.CostEstimate(
            flops=10 * heads * rows * keys * HEAD_SIZE,
            bytes_accessed=6 * q.size + 12 * k.size,
            transcendentals=heads * rows * keys,
        ),
        **PARAMS,
    )(q, do, k, v, q_place, q_start, k_place)


def columns_out(weight, cores):
    wd = lax.axis_size("wd")
    rows = weight.shape[0]
    cut = weight.reshape(rows, wd, cores, -1).transpose(2, 1, 0, 3)
    moved = trade(cut.reshape((cores * wd, rows) + cut.shape[3:]), ("pipe", "wd"))
    return moved.reshape(cores, wd * rows, -1)


def layer_weight(piece):
    full = jnp.concatenate(others(piece, "grp"), axis=0)
    return full, hop(full, "pipe", 1)


def pack_attention(w_query, key_matrix, value_matrix, w_output, cores):
    wd = lax.axis_size("wd")
    rows = w_query.shape[0]
    cut = [
        m.reshape(rows, wd, cores, -1) for m in (w_query, key_matrix, value_matrix, w_output.T)
    ]
    return jnp.concatenate(cut, axis=-1).reshape(rows, -1)


def core_order(own, other, axis):
    core = lax.axis_index("pipe")
    return jnp.where(
        core == 0,
        jnp.concatenate([own, other], axis=axis),
        jnp.concatenate([other, own], axis=axis),
    )


def unpack_attention(own, other, widths):
    query_w, kv_w, out_w = widths
    cuts = (query_w, query_w + kv_w, query_w + 2 * kv_w)

    def split(m):
        return (m[:, : cuts[0]], m[:, cuts[0] : cuts[1]], m[:, cuts[1] : cuts[2]], m[:, cuts[2] :])

    q0, k0, v0, o0 = split(own)
    q1, k1, v1, o1 = split(other)
    return (
        jnp.concatenate([q0, q1], axis=1),
        core_order(k0, k1, 1),
        core_order(v0, v1, 1),
        jnp.concatenate([o0, o1], axis=1),
    )


def core_halves(grad):
    half = grad.shape[1] // 2
    core = lax.axis_index("pipe")
    low, high = grad[:, :half], grad[:, half:]
    return (jnp.where(core == 0, low, high), jnp.where(core == 0, high, low))


def grad_home(own, other):
    total = own + hop(other.astype(BF), "pipe", 1).astype(F32)
    count = lax.axis_size("grp")
    blocks = total.reshape((count, -1) + total.shape[1:])
    mine = sum_others([blocks[k] for k in range(count)], "grp").astype(BF)
    wd = lax.axis_size("wd")
    return trade(mine.reshape((wd, -1) + mine.shape[1:]), "wd")


def layer_forward(x_rows, gains, weights, where):
    w_q, w_k, w_v, w_ot, w_g, w_u, w_dt = weights
    cosine, sine, q_place, q_start, k_place = where
    rows_a = gather_rows(apply_norm(x_rows, gains[0]).astype(BF))
    tok = rows_a.shape[0]
    query = rotary_apply(mm(rows_a, w_q).reshape(tok, -1, HEAD_SIZE), cosine, sine).astype(BF)
    query = query.transpose(1, 0, 2)
    key = rotary_apply(mm(rows_a, w_k).reshape(tok, 1, HEAD_SIZE), cosine, sine).astype(BF)[:, 0]
    value = mm(rows_a, w_v).astype(BF)
    kv_all = jnp.concatenate(others(jnp.concatenate([key, value], axis=1), "grp"), axis=0)
    keys, values = kv_all[:, :HEAD_SIZE], kv_all[:, HEAD_SIZE:]
    context = attend(query, keys, values, q_place, q_start, k_place)
    context = context.transpose(1, 0, 2).reshape(tok, -1)
    mid = x_rows + sum_rows(mm_t(context, w_ot))
    rows_b = gather_rows(apply_norm(mid, gains[1]).astype(BF))
    gate = mm(rows_b, w_g)
    up = mm(rows_b, w_u)
    hidden = (jax.nn.silu(gate) * up).astype(BF)
    out = mid + sum_rows(mm_t(hidden, w_dt))
    return out, (x_rows, rows_a, query, keys, values, context, mid, rows_b, gate, up, hidden)


def layer_backward(grad_out, gains, weights, where, kept):
    w_q, w_k, w_v, w_ot, w_g, w_u, w_dt = weights
    cosine, sine, q_place, q_start, k_place = where
    x_rows, rows_a, query, keys, values, context, mid, rows_b, gate, up, hidden = kept
    tok = rows_a.shape[0]
    grad_mlp = gather_rows(grad_out.astype(BF))
    grad_hidden = mm(grad_mlp, w_dt)
    sig = jax.nn.sigmoid(gate)
    grad_gate = (grad_hidden * up * sig * (1.0 + gate * (1.0 - sig))).astype(BF)
    grad_up = (grad_hidden * gate * sig).astype(BF)
    grad_b = sum_rows(mm_t(grad_gate, w_g) + mm_t(grad_up, w_u))
    half = grad_gate.shape[1] // 2

    def mlp_grad(left, right):
        return grad_home(mm_tl(left, right[:, :half]), mm_tl(left, right[:, half:]))

    home_gate = mlp_grad(rows_b, grad_gate)
    home_up = mlp_grad(rows_b, grad_up)
    home_down = mlp_grad(grad_mlp, hidden)
    grad_mid, gain_b = norm_back(mid, gains[1], grad_b)
    grad_mid = grad_mid + grad_out
    grad_attn = gather_rows(grad_mid.astype(BF))
    grad_context = mm(grad_attn, w_ot).astype(BF)
    grad_context = grad_context.reshape(tok, -1, HEAD_SIZE).transpose(1, 0, 2)
    grad_q, grad_k, grad_v = attend_back(
        query, grad_context, keys, values, q_place, q_start, k_place
    )
    kv = jnp.concatenate([grad_k, grad_v], axis=1)
    kv = kv.reshape((-1, tok) + kv.shape[1:])
    own_kv = sum_others([kv[k] for k in range(kv.shape[0])], "grp").astype(BF)
    grad_k = own_kv[:, :HEAD_SIZE].astype(F32)
    grad_k = rotary_apply(grad_k[:, None, :], cosine, -sine).astype(BF)[:, 0]
    grad_v = own_kv[:, HEAD_SIZE:]
    grad_q = grad_q.transpose(1, 0, 2).astype(F32)
    grad_q = rotary_apply(grad_q, cosine, -sine).astype(BF).reshape(tok, -1)
    grad_a = sum_rows(mm_t(grad_q, w_q) + mm_t(grad_k, w_k) + mm_t(grad_v, w_v))
    grad_in, gain_a = norm_back(x_rows, gains[0], grad_a)
    grad_in = grad_mid + grad_in
    half_q = grad_q.shape[1] // 2
    kv_0, kv_1 = core_halves(grad_k)
    v_0, v_1 = core_halves(grad_v)

    def attn_term(q_half, k_half, v_half, o_half):
        right = jnp.concatenate([q_half, k_half, v_half], axis=1)
        return jnp.concatenate([mm_tl(rows_a, right), mm_tl(grad_attn, o_half)], axis=1)

    home_attn = grad_home(
        attn_term(grad_q[:, :half_q], kv_0, v_0, context[:, :half_q]),
        attn_term(grad_q[:, half_q:], kv_1, v_1, context[:, half_q:]),
    )
    return grad_in, jnp.stack([gain_a, gain_b]), (home_attn, home_gate, home_up, home_down)


def own_layer(first, second):
    core = lax.axis_index("pipe")
    keep = jnp.where(core == 0, first, second)
    return keep, hop(jnp.where(core == 0, second, first), "pipe", 1)


def body(
    block_input,
    cotangent,
    segments,
    norm_gains,
    w_query,
    key_matrix,
    value_matrix,
    w_output,
    w_gate,
    w_up,
    w_down,
):
    core = lax.axis_index("pipe")
    grp = lax.axis_index("grp")
    wd = lax.axis_size("wd")
    groups = lax.axis_size("grp")
    cores = lax.axis_size("pipe")
    tok = block_input.shape[1] * lax.axis_size(CUBE)

    gain_half = trade(
        jnp.broadcast_to(norm_gains, (lax.axis_size(CUBE),) + norm_gains.shape[1:]), CUBE
    )
    gain_half = gain_half.transpose(1, 0, 2).reshape(2, -1)
    gain_own = jnp.concatenate(others(gain_half, "grp"), axis=1)
    gain_other = hop(gain_own, "pipe", 1)
    gains = [
        jnp.where(core == 0, gain_own, gain_other),
        jnp.where(core == 0, gain_other, gain_own),
    ]

    attn_cols = columns_out(
        pack_attention(w_query[0], key_matrix[0], value_matrix[0], w_output[0], cores), cores
    )
    gate_cols = columns_out(w_gate[0], cores)
    up_cols = columns_out(w_up[0], cores)
    down_cols = columns_out(w_down[0].T, cores)
    widths = tuple(n // (wd * cores) for n in (w_query.shape[2], key_matrix.shape[2], w_output.shape[1]))
    weights = []
    for layer in range(2):
        attn = unpack_attention(*layer_weight(attn_cols[layer]), widths)
        mlp = tuple(
            jnp.concatenate(layer_weight(m[layer]), axis=1) for m in (gate_cols, up_cols, down_cols)
        )
        weights.append(attn + mlp)

    seg_row = lax.dynamic_index_in_dim(segments, core, 0, keepdims=False)
    starts = doc_starts(seg_row)
    q_place = grp * tok + jnp.arange(tok, dtype=jnp.int32)
    q_start = lax.dynamic_slice_in_dim(starts, grp * tok, tok)
    cosine, sine = rope_tables(q_place - q_start)
    k_place = relative(jnp.arange(groups * tok, dtype=jnp.int32), 0)
    where = (cosine, sine, q_place[:, None], q_start[:, None], k_place[None, :])

    rows = relative(lax.dynamic_index_in_dim(block_input, core, 0, keepdims=False), 1)
    outs = []
    kept = []
    for layer in range(2):
        out, state = layer_forward(rows.astype(F32), gains[layer], weights[layer], where)
        rows = out.astype(BF)
        outs.append(rows)
        kept.append(state)

    grad = relative(lax.dynamic_index_in_dim(cotangent, core, 0, keepdims=False), 1)
    grads_in = [None, None]
    gain_grads = [None, None]
    homes = [None, None]
    for layer in (1, 0):
        grad_in, gain_grads[layer], homes[layer] = layer_backward(
            grad.astype(F32), gains[layer], weights[layer], where, kept[layer]
        )
        grad = grad_in.astype(BF)
        grads_in[layer] = grad

    def by_batch(pair):
        own, other = own_layer(pair[0], pair[1])
        both = jnp.where(core == 0, jnp.stack([own, other]), jnp.stack([other, own]))
        return relative(both, 2)[None]

    layer_out = by_batch(outs)
    input_grad = by_batch(grads_in)

    keep, extra = own_layer(gain_grads[0], gain_grads[1])
    gain_total = (keep + extra).reshape(2, groups, -1)
    mine = gain_total[:, 0]
    for k in range(1, groups):
        mine = mine + hop(gain_total[:, k], "grp", k)
    mine = mine.reshape(2, lax.axis_size(CUBE), -1).transpose(1, 0, 2)
    grad_norm_gains = jnp.sum(trade(mine, CUBE), axis=0)[None]

    def joined(index):
        own, other = own_layer(homes[0][index], homes[1][index])
        both = jnp.where(core == 0, jnp.stack([own, other]), jnp.stack([other, own]))
        return both.transpose(2, 1, 0, 3).astype(F32)

    attn = joined(0)
    cuts = (widths[0], widths[0] + widths[1], widths[0] + 2 * widths[1])
    rows_d = attn.shape[0]
    grad_wq = attn[..., : cuts[0]].reshape(rows_d, -1)[None]
    grad_wk = attn[..., cuts[0] : cuts[1]].reshape(rows_d, -1)[None]
    grad_wv = attn[..., cuts[1] : cuts[2]].reshape(rows_d, -1)[None]
    grad_wo = attn[..., cuts[2] :].reshape(rows_d, -1).T[None]
    grad_wg = joined(1).reshape(rows_d, -1)[None]
    grad_wu = joined(2).reshape(rows_d, -1)[None]
    grad_wd = joined(3).reshape(rows_d, -1).T[None]
    return (
        layer_out,
        input_grad,
        grad_norm_gains,
        grad_wq,
        grad_wk,
        grad_wv,
        grad_wo,
        grad_wg,
        grad_wu,
        grad_wd,
    )


def solution(mesh):
    sizes = dict(mesh.shape)
    wd = KV_HEADS // sizes["tensor"]
    fine = Mesh(
        mesh.devices.reshape(sizes["pipe"], sizes["dp"] // wd, wd, sizes["tensor"]),
        ("pipe", "grp", "wd", "tensor"),
    )
    dp = ("grp", "wd")
    tokens = P(None, dp + ("tensor",), None)
    outs = P("pipe", None, dp + ("tensor",), None)
    gains = P("pipe", None, dp + ("tensor",))
    tall = P("pipe", dp, "tensor")
    wide = P("pipe", "tensor", dp)
    weights = (tall, tall, tall, wide, tall, tall, wide)
    return jax.shard_map(
        body,
        mesh=fine,
        in_specs=(tokens, tokens, P(), gains) + weights,
        out_specs=(outs, outs, gains) + weights,
        check_vma=False,
    )
```

```python
import jax
import jax.numpy as jnp
from jax import lax
from jax.experimental import pallas as pl
from jax.experimental.pallas import tpu as pltpu
from jax.sharding import Mesh, PartitionSpec as P

HEAD_SIZE = 64
KV_HEADS = 8
EPS = 1e-05
ROPE_BASE = 500000.0
NEG_FILL = -1e30
BF = jnp.bfloat16
F32 = jnp.float32
CUBE = ("wd", "tensor")


def rms_scale(row_values):
    return lax.rsqrt(jnp.mean(row_values * row_values, axis=-1, keepdims=True) + EPS)


def apply_norm(row_values, gain_vector):
    return row_values * rms_scale(row_values) * gain_vector


def norm_back(row_values, gain_vector, grad_normed):
    _, pullback = jax.vjp(apply_norm, row_values, gain_vector)
    return pullback(grad_normed)


def doc_starts(seg_row):
    places = jnp.arange(seg_row.shape[0], dtype=jnp.int32)
    before = jnp.concatenate([seg_row[:1] - 1, seg_row[:-1]])
    return lax.cummax(jnp.where(seg_row != before, places, 0), axis=0)


def rope_tables(positions):
    half_dim = HEAD_SIZE // 2
    freqs = ROPE_BASE ** (-(jnp.arange(half_dim, dtype=F32) * 2.0 / HEAD_SIZE))
    angles = positions.astype(F32)[:, None] * freqs[None, :]
    return (jnp.cos(angles), jnp.sin(angles))


def rotary_apply(head_values, cosine_table, sine_values):
    half_dim = head_values.shape[-1] // 2
    first_half = head_values[..., :half_dim]
    second_half = head_values[..., half_dim:]
    cos_rows = cosine_table[:, None, :]
    sin_rows = sine_values[:, None, :]
    return jnp.concatenate(
        [
            first_half * cos_rows - second_half * sin_rows,
            second_half * cos_rows + first_half * sin_rows,
        ],
        axis=-1,
    )


def mm(left, right):
    return jnp.dot(left, right, preferred_element_type=F32)


def mm_t(left, right):
    return lax.dot_general(left, right, (((1,), (1,)), ((), ())), preferred_element_type=F32)


def mm_tl(left, right):
    return lax.dot_general(left, right, (((0,), (0,)), ((), ())), preferred_element_type=F32)


def trade(blocks, axes):
    return lax.all_to_all(blocks, axes, 0, 0, tiled=True)


def hop(block, axis, step):
    size = lax.axis_size(axis)
    return lax.ppermute(block, axis, [(i, i ^ step) for i in range(size)])


def tie(*values):
    return lax.optimization_barrier(values)


def link_steps():
    steps = []
    step = 1
    while step < lax.axis_size(CUBE):
        steps.append(step)
        step *= 2
    return steps


def lanes_cut(width):
    count = len(link_steps())
    tiles = width // 128
    edges = [128 * (tiles * i // count) for i in range(count)] + [width]
    return list(zip(edges[:-1], edges[1:]))


def turned(steps, by):
    return steps[by:] + steps[:by]


def gather_rows(rows):
    steps = link_steps()
    parts = []
    state = [rows[:, lo:hi] for lo, hi in lanes_cut(rows.shape[1])]
    for phase in range(len(steps)):
        arrived = [hop(x, CUBE, turned(steps, t)[phase]) for t, x in enumerate(state)]
        state = [jnp.concatenate([x, y], axis=0) for x, y in zip(state, arrived)]
    for t, x in enumerate(state):
        order = turned(steps, t)
        cut = x.reshape((2,) * len(steps) + (rows.shape[0], x.shape[1]))
        axes = [order[::-1].index(s) for s in steps[::-1]]
        cut = cut.transpose(axes + [len(steps), len(steps) + 1])
        parts.append(cut.reshape(x.shape))
    return jnp.concatenate(parts, axis=1)


def sum_rows(partial):
    steps = link_steps()
    count = len(steps)
    cut = partial.astype(BF).reshape((2,) * count + (-1, partial.shape[1]))
    state = [cut[..., lo:hi] for lo, hi in lanes_cut(partial.shape[1])]
    left = [steps[::-1]] * count
    for phase in range(count):
        sent = []
        kept = []
        for t, x in enumerate(state):
            at = left[t].index(turned(steps, t)[phase])
            kept.append(lax.index_in_dim(x, 0, at, keepdims=False).astype(F32))
            sent.append(lax.index_in_dim(x, 1, at, keepdims=False).astype(BF))
        arrived = [hop(x, CUBE, turned(steps, t)[phase]) for t, x in enumerate(sent)]
        state = [x + y.astype(F32) for x, y in zip(kept, arrived)]
        left = [
            [s for s in l if s != turned(steps, t)[phase]] for t, l in enumerate(left)
        ]
    return jnp.concatenate(state, axis=-1)


def others(block, axis):
    return [block] + [hop(block, axis, k) for k in range(1, lax.axis_size(axis))]


def sum_others(blocks, axis):
    total = blocks[0].astype(F32)
    for k in range(1, lax.axis_size(axis)):
        total = total + hop(blocks[k].astype(BF), axis, k).astype(F32)
    return total


def relative(values, dim, axis):
    count = lax.axis_size(axis)
    me = lax.axis_index(axis)
    step = 1
    while step < count:
        shape = values.shape
        cut = shape[:dim] + (count // (2 * step), 2, step * (shape[dim] // count)) + shape[dim + 1 :]
        view = values.reshape(cut)
        swapped = jnp.concatenate(
            [lax.slice_in_dim(view, 1, 2, axis=dim + 1), lax.slice_in_dim(view, 0, 1, axis=dim + 1)],
            axis=dim + 1,
        )
        values = jnp.where((me & step) != 0, swapped.reshape(shape), values)
        step *= 2
    return values


def spread_gains(norm_gains):
    me = lax.axis_index(CUBE)
    gain = norm_gains
    for step in link_steps():
        came = hop(gain, CUBE, step)
        gain = jnp.where(
            (me & step) != 0,
            jnp.concatenate([came, gain], axis=1),
            jnp.concatenate([gain, came], axis=1),
        )
    gain = jnp.concatenate(others(gain, "grp"), axis=1)
    other = hop(gain, "pipe", 1)
    core = lax.axis_index("pipe")
    return [jnp.where(core == 0, gain, other), jnp.where(core == 0, other, gain)]


def sum_gains(grads):
    me = lax.axis_index(CUBE)
    keep, extra = own_layer(grads[0], grads[1])
    total = (keep + extra).reshape(2, lax.axis_size("grp"), -1)
    mine = total[:, 0]
    for k in range(1, total.shape[1]):
        mine = mine + hop(total[:, k], "grp", k)
    for step in link_steps()[::-1]:
        half = mine.shape[1] // 2
        low, high = mine[:, :half], mine[:, half:]
        odd = (me & step) != 0
        mine = jnp.where(odd, high, low) + hop(jnp.where(odd, low, high), CUBE, step)
    return mine


def masked_probs(q, k, q_place, q_start, k_place):
    scores = lax.dot_general(q, k, (((1,), (1,)), ((), ())), preferred_element_type=F32)
    scores = scores * HEAD_SIZE ** (-0.5)
    allowed = (k_place <= q_place) & (k_place >= q_start)
    masked = jnp.where(allowed, scores, NEG_FILL)
    exps = jnp.exp(masked - jnp.max(masked, axis=-1, keepdims=True))
    return exps / jnp.sum(exps, axis=-1, keepdims=True)


def attend_kernel(q_ref, k_ref, v_ref, qp_ref, qs_ref, kp_ref, o_ref):
    probs = masked_probs(q_ref[0], k_ref[...], qp_ref[...], qs_ref[...], kp_ref[...])
    o_ref[0] = jnp.dot(probs.astype(BF), v_ref[...], preferred_element_type=F32).astype(BF)


def attend_back_kernel(q_ref, do_ref, k_ref, v_ref, qp_ref, qs_ref, kp_ref, dq_ref, dk_ref, dv_ref):
    @pl.when((pl.program_id(0) == 0) & (pl.program_id(1) == 0))
    def _():
        dk_ref[...] = jnp.zeros_like(dk_ref)
        dv_ref[...] = jnp.zeros_like(dv_ref)

    q = q_ref[0]
    do = do_ref[0]
    k = k_ref[...]
    probs = masked_probs(q, k, qp_ref[...], qs_ref[...], kp_ref[...])
    grad_probs = lax.dot_general(do, v_ref[...], (((1,), (1,)), ((), ())), preferred_element_type=F32)
    delta = jnp.sum(probs * grad_probs, axis=-1, keepdims=True)
    grad_scores = (probs * (grad_probs - delta) * HEAD_SIZE ** (-0.5)).astype(BF)
    dq_ref[0] = jnp.dot(grad_scores, k, preferred_element_type=F32).astype(BF)
    dk_ref[...] += lax.dot_general(
        grad_scores, q, (((0,), (0,)), ((), ())), preferred_element_type=F32
    )
    dv_ref[...] += lax.dot_general(
        probs.astype(BF), do, (((0,), (0,)), ((), ())), preferred_element_type=F32
    )


def attention_specs(heads, rows, keys):
    rows_blk = max(16, min(rows, (512 * 1024) // keys))
    per_head = pl.BlockSpec((1, rows_blk, HEAD_SIZE), lambda b, h: (h, b, 0))
    full = pl.BlockSpec((keys, HEAD_SIZE), lambda b, h: (0, 0))
    row_info = pl.BlockSpec((rows_blk, 1), lambda b, h: (b, 0))
    key_info = pl.BlockSpec((1, keys), lambda b, h: (0, 0))
    return ((rows // rows_blk, heads), per_head, full, row_info, key_info)


PARAMS = dict(
    compiler_params=pltpu.CompilerParams(vmem_limit_bytes=50 * 1024 * 1024),
)


def attend(q, k, v, q_place, q_start, k_place):
    heads, rows, _ = q.shape
    keys = k.shape[0]
    grid, per_head, full, row_info, key_info = attention_specs(heads, rows, keys)
    return pl.pallas_call(
        attend_kernel,
        grid=grid,
        in_specs=[per_head, full, full, row_info, row_info, key_info],
        out_specs=per_head,
        out_shape=jax.ShapeDtypeStruct(q.shape, BF),
        cost_estimate=pl.CostEstimate(
            flops=4 * heads * rows * keys * HEAD_SIZE,
            bytes_accessed=4 * q.size + 4 * k.size,
            transcendentals=heads * rows * keys,
        ),
        **PARAMS,
    )(q, k, v, q_place, q_start, k_place)


def attend_back(q, do, k, v, q_place, q_start, k_place):
    heads, rows, _ = q.shape
    keys = k.shape[0]
    grid, per_head, full, row_info, key_info = attention_specs(heads, rows, keys)
    return pl.pallas_call(
        attend_back_kernel,
        grid=grid,
        in_specs=[per_head, per_head, full, full, row_info, row_info, key_info],
        out_specs=[per_head, full, full],
        out_shape=[
            jax.ShapeDtypeStruct(q.shape, BF),
            jax.ShapeDtypeStruct(k.shape, F32),
            jax.ShapeDtypeStruct(k.shape, F32),
        ],
        cost_estimate=pl.CostEstimate(
            flops=10 * heads * rows * keys * HEAD_SIZE,
            bytes_accessed=6 * q.size + 12 * k.size,
            transcendentals=heads * rows * keys,
        ),
        **PARAMS,
    )(q, do, k, v, q_place, q_start, k_place)


def columns_out(weight, cores):
    wd = lax.axis_size("wd")
    rows = weight.shape[0]
    cut = weight.reshape(rows, wd, cores, -1).transpose(2, 1, 0, 3)
    moved = trade(cut.reshape((cores * wd, rows) + cut.shape[3:]), ("pipe", "wd"))
    return moved.reshape(cores, wd * rows, -1)


def all_rows(piece, after):
    came = []
    for k in range(1, lax.axis_size("grp")):
        if after is not None:
            piece_now, _ = tie(piece, after)
        else:
            piece_now = piece
        after = hop(piece_now, "grp", k)
        came.append(after)
    return [piece] + came


def both_cores(pieces):
    there = [hop(p, "pipe", 1) for p in pieces]
    return jnp.concatenate(pieces, axis=0), jnp.concatenate(there, axis=0)


def pack_attention(w_query, key_matrix, value_matrix, w_output, cores):
    wd = lax.axis_size("wd")
    rows = w_query.shape[0]
    cut = [
        m.reshape(rows, wd, cores, -1) for m in (w_query, key_matrix, value_matrix, w_output.T)
    ]
    return jnp.concatenate(cut, axis=-1).reshape(rows, -1)


def core_order(own, other, axis):
    core = lax.axis_index("pipe")
    return jnp.where(
        core == 0,
        jnp.concatenate([own, other], axis=axis),
        jnp.concatenate([other, own], axis=axis),
    )


def unpack_attention(own, other, widths):
    query_w, kv_w, out_w = widths
    cuts = (query_w, query_w + kv_w, query_w + 2 * kv_w)

    def split(m):
        return (m[:, : cuts[0]], m[:, cuts[0] : cuts[1]], m[:, cuts[1] : cuts[2]], m[:, cuts[2] :])

    q0, k0, v0, o0 = split(own)
    q1, k1, v1, o1 = split(other)
    return (
        jnp.concatenate([q0, q1], axis=1),
        core_order(k0, k1, 1),
        core_order(v0, v1, 1),
        jnp.concatenate([o0, o1], axis=1),
    )


def core_halves(grad):
    half = grad.shape[1] // 2
    core = lax.axis_index("pipe")
    low, high = grad[:, :half], grad[:, half:]
    return (jnp.where(core == 0, low, high), jnp.where(core == 0, high, low))


def grad_half(own, other):
    total = own + hop(other.astype(BF), "pipe", 1).astype(F32)
    count = lax.axis_size("grp")
    return total.reshape((count, -1) + total.shape[1:])


def grad_home(blocks, after):
    total = blocks[0]
    for k in range(1, lax.axis_size("grp")):
        send = blocks[k].astype(BF)
        if after is not None:
            send, _ = tie(send, after)
        after = hop(send, "grp", k)
        total = total + after.astype(F32)
    return total.astype(BF), after


def to_owner(total):
    wd = lax.axis_size("wd")
    return trade(total.reshape((wd, -1) + total.shape[1:]), "wd")


def layer_forward(x_rows, gains, halves, widths, where):
    cosine, sine, q_place, q_start, k_place = where
    rows_a = gather_rows(apply_norm(x_rows, gains[0]).astype(BF))
    w_q, w_k, w_v, w_ot = unpack_attention(*both_cores(halves[0]), widths)
    tok = rows_a.shape[0]
    query = rotary_apply(mm(rows_a, w_q).reshape(tok, -1, HEAD_SIZE), cosine, sine).astype(BF)
    query = query.transpose(1, 0, 2)
    key = rotary_apply(mm(rows_a, w_k).reshape(tok, 1, HEAD_SIZE), cosine, sine).astype(BF)[:, 0]
    value = mm(rows_a, w_v).astype(BF)
    kv_all = jnp.concatenate(others(jnp.concatenate([key, value], axis=1), "grp"), axis=0)
    keys, values = kv_all[:, :HEAD_SIZE], kv_all[:, HEAD_SIZE:]
    context = attend(query, keys, values, q_place, q_start, k_place)
    context, _ = tie(context, halves[1][-1])
    context = context.transpose(1, 0, 2).reshape(tok, -1)
    mid = x_rows + sum_rows(mm_t(context, w_ot))
    mid, _ = tie(mid, halves[2][-1])
    rows_b = gather_rows(apply_norm(mid, gains[1]).astype(BF))
    w_g = jnp.concatenate(both_cores(halves[1]), axis=1)
    w_u = jnp.concatenate(both_cores(halves[2]), axis=1)
    gate = mm(rows_b, w_g)
    up = mm(rows_b, w_u)
    hidden = (jax.nn.silu(gate) * up).astype(BF)
    w_dt = jnp.concatenate(both_cores(halves[3]), axis=1)
    out = mid + sum_rows(mm_t(hidden, w_dt))
    weights = (w_q, w_k, w_v, w_ot, w_g, w_u, w_dt)
    return out, weights, (x_rows, rows_a, query, keys, values, context, mid, rows_b, gate, up, hidden)


def layer_backward(grad_out, gains, weights, where, kept, after, late):
    w_q, w_k, w_v, w_ot, w_g, w_u, w_dt = weights
    cosine, sine, q_place, q_start, k_place = where
    x_rows, rows_a, query, keys, values, context, mid, rows_b, gate, up, hidden = kept
    tok = rows_a.shape[0]
    grad_mlp = gather_rows(grad_out.astype(BF))
    half = hidden.shape[1] // 2

    def mlp_grad(left, right):
        return grad_half(mm_tl(left, right[:, :half]), mm_tl(left, right[:, half:]))

    down_blocks = mlp_grad(grad_mlp, hidden)
    grad_hidden = mm(grad_mlp, w_dt)
    if late:
        grad_hidden, _ = tie(grad_hidden, late[0])
    sig = jax.nn.sigmoid(gate)
    grad_gate = (grad_hidden * up * sig * (1.0 + gate * (1.0 - sig))).astype(BF)
    grad_up = (grad_hidden * gate * sig).astype(BF)
    home_down, after = grad_home(down_blocks, after)
    grad_b = sum_rows(mm_t(grad_gate, w_g) + mm_t(grad_up, w_u))
    if late:
        grad_b, _ = tie(grad_b, late[1])
    gate_blocks = mlp_grad(rows_b, grad_gate)
    up_blocks = mlp_grad(rows_b, grad_up)
    grad_mid, gain_b = norm_back(mid, gains[1], grad_b)
    grad_mid = grad_mid + grad_out
    grad_attn = gather_rows(grad_mid.astype(BF))
    grad_attn, _ = tie(grad_attn, after)
    home_gate, after = grad_home(gate_blocks, after)
    grad_context = mm(grad_attn, w_ot).astype(BF)
    grad_context = grad_context.reshape(tok, -1, HEAD_SIZE).transpose(1, 0, 2)
    grad_q, grad_k, grad_v = attend_back(
        query, grad_context, keys, values, q_place, q_start, k_place
    )
    kv = jnp.concatenate([grad_k, grad_v], axis=1)
    kv = kv.reshape((-1, tok) + kv.shape[1:])
    own_kv = sum_others([kv[k] for k in range(kv.shape[0])], "grp").astype(BF)
    grad_k = own_kv[:, :HEAD_SIZE].astype(F32)
    grad_k = rotary_apply(grad_k[:, None, :], cosine, -sine).astype(BF)[:, 0]
    grad_v = own_kv[:, HEAD_SIZE:]
    grad_q = grad_q.transpose(1, 0, 2).astype(F32)
    grad_q = rotary_apply(grad_q, cosine, -sine).astype(BF).reshape(tok, -1)
    grad_a = sum_rows(mm_t(grad_q, w_q) + mm_t(grad_k, w_k) + mm_t(grad_v, w_v))
    if not late:
        grad_a, _ = tie(grad_a, after)
    home_up, after = grad_home(up_blocks, after)
    still = [after]
    grad_in, gain_a = norm_back(x_rows, gains[0], grad_a)
    grad_in = grad_mid + grad_in
    half_q = grad_q.shape[1] // 2
    kv_0, kv_1 = core_halves(grad_k)
    v_0, v_1 = core_halves(grad_v)

    def attn_term(q_half, k_half, v_half, o_half):
        right = jnp.concatenate([q_half, k_half, v_half], axis=1)
        return jnp.concatenate([mm_tl(rows_a, right), mm_tl(grad_attn, o_half)], axis=1)

    attn_blocks = grad_half(
        attn_term(grad_q[:, :half_q], kv_0, v_0, context[:, :half_q]),
        attn_term(grad_q[:, half_q:], kv_1, v_1, context[:, half_q:]),
    )
    home_attn, after = grad_home(attn_blocks, after)
    still.append(after)
    homes = tuple(to_owner(h) for h in (home_attn, home_gate, home_up, home_down))
    return grad_in, jnp.stack([gain_a, gain_b]), homes, after, still


def own_layer(first, second):
    core = lax.axis_index("pipe")
    keep = jnp.where(core == 0, first, second)
    return keep, hop(jnp.where(core == 0, second, first), "pipe", 1)


def body(
    block_input,
    cotangent,
    segments,
    norm_gains,
    w_query,
    key_matrix,
    value_matrix,
    w_output,
    w_gate,
    w_up,
    w_down,
):
    core = lax.axis_index("pipe")
    grp = lax.axis_index("grp")
    wd = lax.axis_size("wd")
    groups = lax.axis_size("grp")
    cores = lax.axis_size("pipe")
    tok = block_input.shape[1] * lax.axis_size(CUBE)

    gains = spread_gains(norm_gains[0])

    attn_cols = columns_out(
        pack_attention(w_query[0], key_matrix[0], value_matrix[0], w_output[0], cores), cores
    )
    gate_cols = columns_out(w_gate[0], cores)
    up_cols = columns_out(w_up[0], cores)
    down_cols = columns_out(w_down[0].T, cores)
    widths = tuple(n // (wd * cores) for n in (w_query.shape[2], key_matrix.shape[2], w_output.shape[1]))
    halves = []
    after = None
    for layer in range(2):
        own = []
        for cols in (attn_cols, gate_cols, up_cols, down_cols):
            own.append(all_rows(cols[layer], after))
            after = own[-1][-1]
        halves.append(own)

    seg_row = lax.dynamic_index_in_dim(segments, core, 0, keepdims=False)
    starts = doc_starts(seg_row)
    local = relative(jnp.arange(tok, dtype=jnp.int32), 0, CUBE)
    q_place = grp * tok + local
    q_start = relative(lax.dynamic_slice_in_dim(starts, grp * tok, tok), 0, CUBE)
    cosine, sine = rope_tables(q_place - q_start)
    k_place = jnp.concatenate([(grp ^ k) * tok + local for k in range(groups)])
    where = (cosine, sine, q_place[:, None], q_start[:, None], k_place[None, :])

    rows = relative(lax.dynamic_index_in_dim(block_input, core, 0, keepdims=False), 1, "grp")
    outs = []
    kept = []
    weights = []
    for layer in range(2):
        out, full, state = layer_forward(
            rows.astype(F32), gains[layer], halves[layer], widths, where
        )
        rows = out.astype(BF)
        outs.append(rows)
        kept.append(state)
        weights.append(full)

    grad = relative(lax.dynamic_index_in_dim(cotangent, core, 0, keepdims=False), 1, "grp")
    grads_in = [None, None]
    gain_grads = [None, None]
    homes = [None, None]
    after, late = None, None
    for layer in (1, 0):
        grad_in, gain_grads[layer], homes[layer], after, late = layer_backward(
            grad.astype(F32), gains[layer], weights[layer], where, kept[layer], after, late
        )
        grad = grad_in.astype(BF)
        grads_in[layer] = grad

    def by_batch(pair):
        own, other = own_layer(pair[0], pair[1])
        both = jnp.where(core == 0, jnp.stack([own, other]), jnp.stack([other, own]))
        return relative(both, 2, "grp")[None]

    layer_out = by_batch(outs)
    input_grad = by_batch(grads_in)

    grad_norm_gains = sum_gains(gain_grads)[None]

    def joined(index):
        own, other = own_layer(homes[0][index], homes[1][index])
        both = jnp.where(core == 0, jnp.stack([own, other]), jnp.stack([other, own]))
        return both.transpose(2, 1, 0, 3).astype(F32)

    attn = joined(0)
    cuts = (widths[0], widths[0] + widths[1], widths[0] + 2 * widths[1])
    rows_d = attn.shape[0]
    grad_wq = attn[..., : cuts[0]].reshape(rows_d, -1)[None]
    grad_wk = attn[..., cuts[0] : cuts[1]].reshape(rows_d, -1)[None]
    grad_wv = attn[..., cuts[1] : cuts[2]].reshape(rows_d, -1)[None]
    grad_wo = attn[..., cuts[2] :].reshape(rows_d, -1).T[None]
    grad_wg = joined(1).reshape(rows_d, -1)[None]
    grad_wu = joined(2).reshape(rows_d, -1)[None]
    grad_wd = joined(3).reshape(rows_d, -1).T[None]
    return (
        layer_out,
        input_grad,
        grad_norm_gains,
        grad_wq,
        grad_wk,
        grad_wv,
        grad_wo,
        grad_wg,
        grad_wu,
        grad_wd,
    )


def solution(mesh):
    sizes = dict(mesh.shape)
    wd = KV_HEADS // sizes["tensor"]
    fine = Mesh(
        mesh.devices.reshape(sizes["pipe"], sizes["dp"] // wd, wd, sizes["tensor"]),
        ("pipe", "grp", "wd", "tensor"),
    )
    dp = ("grp", "wd")
    tokens = P(None, dp + ("tensor",), None)
    outs = P("pipe", None, dp + ("tensor",), None)
    gains = P("pipe", None, dp + ("tensor",))
    tall = P("pipe", dp, "tensor")
    wide = P("pipe", "tensor", dp)
    weights = (tall, tall, tall, wide, tall, tall, wide)
    return jax.shard_map(
        body,
        mesh=fine,
        in_specs=(tokens, tokens, P(), gains) + weights,
        out_specs=(outs, outs, gains) + weights,
        check_vma=False,
    )
```

```python
import jax
import jax.numpy as jnp
from jax import lax
from jax.experimental import pallas as pl
from jax.experimental.pallas import tpu as pltpu
from jax.sharding import Mesh, PartitionSpec as P

HEAD_SIZE = 64
KV_HEADS = 8
EPS = 1e-05
ROPE_BASE = 500000.0
NEG_FILL = -1e30
BF = jnp.bfloat16
F32 = jnp.float32
CUBE = ("wd", "tensor")


def rms_scale(row_values):
    return lax.rsqrt(jnp.mean(row_values * row_values, axis=-1, keepdims=True) + EPS)


def apply_norm(row_values, gain_vector):
    return row_values * rms_scale(row_values) * gain_vector


def norm_back(row_values, gain_vector, grad_normed):
    _, pullback = jax.vjp(apply_norm, row_values, gain_vector)
    return pullback(grad_normed)


def doc_starts(seg_row):
    places = jnp.arange(seg_row.shape[0], dtype=jnp.int32)
    before = jnp.concatenate([seg_row[:1] - 1, seg_row[:-1]])
    return lax.cummax(jnp.where(seg_row != before, places, 0), axis=0)


def rope_tables(positions):
    half_dim = HEAD_SIZE // 2
    freqs = ROPE_BASE ** (-(jnp.arange(half_dim, dtype=F32) * 2.0 / HEAD_SIZE))
    angles = positions.astype(F32)[:, None] * freqs[None, :]
    return (jnp.cos(angles), jnp.sin(angles))


def rotary_apply(head_values, cosine_table, sine_values):
    half_dim = head_values.shape[-1] // 2
    first_half = head_values[..., :half_dim]
    second_half = head_values[..., half_dim:]
    cos_rows = cosine_table[:, None, :]
    sin_rows = sine_values[:, None, :]
    return jnp.concatenate(
        [
            first_half * cos_rows - second_half * sin_rows,
            second_half * cos_rows + first_half * sin_rows,
        ],
        axis=-1,
    )


def mm(left, right):
    return jnp.dot(left, right, preferred_element_type=F32)


def mm_t(left, right):
    return lax.dot_general(left, right, (((1,), (1,)), ((), ())), preferred_element_type=F32)


def mm_tl(left, right):
    return lax.dot_general(left, right, (((0,), (0,)), ((), ())), preferred_element_type=F32)


def trade(blocks, axes):
    return lax.all_to_all(blocks, axes, 0, 0, tiled=True)


def hop(block, axis, step):
    size = lax.axis_size(axis)
    return lax.ppermute(block, axis, [(i, i ^ step) for i in range(size)])


def tie(*values):
    return lax.optimization_barrier(values)


def link_steps():
    steps = []
    step = 1
    while step < lax.axis_size(CUBE):
        steps.append(step)
        step *= 2
    return steps


def gather_rows(rows):
    count = lax.axis_size(CUBE)
    spread = jnp.broadcast_to(rows[None], (count,) + rows.shape)
    return trade(spread, CUBE).reshape((count * rows.shape[0],) + rows.shape[1:])


def sum_rows(partial):
    count = lax.axis_size(CUBE)
    blocks = partial.astype(BF).reshape((count, -1) + partial.shape[1:])
    return jnp.sum(trade(blocks, CUBE).astype(F32), axis=0)


class Flow:
    def __init__(self):
        self.queue = []
        self.last = None

    def add(self, block):
        box = []
        self.queue.append((block, box))
        return box

    def issue(self):
        block, box = self.queue.pop(0)
        for k in range(1, lax.axis_size("grp")):
            now = block if block.ndim == 2 else block[k - 1]
            if self.last is not None:
                now, _ = tie(now, self.last)
            self.last = hop(now, "grp", k)
            box.append(self.last)

    def step(self, value, count=1):
        for _ in range(min(count, len(self.queue))):
            self.issue()
        value, _ = tie(value, self.last)
        return value

    def need(self, box):
        while not box:
            self.issue()
        return box


def others(block, axis):
    return [block] + [hop(block, axis, k) for k in range(1, lax.axis_size(axis))]


def sum_others(blocks, axis):
    total = blocks[0].astype(F32)
    for k in range(1, lax.axis_size(axis)):
        total = total + hop(blocks[k].astype(BF), axis, k).astype(F32)
    return total


def relative(values, dim, axis):
    count = lax.axis_size(axis)
    me = lax.axis_index(axis)
    step = 1
    while step < count:
        shape = values.shape
        cut = shape[:dim] + (count // (2 * step), 2, step * (shape[dim] // count)) + shape[dim + 1 :]
        view = values.reshape(cut)
        swapped = jnp.concatenate(
            [lax.slice_in_dim(view, 1, 2, axis=dim + 1), lax.slice_in_dim(view, 0, 1, axis=dim + 1)],
            axis=dim + 1,
        )
        values = jnp.where((me & step) != 0, swapped.reshape(shape), values)
        step *= 2
    return values


def spread_gains(norm_gains):
    me = lax.axis_index(CUBE)
    gain = norm_gains
    for step in link_steps():
        came = hop(gain, CUBE, step)
        gain = jnp.where(
            (me & step) != 0,
            jnp.concatenate([came, gain], axis=1),
            jnp.concatenate([gain, came], axis=1),
        )
    gain = jnp.concatenate(others(gain, "grp"), axis=1)
    other = hop(gain, "pipe", 1)
    core = lax.axis_index("pipe")
    return [jnp.where(core == 0, gain, other), jnp.where(core == 0, other, gain)]


def sum_gains(grads):
    me = lax.axis_index(CUBE)
    keep, extra = own_layer(grads[0], grads[1])
    total = (keep + extra).reshape(2, lax.axis_size("grp"), -1)
    mine = total[:, 0]
    for k in range(1, total.shape[1]):
        mine = mine + hop(total[:, k], "grp", k)
    for step in link_steps()[::-1]:
        half = mine.shape[1] // 2
        low, high = mine[:, :half], mine[:, half:]
        odd = (me & step) != 0
        mine = jnp.where(odd, high, low) + hop(jnp.where(odd, low, high), CUBE, step)
    return mine


def masked_probs(q, k, q_place, q_start, k_place):
    scores = lax.dot_general(q, k, (((1,), (1,)), ((), ())), preferred_element_type=F32)
    scores = scores * HEAD_SIZE ** (-0.5)
    allowed = (k_place <= q_place) & (k_place >= q_start)
    masked = jnp.where(allowed, scores, NEG_FILL)
    exps = jnp.exp(masked - jnp.max(masked, axis=-1, keepdims=True))
    return exps / jnp.sum(exps, axis=-1, keepdims=True)


def attend_kernel(q_ref, k_ref, v_ref, qp_ref, qs_ref, kp_ref, o_ref):
    probs = masked_probs(q_ref[0], k_ref[...], qp_ref[...], qs_ref[...], kp_ref[...])
    o_ref[0] = jnp.dot(probs.astype(BF), v_ref[...], preferred_element_type=F32).astype(BF)


def attend_back_kernel(q_ref, do_ref, k_ref, v_ref, qp_ref, qs_ref, kp_ref, dq_ref, dk_ref, dv_ref):
    @pl.when((pl.program_id(0) == 0) & (pl.program_id(1) == 0))
    def _():
        dk_ref[...] = jnp.zeros_like(dk_ref)
        dv_ref[...] = jnp.zeros_like(dv_ref)

    q = q_ref[0]
    do = do_ref[0]
    k = k_ref[...]
    probs = masked_probs(q, k, qp_ref[...], qs_ref[...], kp_ref[...])
    grad_probs = lax.dot_general(do, v_ref[...], (((1,), (1,)), ((), ())), preferred_element_type=F32)
    delta = jnp.sum(probs * grad_probs, axis=-1, keepdims=True)
    grad_scores = (probs * (grad_probs - delta) * HEAD_SIZE ** (-0.5)).astype(BF)
    dq_ref[0] = jnp.dot(grad_scores, k, preferred_element_type=F32).astype(BF)
    dk_ref[...] += lax.dot_general(
        grad_scores, q, (((0,), (0,)), ((), ())), preferred_element_type=F32
    )
    dv_ref[...] += lax.dot_general(
        probs.astype(BF), do, (((0,), (0,)), ((), ())), preferred_element_type=F32
    )


def attention_specs(heads, rows, keys):
    rows_blk = max(16, min(rows, (512 * 1024) // keys))
    per_head = pl.BlockSpec((1, rows_blk, HEAD_SIZE), lambda b, h: (h, b, 0))
    full = pl.BlockSpec((keys, HEAD_SIZE), lambda b, h: (0, 0))
    row_info = pl.BlockSpec((rows_blk, 1), lambda b, h: (b, 0))
    key_info = pl.BlockSpec((1, keys), lambda b, h: (0, 0))
    return ((rows // rows_blk, heads), per_head, full, row_info, key_info)


PARAMS = dict(
    compiler_params=pltpu.CompilerParams(vmem_limit_bytes=50 * 1024 * 1024),
)


def attend(q, k, v, q_place, q_start, k_place):
    heads, rows, _ = q.shape
    keys = k.shape[0]
    grid, per_head, full, row_info, key_info = attention_specs(heads, rows, keys)
    return pl.pallas_call(
        attend_kernel,
        grid=grid,
        in_specs=[per_head, full, full, row_info, row_info, key_info],
        out_specs=per_head,
        out_shape=jax.ShapeDtypeStruct(q.shape, BF),
        cost_estimate=pl.CostEstimate(
            flops=4 * heads * rows * keys * HEAD_SIZE,
            bytes_accessed=4 * q.size + 4 * k.size,
            transcendentals=heads * rows * keys,
        ),
        **PARAMS,
    )(q, k, v, q_place, q_start, k_place)


def attend_back(q, do, k, v, q_place, q_start, k_place):
    heads, rows, _ = q.shape
    keys = k.shape[0]
    grid, per_head, full, row_info, key_info = attention_specs(heads, rows, keys)
    return pl.pallas_call(
        attend_back_kernel,
        grid=grid,
        in_specs=[per_head, per_head, full, full, row_info, row_info, key_info],
        out_specs=[per_head, full, full],
        out_shape=[
            jax.ShapeDtypeStruct(q.shape, BF),
            jax.ShapeDtypeStruct(k.shape, F32),
            jax.ShapeDtypeStruct(k.shape, F32),
        ],
        cost_estimate=pl.CostEstimate(
            flops=10 * heads * rows * keys * HEAD_SIZE,
            bytes_accessed=6 * q.size + 12 * k.size,
            transcendentals=heads * rows * keys,
        ),
        **PARAMS,
    )(q, do, k, v, q_place, q_start, k_place)


def columns_out(weight, cores):
    wd = lax.axis_size("wd")
    rows = weight.shape[0]
    cut = weight.reshape(rows, wd, cores, -1).transpose(2, 1, 0, 3)
    moved = trade(cut.reshape((cores * wd, rows) + cut.shape[3:]), ("pipe", "wd"))
    return moved.reshape(cores, wd * rows, -1)


def in_halves(flow, piece):
    half = piece.shape[1] // 2
    return [(p, flow.add(p)) for p in (piece[:, :half], piece[:, half:])]


def arrived(flow, parts):
    return jnp.concatenate(
        [jnp.concatenate([p] + flow.need(box), axis=0) for p, box in parts], axis=1
    )


def both_cores(flow, parts):
    own = arrived(flow, parts)
    return own, hop(own, "pipe", 1)


def pack_attention(w_query, key_matrix, value_matrix, w_output, cores):
    wd = lax.axis_size("wd")
    rows = w_query.shape[0]
    cut = [
        m.reshape(rows, wd, cores, -1) for m in (w_query, key_matrix, value_matrix, w_output.T)
    ]
    return jnp.concatenate(cut, axis=-1).reshape(rows, -1)


def core_order(own, other, axis):
    core = lax.axis_index("pipe")
    return jnp.where(
        core == 0,
        jnp.concatenate([own, other], axis=axis),
        jnp.concatenate([other, own], axis=axis),
    )


def unpack_attention(own, other, widths):
    query_w, kv_w, out_w = widths
    cuts = (query_w, query_w + kv_w, query_w + 2 * kv_w)

    def split(m):
        return (m[:, : cuts[0]], m[:, cuts[0] : cuts[1]], m[:, cuts[1] : cuts[2]], m[:, cuts[2] :])

    q0, k0, v0, o0 = split(own)
    q1, k1, v1, o1 = split(other)
    return (
        jnp.concatenate([q0, q1], axis=1),
        core_order(k0, k1, 1),
        core_order(v0, v1, 1),
        jnp.concatenate([o0, o1], axis=1),
    )


def core_halves(grad):
    half = grad.shape[1] // 2
    core = lax.axis_index("pipe")
    low, high = grad[:, :half], grad[:, half:]
    return (jnp.where(core == 0, low, high), jnp.where(core == 0, high, low))


def grad_half(flow, own, other):
    total = own + hop(other.astype(BF), "pipe", 1).astype(F32)
    count = lax.axis_size("grp")
    blocks = total.reshape((count, -1) + total.shape[1:])
    half = total.shape[1] // 2
    parts = []
    for b in (blocks[:, :, :half], blocks[:, :, half:]):
        sent = b[1:].astype(BF)
        parts.append((b[0], flow.add(sent if count > 2 else sent[0])))
    return parts


def grad_home(flow, parts):
    sums = []
    for own, box in parts:
        for came in flow.need(box):
            own = own + came.astype(F32)
        sums.append(own.astype(BF))
    total = jnp.concatenate(sums, axis=1)
    wd = lax.axis_size("wd")
    me = lax.axis_index("wd")
    blocks = total.reshape((wd, -1) + total.shape[1:])
    pieces = [lax.dynamic_index_in_dim(blocks, me, 0, keepdims=False)]
    for k in range(1, wd):
        pieces.append(hop(lax.dynamic_index_in_dim(blocks, me ^ k, 0, keepdims=False), "wd", k))
    return jnp.stack(pieces)


def layer_forward(x_rows, gains, flow, parts, widths, where, plan):
    cosine, sine, q_place, q_start, k_place = where
    rows_a = gather_rows(apply_norm(x_rows, gains[0]).astype(BF))
    w_q, w_k, w_v, w_ot = unpack_attention(*both_cores(flow, parts[0]), widths)
    tok = rows_a.shape[0]
    rows_a = flow.step(rows_a, plan[0])
    query = rotary_apply(mm(rows_a, w_q).reshape(tok, -1, HEAD_SIZE), cosine, sine).astype(BF)
    query = query.transpose(1, 0, 2)
    key = rotary_apply(mm(rows_a, w_k).reshape(tok, 1, HEAD_SIZE), cosine, sine).astype(BF)[:, 0]
    value = mm(rows_a, w_v).astype(BF)
    kv_all = jnp.concatenate(others(jnp.concatenate([key, value], axis=1), "grp"), axis=0)
    kv_all = flow.step(kv_all, plan[1])
    keys, values = kv_all[:, :HEAD_SIZE], kv_all[:, HEAD_SIZE:]
    context = attend(query, keys, values, q_place, q_start, k_place)
    context = context.transpose(1, 0, 2).reshape(tok, -1)
    mid = x_rows + sum_rows(mm_t(context, w_ot))
    mid = flow.step(mid, plan[2])
    rows_b = gather_rows(apply_norm(mid, gains[1]).astype(BF))
    rows_b = flow.step(rows_b, plan[3])
    w_g = jnp.concatenate(both_cores(flow, parts[1]), axis=1)
    w_u = jnp.concatenate(both_cores(flow, parts[2]), axis=1)
    gate = mm(rows_b, w_g)
    up = mm(rows_b, w_u)
    hidden = (jax.nn.silu(gate) * up).astype(BF)
    hidden = flow.step(hidden, plan[4])
    w_dt = jnp.concatenate(both_cores(flow, parts[3]), axis=1)
    out = mid + sum_rows(mm_t(hidden, w_dt))
    if plan[5]:
        out = flow.step(out, plan[5])
    weights = (w_q, w_k, w_v, w_ot, w_g, w_u, w_dt)
    return out, weights, (x_rows, rows_a, query, keys, values, context, mid, rows_b, gate, up, hidden)


def layer_backward(grad_out, gains, weights, where, kept, flow, plan):
    w_q, w_k, w_v, w_ot, w_g, w_u, w_dt = weights
    cosine, sine, q_place, q_start, k_place = where
    x_rows, rows_a, query, keys, values, context, mid, rows_b, gate, up, hidden = kept
    tok = rows_a.shape[0]
    grad_mlp = gather_rows(grad_out.astype(BF))
    if plan[0]:
        grad_mlp = flow.step(grad_mlp, plan[0])
    half = hidden.shape[1] // 2

    def mlp_grad(left, right):
        return grad_half(flow, mm_tl(left, right[:, :half]), mm_tl(left, right[:, half:]))

    down_parts = mlp_grad(grad_mlp, hidden)
    grad_hidden = mm(grad_mlp, w_dt)
    sig = jax.nn.sigmoid(gate)
    grad_gate = (grad_hidden * up * sig * (1.0 + gate * (1.0 - sig))).astype(BF)
    grad_up = (grad_hidden * gate * sig).astype(BF)
    grad_b = sum_rows(mm_t(grad_gate, w_g) + mm_t(grad_up, w_u))
    grad_b = flow.step(grad_b, plan[1])
    gate_parts = mlp_grad(rows_b, grad_gate)
    up_parts = mlp_grad(rows_b, grad_up)
    grad_mid, gain_b = norm_back(mid, gains[1], grad_b)
    grad_mid = grad_mid + grad_out
    grad_attn = gather_rows(grad_mid.astype(BF))
    grad_attn = flow.step(grad_attn, plan[2])
    grad_context = mm(grad_attn, w_ot).astype(BF)
    grad_context = grad_context.reshape(tok, -1, HEAD_SIZE).transpose(1, 0, 2)
    grad_q, grad_k, grad_v = attend_back(
        query, grad_context, keys, values, q_place, q_start, k_place
    )
    kv = jnp.concatenate([grad_k, grad_v], axis=1)
    kv = kv.reshape((-1, tok) + kv.shape[1:])
    own_kv = sum_others([kv[k] for k in range(kv.shape[0])], "grp").astype(BF)
    own_kv = flow.step(own_kv, plan[3])
    grad_k = own_kv[:, :HEAD_SIZE].astype(F32)
    grad_k = rotary_apply(grad_k[:, None, :], cosine, -sine).astype(BF)[:, 0]
    grad_v = own_kv[:, HEAD_SIZE:]
    grad_q = grad_q.transpose(1, 0, 2).astype(F32)
    grad_q = rotary_apply(grad_q, cosine, -sine).astype(BF).reshape(tok, -1)
    grad_a = sum_rows(mm_t(grad_q, w_q) + mm_t(grad_k, w_k) + mm_t(grad_v, w_v))
    grad_a = flow.step(grad_a, plan[4])
    grad_in, gain_a = norm_back(x_rows, gains[0], grad_a)
    grad_in = grad_mid + grad_in
    half_q = grad_q.shape[1] // 2
    kv_0, kv_1 = core_halves(grad_k)
    v_0, v_1 = core_halves(grad_v)

    def attn_term(q_half, k_half, v_half, o_half):
        right = jnp.concatenate([q_half, k_half, v_half], axis=1)
        return jnp.concatenate([mm_tl(rows_a, right), mm_tl(grad_attn, o_half)], axis=1)

    attn_parts = grad_half(
        flow,
        attn_term(grad_q[:, :half_q], kv_0, v_0, context[:, :half_q]),
        attn_term(grad_q[:, half_q:], kv_1, v_1, context[:, half_q:]),
    )
    return grad_in, jnp.stack([gain_a, gain_b]), (attn_parts, gate_parts, up_parts, down_parts)


def own_layer(first, second):
    core = lax.axis_index("pipe")
    keep = jnp.where(core == 0, first, second)
    return keep, hop(jnp.where(core == 0, second, first), "pipe", 1)


def body(
    block_input,
    cotangent,
    segments,
    norm_gains,
    w_query,
    key_matrix,
    value_matrix,
    w_output,
    w_gate,
    w_up,
    w_down,
):
    core = lax.axis_index("pipe")
    grp = lax.axis_index("grp")
    wd = lax.axis_size("wd")
    groups = lax.axis_size("grp")
    cores = lax.axis_size("pipe")
    tok = block_input.shape[1] * lax.axis_size(CUBE)

    gains = spread_gains(norm_gains[0])

    packed = pack_attention(w_query[0], key_matrix[0], value_matrix[0], w_output[0], cores)
    packed, gains[0] = tie(packed, gains[0])
    attn_cols = columns_out(packed, cores)
    gate_raw, _ = tie(w_gate[0], attn_cols)
    gate_cols = columns_out(gate_raw, cores)
    up_cols = columns_out(w_up[0], cores)
    down_cols = columns_out(w_down[0].T, cores)
    widths = tuple(n // (wd * cores) for n in (w_query.shape[2], key_matrix.shape[2], w_output.shape[1]))
    flow = Flow()
    parts = [[None] * 4, [None] * 4]
    for layer, kind in ((0, 0), (0, 1), (1, 0), (0, 2), (0, 3), (1, 1), (1, 2), (1, 3)):
        cols = (attn_cols, gate_cols, up_cols, down_cols)[kind][layer]
        if kind:
            parts[layer][kind] = in_halves(flow, cols)
        else:
            parts[layer][kind] = [(cols, flow.add(cols))]

    seg_row = lax.dynamic_index_in_dim(segments, core, 0, keepdims=False)
    starts = doc_starts(seg_row)
    local = jnp.arange(tok, dtype=jnp.int32)
    q_place = grp * tok + local
    q_start = lax.dynamic_slice_in_dim(starts, grp * tok, tok)
    cosine, sine = rope_tables(q_place - q_start)
    k_place = jnp.concatenate([(grp ^ k) * tok + local for k in range(groups)])
    where = (cosine, sine, q_place[:, None], q_start[:, None], k_place[None, :])

    rows = relative(lax.dynamic_index_in_dim(block_input, core, 0, keepdims=False), 1, "grp")
    outs = []
    kept = []
    weights = []
    due = ((1, 1, 2, 2, 1, 1), (1, 1, 1, 1, 1, 0))
    for layer in range(2):
        out, full, state = layer_forward(
            rows.astype(F32), gains[layer], flow, parts[layer], widths, where, due[layer]
        )
        rows = out.astype(BF)
        outs.append(rows)
        kept.append(state)
        weights.append(full)

    grad = relative(lax.dynamic_index_in_dim(cotangent, core, 0, keepdims=False), 1, "grp")
    grads_in = [None, None]
    gain_grads = [None, None]
    flow = Flow()
    kind_parts = [None, None]
    due = ((1, 2, 2, 1, 1), (0, 2, 2, 1, 1))
    for layer in (1, 0):
        grad_in, gain_grads[layer], kind_parts[layer] = layer_backward(
            grad.astype(F32), gains[layer], weights[layer], where, kept[layer], flow, due[layer]
        )
        grad = grad_in.astype(BF)
        grads_in[layer] = grad
    homes = [tuple(grad_home(flow, p) for p in kind_parts[layer]) for layer in range(2)]

    def by_batch(pair):
        own, other = own_layer(pair[0], pair[1])
        both = jnp.where(core == 0, jnp.stack([own, other]), jnp.stack([other, own]))
        return relative(both, 2, "grp")[None]

    layer_out = by_batch(outs)
    input_grad = by_batch(grads_in)

    grad_norm_gains = sum_gains(gain_grads)[None]

    def joined(index):
        own, other = own_layer(homes[0][index], homes[1][index])
        both = jnp.where(core == 0, jnp.stack([own, other]), jnp.stack([other, own]))
        return relative(both, 1, "wd").transpose(2, 1, 0, 3).astype(F32)

    attn = joined(0)
    cuts = (widths[0], widths[0] + widths[1], widths[0] + 2 * widths[1])
    rows_d = attn.shape[0]
    grad_wq = attn[..., : cuts[0]].reshape(rows_d, -1)[None]
    grad_wk = attn[..., cuts[0] : cuts[1]].reshape(rows_d, -1)[None]
    grad_wv = attn[..., cuts[1] : cuts[2]].reshape(rows_d, -1)[None]
    grad_wo = attn[..., cuts[2] :].reshape(rows_d, -1).T[None]
    grad_wg = joined(1).reshape(rows_d, -1)[None]
    grad_wu = joined(2).reshape(rows_d, -1)[None]
    grad_wd = joined(3).reshape(rows_d, -1).T[None]
    return (
        layer_out,
        input_grad,
        grad_norm_gains,
        grad_wq,
        grad_wk,
        grad_wv,
        grad_wo,
        grad_wg,
        grad_wu,
        grad_wd,
    )


def solution(mesh):
    sizes = dict(mesh.shape)
    wd = KV_HEADS // sizes["tensor"]
    fine = Mesh(
        mesh.devices.reshape(sizes["pipe"], sizes["dp"] // wd, wd, sizes["tensor"]),
        ("pipe", "grp", "wd", "tensor"),
    )
    dp = ("grp", "wd")
    tokens = P(None, dp + ("tensor",), None)
    outs = P("pipe", None, dp + ("tensor",), None)
    gains = P("pipe", None, dp + ("tensor",))
    tall = P("pipe", dp, "tensor")
    wide = P("pipe", "tensor", dp)
    weights = (tall, tall, tall, wide, tall, tall, wide)
    return jax.shard_map(
        body,
        mesh=fine,
        in_specs=(tokens, tokens, P(), gains) + weights,
        out_specs=(outs, outs, gains) + weights,
        check_vma=False,
    )
```

```python
import jax
import jax.numpy as jnp
from jax import lax
from jax.experimental import pallas as pl
from jax.experimental.pallas import tpu as pltpu
from jax.sharding import Mesh, PartitionSpec as P

HEAD_SIZE = 64
KV_HEADS = 8
EPS = 1e-05
ROPE_BASE = 500000.0
NEG_FILL = -1e30
BF = jnp.bfloat16
F32 = jnp.float32
CUBE = ("wd", "tensor")


def rms_scale(row_values):
    return lax.rsqrt(jnp.mean(row_values * row_values, axis=-1, keepdims=True) + EPS)


def apply_norm(row_values, gain_vector):
    return row_values * rms_scale(row_values) * gain_vector


def norm_back(row_values, gain_vector, grad_normed):
    _, pullback = jax.vjp(apply_norm, row_values, gain_vector)
    return pullback(grad_normed)


def doc_starts(seg_row):
    places = jnp.arange(seg_row.shape[0], dtype=jnp.int32)
    before = jnp.concatenate([seg_row[:1] - 1, seg_row[:-1]])
    return lax.cummax(jnp.where(seg_row != before, places, 0), axis=0)


def rope_tables(positions):
    half_dim = HEAD_SIZE // 2
    freqs = ROPE_BASE ** (-(jnp.arange(half_dim, dtype=F32) * 2.0 / HEAD_SIZE))
    angles = positions.astype(F32)[:, None] * freqs[None, :]
    return (jnp.cos(angles), jnp.sin(angles))


def rotary_apply(head_values, cosine_table, sine_values):
    half_dim = head_values.shape[-1] // 2
    first_half = head_values[..., :half_dim]
    second_half = head_values[..., half_dim:]
    cos_rows = cosine_table[:, None, :]
    sin_rows = sine_values[:, None, :]
    return jnp.concatenate(
        [
            first_half * cos_rows - second_half * sin_rows,
            second_half * cos_rows + first_half * sin_rows,
        ],
        axis=-1,
    )


def mm(left, right):
    return jnp.dot(left, right, preferred_element_type=F32)


def mm_t(left, right):
    return lax.dot_general(left, right, (((1,), (1,)), ((), ())), preferred_element_type=F32)


def mm_tl(left, right):
    return lax.dot_general(left, right, (((0,), (0,)), ((), ())), preferred_element_type=F32)


def trade(blocks, axes):
    return lax.all_to_all(blocks, axes, 0, 0, tiled=True)


def hop(block, axis, step):
    size = lax.axis_size(axis)
    return lax.ppermute(block, axis, [(i, i ^ step) for i in range(size)])


def tie(*values):
    return lax.optimization_barrier(values)


def link_steps():
    steps = []
    step = 1
    while step < lax.axis_size(CUBE):
        steps.append(step)
        step *= 2
    return steps


def gather_rows(rows):
    count = lax.axis_size(CUBE)
    spread = jnp.broadcast_to(rows[None], (count,) + rows.shape)
    return trade(spread, CUBE).reshape((count * rows.shape[0],) + rows.shape[1:])


def sum_rows(partial):
    count = lax.axis_size(CUBE)
    blocks = partial.astype(BF).reshape((count, -1) + partial.shape[1:])
    return jnp.sum(trade(blocks, CUBE).astype(F32), axis=0)


class Stages:
    def __init__(self):
        self.held = {}

    def run(self, value, step, jobs):
        needed = [[self.held[name] for name in names] for _, _, names in jobs]
        value, needed = lax.optimization_barrier((value, needed))
        out = step(value)
        made = [job(*inputs) for (_, job, _), inputs in zip(jobs, needed)]
        out, made = lax.optimization_barrier((out, made))
        self.held.update((key, result) for (key, _, _), result in zip(jobs, made))
        return out


def others(block, axis):
    return [block] + [hop(block, axis, k) for k in range(1, lax.axis_size(axis))]


def sum_others(blocks, axis):
    total = blocks[0].astype(F32)
    for k in range(1, lax.axis_size(axis)):
        total = total + hop(blocks[k].astype(BF), axis, k).astype(F32)
    return total


def relative(values, dim, axis):
    count = lax.axis_size(axis)
    me = lax.axis_index(axis)
    step = 1
    while step < count:
        shape = values.shape
        cut = shape[:dim] + (count // (2 * step), 2, step * (shape[dim] // count)) + shape[dim + 1 :]
        view = values.reshape(cut)
        swapped = jnp.concatenate(
            [lax.slice_in_dim(view, 1, 2, axis=dim + 1), lax.slice_in_dim(view, 0, 1, axis=dim + 1)],
            axis=dim + 1,
        )
        values = jnp.where((me & step) != 0, swapped.reshape(shape), values)
        step *= 2
    return values


def spread_gains(norm_gains):
    me = lax.axis_index(CUBE)
    gain = norm_gains
    for step in link_steps():
        came = hop(gain, CUBE, step)
        gain = jnp.where(
            (me & step) != 0,
            jnp.concatenate([came, gain], axis=1),
            jnp.concatenate([gain, came], axis=1),
        )
    gain = jnp.concatenate(others(gain, "grp"), axis=1)
    other = hop(gain, "pipe", 1)
    core = lax.axis_index("pipe")
    return [jnp.where(core == 0, gain, other), jnp.where(core == 0, other, gain)]


def sum_gains(grads):
    me = lax.axis_index(CUBE)
    keep, extra = own_layer(grads[0], grads[1])
    total = (keep + extra).reshape(2, lax.axis_size("grp"), -1)
    mine = total[:, 0]
    for k in range(1, total.shape[1]):
        mine = mine + hop(total[:, k], "grp", k)
    for step in link_steps()[::-1]:
        half = mine.shape[1] // 2
        low, high = mine[:, :half], mine[:, half:]
        odd = (me & step) != 0
        mine = jnp.where(odd, high, low) + hop(jnp.where(odd, low, high), CUBE, step)
    return mine


def masked_probs(q, k, q_place, q_start, k_place):
    scores = lax.dot_general(q, k, (((1,), (1,)), ((), ())), preferred_element_type=F32)
    scores = scores * HEAD_SIZE ** (-0.5)
    allowed = (k_place <= q_place) & (k_place >= q_start)
    masked = jnp.where(allowed, scores, NEG_FILL)
    exps = jnp.exp(masked - jnp.max(masked, axis=-1, keepdims=True))
    return exps / jnp.sum(exps, axis=-1, keepdims=True)


def attend_kernel(q_ref, k_ref, v_ref, qp_ref, qs_ref, kp_ref, o_ref):
    probs = masked_probs(q_ref[0], k_ref[...], qp_ref[...], qs_ref[...], kp_ref[...])
    o_ref[0] = jnp.dot(probs.astype(BF), v_ref[...], preferred_element_type=F32).astype(BF)


def attend_back_kernel(q_ref, do_ref, k_ref, v_ref, qp_ref, qs_ref, kp_ref, dq_ref, dk_ref, dv_ref):
    @pl.when((pl.program_id(0) == 0) & (pl.program_id(1) == 0))
    def _():
        dk_ref[...] = jnp.zeros_like(dk_ref)
        dv_ref[...] = jnp.zeros_like(dv_ref)

    q = q_ref[0]
    do = do_ref[0]
    k = k_ref[...]
    probs = masked_probs(q, k, qp_ref[...], qs_ref[...], kp_ref[...])
    grad_probs = lax.dot_general(do, v_ref[...], (((1,), (1,)), ((), ())), preferred_element_type=F32)
    delta = jnp.sum(probs * grad_probs, axis=-1, keepdims=True)
    grad_scores = (probs * (grad_probs - delta) * HEAD_SIZE ** (-0.5)).astype(BF)
    dq_ref[0] = jnp.dot(grad_scores, k, preferred_element_type=F32).astype(BF)
    dk_ref[...] += lax.dot_general(
        grad_scores, q, (((0,), (0,)), ((), ())), preferred_element_type=F32
    )
    dv_ref[...] += lax.dot_general(
        probs.astype(BF), do, (((0,), (0,)), ((), ())), preferred_element_type=F32
    )


def attention_specs(heads, rows, keys):
    rows_blk = max(16, min(rows, (512 * 1024) // keys))
    per_head = pl.BlockSpec((1, rows_blk, HEAD_SIZE), lambda b, h: (h, b, 0))
    full = pl.BlockSpec((keys, HEAD_SIZE), lambda b, h: (0, 0))
    row_info = pl.BlockSpec((rows_blk, 1), lambda b, h: (b, 0))
    key_info = pl.BlockSpec((1, keys), lambda b, h: (0, 0))
    return ((rows // rows_blk, heads), per_head, full, row_info, key_info)


PARAMS = dict(
    compiler_params=pltpu.CompilerParams(vmem_limit_bytes=50 * 1024 * 1024),
)


def attend(q, k, v, q_place, q_start, k_place):
    heads, rows, _ = q.shape
    keys = k.shape[0]
    grid, per_head, full, row_info, key_info = attention_specs(heads, rows, keys)
    return pl.pallas_call(
        attend_kernel,
        grid=grid,
        in_specs=[per_head, full, full, row_info, row_info, key_info],
        out_specs=per_head,
        out_shape=jax.ShapeDtypeStruct(q.shape, BF),
        cost_estimate=pl.CostEstimate(
            flops=4 * heads * rows * keys * HEAD_SIZE,
            bytes_accessed=4 * q.size + 4 * k.size,
            transcendentals=heads * rows * keys,
        ),
        **PARAMS,
    )(q, k, v, q_place, q_start, k_place)


def attend_back(q, do, k, v, q_place, q_start, k_place):
    heads, rows, _ = q.shape
    keys = k.shape[0]
    grid, per_head, full, row_info, key_info = attention_specs(heads, rows, keys)
    return pl.pallas_call(
        attend_back_kernel,
        grid=grid,
        in_specs=[per_head, per_head, full, full, row_info, row_info, key_info],
        out_specs=[per_head, full, full],
        out_shape=[
            jax.ShapeDtypeStruct(q.shape, BF),
            jax.ShapeDtypeStruct(k.shape, F32),
            jax.ShapeDtypeStruct(k.shape, F32),
        ],
        cost_estimate=pl.CostEstimate(
            flops=10 * heads * rows * keys * HEAD_SIZE,
            bytes_accessed=6 * q.size + 12 * k.size,
            transcendentals=heads * rows * keys,
        ),
        **PARAMS,
    )(q, do, k, v, q_place, q_start, k_place)


def to_blocks(weight, cores):
    wd = lax.axis_size("wd")
    rows = weight.shape[0]
    cut = weight.reshape(rows, wd, cores, -1).transpose(2, 1, 0, 3)
    return cut.reshape((cores * wd, rows) + cut.shape[3:])


def columns_out(blocks):
    moved = trade(blocks, ("pipe", "wd"))
    return moved.reshape((2, -1) + moved.shape[2:])


def exchange(piece):
    return [hop(piece, "grp", k) for k in range(1, lax.axis_size("grp"))]


def piece_of(layer, part=None):
    def take(cols):
        rows = cols.shape[1] // 2
        if part is None:
            return exchange(cols[layer])
        return exchange(cols[layer, part * rows : (part + 1) * rows])

    return take


def whole(layer):
    def join(cols, *came):
        pieces = [cols[layer]]
        for k in range(len(came[0])):
            pieces += [c[k] for c in came]
        there = [hop(p, "pipe", 1) for p in pieces]
        return jnp.concatenate(pieces, axis=0), jnp.concatenate(there, axis=0)

    return join


def pack_attention(w_query, key_matrix, value_matrix, w_output, cores):
    wd = lax.axis_size("wd")
    rows = w_query.shape[0]
    cut = [
        m.reshape(rows, wd, cores, -1) for m in (w_query, key_matrix, value_matrix, w_output.T)
    ]
    return jnp.concatenate(cut, axis=-1).reshape(rows, -1)


def core_order(own, other, axis):
    core = lax.axis_index("pipe")
    return jnp.where(
        core == 0,
        jnp.concatenate([own, other], axis=axis),
        jnp.concatenate([other, own], axis=axis),
    )


def unpack_attention(own, other, widths):
    query_w, kv_w, out_w = widths
    cuts = (query_w, query_w + kv_w, query_w + 2 * kv_w)

    def split(m):
        return (m[:, : cuts[0]], m[:, cuts[0] : cuts[1]], m[:, cuts[1] : cuts[2]], m[:, cuts[2] :])

    q0, k0, v0, o0 = split(own)
    q1, k1, v1, o1 = split(other)
    return (
        jnp.concatenate([q0, q1], axis=1),
        core_order(k0, k1, 1),
        core_order(v0, v1, 1),
        jnp.concatenate([o0, o1], axis=1),
    )


def core_halves(grad):
    half = grad.shape[1] // 2
    core = lax.axis_index("pipe")
    low, high = grad[:, :half], grad[:, half:]
    return (jnp.where(core == 0, low, high), jnp.where(core == 0, high, low))


def grad_pair(own, other):
    total = own + hop(other.astype(BF), "pipe", 1).astype(F32)
    return total.reshape((lax.axis_size("grp"), -1) + total.shape[1:])


def mlp_pair(left, right):
    half = right.shape[1] // 2
    return grad_pair(mm_tl(left, right[:, :half]), mm_tl(left, right[:, half:]))


def grad_part(part):
    def add(blocks):
        rows = blocks.shape[1] // 2
        cut = blocks[:, part * rows : (part + 1) * rows]
        total = cut[0]
        for k in range(1, blocks.shape[0]):
            total = total + hop(cut[k].astype(BF), "grp", k).astype(F32)
        return total.astype(BF)

    return add


def grad_home(low, high):
    wd = lax.axis_size("wd")
    me = lax.axis_index("wd")
    blocks = jnp.concatenate([low, high], axis=0).reshape((wd, -1) + low.shape[1:])
    pieces = [lax.dynamic_index_in_dim(blocks, me, 0, keepdims=False)]
    for k in range(1, wd):
        pieces.append(hop(lax.dynamic_index_in_dim(blocks, me ^ k, 0, keepdims=False), "wd", k))
    return jnp.stack(pieces)


def place_kernel(turned, at_ref, keep_ref, got_ref, out_ref):
    mine = pl.program_id(1) == at_ref[1]

    def put(ref):
        block = ref[0].astype(F32)
        out_ref[...] = block.T if turned else block

    @pl.when(mine)
    def _():
        put(keep_ref)

    @pl.when(jnp.logical_not(mine))
    def _():
        put(got_ref)


def place(keep, got, turned):
    wd, rows, cols = keep.shape
    at = jnp.stack([lax.axis_index("wd"), lax.axis_index("pipe")]).astype(jnp.int32)
    cores = lax.axis_size("pipe")
    source = pl.BlockSpec((1, rows, cols), lambda w, c, at_ref: (w ^ at_ref[0], 0, 0))
    if turned:
        shape, target = (wd * cores * cols, rows), (cols, rows)
        out = pl.BlockSpec(target, lambda w, c, at_ref: (w * cores + c, 0))
    else:
        shape, target = (rows, wd * cores * cols), (rows, cols)
        out = pl.BlockSpec(target, lambda w, c, at_ref: (0, w * cores + c))
    return pl.pallas_call(
        lambda *refs: place_kernel(turned, *refs),
        grid_spec=pltpu.PrefetchScalarGridSpec(
            num_scalar_prefetch=1, grid=(wd, cores), in_specs=[source, source], out_specs=out
        ),
        out_shape=jax.ShapeDtypeStruct(shape, F32),
        cost_estimate=pl.CostEstimate(
            flops=keep.size, bytes_accessed=12 * keep.size, transcendentals=0
        ),
    )(at, keep, got)


def layer_forward(stages, layer, x_rows, gains, where, jobs):
    held = stages.held
    cosine, sine, q_place, q_start, k_place = where
    normed = apply_norm(x_rows, gains[0]).astype(BF)
    rows_a = stages.run(normed, gather_rows, jobs[0])
    w_q, w_k, w_v, w_ot = held["attn", layer]
    tok = rows_a.shape[0]

    def project(rows):
        query = rotary_apply(mm(rows, w_q).reshape(tok, -1, HEAD_SIZE), cosine, sine).astype(BF)
        key = rotary_apply(mm(rows, w_k).reshape(tok, 1, HEAD_SIZE), cosine, sine).astype(BF)[:, 0]
        value = mm(rows, w_v).astype(BF)
        kv = jnp.concatenate([key, value], axis=1)
        return query.transpose(1, 0, 2), jnp.concatenate(others(kv, "grp"), axis=0)

    query, kv_all = stages.run(rows_a, project, jobs[1])
    keys, values = kv_all[:, :HEAD_SIZE], kv_all[:, HEAD_SIZE:]

    def attention(q):
        context = attend(q, keys, values, q_place, q_start, k_place)
        context = context.transpose(1, 0, 2).reshape(tok, -1)
        return context, x_rows + sum_rows(mm_t(context, w_ot))

    context, mid = stages.run(query, attention, jobs[2])
    rows_b = stages.run(
        mid, lambda m: gather_rows(apply_norm(m, gains[1]).astype(BF)), jobs[3]
    )
    w_gu = held["gu", layer]

    def ahead(rows):
        both = mm(rows, w_gu)
        half = both.shape[1] // 2
        gate, up = both[:, :half], both[:, half:]
        return gate, up, (jax.nn.silu(gate) * up).astype(BF)

    gate, up, hidden = stages.run(rows_b, ahead, jobs[4])
    return x_rows, rows_a, query, keys, values, context, mid, rows_b, gate, up, hidden


def layer_backward(stages, layer, grad_out, grad_mlp, gains, where, kept, also, jobs):
    held = stages.held
    cosine, sine, q_place, q_start, k_place = where
    x_rows, rows_a, query, keys, values, context, mid, rows_b, gate, up, hidden = kept
    w_q, w_k, w_v, w_ot = held["attn", layer]
    w_gu, w_dt = held["gu", layer], held["down", layer]
    tok = rows_a.shape[0]
    held["rows_b"], held["hidden"] = rows_b, hidden
    held["grad_mlp"] = grad_mlp

    def feed_back(rows):
        grad_hidden = mm(rows, w_dt)
        sig = jax.nn.sigmoid(gate)
        grad_gate = (grad_hidden * up * sig * (1.0 + gate * (1.0 - sig))).astype(BF)
        grad_up = (grad_hidden * gate * sig).astype(BF)
        both = jnp.concatenate([grad_gate, grad_up], axis=1)
        return grad_gate, grad_up, mm_t(both, w_gu).astype(BF), also(hidden)

    grad_gate, grad_up, partial, extra = stages.run(grad_mlp, feed_back, jobs[0])
    held["grad_gate"], held["grad_up"] = grad_gate, grad_up
    grad_b = stages.run(partial, sum_rows, jobs[1])
    grad_mid, gain_b = norm_back(mid, gains[1], grad_b)
    grad_mid = grad_mid + grad_out
    grad_attn = stages.run(grad_mid.astype(BF), gather_rows, jobs[2])

    def attention_back(rows):
        grad_context = mm(rows, w_ot).astype(BF)
        grad_context = grad_context.reshape(tok, -1, HEAD_SIZE).transpose(1, 0, 2)
        grad_q, grad_k, grad_v = attend_back(
            query, grad_context, keys, values, q_place, q_start, k_place
        )
        kv = jnp.concatenate([grad_k, grad_v], axis=1)
        kv = kv.reshape((-1, tok) + kv.shape[1:])
        own_kv = sum_others([kv[k] for k in range(kv.shape[0])], "grp").astype(BF)
        grad_k = own_kv[:, :HEAD_SIZE].astype(F32)
        grad_k = rotary_apply(grad_k[:, None, :], cosine, -sine).astype(BF)[:, 0]
        grad_v = own_kv[:, HEAD_SIZE:]
        grad_q = grad_q.transpose(1, 0, 2).astype(F32)
        grad_q = rotary_apply(grad_q, cosine, -sine).astype(BF).reshape(tok, -1)
        partial = mm_t(grad_q, w_q) + mm_t(grad_k, w_k) + mm_t(grad_v, w_v)
        return grad_q, grad_k, grad_v, partial.astype(BF)

    grad_q, grad_k, grad_v, partial = stages.run(grad_attn, attention_back, jobs[3])

    def attn_pair(g_q, g_k, g_v):
        half_q = g_q.shape[1] // 2
        kv_0, kv_1 = core_halves(g_k)
        v_0, v_1 = core_halves(g_v)

        def term(q_half, k_half, v_half, o_half):
            right = jnp.concatenate([q_half, k_half, v_half], axis=1)
            return jnp.concatenate([mm_tl(rows_a, right), mm_tl(grad_attn, o_half)], axis=1)

        return grad_pair(
            term(g_q[:, :half_q], kv_0, v_0, context[:, :half_q]),
            term(g_q[:, half_q:], kv_1, v_1, context[:, half_q:]),
        )

    held["g_q"], held["g_k"], held["g_v"] = grad_q, grad_k, grad_v
    held["attn_pair"] = attn_pair
    grad_a = stages.run(partial, sum_rows, jobs[4](attn_pair))
    grad_in, gain_a = norm_back(x_rows, gains[0], grad_a)
    return grad_mid + grad_in, jnp.stack([gain_a, gain_b]), extra


def own_layer(first, second):
    core = lax.axis_index("pipe")
    keep = jnp.where(core == 0, first, second)
    return keep, hop(jnp.where(core == 0, second, first), "pipe", 1)


def body(
    block_input,
    cotangent,
    segments,
    norm_gains,
    w_query,
    key_matrix,
    value_matrix,
    w_output,
    w_gate,
    w_up,
    w_down,
):
    core = lax.axis_index("pipe")
    grp = lax.axis_index("grp")
    wd = lax.axis_size("wd")
    groups = lax.axis_size("grp")
    cores = lax.axis_size("pipe")
    tok = block_input.shape[1] * lax.axis_size(CUBE)

    gains = spread_gains(norm_gains[0])

    stages = Stages()
    held = stages.held
    packed = pack_attention(w_query[0], key_matrix[0], value_matrix[0], w_output[0], cores)
    packed, gains = lax.optimization_barrier((packed, gains))
    attn_cols = columns_out(to_blocks(packed, cores))
    held["gate_out"] = to_blocks(w_gate[0], cores)
    held["up_out"] = to_blocks(w_up[0], cores)
    held["down_out"] = to_blocks(w_down[0].T, cores)
    widths = tuple(n // (wd * cores) for n in (w_query.shape[2], key_matrix.shape[2], w_output.shape[1]))

    def move(name):
        return (name, columns_out, (name + "_out",))

    def swap(name, layer, part=None):
        return ((name, layer, part), piece_of(layer, part), (name,))

    def parts(name, layer):
        if name == "attn_cols":
            return (name, (name, layer, None))
        return (name, (name, layer, 0), (name, layer, 1))

    def attn_ready(layer):
        def ready(*values):
            return unpack_attention(*whole(layer)(*values), widths)

        return (("attn", layer), ready, parts("attn_cols", layer))

    def gate_up_ready(layer):
        def ready(*values):
            half = len(values) // 2
            pairs = whole(layer)(*values[:half]), whole(layer)(*values[half:])
            return jnp.concatenate(pairs[0] + pairs[1], axis=1)

        return (("gu", layer), ready, parts("gate", layer) + parts("up", layer))

    def down_ready(layer):
        def ready(*values):
            return jnp.concatenate(whole(layer)(*values), axis=1)

        return (("down", layer), ready, parts("down", layer))

    seg_row = lax.dynamic_index_in_dim(segments, core, 0, keepdims=False)
    starts = doc_starts(seg_row)
    local = jnp.arange(tok, dtype=jnp.int32)
    q_place = grp * tok + local
    q_start = lax.dynamic_slice_in_dim(starts, grp * tok, tok)
    cosine, sine = rope_tables(q_place - q_start)
    k_place = jnp.concatenate([(grp ^ k) * tok + local for k in range(groups)])
    where = (cosine, sine, q_place[:, None], q_start[:, None], k_place[None, :])

    rows = relative(lax.dynamic_index_in_dim(block_input, core, 0, keepdims=False), 1, "grp")
    grad = relative(lax.dynamic_index_in_dim(cotangent, core, 0, keepdims=False), 1, "grp")
    held["attn_cols"] = attn_cols
    rows = stages.run(rows, lambda r: r, [move("gate"), swap("attn_cols", 0)])
    kept = [None, None]
    outs = [None, None]
    kept[0] = layer_forward(
        stages,
        0,
        rows.astype(F32),
        gains[0],
        where,
        (
            [attn_ready(0), swap("gate", 0, 0)],
            [move("up"), swap("gate", 0, 1)],
            [move("down"), swap("up", 0, 0), swap("up", 0, 1)],
            [gate_up_ready(0), swap("down", 0, 0)],
            [swap("down", 0, 1)],
        ),
    )

    def close(hidden, layer):
        return (kept[layer][6] + sum_rows(mm_t(hidden, held["down", layer]))).astype(BF)

    hidden = stages.run(kept[0][-1], lambda h: h, [down_ready(0)])
    outs[0] = stages.run(hidden, lambda h: close(h, 0), [swap("attn_cols", 1)])
    held["cotangent"] = grad
    kept[1] = layer_forward(
        stages,
        1,
        outs[0].astype(F32),
        gains[1],
        where,
        (
            [attn_ready(1), swap("gate", 1, 0)],
            [swap("gate", 1, 1)],
            [swap("up", 1, 0), swap("up", 1, 1)],
            [gate_up_ready(1), swap("down", 1, 0)],
            [swap("down", 1, 1), ("last", lambda g: gather_rows(g), ("cotangent",))],
        ),
    )
    hidden = stages.run(kept[1][-1], lambda h: h, [down_ready(1)])

    def grad_of(name, layer):
        sources = {
            "down": ("grad_mlp", "hidden"),
            "gate": ("rows_b", "grad_gate"),
            "up": ("rows_b", "grad_up"),
        }[name]
        return (("pair", name, layer), mlp_pair, sources)

    def grad_swap(name, layer, part):
        return (("part", name, layer, part), grad_part(part), (("pair", name, layer),))

    def home(name, layer):
        keys = tuple(("part", name, layer, part) for part in range(2))
        return (("home", name, layer), grad_home, keys)

    def attn_grad(layer):
        return lambda pair: (("pair", "attn", layer), pair, ("g_q", "g_k", "g_v"))

    grads_in = [None, None]
    gain_grads = [None, None]
    grad_in, gain_grads[1], outs[1] = layer_backward(
        stages,
        1,
        grad.astype(F32),
        held["last"],
        gains[1],
        where,
        kept[1][:-1] + (hidden,),
        lambda h: close(h, 1),
        (
            [grad_of("down", 1)],
            [grad_swap("down", 1, 0), grad_of("gate", 1)],
            [grad_swap("down", 1, 1), grad_of("up", 1)],
            [grad_swap("gate", 1, 0), grad_swap("gate", 1, 1)],
            lambda pair: [grad_swap("up", 1, 0), home("down", 1)],
        ),
    )
    grads_in[1] = grad_in.astype(BF)
    grad_mlp = stages.run(
        grads_in[1],
        gather_rows,
        [grad_swap("up", 1, 1), attn_grad(1)(held["attn_pair"]), home("gate", 1)],
    )
    grad_in, gain_grads[0], _ = layer_backward(
        stages,
        0,
        grads_in[1].astype(F32),
        grad_mlp,
        gains[0],
        where,
        kept[0],
        lambda h: (),
        (
            [grad_of("down", 0), grad_swap("attn", 1, 0), grad_swap("attn", 1, 1)],
            [grad_swap("down", 0, 0), grad_of("gate", 0), home("up", 1)],
            [grad_swap("down", 0, 1), grad_of("up", 0), home("attn", 1)],
            [grad_swap("gate", 0, 0), grad_swap("gate", 0, 1)],
            lambda pair: [grad_swap("up", 0, 0), home("down", 0), attn_grad(0)(pair)],
        ),
    )
    grads_in[0] = grad_in.astype(BF)
    for key, job, names in (
        grad_swap("attn", 0, 0),
        grad_swap("attn", 0, 1),
        grad_swap("up", 0, 1),
        home("gate", 0),
        home("attn", 0),
        home("up", 0),
    ):
        held[key] = job(*[held[name] for name in names])

    def by_batch(pair):
        own, other = own_layer(pair[0], pair[1])
        both = jnp.where(core == 0, jnp.stack([own, other]), jnp.stack([other, own]))
        return relative(both, 2, "grp")[None]

    layer_out = by_batch(outs)
    input_grad = by_batch(grads_in)

    grad_norm_gains = sum_gains(gain_grads)[None]

    def both(name):
        return own_layer(held["home", name, 0], held["home", name, 1])

    keep, got = both("attn")
    cuts = (0, widths[0], widths[0] + widths[1], widths[0] + 2 * widths[1], keep.shape[2])
    q_pair, k_pair, v_pair, o_pair = (
        (keep[..., lo:hi], got[..., lo:hi]) for lo, hi in zip(cuts[:-1], cuts[1:])
    )

    def small(pair):
        order = jnp.where(core == 0, jnp.stack(pair), jnp.stack(pair[::-1]))
        order = relative(order, 1, "wd").transpose(2, 1, 0, 3).astype(F32)
        return order.reshape(order.shape[0], -1)[None]

    grad_wq = place(*q_pair, False)[None]
    grad_wk = small(k_pair)
    grad_wv = small(v_pair)
    grad_wo = place(*o_pair, True)[None]
    grad_wg = place(*both("gate"), False)[None]
    grad_wu = place(*both("up"), False)[None]
    grad_wd = place(*both("down"), True)[None]
    return (
        layer_out,
        input_grad,
        grad_norm_gains,
        grad_wq,
        grad_wk,
        grad_wv,
        grad_wo,
        grad_wg,
        grad_wu,
        grad_wd,
    )


def solution(mesh):
    sizes = dict(mesh.shape)
    wd = KV_HEADS // sizes["tensor"]
    fine = Mesh(
        mesh.devices.reshape(sizes["pipe"], sizes["dp"] // wd, wd, sizes["tensor"]),
        ("pipe", "grp", "wd", "tensor"),
    )
    dp = ("grp", "wd")
    tokens = P(None, dp + ("tensor",), None)
    outs = P("pipe", None, dp + ("tensor",), None)
    gains = P("pipe", None, dp + ("tensor",))
    tall = P("pipe", dp, "tensor")
    wide = P("pipe", "tensor", dp)
    weights = (tall, tall, tall, wide, tall, tall, wide)
    return jax.shard_map(
        body,
        mesh=fine,
        in_specs=(tokens, tokens, P(), gains) + weights,
        out_specs=(outs, outs, gains) + weights,
        check_vma=False,
    )
```

```python
import jax
import jax.numpy as jnp
from jax import lax
from jax.experimental import pallas as pl
from jax.experimental.pallas import tpu as pltpu
from jax.sharding import Mesh, PartitionSpec as P

HEAD_SIZE = 64
KV_HEADS = 8
EPS = 1e-05
ROPE_BASE = 500000.0
NEG_FILL = -1e30
BF = jnp.bfloat16
F32 = jnp.float32
CUBE = ("wd", "tensor")


def rms_scale(row_values):
    return lax.rsqrt(jnp.mean(row_values * row_values, axis=-1, keepdims=True) + EPS)


def apply_norm(row_values, gain_vector):
    return row_values * rms_scale(row_values) * gain_vector


def norm_back(row_values, gain_vector, grad_normed):
    _, pullback = jax.vjp(apply_norm, row_values, gain_vector)
    return pullback(grad_normed)


def doc_starts(seg_row):
    places = jnp.arange(seg_row.shape[0], dtype=jnp.int32)
    before = jnp.concatenate([seg_row[:1] - 1, seg_row[:-1]])
    return lax.cummax(jnp.where(seg_row != before, places, 0), axis=0)


def rope_tables(positions):
    half_dim = HEAD_SIZE // 2
    freqs = ROPE_BASE ** (-(jnp.arange(half_dim, dtype=F32) * 2.0 / HEAD_SIZE))
    angles = positions.astype(F32)[:, None] * freqs[None, :]
    return (jnp.cos(angles), jnp.sin(angles))


def rotary_apply(head_values, cosine_table, sine_values):
    half_dim = head_values.shape[-1] // 2
    first_half = head_values[..., :half_dim]
    second_half = head_values[..., half_dim:]
    cos_rows = cosine_table[:, None, :]
    sin_rows = sine_values[:, None, :]
    return jnp.concatenate(
        [
            first_half * cos_rows - second_half * sin_rows,
            second_half * cos_rows + first_half * sin_rows,
        ],
        axis=-1,
    )


def mm(left, right):
    return jnp.dot(left, right, preferred_element_type=F32)


def mm_t(left, right):
    return lax.dot_general(left, right, (((1,), (1,)), ((), ())), preferred_element_type=F32)


def mm_tl(left, right):
    return lax.dot_general(left, right, (((0,), (0,)), ((), ())), preferred_element_type=F32)


def trade(blocks, axes):
    return lax.all_to_all(blocks, axes, 0, 0, tiled=True)


def hop(block, axis, step):
    size = lax.axis_size(axis)
    return lax.ppermute(block, axis, [(i, i ^ step) for i in range(size)])


def tie(*values):
    return lax.optimization_barrier(values)


def link_steps():
    steps = []
    step = 1
    while step < lax.axis_size(CUBE):
        steps.append(step)
        step *= 2
    return steps


FAR, NEAR, SIDE = 4, 2, 1
ROW_ORDER = (0, FAR, NEAR, FAR | NEAR, SIDE, FAR | SIDE, NEAR | SIDE, FAR | NEAR | SIDE)


def cube(block, step):
    return hop(block, CUBE, step)


def gather_rows(rows):
    two = jnp.concatenate([rows, cube(rows, FAR)], axis=0)
    n, half = two.shape[0], two.shape[1] // 2
    left, right = two[:, :half], two[:, half:]
    left_came, right_came = cube(left, NEAR), cube(right, SIDE)
    left = jnp.concatenate([left, left_came], axis=0)
    right = jnp.concatenate([right, right_came], axis=0)
    left_came, right_came = cube(left, SIDE), cube(right, NEAR)
    left = jnp.concatenate([left, left_came], axis=0)
    right = jnp.concatenate([right[:n], right_came[:n], right[n:], right_came[n:]], axis=0)
    return jnp.concatenate([left, right], axis=1)


def sum_rows(partial):
    partial = partial.astype(BF)
    n, half = partial.shape[0] // 4, partial.shape[1] // 2
    left, right = partial[:, :half], partial[:, half:]
    left_came = cube(left[2 * n :], SIDE)
    right_came = cube(jnp.concatenate([right[n : 2 * n], right[3 * n :]], axis=0), NEAR)
    left = left[: 2 * n].astype(F32) + left_came.astype(F32)
    right_came = right_came.astype(F32)
    low = right[:n].astype(F32) + right_came[:n]
    high = right[2 * n : 3 * n].astype(F32) + right_came[n:]
    left_came = cube(left[n:].astype(BF), NEAR)
    right_came = cube(high.astype(BF), SIDE)
    left = left[:n] + left_came.astype(F32)
    right = low + right_came.astype(F32)
    both = jnp.concatenate([left, right], axis=1)
    rows = n // 2
    return both[:rows] + cube(both[rows:].astype(BF), FAR).astype(F32)


class Stages:
    def __init__(self):
        self.held = {}

    def run(self, value, step, jobs):
        needed = [[self.held[name] for name in names] for _, _, names in jobs]
        value, needed = lax.optimization_barrier((value, needed))
        out = step(value)
        made = [job(*inputs) for (_, job, _), inputs in zip(jobs, needed)]
        out, made = lax.optimization_barrier((out, made))
        self.held.update((key, result) for (key, _, _), result in zip(jobs, made))
        return out


def others(block, axis):
    return [block] + [hop(block, axis, k) for k in range(1, lax.axis_size(axis))]


def sum_others(blocks, axis):
    total = blocks[0].astype(F32)
    for k in range(1, lax.axis_size(axis)):
        total = total + hop(blocks[k].astype(BF), axis, k).astype(F32)
    return total


def relative(values, dim, axis):
    count = lax.axis_size(axis)
    me = lax.axis_index(axis)
    step = 1
    while step < count:
        shape = values.shape
        cut = shape[:dim] + (count // (2 * step), 2, step * (shape[dim] // count)) + shape[dim + 1 :]
        view = values.reshape(cut)
        swapped = jnp.concatenate(
            [lax.slice_in_dim(view, 1, 2, axis=dim + 1), lax.slice_in_dim(view, 0, 1, axis=dim + 1)],
            axis=dim + 1,
        )
        values = jnp.where((me & step) != 0, swapped.reshape(shape), values)
        step *= 2
    return values


def spread_gains(norm_gains):
    me = lax.axis_index(CUBE)
    gain = norm_gains
    for step in link_steps():
        came = hop(gain, CUBE, step)
        gain = jnp.where(
            (me & step) != 0,
            jnp.concatenate([came, gain], axis=1),
            jnp.concatenate([gain, came], axis=1),
        )
    gain = jnp.concatenate(others(gain, "grp"), axis=1)
    other = hop(gain, "pipe", 1)
    core = lax.axis_index("pipe")
    return [jnp.where(core == 0, gain, other), jnp.where(core == 0, other, gain)]


def sum_gains(grads):
    me = lax.axis_index(CUBE)
    keep, extra = own_layer(grads[0], grads[1])
    total = (keep + extra).reshape(2, lax.axis_size("grp"), -1)
    mine = total[:, 0]
    for k in range(1, total.shape[1]):
        mine = mine + hop(total[:, k], "grp", k)
    for step in link_steps()[::-1]:
        half = mine.shape[1] // 2
        low, high = mine[:, :half], mine[:, half:]
        odd = (me & step) != 0
        mine = jnp.where(odd, high, low) + hop(jnp.where(odd, low, high), CUBE, step)
    return mine


def masked_probs(q, k, q_place, q_start, k_place):
    scores = lax.dot_general(q, k, (((1,), (1,)), ((), ())), preferred_element_type=F32)
    scores = scores * HEAD_SIZE ** (-0.5)
    allowed = (k_place <= q_place) & (k_place >= q_start)
    masked = jnp.where(allowed, scores, NEG_FILL)
    exps = jnp.exp(masked - jnp.max(masked, axis=-1, keepdims=True))
    return exps / jnp.sum(exps, axis=-1, keepdims=True)


def attend_kernel(q_ref, k_ref, v_ref, qp_ref, qs_ref, kp_ref, o_ref):
    probs = masked_probs(q_ref[0], k_ref[...], qp_ref[...], qs_ref[...], kp_ref[...])
    o_ref[0] = jnp.dot(probs.astype(BF), v_ref[...], preferred_element_type=F32).astype(BF)


def attend_back_kernel(q_ref, do_ref, k_ref, v_ref, qp_ref, qs_ref, kp_ref, dq_ref, dk_ref, dv_ref):
    @pl.when((pl.program_id(0) == 0) & (pl.program_id(1) == 0))
    def _():
        dk_ref[...] = jnp.zeros_like(dk_ref)
        dv_ref[...] = jnp.zeros_like(dv_ref)

    q = q_ref[0]
    do = do_ref[0]
    k = k_ref[...]
    probs = masked_probs(q, k, qp_ref[...], qs_ref[...], kp_ref[...])
    grad_probs = lax.dot_general(do, v_ref[...], (((1,), (1,)), ((), ())), preferred_element_type=F32)
    delta = jnp.sum(probs * grad_probs, axis=-1, keepdims=True)
    grad_scores = (probs * (grad_probs - delta) * HEAD_SIZE ** (-0.5)).astype(BF)
    dq_ref[0] = jnp.dot(grad_scores, k, preferred_element_type=F32).astype(BF)
    dk_ref[...] += lax.dot_general(
        grad_scores, q, (((0,), (0,)), ((), ())), preferred_element_type=F32
    )
    dv_ref[...] += lax.dot_general(
        probs.astype(BF), do, (((0,), (0,)), ((), ())), preferred_element_type=F32
    )


def attention_specs(heads, rows, keys):
    rows_blk = max(16, min(rows, (512 * 1024) // keys))
    per_head = pl.BlockSpec((1, rows_blk, HEAD_SIZE), lambda b, h: (h, b, 0))
    full = pl.BlockSpec((keys, HEAD_SIZE), lambda b, h: (0, 0))
    row_info = pl.BlockSpec((rows_blk, 1), lambda b, h: (b, 0))
    key_info = pl.BlockSpec((1, keys), lambda b, h: (0, 0))
    return ((rows // rows_blk, heads), per_head, full, row_info, key_info)


PARAMS = dict(
    compiler_params=pltpu.CompilerParams(vmem_limit_bytes=50 * 1024 * 1024),
)


def attend(q, k, v, q_place, q_start, k_place):
    heads, rows, _ = q.shape
    keys = k.shape[0]
    grid, per_head, full, row_info, key_info = attention_specs(heads, rows, keys)
    return pl.pallas_call(
        attend_kernel,
        grid=grid,
        in_specs=[per_head, full, full, row_info, row_info, key_info],
        out_specs=per_head,
        out_shape=jax.ShapeDtypeStruct(q.shape, BF),
        cost_estimate=pl.CostEstimate(
            flops=4 * heads * rows * keys * HEAD_SIZE,
            bytes_accessed=4 * q.size + 4 * k.size,
            transcendentals=heads * rows * keys,
        ),
        **PARAMS,
    )(q, k, v, q_place, q_start, k_place)


def attend_back(q, do, k, v, q_place, q_start, k_place):
    heads, rows, _ = q.shape
    keys = k.shape[0]
    grid, per_head, full, row_info, key_info = attention_specs(heads, rows, keys)
    return pl.pallas_call(
        attend_back_kernel,
        grid=grid,
        in_specs=[per_head, per_head, full, full, row_info, row_info, key_info],
        out_specs=[per_head, full, full],
        out_shape=[
            jax.ShapeDtypeStruct(q.shape, BF),
            jax.ShapeDtypeStruct(k.shape, F32),
            jax.ShapeDtypeStruct(k.shape, F32),
        ],
        cost_estimate=pl.CostEstimate(
            flops=10 * heads * rows * keys * HEAD_SIZE,
            bytes_accessed=6 * q.size + 12 * k.size,
            transcendentals=heads * rows * keys,
        ),
        **PARAMS,
    )(q, do, k, v, q_place, q_start, k_place)


def to_blocks(weight, cores):
    wd = lax.axis_size("wd")
    rows = weight.shape[0]
    cut = weight.reshape(rows, wd, cores, -1).transpose(2, 1, 0, 3)
    return cut.reshape((cores * wd, rows) + cut.shape[3:])


def columns_out(blocks):
    moved = trade(blocks, ("pipe", "wd"))
    return moved.reshape((2, -1) + moved.shape[2:])


def exchange(piece):
    return [hop(piece, "grp", k) for k in range(1, lax.axis_size("grp"))]


def piece_of(layer, part=None):
    def take(cols):
        rows = cols.shape[1] // 2
        if part is None:
            return exchange(cols[layer])
        return exchange(cols[layer, part * rows : (part + 1) * rows])

    return take


def put_kernel(spots, *refs):
    pieces, out, sems = refs[: len(spots)], refs[len(spots)], refs[len(spots) + 1]
    copies = []
    for i, (row, rows, col, cols) in enumerate(spots):
        target = out.at[pl.ds(row, rows), pl.ds(col, cols)]
        copies.append(pltpu.make_async_copy(pieces[i], target, sems.at[i]))
    for copy in copies:
        copy.start()
    for copy in copies:
        copy.wait()


def put_together(columns):
    spots, pieces = [], []
    col = 0
    for stack in columns:
        row = 0
        for piece in stack:
            spots.append((row, piece.shape[0], col, piece.shape[1]))
            pieces.append(piece)
            row += piece.shape[0]
        col += stack[0].shape[1]
    anywhere = pl.BlockSpec(memory_space=pl.ANY)
    return pl.pallas_call(
        lambda *refs: put_kernel(spots, *refs),
        in_specs=[anywhere] * len(pieces),
        out_specs=anywhere,
        out_shape=jax.ShapeDtypeStruct((row, col), BF),
        scratch_shapes=[pltpu.SemaphoreType.DMA((len(pieces),))],
        cost_estimate=pl.CostEstimate(flops=0, bytes_accessed=4 * row * col, transcendentals=0),
    )(*pieces)


def stacked(layer):
    def join(cols, *came):
        pieces = [cols[layer]]
        for k in range(len(came[0])):
            pieces += [c[k] for c in came]
        return pieces

    return join


def crossed(pieces):
    return [hop(p, "pipe", 1) for p in pieces]


def pack_attention(w_query, key_matrix, value_matrix, w_output, cores):
    wd = lax.axis_size("wd")
    rows = w_query.shape[0]
    cut = [
        m.reshape(rows, wd, cores, -1) for m in (w_query, key_matrix, value_matrix, w_output.T)
    ]
    return jnp.concatenate(cut, axis=-1).reshape(rows, -1)


def core_order(own, other, axis):
    core = lax.axis_index("pipe")
    return jnp.where(
        core == 0,
        jnp.concatenate([own, other], axis=axis),
        jnp.concatenate([other, own], axis=axis),
    )


def unpack_attention(own, other, widths):
    query_w, kv_w, out_w = widths
    cuts = (query_w, query_w + kv_w, query_w + 2 * kv_w)

    def split(m):
        return (m[:, : cuts[0]], m[:, cuts[0] : cuts[1]], m[:, cuts[1] : cuts[2]], m[:, cuts[2] :])

    q0, k0, v0, o0 = split(own)
    q1, k1, v1, o1 = split(other)
    return (
        jnp.concatenate([q0, q1], axis=1),
        core_order(k0, k1, 1),
        core_order(v0, v1, 1),
        jnp.concatenate([o0, o1], axis=1),
    )


def core_halves(grad):
    half = grad.shape[1] // 2
    core = lax.axis_index("pipe")
    low, high = grad[:, :half], grad[:, half:]
    return (jnp.where(core == 0, low, high), jnp.where(core == 0, high, low))


def grad_pair(own, other):
    total = own + hop(other.astype(BF), "pipe", 1).astype(F32)
    return total.reshape((lax.axis_size("grp"), -1) + total.shape[1:])


def mlp_pair(left, right):
    half = right.shape[1] // 2
    return grad_pair(mm_tl(left, right[:, :half]), mm_tl(left, right[:, half:]))


def grad_part(part):
    def add(blocks):
        rows = blocks.shape[1] // 2
        cut = blocks[:, part * rows : (part + 1) * rows]
        total = cut[0]
        for k in range(1, blocks.shape[0]):
            total = total + hop(cut[k].astype(BF), "grp", k).astype(F32)
        return total.astype(BF)

    return add


def grad_home(low, high):
    wd = lax.axis_size("wd")
    me = lax.axis_index("wd")
    blocks = jnp.concatenate([low, high], axis=0).reshape((wd, -1) + low.shape[1:])
    pieces = [lax.dynamic_index_in_dim(blocks, me, 0, keepdims=False)]
    for k in range(1, wd):
        pieces.append(hop(lax.dynamic_index_in_dim(blocks, me ^ k, 0, keepdims=False), "wd", k))
    return jnp.stack(pieces)


def place_kernel(turned, at_ref, keep_ref, got_ref, out_ref):
    mine = pl.program_id(1) == at_ref[1]

    def put(ref):
        block = ref[0].astype(F32)
        out_ref[...] = block.T if turned else block

    @pl.when(mine)
    def _():
        put(keep_ref)

    @pl.when(jnp.logical_not(mine))
    def _():
        put(got_ref)


def place(keep, got, turned):
    wd, rows, cols = keep.shape
    at = jnp.stack([lax.axis_index("wd"), lax.axis_index("pipe")]).astype(jnp.int32)
    cores = lax.axis_size("pipe")
    source = pl.BlockSpec((1, rows, cols), lambda w, c, at_ref: (w ^ at_ref[0], 0, 0))
    if turned:
        shape, target = (wd * cores * cols, rows), (cols, rows)
        out = pl.BlockSpec(target, lambda w, c, at_ref: (w * cores + c, 0))
    else:
        shape, target = (rows, wd * cores * cols), (rows, cols)
        out = pl.BlockSpec(target, lambda w, c, at_ref: (0, w * cores + c))
    return pl.pallas_call(
        lambda *refs: place_kernel(turned, *refs),
        grid_spec=pltpu.PrefetchScalarGridSpec(
            num_scalar_prefetch=1, grid=(wd, cores), in_specs=[source, source], out_specs=out
        ),
        out_shape=jax.ShapeDtypeStruct(shape, F32),
        cost_estimate=pl.CostEstimate(
            flops=keep.size, bytes_accessed=12 * keep.size, transcendentals=0
        ),
    )(at, keep, got)


def layer_forward(stages, layer, x_rows, gains, where, jobs, before):
    held = stages.held
    cosine, sine, q_place, q_start, k_place = where
    normed = apply_norm(x_rows, gains[0]).astype(BF)
    rows_a = stages.run(normed, gather_rows, jobs[0]) if jobs[0] else gather_rows(normed)
    w_q, w_k, w_v, w_ot = held["attn", layer]
    tok = rows_a.shape[0]

    def project(rows):
        query = rotary_apply(mm(rows, w_q).reshape(tok, -1, HEAD_SIZE), cosine, sine).astype(BF)
        key = rotary_apply(mm(rows, w_k).reshape(tok, 1, HEAD_SIZE), cosine, sine).astype(BF)[:, 0]
        value = mm(rows, w_v).astype(BF)
        kv = jnp.concatenate([key, value], axis=1)
        return query.transpose(1, 0, 2), jnp.concatenate(others(kv, "grp"), axis=0)

    query, kv_all = stages.run(rows_a, project, jobs[1])
    keys, values = kv_all[:, :HEAD_SIZE], kv_all[:, HEAD_SIZE:]

    def attention(q):
        context = attend(q, keys, values, q_place, q_start, k_place)
        context = context.transpose(1, 0, 2).reshape(tok, -1)
        return context, x_rows + sum_rows(mm_t(context, w_ot))

    context, mid = stages.run(query, attention, jobs[2])
    rows_b = stages.run(
        mid, lambda m: gather_rows(apply_norm(m, gains[1]).astype(BF)), jobs[3]
    )
    for more in before:
        rows_b = stages.run(rows_b, lambda r: r, more)
    w_gu = held["gu", layer]

    def ahead(rows):
        both = mm(rows, w_gu)
        half = both.shape[1] // 2
        gate, up = both[:, :half], both[:, half:]
        return gate, up, (jax.nn.silu(gate) * up).astype(BF)

    gate, up, hidden = stages.run(rows_b, ahead, jobs[4])
    return x_rows, rows_a, query, keys, values, context, mid, rows_b, gate, up, hidden


def layer_backward(stages, layer, grad_out, grad_mlp, gains, where, kept, also, jobs):
    held = stages.held
    cosine, sine, q_place, q_start, k_place = where
    x_rows, rows_a, query, keys, values, context, mid, rows_b, gate, up, hidden = kept
    w_q, w_k, w_v, w_ot = held["attn", layer]
    w_gu, w_dt = held["gu", layer], held["down", layer]
    tok = rows_a.shape[0]
    held["rows_b"], held["hidden"] = rows_b, hidden
    held["grad_mlp"] = grad_mlp

    def feed_back(rows):
        grad_hidden = mm(rows, w_dt)
        sig = jax.nn.sigmoid(gate)
        grad_gate = (grad_hidden * up * sig * (1.0 + gate * (1.0 - sig))).astype(BF)
        grad_up = (grad_hidden * gate * sig).astype(BF)
        both = jnp.concatenate([grad_gate, grad_up], axis=1)
        return grad_gate, grad_up, mm_t(both, w_gu).astype(BF), also(hidden)

    grad_gate, grad_up, partial, extra = stages.run(grad_mlp, feed_back, jobs[0])
    held["grad_gate"], held["grad_up"] = grad_gate, grad_up
    grad_b = stages.run(partial, sum_rows, jobs[1])
    grad_mid, gain_b = norm_back(mid, gains[1], grad_b)
    grad_mid = grad_mid + grad_out
    grad_attn = stages.run(grad_mid.astype(BF), gather_rows, jobs[2])

    def attention_back(rows):
        grad_context = mm(rows, w_ot).astype(BF)
        grad_context = grad_context.reshape(tok, -1, HEAD_SIZE).transpose(1, 0, 2)
        grad_q, grad_k, grad_v = attend_back(
            query, grad_context, keys, values, q_place, q_start, k_place
        )
        kv = jnp.concatenate([grad_k, grad_v], axis=1)
        kv = kv.reshape((-1, tok) + kv.shape[1:])
        own_kv = sum_others([kv[k] for k in range(kv.shape[0])], "grp").astype(BF)
        grad_k = own_kv[:, :HEAD_SIZE].astype(F32)
        grad_k = rotary_apply(grad_k[:, None, :], cosine, -sine).astype(BF)[:, 0]
        grad_v = own_kv[:, HEAD_SIZE:]
        grad_q = grad_q.transpose(1, 0, 2).astype(F32)
        grad_q = rotary_apply(grad_q, cosine, -sine).astype(BF).reshape(tok, -1)
        partial = mm_t(grad_q, w_q) + mm_t(grad_k, w_k) + mm_t(grad_v, w_v)
        return grad_q, grad_k, grad_v, partial.astype(BF)

    grad_q, grad_k, grad_v, partial = stages.run(grad_attn, attention_back, jobs[3])

    def attn_pair(g_q, g_k, g_v):
        half_q = g_q.shape[1] // 2
        kv_0, kv_1 = core_halves(g_k)
        v_0, v_1 = core_halves(g_v)

        def term(q_half, k_half, v_half, o_half):
            right = jnp.concatenate([q_half, k_half, v_half], axis=1)
            return jnp.concatenate([mm_tl(rows_a, right), mm_tl(grad_attn, o_half)], axis=1)

        return grad_pair(
            term(g_q[:, :half_q], kv_0, v_0, context[:, :half_q]),
            term(g_q[:, half_q:], kv_1, v_1, context[:, half_q:]),
        )

    held["g_q"], held["g_k"], held["g_v"] = grad_q, grad_k, grad_v
    held["attn_pair"] = attn_pair
    grad_a = stages.run(partial, sum_rows, jobs[4](attn_pair))
    grad_in, gain_a = norm_back(x_rows, gains[0], grad_a)
    return grad_mid + grad_in, jnp.stack([gain_a, gain_b]), extra


def own_layer(first, second):
    core = lax.axis_index("pipe")
    keep = jnp.where(core == 0, first, second)
    return keep, hop(jnp.where(core == 0, second, first), "pipe", 1)


def body(
    block_input,
    cotangent,
    segments,
    norm_gains,
    w_query,
    key_matrix,
    value_matrix,
    w_output,
    w_gate,
    w_up,
    w_down,
):
    core = lax.axis_index("pipe")
    grp = lax.axis_index("grp")
    wd = lax.axis_size("wd")
    groups = lax.axis_size("grp")
    cores = lax.axis_size("pipe")
    tok = block_input.shape[1] * lax.axis_size(CUBE)

    gains = spread_gains(norm_gains[0])

    stages = Stages()
    held = stages.held
    packed = pack_attention(w_query[0], key_matrix[0], value_matrix[0], w_output[0], cores)
    held["attn"] = columns_out(to_blocks(packed, cores))
    held["gate"] = columns_out(to_blocks(w_gate[0], cores))
    held["up_out"] = to_blocks(w_up[0], cores)
    held["down_out"] = to_blocks(w_down[0].T, cores)
    widths = tuple(n // (wd * cores) for n in (w_query.shape[2], key_matrix.shape[2], w_output.shape[1]))

    def move(name):
        return (name, columns_out, (name + "_out",))

    def swap(name, layer, part=None):
        return ((name, layer, part), piece_of(layer, part), (name,))

    def parts(name, layer):
        if name == "attn":
            return (name, (name, layer, None))
        return (name, (name, layer, 0), (name, layer, 1))

    def attn_ready(layer):
        def ready(*values):
            own = stacked(layer)(*values)
            there = crossed(own)
            return unpack_attention(
                jnp.concatenate(own, axis=0), jnp.concatenate(there, axis=0), widths
            )

        return (("attn", layer), ready, parts("attn", layer))

    def cross(name, layer):
        def ready(*values):
            own = stacked(layer)(*values)
            return own, crossed(own)

        return (("cross", name, layer), ready, parts(name, layer))

    def gate_up_ready(layer):
        def ready(gate, up):
            return put_together([gate[0], gate[1], up[0], up[1]])

        return (("gu", layer), ready, (("cross", "gate", layer), ("cross", "up", layer)))

    def down_ready(layer):
        return (("down", layer), lambda d: put_together([d[0], d[1]]), (("cross", "down", layer),))

    seg_row = lax.dynamic_index_in_dim(segments, core, 0, keepdims=False)
    starts = doc_starts(seg_row)
    rows_own = tok // lax.axis_size(CUBE)

    def in_row_order(values):
        values = relative(values, 0, CUBE)
        return jnp.concatenate(
            [values[j * rows_own : (j + 1) * rows_own] for j in ROW_ORDER], axis=0
        )

    local = in_row_order(jnp.arange(tok, dtype=jnp.int32))
    q_place = grp * tok + local
    q_start = in_row_order(lax.dynamic_slice_in_dim(starts, grp * tok, tok))
    cosine, sine = rope_tables(q_place - q_start)
    k_place = jnp.concatenate([(grp ^ k) * tok + local for k in range(groups)])
    where = (cosine, sine, q_place[:, None], q_start[:, None], k_place[None, :])

    rows = relative(lax.dynamic_index_in_dim(block_input, core, 0, keepdims=False), 1, "grp")
    grad = relative(lax.dynamic_index_in_dim(cotangent, core, 0, keepdims=False), 1, "grp")
    held["cotangent"] = grad
    for key, job, names in (swap("attn", 0), attn_ready(0)):
        held[key] = job(*[held[name] for name in names])
    kept = [None, None]
    outs = [None, None]
    kept[0] = layer_forward(
        stages,
        0,
        rows.astype(F32),
        gains[0],
        where,
        (
            [],
            [move("up"), swap("gate", 0, 0)],
            [move("down"), swap("gate", 0, 1), swap("up", 0, 0)],
            [swap("up", 0, 1), swap("down", 0, 0), cross("gate", 0)],
            [swap("down", 0, 1)],
        ),
        [[cross("up", 0)], [gate_up_ready(0)]],
    )

    def close(hidden, layer):
        return (kept[layer][6] + sum_rows(mm_t(hidden, held["down", layer]))).astype(BF)

    hidden = kept[0][-1]
    for jobs in ([cross("down", 0)], [down_ready(0)]):
        hidden = stages.run(hidden, lambda h: h, jobs)
    outs[0] = stages.run(hidden, lambda h: close(h, 0), [swap("attn", 1), swap("gate", 1, 0)])
    kept[1] = layer_forward(
        stages,
        1,
        outs[0].astype(F32),
        gains[1],
        where,
        (
            [swap("gate", 1, 1), attn_ready(1)],
            [swap("up", 1, 0), ("last", gather_rows, ("cotangent",))],
            [swap("up", 1, 1), swap("down", 1, 0), cross("gate", 1)],
            [swap("down", 1, 1), cross("up", 1)],
            [cross("down", 1)],
        ),
        [[gate_up_ready(1)]],
    )
    hidden = stages.run(kept[1][-1], lambda h: h, [down_ready(1)])

    def grad_of(name, layer):
        sources = {
            "down": ("grad_mlp", "hidden"),
            "gate": ("rows_b", "grad_gate"),
            "up": ("rows_b", "grad_up"),
        }[name]
        return (("pair", name, layer), mlp_pair, sources)

    def grad_swap(name, layer, part):
        return (("part", name, layer, part), grad_part(part), (("pair", name, layer),))

    def home(name, layer):
        keys = tuple(("part", name, layer, part) for part in range(2))
        return (("home", name, layer), grad_home, keys)

    def attn_grad(layer):
        return lambda pair: (("pair", "attn", layer), pair, ("g_q", "g_k", "g_v"))

    grads_in = [None, None]
    gain_grads = [None, None]
    grad_in, gain_grads[1], outs[1] = layer_backward(
        stages,
        1,
        grad.astype(F32),
        held["last"],
        gains[1],
        where,
        kept[1][:-1] + (hidden,),
        lambda h: close(h, 1),
        (
            [grad_of("down", 1)],
            [grad_swap("down", 1, 0), grad_of("gate", 1)],
            [grad_swap("down", 1, 1), grad_of("up", 1)],
            [grad_swap("gate", 1, 0), grad_swap("gate", 1, 1), home("down", 1)],
            lambda pair: [grad_swap("up", 1, 0), attn_grad(1)(pair)],
        ),
    )
    grads_in[1] = grad_in.astype(BF)
    grad_mlp = stages.run(grads_in[1], gather_rows, [grad_swap("up", 1, 1)])
    grad_in, gain_grads[0], _ = layer_backward(
        stages,
        0,
        grads_in[1].astype(F32),
        grad_mlp,
        gains[0],
        where,
        kept[0],
        lambda h: (),
        (
            [grad_of("down", 0), grad_swap("attn", 1, 0), grad_swap("attn", 1, 1), home("gate", 1)],
            [grad_swap("down", 0, 0), grad_of("gate", 0)],
            [grad_swap("down", 0, 1), grad_of("up", 0)],
            [grad_swap("gate", 0, 0), grad_swap("gate", 0, 1), home("up", 1), home("down", 0)],
            lambda pair: [grad_swap("up", 0, 0), attn_grad(0)(pair)],
        ),
    )
    grads_in[0] = grad_in.astype(BF)
    for key, job, names in (
        grad_swap("attn", 0, 0),
        grad_swap("attn", 0, 1),
        home("attn", 1),
        grad_swap("up", 0, 1),
        home("gate", 0),
        home("attn", 0),
        home("up", 0),
    ):
        held[key] = job(*[held[name] for name in names])

    def by_batch(pair):
        own, other = own_layer(pair[0], pair[1])
        both = jnp.where(core == 0, jnp.stack([own, other]), jnp.stack([other, own]))
        return relative(both, 2, "grp")[None]

    layer_out = by_batch(outs)
    input_grad = by_batch(grads_in)

    grad_norm_gains = sum_gains(gain_grads)[None]

    def both(name):
        return own_layer(held["home", name, 0], held["home", name, 1])

    keep, got = both("attn")
    cuts = (0, widths[0], widths[0] + widths[1], widths[0] + 2 * widths[1], keep.shape[2])
    q_pair, k_pair, v_pair, o_pair = (
        (keep[..., lo:hi], got[..., lo:hi]) for lo, hi in zip(cuts[:-1], cuts[1:])
    )

    def small(pair):
        order = jnp.where(core == 0, jnp.stack(pair), jnp.stack(pair[::-1]))
        order = relative(order, 1, "wd").transpose(2, 1, 0, 3).astype(F32)
        return order.reshape(order.shape[0], -1)[None]

    grad_wq = place(*q_pair, False)[None]
    grad_wk = small(k_pair)
    grad_wv = small(v_pair)
    grad_wo = place(*o_pair, True)[None]
    grad_wg = place(*both("gate"), False)[None]
    grad_wu = place(*both("up"), False)[None]
    grad_wd = place(*both("down"), True)[None]
    return (
        layer_out,
        input_grad,
        grad_norm_gains,
        grad_wq,
        grad_wk,
        grad_wv,
        grad_wo,
        grad_wg,
        grad_wu,
        grad_wd,
    )


def solution(mesh):
    sizes = dict(mesh.shape)
    wd = KV_HEADS // sizes["tensor"]
    fine = Mesh(
        mesh.devices.reshape(sizes["pipe"], sizes["dp"] // wd, wd, sizes["tensor"]),
        ("pipe", "grp", "wd", "tensor"),
    )
    dp = ("grp", "wd")
    tokens = P(None, dp + ("tensor",), None)
    outs = P("pipe", None, dp + ("tensor",), None)
    gains = P("pipe", None, dp + ("tensor",))
    tall = P("pipe", dp, "tensor")
    wide = P("pipe", "tensor", dp)
    weights = (tall, tall, tall, wide, tall, tall, wide)
    return jax.shard_map(
        body,
        mesh=fine,
        in_specs=(tokens, tokens, P(), gains) + weights,
        out_specs=(outs, outs, gains) + weights,
        check_vma=False,
    )
```

```python
import jax
import jax.numpy as jnp
from jax import lax
from jax.experimental import pallas as pl
from jax.experimental.pallas import tpu as pltpu
from jax.sharding import Mesh, PartitionSpec as P

HEAD_SIZE = 64
KV_HEADS = 8
EPS = 1e-05
ROPE_BASE = 500000.0
NEG_FILL = -1e30
BF = jnp.bfloat16
F32 = jnp.float32
CUBE = ("wd", "tensor")


def rms_scale(row_values):
    return lax.rsqrt(jnp.mean(row_values * row_values, axis=-1, keepdims=True) + EPS)


def apply_norm(row_values, gain_vector):
    return row_values * rms_scale(row_values) * gain_vector


def norm_back(row_values, gain_vector, grad_normed):
    _, pullback = jax.vjp(apply_norm, row_values, gain_vector)
    return pullback(grad_normed)


def doc_starts(seg_row):
    places = jnp.arange(seg_row.shape[0], dtype=jnp.int32)
    before = jnp.concatenate([seg_row[:1] - 1, seg_row[:-1]])
    return lax.cummax(jnp.where(seg_row != before, places, 0), axis=0)


def rope_tables(positions):
    half_dim = HEAD_SIZE // 2
    freqs = ROPE_BASE ** (-(jnp.arange(half_dim, dtype=F32) * 2.0 / HEAD_SIZE))
    angles = positions.astype(F32)[:, None] * freqs[None, :]
    return (jnp.cos(angles), jnp.sin(angles))


def rotary_apply(head_values, cosine_table, sine_values):
    half_dim = head_values.shape[-1] // 2
    first_half = head_values[..., :half_dim]
    second_half = head_values[..., half_dim:]
    cos_rows = cosine_table[:, None, :]
    sin_rows = sine_values[:, None, :]
    return jnp.concatenate(
        [
            first_half * cos_rows - second_half * sin_rows,
            second_half * cos_rows + first_half * sin_rows,
        ],
        axis=-1,
    )


def mm(left, right):
    return jnp.dot(left, right, preferred_element_type=F32)


def mm_t(left, right):
    return lax.dot_general(left, right, (((1,), (1,)), ((), ())), preferred_element_type=F32)


def mm_tl(left, right):
    return lax.dot_general(left, right, (((0,), (0,)), ((), ())), preferred_element_type=F32)


def trade(blocks, axes):
    return lax.all_to_all(blocks, axes, 0, 0, tiled=True)


def hop(block, axis, step):
    size = lax.axis_size(axis)
    return lax.ppermute(block, axis, [(i, i ^ step) for i in range(size)])


def tie(*values):
    return lax.optimization_barrier(values)


def link_steps():
    steps = []
    step = 1
    while step < lax.axis_size(CUBE):
        steps.append(step)
        step *= 2
    return steps


FAR, NEAR, SIDE = 4, 2, 1
ROW_ORDER = (0, FAR, NEAR, FAR | NEAR, SIDE, FAR | SIDE, NEAR | SIDE, FAR | NEAR | SIDE)


def cube(block, step):
    return hop(block, CUBE, step)


def join_kernel(left_ref, left_came_ref, right_ref, right_came_ref, out_ref):
    half = left_ref.shape[1]
    block = pl.program_id(0)

    @pl.when(block < 2)
    def _():
        out_ref[:, :half] = left_ref[...]

    @pl.when(block >= 2)
    def _():
        out_ref[:, :half] = left_came_ref[...]

    @pl.when(block % 2 == 0)
    def _():
        out_ref[:, half:] = right_ref[...]

    @pl.when(block % 2 == 1)
    def _():
        out_ref[:, half:] = right_came_ref[...]


def join_halves(left, left_came, right, right_came):
    rows, half = left.shape[0] // 2, left.shape[1]

    def spec(place):
        return pl.BlockSpec((rows, half), lambda i: (place(i), 0))

    return pl.pallas_call(
        join_kernel,
        grid=(4,),
        in_specs=[
            spec(lambda i: jnp.minimum(i, 1)),
            spec(lambda i: jnp.maximum(i - 2, 0)),
            spec(lambda i: i // 2),
            spec(lambda i: i // 2),
        ],
        out_specs=pl.BlockSpec((rows, 2 * half), lambda i: (i, 0)),
        out_shape=jax.ShapeDtypeStruct((4 * rows, 2 * half), left.dtype),
        cost_estimate=pl.CostEstimate(
            flops=0, bytes_accessed=32 * rows * half, transcendentals=0
        ),
    )(left, left_came, right, right_came)


def gather_rows(rows):
    two = jnp.concatenate([rows, cube(rows, FAR)], axis=0)
    half = two.shape[1] // 2
    left, right = two[:, :half], two[:, half:]
    left_came, right_came = cube(left, NEAR), cube(right, SIDE)
    left = jnp.concatenate([left, left_came], axis=0)
    right = jnp.concatenate([right, right_came], axis=0)
    return join_halves(left, cube(left, SIDE), right, cube(right, NEAR))


def sum_rows(partial):
    partial = partial.astype(BF)
    n, half = partial.shape[0] // 4, partial.shape[1] // 2
    left, right = partial[:, :half], partial[:, half:]
    left_came = cube(left[2 * n :], SIDE)
    right_came = cube(jnp.concatenate([right[n : 2 * n], right[3 * n :]], axis=0), NEAR)
    left = left[: 2 * n].astype(F32) + left_came.astype(F32)
    right_came = right_came.astype(F32)
    low = right[:n].astype(F32) + right_came[:n]
    high = right[2 * n : 3 * n].astype(F32) + right_came[n:]
    left_came = cube(left[n:].astype(BF), NEAR)
    right_came = cube(high.astype(BF), SIDE)
    left = left[:n] + left_came.astype(F32)
    right = low + right_came.astype(F32)
    both = jnp.concatenate([left, right], axis=1)
    rows = n // 2
    return both[:rows] + cube(both[rows:].astype(BF), FAR).astype(F32)


class Stages:
    def __init__(self):
        self.held = {}

    def run(self, value, step, jobs):
        needed = [[self.held[name] for name in names] for _, _, names in jobs]
        value, needed = lax.optimization_barrier((value, needed))
        out = step(value)
        made = [job(*inputs) for (_, job, _), inputs in zip(jobs, needed)]
        out, made = lax.optimization_barrier((out, made))
        self.held.update((key, result) for (key, _, _), result in zip(jobs, made))
        return out


def others(block, axis):
    return [block] + [hop(block, axis, k) for k in range(1, lax.axis_size(axis))]


def sum_others(blocks, axis):
    total = blocks[0].astype(F32)
    for k in range(1, lax.axis_size(axis)):
        total = total + hop(blocks[k].astype(BF), axis, k).astype(F32)
    return total


def relative(values, dim, axis):
    count = lax.axis_size(axis)
    me = lax.axis_index(axis)
    step = 1
    while step < count:
        shape = values.shape
        cut = shape[:dim] + (count // (2 * step), 2, step * (shape[dim] // count)) + shape[dim + 1 :]
        view = values.reshape(cut)
        swapped = jnp.concatenate(
            [lax.slice_in_dim(view, 1, 2, axis=dim + 1), lax.slice_in_dim(view, 0, 1, axis=dim + 1)],
            axis=dim + 1,
        )
        values = jnp.where((me & step) != 0, swapped.reshape(shape), values)
        step *= 2
    return values


def spread_gains(norm_gains):
    me = lax.axis_index(CUBE)
    gain = norm_gains
    for step in link_steps():
        came = hop(gain, CUBE, step)
        gain = jnp.where(
            (me & step) != 0,
            jnp.concatenate([came, gain], axis=1),
            jnp.concatenate([gain, came], axis=1),
        )
    gain = jnp.concatenate(others(gain, "grp"), axis=1)
    other = hop(gain, "pipe", 1)
    core = lax.axis_index("pipe")
    return [jnp.where(core == 0, gain, other), jnp.where(core == 0, other, gain)]


def sum_gains(grads):
    me = lax.axis_index(CUBE)
    keep, extra = own_layer(grads[0], grads[1])
    total = (keep + extra).reshape(2, lax.axis_size("grp"), -1)
    mine = total[:, 0]
    for k in range(1, total.shape[1]):
        mine = mine + hop(total[:, k], "grp", k)
    for step in link_steps()[::-1]:
        half = mine.shape[1] // 2
        low, high = mine[:, :half], mine[:, half:]
        odd = (me & step) != 0
        mine = jnp.where(odd, high, low) + hop(jnp.where(odd, low, high), CUBE, step)
    return mine


def masked_probs(q, k, q_place, q_start, k_place):
    scores = lax.dot_general(q, k, (((1,), (1,)), ((), ())), preferred_element_type=F32)
    scores = scores * HEAD_SIZE ** (-0.5)
    allowed = (k_place <= q_place) & (k_place >= q_start)
    masked = jnp.where(allowed, scores, NEG_FILL)
    exps = jnp.exp(masked - jnp.max(masked, axis=-1, keepdims=True))
    return exps / jnp.sum(exps, axis=-1, keepdims=True)


def attend_kernel(q_ref, k_ref, v_ref, qp_ref, qs_ref, kp_ref, o_ref):
    probs = masked_probs(q_ref[0], k_ref[...], qp_ref[...], qs_ref[...], kp_ref[...])
    o_ref[0] = jnp.dot(probs.astype(BF), v_ref[...], preferred_element_type=F32).astype(BF)


def attend_back_kernel(q_ref, do_ref, k_ref, v_ref, qp_ref, qs_ref, kp_ref, dq_ref, dk_ref, dv_ref):
    @pl.when((pl.program_id(0) == 0) & (pl.program_id(1) == 0))
    def _():
        dk_ref[...] = jnp.zeros_like(dk_ref)
        dv_ref[...] = jnp.zeros_like(dv_ref)

    q = q_ref[0]
    do = do_ref[0]
    k = k_ref[...]
    probs = masked_probs(q, k, qp_ref[...], qs_ref[...], kp_ref[...])
    grad_probs = lax.dot_general(do, v_ref[...], (((1,), (1,)), ((), ())), preferred_element_type=F32)
    delta = jnp.sum(probs * grad_probs, axis=-1, keepdims=True)
    grad_scores = (probs * (grad_probs - delta) * HEAD_SIZE ** (-0.5)).astype(BF)
    dq_ref[0] = jnp.dot(grad_scores, k, preferred_element_type=F32).astype(BF)
    dk_ref[...] += lax.dot_general(
        grad_scores, q, (((0,), (0,)), ((), ())), preferred_element_type=F32
    )
    dv_ref[...] += lax.dot_general(
        probs.astype(BF), do, (((0,), (0,)), ((), ())), preferred_element_type=F32
    )


def attention_specs(heads, rows, keys):
    rows_blk = max(16, min(rows, (512 * 1024) // keys))
    per_head = pl.BlockSpec((1, rows_blk, HEAD_SIZE), lambda b, h: (h, b, 0))
    full = pl.BlockSpec((keys, HEAD_SIZE), lambda b, h: (0, 0))
    row_info = pl.BlockSpec((rows_blk, 1), lambda b, h: (b, 0))
    key_info = pl.BlockSpec((1, keys), lambda b, h: (0, 0))
    return ((rows // rows_blk, heads), per_head, full, row_info, key_info)


PARAMS = dict(
    compiler_params=pltpu.CompilerParams(vmem_limit_bytes=50 * 1024 * 1024),
)


def attend(q, k, v, q_place, q_start, k_place):
    heads, rows, _ = q.shape
    keys = k.shape[0]
    grid, per_head, full, row_info, key_info = attention_specs(heads, rows, keys)
    return pl.pallas_call(
        attend_kernel,
        grid=grid,
        in_specs=[per_head, full, full, row_info, row_info, key_info],
        out_specs=per_head,
        out_shape=jax.ShapeDtypeStruct(q.shape, BF),
        cost_estimate=pl.CostEstimate(
            flops=4 * heads * rows * keys * HEAD_SIZE,
            bytes_accessed=4 * q.size + 4 * k.size,
            transcendentals=heads * rows * keys,
        ),
        **PARAMS,
    )(q, k, v, q_place, q_start, k_place)


def attend_back(q, do, k, v, q_place, q_start, k_place):
    heads, rows, _ = q.shape
    keys = k.shape[0]
    grid, per_head, full, row_info, key_info = attention_specs(heads, rows, keys)
    return pl.pallas_call(
        attend_back_kernel,
        grid=grid,
        in_specs=[per_head, per_head, full, full, row_info, row_info, key_info],
        out_specs=[per_head, full, full],
        out_shape=[
            jax.ShapeDtypeStruct(q.shape, BF),
            jax.ShapeDtypeStruct(k.shape, F32),
            jax.ShapeDtypeStruct(k.shape, F32),
        ],
        cost_estimate=pl.CostEstimate(
            flops=10 * heads * rows * keys * HEAD_SIZE,
            bytes_accessed=6 * q.size + 12 * k.size,
            transcendentals=heads * rows * keys,
        ),
        **PARAMS,
    )(q, do, k, v, q_place, q_start, k_place)


def to_blocks(weight, cores):
    wd = lax.axis_size("wd")
    rows = weight.shape[0]
    cut = weight.reshape(rows, wd, cores, -1).transpose(2, 1, 0, 3)
    return cut.reshape((cores * wd, rows) + cut.shape[3:])


def columns_out(blocks):
    moved = trade(blocks, ("pipe", "wd"))
    return moved.reshape((2, -1) + moved.shape[2:])


def exchange(piece):
    return [hop(piece, "grp", k) for k in range(1, lax.axis_size("grp"))]


def piece_of(layer, part=None):
    def take(cols):
        rows = cols.shape[1] // 2
        if part is None:
            return exchange(cols[layer])
        return exchange(cols[layer, part * rows : (part + 1) * rows])

    return take


def put_kernel(spots, *refs):
    pieces, out = refs[: len(spots)], refs[len(spots)]
    block = pl.program_id(0)
    for piece, (first, count, col, cols) in zip(pieces, spots):

        def put(piece=piece, col=col, cols=cols):
            out[:, col : col + cols] = piece[...]

        pl.when((block >= first) & (block < first + count))(put)


def put_together(columns):
    block = min([256] + [piece.shape[0] for stack in columns for piece in stack])
    spots, pieces, specs = [], [], []
    col = 0
    for stack in columns:
        first = 0
        for piece in stack:
            count, cols = piece.shape[0] // block, piece.shape[1]
            spots.append((first, count, col, cols))
            pieces.append(piece)

            def at(i, first=first, count=count):
                return (jnp.clip(i - first, 0, count - 1), 0)

            specs.append(pl.BlockSpec((block, cols), at))
            first += count
        col += cols
    return pl.pallas_call(
        lambda *refs: put_kernel(spots, *refs),
        grid=(first,),
        in_specs=specs,
        out_specs=pl.BlockSpec((block, col), lambda i: (i, 0)),
        out_shape=jax.ShapeDtypeStruct((first * block, col), BF),
        cost_estimate=pl.CostEstimate(
            flops=0, bytes_accessed=4 * first * block * col, transcendentals=0
        ),
        **PARAMS,
    )(*pieces)


def stacked(layer):
    def join(cols, *came):
        pieces = [cols[layer]]
        for k in range(len(came[0])):
            pieces += [c[k] for c in came]
        return pieces

    return join


def crossed(pieces):
    return [hop(p, "pipe", 1) for p in pieces]


def pack_attention(w_query, key_matrix, value_matrix, w_output, cores):
    wd = lax.axis_size("wd")
    rows = w_query.shape[0]
    cut = [
        m.reshape(rows, wd, cores, -1) for m in (w_query, key_matrix, value_matrix, w_output.T)
    ]
    return jnp.concatenate(cut, axis=-1).reshape(rows, -1)


def core_order(own, other, axis):
    core = lax.axis_index("pipe")
    return jnp.where(
        core == 0,
        jnp.concatenate([own, other], axis=axis),
        jnp.concatenate([other, own], axis=axis),
    )


def unpack_attention(own, other, widths):
    query_w, kv_w, out_w = widths
    cuts = (query_w, query_w + kv_w, query_w + 2 * kv_w)

    def split(m):
        return (m[:, : cuts[0]], m[:, cuts[0] : cuts[1]], m[:, cuts[1] : cuts[2]], m[:, cuts[2] :])

    q0, k0, v0, o0 = split(own)
    q1, k1, v1, o1 = split(other)
    return (
        jnp.concatenate([q0, q1], axis=1),
        core_order(k0, k1, 1),
        core_order(v0, v1, 1),
        jnp.concatenate([o0, o1], axis=1),
    )


def core_halves(grad):
    half = grad.shape[1] // 2
    core = lax.axis_index("pipe")
    low, high = grad[:, :half], grad[:, half:]
    return (jnp.where(core == 0, low, high), jnp.where(core == 0, high, low))


def grad_pair(own, other):
    total = own + hop(other.astype(BF), "pipe", 1).astype(F32)
    return total.reshape((lax.axis_size("grp"), -1) + total.shape[1:])


def mlp_pair(left, right):
    half = right.shape[1] // 2
    return grad_pair(mm_tl(left, right[:, :half]), mm_tl(left, right[:, half:]))


def grad_part(part):
    def add(blocks):
        rows = blocks.shape[1] // 2
        cut = blocks[:, part * rows : (part + 1) * rows]
        total = cut[0]
        for k in range(1, blocks.shape[0]):
            total = total + hop(cut[k].astype(BF), "grp", k).astype(F32)
        return total.astype(BF)

    return add


def grad_home(low, high):
    wd = lax.axis_size("wd")
    me = lax.axis_index("wd")
    blocks = jnp.concatenate([low, high], axis=0).reshape((wd, -1) + low.shape[1:])
    pieces = [lax.dynamic_index_in_dim(blocks, me, 0, keepdims=False)]
    for k in range(1, wd):
        pieces.append(hop(lax.dynamic_index_in_dim(blocks, me ^ k, 0, keepdims=False), "wd", k))
    return jnp.stack(pieces)


def place_kernel(turned, at_ref, keep_ref, got_ref, out_ref):
    mine = pl.program_id(1) == at_ref[1]

    def put(ref):
        block = ref[0].astype(F32)
        out_ref[...] = block.T if turned else block

    @pl.when(mine)
    def _():
        put(keep_ref)

    @pl.when(jnp.logical_not(mine))
    def _():
        put(got_ref)


def place(keep, got, turned):
    wd, rows, cols = keep.shape
    at = jnp.stack([lax.axis_index("wd"), lax.axis_index("pipe")]).astype(jnp.int32)
    cores = lax.axis_size("pipe")
    source = pl.BlockSpec((1, rows, cols), lambda w, c, at_ref: (w ^ at_ref[0], 0, 0))
    if turned:
        shape, target = (wd * cores * cols, rows), (cols, rows)
        out = pl.BlockSpec(target, lambda w, c, at_ref: (w * cores + c, 0))
    else:
        shape, target = (rows, wd * cores * cols), (rows, cols)
        out = pl.BlockSpec(target, lambda w, c, at_ref: (0, w * cores + c))
    return pl.pallas_call(
        lambda *refs: place_kernel(turned, *refs),
        grid_spec=pltpu.PrefetchScalarGridSpec(
            num_scalar_prefetch=1, grid=(wd, cores), in_specs=[source, source], out_specs=out
        ),
        out_shape=jax.ShapeDtypeStruct(shape, F32),
        cost_estimate=pl.CostEstimate(
            flops=keep.size, bytes_accessed=12 * keep.size, transcendentals=0
        ),
    )(at, keep, got)


def layer_forward(stages, layer, x_rows, gains, where, jobs):
    held = stages.held
    cosine, sine, q_place, q_start, k_place = where
    normed = apply_norm(x_rows, gains[0]).astype(BF)
    rows_a = stages.run(normed, gather_rows, jobs[0])
    w_q, w_k, w_v, w_ot = held["attn", layer]
    tok = rows_a.shape[0]

    def project(rows):
        query = rotary_apply(mm(rows, w_q).reshape(tok, -1, HEAD_SIZE), cosine, sine).astype(BF)
        key = rotary_apply(mm(rows, w_k).reshape(tok, 1, HEAD_SIZE), cosine, sine).astype(BF)[:, 0]
        value = mm(rows, w_v).astype(BF)
        kv = jnp.concatenate([key, value], axis=1)
        return query.transpose(1, 0, 2), jnp.concatenate(others(kv, "grp"), axis=0)

    query, kv_all = stages.run(rows_a, project, jobs[1])
    keys, values = kv_all[:, :HEAD_SIZE], kv_all[:, HEAD_SIZE:]

    def attention(q):
        context = attend(q, keys, values, q_place, q_start, k_place)
        context = context.transpose(1, 0, 2).reshape(tok, -1)
        return context, mm_t(context, w_ot).astype(BF)

    context, partial = stages.run(query, attention, jobs[2])
    mid = stages.run(partial, lambda p: x_rows + sum_rows(p), jobs[3])
    rows_b = stages.run(
        mid, lambda m: gather_rows(apply_norm(m, gains[1]).astype(BF)), jobs[4]
    )
    rows_b = stages.run(rows_b, lambda r: r, jobs[5])
    w_gu = held["gu", layer]

    def ahead(rows):
        both = mm(rows, w_gu)
        half = both.shape[1] // 2
        gate, up = both[:, :half], both[:, half:]
        return gate, up, (jax.nn.silu(gate) * up).astype(BF)

    gate, up, hidden = stages.run(rows_b, ahead, jobs[6])
    return x_rows, rows_a, query, keys, values, context, mid, rows_b, gate, up, hidden


def layer_backward(stages, layer, grad_out, grad_mlp, gains, where, kept, also, jobs):
    held = stages.held
    cosine, sine, q_place, q_start, k_place = where
    x_rows, rows_a, query, keys, values, context, mid, rows_b, gate, up, hidden = kept
    w_q, w_k, w_v, w_ot = held["attn", layer]
    w_gu, w_dt = held["gu", layer], held["down", layer]
    tok = rows_a.shape[0]
    held["rows_b"], held["hidden"] = rows_b, hidden
    held["grad_mlp"] = grad_mlp

    def feed_back(rows):
        grad_hidden = mm(rows, w_dt)
        sig = jax.nn.sigmoid(gate)
        grad_gate = (grad_hidden * up * sig * (1.0 + gate * (1.0 - sig))).astype(BF)
        grad_up = (grad_hidden * gate * sig).astype(BF)
        both = jnp.concatenate([grad_gate, grad_up], axis=1)
        return grad_gate, grad_up, mm_t(both, w_gu).astype(BF), also(hidden)

    grad_gate, grad_up, partial, extra = stages.run(grad_mlp, feed_back, jobs[0])
    held["grad_gate"], held["grad_up"] = grad_gate, grad_up
    grad_b = stages.run(partial, sum_rows, jobs[1])
    grad_mid, gain_b = norm_back(mid, gains[1], grad_b)
    grad_mid = grad_mid + grad_out
    grad_attn = stages.run(grad_mid.astype(BF), gather_rows, jobs[2])

    def attention_back(rows):
        grad_context = mm(rows, w_ot).astype(BF)
        grad_context = grad_context.reshape(tok, -1, HEAD_SIZE).transpose(1, 0, 2)
        return attend_back(query, grad_context, keys, values, q_place, q_start, k_place)

    def keys_back(grads):
        grad_q, grad_k, grad_v = grads
        kv = jnp.concatenate([grad_k, grad_v], axis=1)
        kv = kv.reshape((-1, tok) + kv.shape[1:])
        own_kv = sum_others([kv[k] for k in range(kv.shape[0])], "grp").astype(BF)
        grad_k = own_kv[:, :HEAD_SIZE].astype(F32)
        grad_k = rotary_apply(grad_k[:, None, :], cosine, -sine).astype(BF)[:, 0]
        grad_v = own_kv[:, HEAD_SIZE:]
        grad_q = grad_q.transpose(1, 0, 2).astype(F32)
        grad_q = rotary_apply(grad_q, cosine, -sine).astype(BF).reshape(tok, -1)
        partial = mm_t(grad_q, w_q) + mm_t(grad_k, w_k) + mm_t(grad_v, w_v)
        return grad_q, grad_k, grad_v, partial.astype(BF)

    grads = stages.run(grad_attn, attention_back, jobs[3])
    grad_q, grad_k, grad_v, partial = stages.run(grads, keys_back, jobs[4])

    def attn_pair(g_q, g_k, g_v):
        half_q = g_q.shape[1] // 2
        kv_0, kv_1 = core_halves(g_k)
        v_0, v_1 = core_halves(g_v)

        def term(q_half, k_half, v_half, o_half):
            right = jnp.concatenate([q_half, k_half, v_half], axis=1)
            return jnp.concatenate([mm_tl(rows_a, right), mm_tl(grad_attn, o_half)], axis=1)

        return grad_pair(
            term(g_q[:, :half_q], kv_0, v_0, context[:, :half_q]),
            term(g_q[:, half_q:], kv_1, v_1, context[:, half_q:]),
        )

    held["g_q"], held["g_k"], held["g_v"] = grad_q, grad_k, grad_v
    held["attn_pair"] = attn_pair
    grad_a = stages.run(partial, sum_rows, jobs[5](attn_pair))
    grad_in, gain_a = norm_back(x_rows, gains[0], grad_a)
    return grad_mid + grad_in, jnp.stack([gain_a, gain_b]), extra


def own_layer(first, second):
    core = lax.axis_index("pipe")
    keep = jnp.where(core == 0, first, second)
    return keep, hop(jnp.where(core == 0, second, first), "pipe", 1)


def body(
    block_input,
    cotangent,
    segments,
    norm_gains,
    w_query,
    key_matrix,
    value_matrix,
    w_output,
    w_gate,
    w_up,
    w_down,
):
    core = lax.axis_index("pipe")
    grp = lax.axis_index("grp")
    wd = lax.axis_size("wd")
    groups = lax.axis_size("grp")
    cores = lax.axis_size("pipe")
    tok = block_input.shape[1] * lax.axis_size(CUBE)

    gains = spread_gains(norm_gains[0])

    stages = Stages()
    held = stages.held
    packed = pack_attention(w_query[0], key_matrix[0], value_matrix[0], w_output[0], cores)
    held["attn"] = columns_out(to_blocks(packed, cores))
    held["gate"] = columns_out(to_blocks(w_gate[0], cores))
    held["up_out"] = to_blocks(w_up[0], cores)
    held["down_out"] = to_blocks(w_down[0].T, cores)
    widths = tuple(n // (wd * cores) for n in (w_query.shape[2], key_matrix.shape[2], w_output.shape[1]))

    def move(name):
        return (name, columns_out, (name + "_out",))

    def swap(name, layer, part=None):
        return ((name, layer, part), piece_of(layer, part), (name,))

    def parts(name, layer):
        if name == "attn":
            return (name, (name, layer, None))
        return (name, (name, layer, 0), (name, layer, 1))

    def attn_ready(layer):
        def ready(*values):
            own = stacked(layer)(*values)
            there = crossed(own)
            return unpack_attention(
                jnp.concatenate(own, axis=0), jnp.concatenate(there, axis=0), widths
            )

        return (("attn", layer), ready, parts("attn", layer))

    def cross(name, layer):
        def ready(*values):
            own = stacked(layer)(*values)
            return own, crossed(own)

        return (("cross", name, layer), ready, parts(name, layer))

    def gate_up_ready(layer):
        def ready(gate, up):
            return put_together([gate[0], gate[1], up[0], up[1]])

        return (("gu", layer), ready, (("cross", "gate", layer), ("cross", "up", layer)))

    def down_ready(layer):
        return (("down", layer), lambda d: put_together([d[0], d[1]]), (("cross", "down", layer),))

    seg_row = lax.dynamic_index_in_dim(segments, core, 0, keepdims=False)
    starts = doc_starts(seg_row)
    rows_own = tok // lax.axis_size(CUBE)

    def in_row_order(values):
        values = relative(values, 0, CUBE)
        return jnp.concatenate(
            [values[j * rows_own : (j + 1) * rows_own] for j in ROW_ORDER], axis=0
        )

    local = in_row_order(jnp.arange(tok, dtype=jnp.int32))
    q_place = grp * tok + local
    q_start = in_row_order(lax.dynamic_slice_in_dim(starts, grp * tok, tok))
    cosine, sine = rope_tables(q_place - q_start)
    k_place = jnp.concatenate([(grp ^ k) * tok + local for k in range(groups)])
    where = (cosine, sine, q_place[:, None], q_start[:, None], k_place[None, :])

    rows = relative(lax.dynamic_index_in_dim(block_input, core, 0, keepdims=False), 1, "grp")
    grad = relative(lax.dynamic_index_in_dim(cotangent, core, 0, keepdims=False), 1, "grp")
    held["cotangent"] = grad
    key, job, names = swap("attn", 0)
    held[key] = job(held["attn"])
    ahead = (rows, held[key], held["gate"])
    rows, held[key], held["gate"] = lax.optimization_barrier(ahead)
    kept = [None, None]
    outs = [None, None]
    kept[0] = layer_forward(
        stages,
        0,
        rows.astype(F32),
        gains[0],
        where,
        (
            [attn_ready(0), swap("gate", 0, 0)],
            [move("up"), swap("gate", 0, 1)],
            [move("down"), swap("up", 0, 0)],
            [swap("up", 0, 1), cross("gate", 0)],
            [swap("down", 0, 0), cross("up", 0)],
            [swap("down", 0, 1), gate_up_ready(0)],
            [cross("down", 0)],
        ),
    )

    def close(hidden, layer):
        return (kept[layer][6] + sum_rows(mm_t(hidden, held["down", layer]))).astype(BF)

    hidden = kept[0][-1]
    hidden = stages.run(hidden, lambda h: h, [down_ready(0), swap("attn", 1)])
    outs[0] = stages.run(hidden, lambda h: close(h, 0), [swap("gate", 1, 0)])
    kept[1] = layer_forward(
        stages,
        1,
        outs[0].astype(F32),
        gains[1],
        where,
        (
            [swap("gate", 1, 1), attn_ready(1)],
            [swap("up", 1, 0), ("last", gather_rows, ("cotangent",))],
            [swap("up", 1, 1)],
            [swap("down", 1, 0), cross("gate", 1)],
            [swap("down", 1, 1), cross("up", 1)],
            [gate_up_ready(1)],
            [cross("down", 1)],
        ),
    )
    hidden = stages.run(kept[1][-1], lambda h: h, [down_ready(1)])

    def grad_of(name, layer):
        sources = {
            "down": ("grad_mlp", "hidden"),
            "gate": ("rows_b", "grad_gate"),
            "up": ("rows_b", "grad_up"),
        }[name]
        return (("pair", name, layer), mlp_pair, sources)

    def grad_swap(name, layer, part):
        return (("part", name, layer, part), grad_part(part), (("pair", name, layer),))

    def home(name, layer):
        keys = tuple(("part", name, layer, part) for part in range(2))
        return (("home", name, layer), grad_home, keys)

    def attn_grad(layer):
        return lambda pair: (("pair", "attn", layer), pair, ("g_q", "g_k", "g_v"))

    grads_in = [None, None]
    gain_grads = [None, None]
    grad_in, gain_grads[1], outs[1] = layer_backward(
        stages,
        1,
        grad.astype(F32),
        held["last"],
        gains[1],
        where,
        kept[1][:-1] + (hidden,),
        lambda h: close(h, 1),
        (
            [grad_of("down", 1)],
            [grad_swap("down", 1, 0), grad_of("gate", 1)],
            [grad_swap("down", 1, 1), grad_of("up", 1)],
            [grad_swap("gate", 1, 0)],
            [grad_swap("gate", 1, 1), home("down", 1)],
            lambda pair: [grad_swap("up", 1, 0), attn_grad(1)(pair)],
        ),
    )
    grads_in[1] = grad_in.astype(BF)
    grad_mlp = stages.run(grads_in[1], gather_rows, [grad_swap("up", 1, 1), home("gate", 1)])
    grad_in, gain_grads[0], _ = layer_backward(
        stages,
        0,
        grads_in[1].astype(F32),
        grad_mlp,
        gains[0],
        where,
        kept[0],
        lambda h: (),
        (
            [grad_of("down", 0), grad_swap("attn", 1, 0), grad_swap("attn", 1, 1)],
            [grad_swap("down", 0, 0), grad_of("gate", 0), home("up", 1)],
            [grad_swap("down", 0, 1), grad_of("up", 0)],
            [grad_swap("gate", 0, 0)],
            [grad_swap("gate", 0, 1), home("down", 0)],
            lambda pair: [grad_swap("up", 0, 0), attn_grad(0)(pair), home("gate", 0)],
        ),
    )
    grads_in[0] = grad_in.astype(BF)
    for key, job, names in (
        grad_swap("attn", 0, 0),
        grad_swap("attn", 0, 1),
        home("attn", 1),
        grad_swap("up", 0, 1),
        home("attn", 0),
        home("up", 0),
    ):
        held[key] = job(*[held[name] for name in names])

    def by_batch(pair):
        own, other = own_layer(pair[0], pair[1])
        both = jnp.where(core == 0, jnp.stack([own, other]), jnp.stack([other, own]))
        return relative(both, 2, "grp")[None]

    layer_out = by_batch(outs)
    input_grad = by_batch(grads_in)

    grad_norm_gains = sum_gains(gain_grads)[None]

    def both(name):
        return own_layer(held["home", name, 0], held["home", name, 1])

    keep, got = both("attn")
    cuts = (0, widths[0], widths[0] + widths[1], widths[0] + 2 * widths[1], keep.shape[2])
    q_pair, k_pair, v_pair, o_pair = (
        (keep[..., lo:hi], got[..., lo:hi]) for lo, hi in zip(cuts[:-1], cuts[1:])
    )

    def small(pair):
        order = jnp.where(core == 0, jnp.stack(pair), jnp.stack(pair[::-1]))
        order = relative(order, 1, "wd").transpose(2, 1, 0, 3).astype(F32)
        return order.reshape(order.shape[0], -1)[None]

    grad_wq = place(*q_pair, False)[None]
    grad_wk = small(k_pair)
    grad_wv = small(v_pair)
    grad_wo = place(*o_pair, True)[None]
    grad_wg = place(*both("gate"), False)[None]
    grad_wu = place(*both("up"), False)[None]
    grad_wd = place(*both("down"), True)[None]
    return (
        layer_out,
        input_grad,
        grad_norm_gains,
        grad_wq,
        grad_wk,
        grad_wv,
        grad_wo,
        grad_wg,
        grad_wu,
        grad_wd,
    )


def solution(mesh):
    sizes = dict(mesh.shape)
    wd = KV_HEADS // sizes["tensor"]
    fine = Mesh(
        mesh.devices.reshape(sizes["pipe"], sizes["dp"] // wd, wd, sizes["tensor"]),
        ("pipe", "grp", "wd", "tensor"),
    )
    dp = ("grp", "wd")
    tokens = P(None, dp + ("tensor",), None)
    outs = P("pipe", None, dp + ("tensor",), None)
    gains = P("pipe", None, dp + ("tensor",))
    tall = P("pipe", dp, "tensor")
    wide = P("pipe", "tensor", dp)
    weights = (tall, tall, tall, wide, tall, tall, wide)
    return jax.shard_map(
        body,
        mesh=fine,
        in_specs=(tokens, tokens, P(), gains) + weights,
        out_specs=(outs, outs, gains) + weights,
        check_vma=False,
    )
```

```python
import jax
import jax.numpy as jnp
from jax import lax
from jax.experimental import pallas as pl
from jax.experimental.pallas import tpu as pltpu
from jax.sharding import Mesh, PartitionSpec as P

HEAD_SIZE = 64
KV_HEADS = 8
EPS = 1e-05
ROPE_BASE = 500000.0
NEG_FILL = -1e30
BF = jnp.bfloat16
F32 = jnp.float32
CUBE = ("wd", "tensor")


def rms_scale(row_values):
    return lax.rsqrt(jnp.mean(row_values * row_values, axis=-1, keepdims=True) + EPS)


def apply_norm(row_values, gain_vector):
    return row_values * rms_scale(row_values) * gain_vector


def norm_back(row_values, gain_vector, grad_normed):
    _, pullback = jax.vjp(apply_norm, row_values, gain_vector)
    return pullback(grad_normed)


def doc_starts(seg_row):
    places = jnp.arange(seg_row.shape[0], dtype=jnp.int32)
    before = jnp.concatenate([seg_row[:1] - 1, seg_row[:-1]])
    return lax.cummax(jnp.where(seg_row != before, places, 0), axis=0)


def rope_tables(positions):
    half_dim = HEAD_SIZE // 2
    freqs = ROPE_BASE ** (-(jnp.arange(half_dim, dtype=F32) * 2.0 / HEAD_SIZE))
    angles = positions.astype(F32)[:, None] * freqs[None, :]
    return (jnp.cos(angles), jnp.sin(angles))


def rotary_apply(head_values, cosine_table, sine_values):
    half_dim = head_values.shape[-1] // 2
    first_half = head_values[..., :half_dim]
    second_half = head_values[..., half_dim:]
    cos_rows = cosine_table[:, None, :]
    sin_rows = sine_values[:, None, :]
    return jnp.concatenate(
        [
            first_half * cos_rows - second_half * sin_rows,
            second_half * cos_rows + first_half * sin_rows,
        ],
        axis=-1,
    )


def mm(left, right):
    return jnp.dot(left, right, preferred_element_type=F32)


def mm_t(left, right):
    return lax.dot_general(left, right, (((1,), (1,)), ((), ())), preferred_element_type=F32)


def mm_tl(left, right):
    return lax.dot_general(left, right, (((0,), (0,)), ((), ())), preferred_element_type=F32)


def trade(blocks, axes):
    return lax.all_to_all(blocks, axes, 0, 0, tiled=True)


def hop(block, axis, step):
    size = lax.axis_size(axis)
    return lax.ppermute(block, axis, [(i, i ^ step) for i in range(size)])


def tie(*values):
    return lax.optimization_barrier(values)


def link_steps():
    steps = []
    step = 1
    while step < lax.axis_size(CUBE):
        steps.append(step)
        step *= 2
    return steps


FAR, NEAR, SIDE = 4, 2, 1
ROW_ORDER = (0, FAR, NEAR, FAR | NEAR, SIDE, FAR | SIDE, NEAR | SIDE, FAR | NEAR | SIDE)


def cube(block, step):
    return hop(block, CUBE, step)


def join_kernel(left_ref, left_came_ref, right_ref, right_came_ref, out_ref):
    half = left_ref.shape[1]
    block = pl.program_id(0)

    @pl.when(block < 2)
    def _():
        out_ref[:, :half] = left_ref[...]

    @pl.when(block >= 2)
    def _():
        out_ref[:, :half] = left_came_ref[...]

    @pl.when(block % 2 == 0)
    def _():
        out_ref[:, half:] = right_ref[...]

    @pl.when(block % 2 == 1)
    def _():
        out_ref[:, half:] = right_came_ref[...]


def join_halves(left, left_came, right, right_came):
    rows, half = left.shape[0] // 2, left.shape[1]

    def spec(place):
        return pl.BlockSpec((rows, half), lambda i: (place(i), 0))

    return pl.pallas_call(
        join_kernel,
        grid=(4,),
        in_specs=[
            spec(lambda i: jnp.minimum(i, 1)),
            spec(lambda i: jnp.maximum(i - 2, 0)),
            spec(lambda i: i // 2),
            spec(lambda i: i // 2),
        ],
        out_specs=pl.BlockSpec((rows, 2 * half), lambda i: (i, 0)),
        out_shape=jax.ShapeDtypeStruct((4 * rows, 2 * half), left.dtype),
        cost_estimate=pl.CostEstimate(
            flops=0, bytes_accessed=32 * rows * half, transcendentals=0
        ),
    )(left, left_came, right, right_came)


def gather_rows(rows):
    two = jnp.concatenate([rows, cube(rows, FAR)], axis=0)
    half = two.shape[1] // 2
    left, right = two[:, :half], two[:, half:]
    left_came, right_came = cube(left, NEAR), cube(right, SIDE)
    left = jnp.concatenate([left, left_came], axis=0)
    right = jnp.concatenate([right, right_came], axis=0)
    return join_halves(left, cube(left, SIDE), right, cube(right, NEAR))


def sum_rows(partial):
    partial = partial.astype(BF)
    n, half = partial.shape[0] // 4, partial.shape[1] // 2
    left, right = partial[:, :half], partial[:, half:]
    left_came = cube(left[2 * n :], SIDE)
    right_came = cube(jnp.concatenate([right[n : 2 * n], right[3 * n :]], axis=0), NEAR)
    left = left[: 2 * n].astype(F32) + left_came.astype(F32)
    right_came = right_came.astype(F32)
    low = right[:n].astype(F32) + right_came[:n]
    high = right[2 * n : 3 * n].astype(F32) + right_came[n:]
    left_came = cube(left[n:].astype(BF), NEAR)
    right_came = cube(high.astype(BF), SIDE)
    left = left[:n] + left_came.astype(F32)
    right = low + right_came.astype(F32)
    both = jnp.concatenate([left, right], axis=1)
    rows = n // 2
    return both[:rows] + cube(both[rows:].astype(BF), FAR).astype(F32)


class Stages:
    def __init__(self):
        self.held = {}

    def run(self, value, step, jobs):
        needed = [[self.held[name] for name in names] for _, _, names in jobs]
        value, needed = lax.optimization_barrier((value, needed))
        out = step(value)
        made = [job(*inputs) for (_, job, _), inputs in zip(jobs, needed)]
        out, made = lax.optimization_barrier((out, made))
        self.held.update((key, result) for (key, _, _), result in zip(jobs, made))
        return out


def others(block, axis):
    return [block] + [hop(block, axis, k) for k in range(1, lax.axis_size(axis))]


def sum_others(blocks, axis):
    total = blocks[0].astype(F32)
    for k in range(1, lax.axis_size(axis)):
        total = total + hop(blocks[k].astype(BF), axis, k).astype(F32)
    return total


def relative(values, dim, axis):
    count = lax.axis_size(axis)
    me = lax.axis_index(axis)
    step = 1
    while step < count:
        shape = values.shape
        cut = shape[:dim] + (count // (2 * step), 2, step * (shape[dim] // count)) + shape[dim + 1 :]
        view = values.reshape(cut)
        swapped = jnp.concatenate(
            [lax.slice_in_dim(view, 1, 2, axis=dim + 1), lax.slice_in_dim(view, 0, 1, axis=dim + 1)],
            axis=dim + 1,
        )
        values = jnp.where((me & step) != 0, swapped.reshape(shape), values)
        step *= 2
    return values


def spread_gains(norm_gains):
    me = lax.axis_index(CUBE)
    gain = norm_gains
    for step in link_steps():
        came = hop(gain, CUBE, step)
        gain = jnp.where(
            (me & step) != 0,
            jnp.concatenate([came, gain], axis=1),
            jnp.concatenate([gain, came], axis=1),
        )
    gain = jnp.concatenate(others(gain, "grp"), axis=1)
    other = hop(gain, "pipe", 1)
    core = lax.axis_index("pipe")
    return [jnp.where(core == 0, gain, other), jnp.where(core == 0, other, gain)]


def sum_gains(grads):
    me = lax.axis_index(CUBE)
    keep, extra = own_layer(grads[0], grads[1])
    total = (keep + extra).reshape(2, lax.axis_size("grp"), -1)
    mine = total[:, 0]
    for k in range(1, total.shape[1]):
        mine = mine + hop(total[:, k], "grp", k)
    for step in link_steps()[::-1]:
        half = mine.shape[1] // 2
        low, high = mine[:, :half], mine[:, half:]
        odd = (me & step) != 0
        mine = jnp.where(odd, high, low) + hop(jnp.where(odd, low, high), CUBE, step)
    return mine


def masked_probs(q, k, q_place, q_start, k_place):
    scores = lax.dot_general(q, k, (((1,), (1,)), ((), ())), preferred_element_type=F32)
    scores = scores * HEAD_SIZE ** (-0.5)
    allowed = (k_place <= q_place) & (k_place >= q_start)
    masked = jnp.where(allowed, scores, NEG_FILL)
    exps = jnp.exp(masked - jnp.max(masked, axis=-1, keepdims=True))
    return exps / jnp.sum(exps, axis=-1, keepdims=True)


def attend_kernel(q_ref, k_ref, v_ref, qp_ref, qs_ref, kp_ref, o_ref):
    probs = masked_probs(q_ref[0], k_ref[...], qp_ref[...], qs_ref[...], kp_ref[...])
    o_ref[0] = jnp.dot(probs.astype(BF), v_ref[...], preferred_element_type=F32).astype(BF)


def attend_back_kernel(q_ref, do_ref, k_ref, v_ref, qp_ref, qs_ref, kp_ref, dq_ref, dk_ref, dv_ref):
    @pl.when((pl.program_id(0) == 0) & (pl.program_id(1) == 0))
    def _():
        dk_ref[...] = jnp.zeros_like(dk_ref)
        dv_ref[...] = jnp.zeros_like(dv_ref)

    q = q_ref[0]
    do = do_ref[0]
    k = k_ref[...]
    probs = masked_probs(q, k, qp_ref[...], qs_ref[...], kp_ref[...])
    grad_probs = lax.dot_general(do, v_ref[...], (((1,), (1,)), ((), ())), preferred_element_type=F32)
    delta = jnp.sum(probs * grad_probs, axis=-1, keepdims=True)
    grad_scores = (probs * (grad_probs - delta) * HEAD_SIZE ** (-0.5)).astype(BF)
    dq_ref[0] = jnp.dot(grad_scores, k, preferred_element_type=F32).astype(BF)
    dk_ref[...] += lax.dot_general(
        grad_scores, q, (((0,), (0,)), ((), ())), preferred_element_type=F32
    )
    dv_ref[...] += lax.dot_general(
        probs.astype(BF), do, (((0,), (0,)), ((), ())), preferred_element_type=F32
    )


def attention_specs(heads, rows, keys):
    rows_blk = max(16, min(rows, (512 * 1024) // keys))
    per_head = pl.BlockSpec((1, rows_blk, HEAD_SIZE), lambda b, h: (h, b, 0))
    full = pl.BlockSpec((keys, HEAD_SIZE), lambda b, h: (0, 0))
    row_info = pl.BlockSpec((rows_blk, 1), lambda b, h: (b, 0))
    key_info = pl.BlockSpec((1, keys), lambda b, h: (0, 0))
    return ((rows // rows_blk, heads), per_head, full, row_info, key_info)


PARAMS = dict(
    compiler_params=pltpu.CompilerParams(vmem_limit_bytes=50 * 1024 * 1024),
)


def attend(q, k, v, q_place, q_start, k_place):
    heads, rows, _ = q.shape
    keys = k.shape[0]
    grid, per_head, full, row_info, key_info = attention_specs(heads, rows, keys)
    return pl.pallas_call(
        attend_kernel,
        grid=grid,
        in_specs=[per_head, full, full, row_info, row_info, key_info],
        out_specs=per_head,
        out_shape=jax.ShapeDtypeStruct(q.shape, BF),
        cost_estimate=pl.CostEstimate(
            flops=4 * heads * rows * keys * HEAD_SIZE,
            bytes_accessed=4 * q.size + 4 * k.size,
            transcendentals=heads * rows * keys,
        ),
        **PARAMS,
    )(q, k, v, q_place, q_start, k_place)


def attend_back(q, do, k, v, q_place, q_start, k_place):
    heads, rows, _ = q.shape
    keys = k.shape[0]
    grid, per_head, full, row_info, key_info = attention_specs(heads, rows, keys)
    return pl.pallas_call(
        attend_back_kernel,
        grid=grid,
        in_specs=[per_head, per_head, full, full, row_info, row_info, key_info],
        out_specs=[per_head, full, full],
        out_shape=[
            jax.ShapeDtypeStruct(q.shape, BF),
            jax.ShapeDtypeStruct(k.shape, F32),
            jax.ShapeDtypeStruct(k.shape, F32),
        ],
        cost_estimate=pl.CostEstimate(
            flops=10 * heads * rows * keys * HEAD_SIZE,
            bytes_accessed=6 * q.size + 12 * k.size,
            transcendentals=heads * rows * keys,
        ),
        **PARAMS,
    )(q, do, k, v, q_place, q_start, k_place)


def to_blocks(weight, cores):
    wd = lax.axis_size("wd")
    rows = weight.shape[0]
    cut = weight.reshape(rows, wd, cores, -1).transpose(2, 1, 0, 3)
    return cut.reshape((cores * wd, rows) + cut.shape[3:])


def columns_out(blocks):
    moved = trade(blocks, ("pipe", "wd"))
    return moved.reshape((2, -1) + moved.shape[2:])


def exchange(piece):
    return [hop(piece, "grp", k) for k in range(1, lax.axis_size("grp"))]


def piece_of(layer, part=None):
    def take(cols):
        rows = cols.shape[1] // 2
        if part is None:
            return exchange(cols[layer])
        return exchange(cols[layer, part * rows : (part + 1) * rows])

    return take


def put_kernel(spots, *refs):
    pieces, out = refs[: len(spots)], refs[len(spots)]
    block = pl.program_id(0)
    for piece, (first, count, col, cols) in zip(pieces, spots):

        def put(piece=piece, col=col, cols=cols):
            out[:, col : col + cols] = piece[...]

        pl.when((block >= first) & (block < first + count))(put)


def put_together(columns):
    block = min([256] + [piece.shape[0] for stack in columns for piece in stack])
    spots, pieces, specs = [], [], []
    col = 0
    for stack in columns:
        first = 0
        for piece in stack:
            count, cols = piece.shape[0] // block, piece.shape[1]
            spots.append((first, count, col, cols))
            pieces.append(piece)

            def at(i, first=first, count=count):
                return (jnp.clip(i - first, 0, count - 1), 0)

            specs.append(pl.BlockSpec((block, cols), at))
            first += count
        col += cols
    return pl.pallas_call(
        lambda *refs: put_kernel(spots, *refs),
        grid=(first,),
        in_specs=specs,
        out_specs=pl.BlockSpec((block, col), lambda i: (i, 0)),
        out_shape=jax.ShapeDtypeStruct((first * block, col), BF),
        cost_estimate=pl.CostEstimate(
            flops=0, bytes_accessed=4 * first * block * col, transcendentals=0
        ),
        **PARAMS,
    )(*pieces)


def stacked(layer):
    def join(cols, *came):
        pieces = [cols[layer]]
        for k in range(len(came[0])):
            pieces += [c[k] for c in came]
        return pieces

    return join


def crossed(pieces):
    return [hop(p, "pipe", 1) for p in pieces]


def pack_attention(w_query, key_matrix, value_matrix, w_output, cores):
    wd = lax.axis_size("wd")
    rows = w_query.shape[0]
    cut = [
        m.reshape(rows, wd, cores, -1) for m in (w_query, key_matrix, value_matrix, w_output.T)
    ]
    return jnp.concatenate(cut, axis=-1).reshape(rows, -1)


def core_order(own, other, axis):
    core = lax.axis_index("pipe")
    return jnp.where(
        core == 0,
        jnp.concatenate([own, other], axis=axis),
        jnp.concatenate([other, own], axis=axis),
    )


def unpack_attention(own, other, widths):
    query_w, kv_w, out_w = widths
    cuts = (query_w, query_w + kv_w, query_w + 2 * kv_w)

    def split(m):
        return (m[:, : cuts[0]], m[:, cuts[0] : cuts[1]], m[:, cuts[1] : cuts[2]], m[:, cuts[2] :])

    q0, k0, v0, o0 = split(own)
    q1, k1, v1, o1 = split(other)
    return (
        jnp.concatenate([q0, q1], axis=1),
        core_order(k0, k1, 1),
        core_order(v0, v1, 1),
        jnp.concatenate([o0, o1], axis=1),
    )


def core_halves(grad):
    half = grad.shape[1] // 2
    core = lax.axis_index("pipe")
    low, high = grad[:, :half], grad[:, half:]
    return (jnp.where(core == 0, low, high), jnp.where(core == 0, high, low))


def grad_pair(own, other):
    total = own + hop(other.astype(BF), "pipe", 1).astype(F32)
    return total.reshape((lax.axis_size("grp"), -1) + total.shape[1:])


def mlp_pair(left, right):
    half = right.shape[1] // 2
    return grad_pair(mm_tl(left, right[:, :half]), mm_tl(left, right[:, half:]))


def grad_part(part):
    def add(blocks):
        rows = blocks.shape[1] // 2
        cut = blocks[:, part * rows : (part + 1) * rows]
        total = cut[0]
        for k in range(1, blocks.shape[0]):
            total = total + hop(cut[k].astype(BF), "grp", k).astype(F32)
        return total.astype(BF)

    return add


def grad_home(low, high):
    wd = lax.axis_size("wd")
    me = lax.axis_index("wd")
    blocks = jnp.concatenate([low, high], axis=0).reshape((wd, -1) + low.shape[1:])
    pieces = [lax.dynamic_index_in_dim(blocks, me, 0, keepdims=False)]
    for k in range(1, wd):
        pieces.append(hop(lax.dynamic_index_in_dim(blocks, me ^ k, 0, keepdims=False), "wd", k))
    return jnp.stack(pieces)


def place_kernel(turned, at_ref, keep_ref, got_ref, out_ref):
    mine = pl.program_id(1) == at_ref[1]

    def put(ref):
        block = ref[0].astype(F32)
        out_ref[...] = block.T if turned else block

    @pl.when(mine)
    def _():
        put(keep_ref)

    @pl.when(jnp.logical_not(mine))
    def _():
        put(got_ref)


def place(keep, got, turned):
    wd, rows, cols = keep.shape
    at = jnp.stack([lax.axis_index("wd"), lax.axis_index("pipe")]).astype(jnp.int32)
    cores = lax.axis_size("pipe")
    source = pl.BlockSpec((1, rows, cols), lambda w, c, at_ref: (w ^ at_ref[0], 0, 0))
    if turned:
        shape, target = (wd * cores * cols, rows), (cols, rows)
        out = pl.BlockSpec(target, lambda w, c, at_ref: (w * cores + c, 0))
    else:
        shape, target = (rows, wd * cores * cols), (rows, cols)
        out = pl.BlockSpec(target, lambda w, c, at_ref: (0, w * cores + c))
    return pl.pallas_call(
        lambda *refs: place_kernel(turned, *refs),
        grid_spec=pltpu.PrefetchScalarGridSpec(
            num_scalar_prefetch=1, grid=(wd, cores), in_specs=[source, source], out_specs=out
        ),
        out_shape=jax.ShapeDtypeStruct(shape, F32),
        cost_estimate=pl.CostEstimate(
            flops=keep.size, bytes_accessed=12 * keep.size, transcendentals=0
        ),
    )(at, keep, got)


def layer_forward(stages, layer, x_rows, gains, where, jobs):
    held = stages.held
    cosine, sine, q_place, q_start, k_place = where
    normed = apply_norm(x_rows, gains[0]).astype(BF)
    rows_a = stages.run(normed, gather_rows, jobs[0])
    w_q, w_k, w_v, w_ot = held["attn", layer]
    tok = rows_a.shape[0]

    def project(rows):
        key = rotary_apply(mm(rows, w_k).reshape(tok, 1, HEAD_SIZE), cosine, sine).astype(BF)[:, 0]
        value = mm(rows, w_v).astype(BF)
        return jnp.concatenate([key, value], axis=1)

    def queries(rows):
        query = rotary_apply(mm(rows, w_q).reshape(tok, -1, HEAD_SIZE), cosine, sine).astype(BF)
        return query.transpose(1, 0, 2)

    held["rows_a"] = rows_a
    kv_all = stages.run(
        project(rows_a),
        lambda kv: jnp.concatenate(others(kv, "grp"), axis=0),
        [("query", queries, ("rows_a",))] + jobs[1],
    )
    query = held["query"]
    keys, values = kv_all[:, :HEAD_SIZE], kv_all[:, HEAD_SIZE:]

    def attention(q):
        context = attend(q, keys, values, q_place, q_start, k_place)
        context = context.transpose(1, 0, 2).reshape(tok, -1)
        return context, mm_t(context, w_ot).astype(BF)

    context, partial = stages.run(query, attention, jobs[2])
    mid = stages.run(partial, lambda p: x_rows + sum_rows(p), jobs[3])
    rows_b = stages.run(
        mid, lambda m: gather_rows(apply_norm(m, gains[1]).astype(BF)), jobs[4]
    )
    rows_b = stages.run(rows_b, lambda r: r, jobs[5])
    w_gu = held["gu", layer]

    def ahead(rows):
        both = mm(rows, w_gu)
        half = both.shape[1] // 2
        gate, up = both[:, :half], both[:, half:]
        return gate, up, (jax.nn.silu(gate) * up).astype(BF)

    gate, up, hidden = stages.run(rows_b, ahead, jobs[6])
    return x_rows, rows_a, query, keys, values, context, mid, rows_b, gate, up, hidden


def layer_backward(stages, layer, grad_out, grad_mlp, gains, where, kept, also, jobs):
    held = stages.held
    cosine, sine, q_place, q_start, k_place = where
    x_rows, rows_a, query, keys, values, context, mid, rows_b, gate, up, hidden = kept
    w_q, w_k, w_v, w_ot = held["attn", layer]
    w_gu, w_dt = held["gu", layer], held["down", layer]
    tok = rows_a.shape[0]
    held["rows_b"], held["hidden"], held["grad_mlp"] = rows_b, hidden, grad_mlp

    def feed_back(rows):
        grad_hidden = mm(rows, w_dt)
        sig = jax.nn.sigmoid(gate)
        grad_gate = (grad_hidden * up * sig * (1.0 + gate * (1.0 - sig))).astype(BF)
        grad_up = (grad_hidden * gate * sig).astype(BF)
        both = jnp.concatenate([grad_gate, grad_up], axis=1)
        return grad_gate, grad_up, mm_t(both, w_gu).astype(BF), also(hidden)

    grad_gate, grad_up, partial, extra = stages.run(grad_mlp, feed_back, jobs[0])
    held["grad_gate"], held["grad_up"] = grad_gate, grad_up
    grad_b = stages.run(partial, sum_rows, jobs[1])
    grad_mid, gain_b = norm_back(mid, gains[1], grad_b)
    grad_mid = grad_mid + grad_out
    grad_attn = stages.run(grad_mid.astype(BF), gather_rows, jobs[2])

    def attention_back(rows):
        grad_context = mm(rows, w_ot).astype(BF)
        grad_context = grad_context.reshape(tok, -1, HEAD_SIZE).transpose(1, 0, 2)
        return attend_back(query, grad_context, keys, values, q_place, q_start, k_place)

    def keys_back(grads):
        kv = jnp.concatenate(grads, axis=1)
        kv = kv.reshape((-1, tok) + kv.shape[1:])
        return sum_others([kv[k] for k in range(kv.shape[0])], "grp").astype(BF)

    def queries_back(grad_q):
        grad_q = grad_q.transpose(1, 0, 2).astype(F32)
        grad_q = rotary_apply(grad_q, cosine, -sine).astype(BF).reshape(tok, -1)
        return grad_q, mm_t(grad_q, w_q)

    held["grad_q"], *grads = stages.run(grad_attn, attention_back, jobs[3])
    own_kv = stages.run(grads, keys_back, [("g_q", queries_back, ("grad_q",))] + jobs[4])
    grad_q, partial = held["g_q"]
    grad_k = own_kv[:, :HEAD_SIZE].astype(F32)
    grad_k = rotary_apply(grad_k[:, None, :], cosine, -sine).astype(BF)[:, 0]
    grad_v = own_kv[:, HEAD_SIZE:]
    partial = (partial + mm_t(grad_k, w_k) + mm_t(grad_v, w_v)).astype(BF)

    def attn_pair(g_q, g_k, g_v):
        half_q = g_q.shape[1] // 2
        kv_0, kv_1 = core_halves(g_k)
        v_0, v_1 = core_halves(g_v)

        def term(q_half, k_half, v_half, o_half):
            right = jnp.concatenate([q_half, k_half, v_half], axis=1)
            return jnp.concatenate([mm_tl(rows_a, right), mm_tl(grad_attn, o_half)], axis=1)

        return grad_pair(
            term(g_q[:, :half_q], kv_0, v_0, context[:, :half_q]),
            term(g_q[:, half_q:], kv_1, v_1, context[:, half_q:]),
        )

    held["g_q"], held["g_k"], held["g_v"] = grad_q, grad_k, grad_v
    grad_a = stages.run(partial, sum_rows, jobs[5](attn_pair))
    grad_in, gain_a = norm_back(x_rows, gains[0], grad_a)
    return grad_mid + grad_in, jnp.stack([gain_a, gain_b]), extra


def own_layer(first, second):
    core = lax.axis_index("pipe")
    keep = jnp.where(core == 0, first, second)
    return keep, hop(jnp.where(core == 0, second, first), "pipe", 1)


def body(
    block_input,
    cotangent,
    segments,
    norm_gains,
    w_query,
    key_matrix,
    value_matrix,
    w_output,
    w_gate,
    w_up,
    w_down,
):
    core = lax.axis_index("pipe")
    grp = lax.axis_index("grp")
    wd = lax.axis_size("wd")
    groups = lax.axis_size("grp")
    cores = lax.axis_size("pipe")
    tok = block_input.shape[1] * lax.axis_size(CUBE)

    stages = Stages()
    held = stages.held
    packed = pack_attention(w_query[0], key_matrix[0], value_matrix[0], w_output[0], cores)
    attn_cols = columns_out(to_blocks(packed, cores))
    held["attn"], first_gains = lax.optimization_barrier((attn_cols, norm_gains[0]))
    gains = spread_gains(first_gains)
    held["gate_out"] = to_blocks(w_gate[0], cores)
    held["up_out"] = to_blocks(w_up[0], cores)
    held["down_out"] = to_blocks(w_down[0].T, cores)
    widths = tuple(n // (wd * cores) for n in (w_query.shape[2], key_matrix.shape[2], w_output.shape[1]))

    def move(name):
        return (name, columns_out, (name + "_out",))

    def swap(name, layer, part=None):
        return ((name, layer, part), piece_of(layer, part), (name,))

    def parts(name, layer):
        if name == "attn":
            return (name, (name, layer, None))
        return (name, (name, layer, 0), (name, layer, 1))

    def attn_ready(layer):
        def ready(*values):
            own = stacked(layer)(*values)
            there = crossed(own)
            return unpack_attention(
                jnp.concatenate(own, axis=0), jnp.concatenate(there, axis=0), widths
            )

        return (("attn", layer), ready, parts("attn", layer))

    def cross(name, layer):
        def ready(*values):
            own = stacked(layer)(*values)
            return own, crossed(own)

        return (("cross", name, layer), ready, parts(name, layer))

    def gate_up_ready(layer):
        def ready(gate, up):
            return put_together([gate[0], gate[1], up[0], up[1]])

        return (("gu", layer), ready, (("cross", "gate", layer), ("cross", "up", layer)))

    def down_ready(layer):
        return (("down", layer), lambda d: put_together([d[0], d[1]]), (("cross", "down", layer),))

    seg_row = lax.dynamic_index_in_dim(segments, core, 0, keepdims=False)
    starts = doc_starts(seg_row)
    rows_own = tok // lax.axis_size(CUBE)

    def in_row_order(values):
        values = relative(values, 0, CUBE)
        return jnp.concatenate(
            [values[j * rows_own : (j + 1) * rows_own] for j in ROW_ORDER], axis=0
        )

    local = in_row_order(jnp.arange(tok, dtype=jnp.int32))
    q_place = grp * tok + local
    q_start = in_row_order(lax.dynamic_slice_in_dim(starts, grp * tok, tok))
    cosine, sine = rope_tables(q_place - q_start)
    k_place = jnp.concatenate([(grp ^ k) * tok + local for k in range(groups)])
    where = (cosine, sine, q_place[:, None], q_start[:, None], k_place[None, :])

    rows = relative(lax.dynamic_index_in_dim(block_input, core, 0, keepdims=False), 1, "grp")
    grad = relative(lax.dynamic_index_in_dim(cotangent, core, 0, keepdims=False), 1, "grp")
    held["cotangent"] = grad
    key, job, names = swap("attn", 0)
    held[key] = job(held["attn"])
    rows, held[key], gains = lax.optimization_barrier((rows, held[key], gains))
    kept = [None, None]
    outs = [None, None]
    kept[0] = layer_forward(
        stages,
        0,
        rows.astype(F32),
        gains[0],
        where,
        (
            [attn_ready(0), swap("attn", 1), move("gate")],
            [swap("gate", 0, 0), move("up")],
            [swap("gate", 0, 1), move("down")],
            [swap("up", 0, 0), swap("up", 0, 1)],
            [swap("down", 0, 0), cross("gate", 0), cross("up", 0)],
            [swap("down", 0, 1), gate_up_ready(0)],
            [cross("down", 0)],
        ),
    )

    def close(hidden, layer):
        return (kept[layer][6] + sum_rows(mm_t(hidden, held["down", layer]))).astype(BF)

    hidden = kept[0][-1]
    hidden = stages.run(hidden, lambda h: h, [down_ready(0)])
    outs[0] = stages.run(hidden, lambda h: close(h, 0), [swap("gate", 1, 0)])
    kept[1] = layer_forward(
        stages,
        1,
        outs[0].astype(F32),
        gains[1],
        where,
        (
            [swap("gate", 1, 1), attn_ready(1)],
            [swap("up", 1, 0)],
            [swap("up", 1, 1), ("last", gather_rows, ("cotangent",))],
            [swap("down", 1, 0), cross("gate", 1)],
            [swap("down", 1, 1), cross("up", 1)],
            [gate_up_ready(1)],
            [cross("down", 1)],
        ),
    )

    def grad_of(name, layer):
        sources = {
            "down": ("grad_mlp", "hidden"),
            "gate": ("rows_b", "grad_gate"),
            "up": ("rows_b", "grad_up"),
        }[name]
        return (("pair", name, layer), mlp_pair, sources)

    def grad_swap(name, layer, part):
        return (("part", name, layer, part), grad_part(part), (("pair", name, layer),))

    def home(name, layer):
        keys = tuple(("part", name, layer, part) for part in range(2))
        return (("home", name, layer), grad_home, keys)

    def attn_grad(layer):
        return lambda pair: (("pair", "attn", layer), pair, ("g_q", "g_k", "g_v"))

    def final(name, turned):
        def ready(first, second):
            return place(*own_layer(first, second), turned)

        return (("final", name), ready, (("home", name, 0), ("home", name, 1)))

    held["hidden"], held["grad_mlp"] = kept[1][-1], held["last"]
    hidden = stages.run(kept[1][-1], lambda h: h, [down_ready(1), grad_of("down", 1)])

    grads_in = [None, None]
    gain_grads = [None, None]
    grad_in, gain_grads[1], outs[1] = layer_backward(
        stages,
        1,
        grad.astype(F32),
        held["last"],
        gains[1],
        where,
        kept[1][:-1] + (hidden,),
        lambda h: close(h, 1),
        (
            [grad_swap("down", 1, 0)],
            [grad_swap("down", 1, 1), grad_of("gate", 1)],
            [grad_of("up", 1), home("down", 1)],
            [grad_swap("gate", 1, 0)],
            [grad_swap("gate", 1, 1)],
            lambda pair: [grad_swap("up", 1, 0), attn_grad(1)(pair)],
        ),
    )
    grads_in[1] = grad_in.astype(BF)
    grad_mlp = stages.run(grads_in[1], gather_rows, [grad_swap("up", 1, 1), home("gate", 1)])
    grad_in, gain_grads[0], _ = layer_backward(
        stages,
        0,
        grads_in[1].astype(F32),
        grad_mlp,
        gains[0],
        where,
        kept[0],
        lambda h: (),
        (
            [grad_of("down", 0), grad_swap("attn", 1, 0), grad_swap("attn", 1, 1)],
            [grad_swap("down", 0, 0), grad_of("gate", 0), home("up", 1)],
            [grad_swap("down", 0, 1), grad_of("up", 0)],
            [grad_swap("gate", 0, 0), home("attn", 1)],
            [grad_swap("gate", 0, 1), home("down", 0)],
            lambda pair: [grad_swap("up", 0, 0), attn_grad(0)(pair), final("down", True)],
        ),
    )
    grads_in[0] = grad_in.astype(BF)
    tail = grads_in[0]
    for jobs in (
        [grad_swap("attn", 0, 0), grad_swap("attn", 0, 1), home("gate", 0)],
        [grad_swap("up", 0, 1), home("attn", 0), final("gate", False)],
        [home("up", 0)],
    ):
        tail = stages.run(tail, lambda t: t, jobs)

    def by_batch(pair):
        own, other = own_layer(pair[0], pair[1])
        both = jnp.where(core == 0, jnp.stack([own, other]), jnp.stack([other, own]))
        return relative(both, 2, "grp")[None]

    layer_out = by_batch(outs)
    input_grad = by_batch(grads_in)

    grad_norm_gains = sum_gains(gain_grads)[None]

    def both(name):
        return own_layer(held["home", name, 0], held["home", name, 1])

    keep, got = both("attn")
    cuts = (0, widths[0], widths[0] + widths[1], widths[0] + 2 * widths[1], keep.shape[2])
    q_pair, k_pair, v_pair, o_pair = (
        (keep[..., lo:hi], got[..., lo:hi]) for lo, hi in zip(cuts[:-1], cuts[1:])
    )

    def small(pair):
        order = jnp.where(core == 0, jnp.stack(pair), jnp.stack(pair[::-1]))
        order = relative(order, 1, "wd").transpose(2, 1, 0, 3).astype(F32)
        return order.reshape(order.shape[0], -1)[None]

    grad_wq = place(*q_pair, False)[None]
    grad_wk = small(k_pair)
    grad_wv = small(v_pair)
    grad_wo = place(*o_pair, True)[None]
    grad_wg = held["final", "gate"][None]
    grad_wu = place(*both("up"), False)[None]
    grad_wd = held["final", "down"][None]
    return (
        layer_out,
        input_grad,
        grad_norm_gains,
        grad_wq,
        grad_wk,
        grad_wv,
        grad_wo,
        grad_wg,
        grad_wu,
        grad_wd,
    )


def solution(mesh):
    sizes = dict(mesh.shape)
    wd = KV_HEADS // sizes["tensor"]
    fine = Mesh(
        mesh.devices.reshape(sizes["pipe"], sizes["dp"] // wd, wd, sizes["tensor"]),
        ("pipe", "grp", "wd", "tensor"),
    )
    dp = ("grp", "wd")
    tokens = P(None, dp + ("tensor",), None)
    outs = P("pipe", None, dp + ("tensor",), None)
    gains = P("pipe", None, dp + ("tensor",))
    tall = P("pipe", dp, "tensor")
    wide = P("pipe", "tensor", dp)
    weights = (tall, tall, tall, wide, tall, tall, wide)
    return jax.shard_map(
        body,
        mesh=fine,
        in_specs=(tokens, tokens, P(), gains) + weights,
        out_specs=(outs, outs, gains) + weights,
        check_vma=False,
    )
```

```python
import jax
import jax.numpy as jnp
from jax import lax
from jax.experimental import pallas as pl
from jax.experimental.pallas import tpu as pltpu
from jax.sharding import Mesh, PartitionSpec as P

HEAD_SIZE = 64
KV_HEADS = 8
EPS = 1e-05
ROPE_BASE = 500000.0
NEG_FILL = -1e30
BF = jnp.bfloat16
F32 = jnp.float32
CUBE = ("wd", "tensor")


def rms_scale(row_values):
    return lax.rsqrt(jnp.mean(row_values * row_values, axis=-1, keepdims=True) + EPS)


def apply_norm(row_values, gain_vector):
    return row_values * rms_scale(row_values) * gain_vector


def norm_back(row_values, gain_vector, grad_normed):
    _, pullback = jax.vjp(apply_norm, row_values, gain_vector)
    return pullback(grad_normed)


def doc_starts(seg_row):
    places = jnp.arange(seg_row.shape[0], dtype=jnp.int32)
    before = jnp.concatenate([seg_row[:1] - 1, seg_row[:-1]])
    return lax.cummax(jnp.where(seg_row != before, places, 0), axis=0)


def rope_tables(positions):
    half_dim = HEAD_SIZE // 2
    freqs = ROPE_BASE ** (-(jnp.arange(half_dim, dtype=F32) * 2.0 / HEAD_SIZE))
    angles = positions.astype(F32)[:, None] * freqs[None, :]
    return (jnp.cos(angles), jnp.sin(angles))


def rotary_apply(head_values, cosine_table, sine_values):
    half_dim = head_values.shape[-1] // 2
    first_half = head_values[..., :half_dim]
    second_half = head_values[..., half_dim:]
    cos_rows = cosine_table[:, None, :]
    sin_rows = sine_values[:, None, :]
    return jnp.concatenate(
        [
            first_half * cos_rows - second_half * sin_rows,
            second_half * cos_rows + first_half * sin_rows,
        ],
        axis=-1,
    )


def mm(left, right):
    return jnp.dot(left, right, preferred_element_type=F32)


def mm_t(left, right):
    return lax.dot_general(left, right, (((1,), (1,)), ((), ())), preferred_element_type=F32)


def mm_tl(left, right):
    return lax.dot_general(left, right, (((0,), (0,)), ((), ())), preferred_element_type=F32)


def trade(blocks, axes):
    return lax.all_to_all(blocks, axes, 0, 0, tiled=True)


def hop(block, axis, step):
    size = lax.axis_size(axis)
    return lax.ppermute(block, axis, [(i, i ^ step) for i in range(size)])


def tie(*values):
    return lax.optimization_barrier(values)


def link_steps():
    steps = []
    step = 1
    while step < lax.axis_size(CUBE):
        steps.append(step)
        step *= 2
    return steps


FAR, NEAR, SIDE = 4, 2, 1
ROW_ORDER = (0, FAR, NEAR, FAR | NEAR, SIDE, FAR | SIDE, NEAR | SIDE, FAR | NEAR | SIDE)


def cube(block, step):
    return hop(block, CUBE, step)


def join_kernel(left_ref, left_came_ref, right_ref, right_came_ref, out_ref):
    half = left_ref.shape[1]
    block = pl.program_id(0)

    @pl.when(block < 2)
    def _():
        out_ref[:, :half] = left_ref[...]

    @pl.when(block >= 2)
    def _():
        out_ref[:, :half] = left_came_ref[...]

    @pl.when(block % 2 == 0)
    def _():
        out_ref[:, half:] = right_ref[...]

    @pl.when(block % 2 == 1)
    def _():
        out_ref[:, half:] = right_came_ref[...]


def join_halves(left, left_came, right, right_came):
    rows, half = left.shape[0] // 2, left.shape[1]

    def spec(place):
        return pl.BlockSpec((rows, half), lambda i: (place(i), 0))

    return pl.pallas_call(
        join_kernel,
        grid=(4,),
        in_specs=[
            spec(lambda i: jnp.minimum(i, 1)),
            spec(lambda i: jnp.maximum(i - 2, 0)),
            spec(lambda i: i // 2),
            spec(lambda i: i // 2),
        ],
        out_specs=pl.BlockSpec((rows, 2 * half), lambda i: (i, 0)),
        out_shape=jax.ShapeDtypeStruct((4 * rows, 2 * half), left.dtype),
        cost_estimate=pl.CostEstimate(
            flops=0, bytes_accessed=32 * rows * half, transcendentals=0
        ),
    )(left, left_came, right, right_came)


def gather_far(rows):
    return jnp.concatenate([rows, cube(rows, FAR)], axis=0)


def gather_across(rows):
    half = rows.shape[1] // 2
    left, right = rows[:, :half], rows[:, half:]
    left_came, right_came = cube(left, NEAR), cube(right, SIDE)
    left = jnp.concatenate([left, left_came], axis=0)
    return left, jnp.concatenate([right, right_came], axis=0)


def gather_last(pair):
    left, right = pair
    return join_halves(left, cube(left, SIDE), right, cube(right, NEAR))


def gather_rows(stages, rows, jobs):
    for step, more in zip((gather_far, gather_across, gather_last), jobs):
        rows = stages.run(rows, step, more)
    return rows


def sum_rows(stages, partial, jobs):
    n = partial.shape[0] // 4
    half = partial.shape[1] // 2

    def across(x):
        left, right = x[:, :half], x[:, half:]
        left_came = cube(left[2 * n :], SIDE)
        right_came = cube(jnp.concatenate([right[n : 2 * n], right[3 * n :]], axis=0), NEAR)
        left = left[: 2 * n].astype(F32) + left_came.astype(F32)
        right_came = right_came.astype(F32)
        low = right[:n].astype(F32) + right_came[:n]
        high = right[2 * n : 3 * n].astype(F32) + right_came[n:]
        return left[:n], left[n:].astype(BF), low, high.astype(BF)

    def again(parts):
        left, left_out, right, right_out = parts
        left_came = cube(left_out, NEAR)
        right_came = cube(right_out, SIDE)
        both = [left + left_came.astype(F32), right + right_came.astype(F32)]
        both = jnp.concatenate(both, axis=1)
        return both[: n // 2], both[n // 2 :].astype(BF)

    def far(parts):
        return parts[0] + cube(parts[1], FAR).astype(F32)

    value = partial
    for step, more in zip((across, again, far), jobs):
        value = stages.run(value, step, more)
    return value


class Stages:
    def __init__(self):
        self.held = {}

    def run(self, value, step, jobs):
        needed = [[self.held[name] for name in job[2]] for job in jobs]
        value, needed = lax.optimization_barrier((value, needed))
        out = step(value)
        made = [job[1](*inputs) for job, inputs in zip(jobs, needed)]
        due = [m for m, job in zip(made, jobs) if len(job) == 3]
        out, due = lax.optimization_barrier((out, due))
        for job, result in zip(jobs, made):
            self.held[job[0]] = due.pop(0) if len(job) == 3 else result
        return out


class Bulk:
    def __init__(self, order, job):
        self.order = [[name, layer, 0, units] for name, layer, units in order]
        self.job = job
        self.keys = {}

    def take(self, count):
        jobs = []
        while count and self.order:
            name, layer, done, units = entry = self.order[0]
            some = min(count, units - done)
            key = ("unit", name, layer, done)
            make, source = self.job(name, layer, done, some, units)
            jobs.append((key, make, (source,)))
            self.keys.setdefault((name, layer), []).append(key)
            entry[2] += some
            count -= some
            if entry[2] == units:
                self.order.pop(0)
        return jobs

    def parts(self, name, layer):
        return tuple(self.keys[name, layer])


def others(block, axis):
    return [block] + [hop(block, axis, k) for k in range(1, lax.axis_size(axis))]


def sum_others(blocks, axis):
    total = blocks[0].astype(F32)
    for k in range(1, lax.axis_size(axis)):
        total = total + hop(blocks[k].astype(BF), axis, k).astype(F32)
    return total


def relative(values, dim, axis):
    count = lax.axis_size(axis)
    me = lax.axis_index(axis)
    step = 1
    while step < count:
        shape = values.shape
        cut = shape[:dim] + (count // (2 * step), 2, step * (shape[dim] // count)) + shape[dim + 1 :]
        view = values.reshape(cut)
        swapped = jnp.concatenate(
            [lax.slice_in_dim(view, 1, 2, axis=dim + 1), lax.slice_in_dim(view, 0, 1, axis=dim + 1)],
            axis=dim + 1,
        )
        values = jnp.where((me & step) != 0, swapped.reshape(shape), values)
        step *= 2
    return values


def spread_gains(norm_gains):
    me = lax.axis_index(CUBE)
    gain = norm_gains
    for step in link_steps():
        came = hop(gain, CUBE, step)
        gain = jnp.where(
            (me & step) != 0,
            jnp.concatenate([came, gain], axis=1),
            jnp.concatenate([gain, came], axis=1),
        )
    gain = jnp.concatenate(others(gain, "grp"), axis=1)
    other = hop(gain, "pipe", 1)
    core = lax.axis_index("pipe")
    return [jnp.where(core == 0, gain, other), jnp.where(core == 0, other, gain)]


def sum_gains(grads):
    me = lax.axis_index(CUBE)
    keep, extra = own_layer(grads[0], grads[1])
    total = (keep + extra).reshape(2, lax.axis_size("grp"), -1)
    mine = total[:, 0]
    for k in range(1, total.shape[1]):
        mine = mine + hop(total[:, k], "grp", k)
    for step in link_steps()[::-1]:
        half = mine.shape[1] // 2
        low, high = mine[:, :half], mine[:, half:]
        odd = (me & step) != 0
        mine = jnp.where(odd, high, low) + hop(jnp.where(odd, low, high), CUBE, step)
    return mine


def masked_probs(q, k, q_place, q_start, k_place):
    scores = lax.dot_general(q, k, (((1,), (1,)), ((), ())), preferred_element_type=F32)
    scores = scores * HEAD_SIZE ** (-0.5)
    allowed = (k_place <= q_place) & (k_place >= q_start)
    masked = jnp.where(allowed, scores, NEG_FILL)
    exps = jnp.exp(masked - jnp.max(masked, axis=-1, keepdims=True))
    return exps / jnp.sum(exps, axis=-1, keepdims=True)


def attend_kernel(q_ref, k_ref, v_ref, qp_ref, qs_ref, kp_ref, o_ref):
    probs = masked_probs(q_ref[0], k_ref[...], qp_ref[...], qs_ref[...], kp_ref[...])
    o_ref[0] = jnp.dot(probs.astype(BF), v_ref[...], preferred_element_type=F32).astype(BF)


def attend_back_kernel(q_ref, do_ref, k_ref, v_ref, qp_ref, qs_ref, kp_ref, dq_ref, dk_ref, dv_ref):
    @pl.when((pl.program_id(0) == 0) & (pl.program_id(1) == 0))
    def _():
        dk_ref[...] = jnp.zeros_like(dk_ref)
        dv_ref[...] = jnp.zeros_like(dv_ref)

    q = q_ref[0]
    do = do_ref[0]
    k = k_ref[...]
    probs = masked_probs(q, k, qp_ref[...], qs_ref[...], kp_ref[...])
    grad_probs = lax.dot_general(do, v_ref[...], (((1,), (1,)), ((), ())), preferred_element_type=F32)
    delta = jnp.sum(probs * grad_probs, axis=-1, keepdims=True)
    grad_scores = (probs * (grad_probs - delta) * HEAD_SIZE ** (-0.5)).astype(BF)
    dq_ref[0] = jnp.dot(grad_scores, k, preferred_element_type=F32).astype(BF)
    dk_ref[...] += lax.dot_general(
        grad_scores, q, (((0,), (0,)), ((), ())), preferred_element_type=F32
    )
    dv_ref[...] += lax.dot_general(
        probs.astype(BF), do, (((0,), (0,)), ((), ())), preferred_element_type=F32
    )


def attention_specs(heads, rows, keys):
    rows_blk = max(16, min(rows, (512 * 1024) // keys))
    per_head = pl.BlockSpec((1, rows_blk, HEAD_SIZE), lambda b, h: (h, b, 0))
    full = pl.BlockSpec((keys, HEAD_SIZE), lambda b, h: (0, 0))
    row_info = pl.BlockSpec((rows_blk, 1), lambda b, h: (b, 0))
    key_info = pl.BlockSpec((1, keys), lambda b, h: (0, 0))
    return ((rows // rows_blk, heads), per_head, full, row_info, key_info)


PARAMS = dict(
    compiler_params=pltpu.CompilerParams(vmem_limit_bytes=50 * 1024 * 1024),
)


def attend(q, k, v, q_place, q_start, k_place):
    heads, rows, _ = q.shape
    keys = k.shape[0]
    grid, per_head, full, row_info, key_info = attention_specs(heads, rows, keys)
    return pl.pallas_call(
        attend_kernel,
        grid=grid,
        in_specs=[per_head, full, full, row_info, row_info, key_info],
        out_specs=per_head,
        out_shape=jax.ShapeDtypeStruct(q.shape, BF),
        cost_estimate=pl.CostEstimate(
            flops=4 * heads * rows * keys * HEAD_SIZE,
            bytes_accessed=4 * q.size + 4 * k.size,
            transcendentals=heads * rows * keys,
        ),
        **PARAMS,
    )(q, k, v, q_place, q_start, k_place)


def attend_back(q, do, k, v, q_place, q_start, k_place):
    heads, rows, _ = q.shape
    keys = k.shape[0]
    grid, per_head, full, row_info, key_info = attention_specs(heads, rows, keys)
    return pl.pallas_call(
        attend_back_kernel,
        grid=grid,
        in_specs=[per_head, per_head, full, full, row_info, row_info, key_info],
        out_specs=[per_head, full, full],
        out_shape=[
            jax.ShapeDtypeStruct(q.shape, BF),
            jax.ShapeDtypeStruct(k.shape, F32),
            jax.ShapeDtypeStruct(k.shape, F32),
        ],
        cost_estimate=pl.CostEstimate(
            flops=10 * heads * rows * keys * HEAD_SIZE,
            bytes_accessed=6 * q.size + 12 * k.size,
            transcendentals=heads * rows * keys,
        ),
        **PARAMS,
    )(q, do, k, v, q_place, q_start, k_place)


def to_blocks(weight, cores):
    wd = lax.axis_size("wd")
    rows = weight.shape[0]
    cut = weight.reshape(rows, wd, cores, -1).transpose(2, 1, 0, 3)
    return cut.reshape((cores * wd, rows) + cut.shape[3:])


def columns_out(blocks):
    moved = trade(blocks, ("pipe", "wd"))
    return moved.reshape((2, -1) + moved.shape[2:])


def exchange(piece):
    return [hop(piece, "grp", k) for k in range(1, lax.axis_size("grp"))]


def weight_unit(name, layer, done, some, units):
    def take(cols):
        rows = cols.shape[1] // units
        return exchange(cols[layer, done * rows : (done + some) * rows])

    return take, name


def grad_unit(name, layer, done, some, units):
    def add(blocks):
        rows = blocks.shape[1] // units
        cut = blocks[:, done * rows : (done + some) * rows]
        total = cut[0]
        for k in range(1, blocks.shape[0]):
            total = total + hop(cut[k].astype(BF), "grp", k).astype(F32)
        return total.astype(BF)

    return add, ("pair", name, layer)


def put_kernel(spots, *refs):
    pieces, out = refs[: len(spots)], refs[len(spots)]
    block = pl.program_id(0)
    for piece, (first, count, col, cols) in zip(pieces, spots):

        def put(piece=piece, col=col, cols=cols):
            out[:, col : col + cols] = piece[...]

        pl.when((block >= first) & (block < first + count))(put)


def put_together(columns):
    block = min([256] + [piece.shape[0] for stack in columns for piece in stack])
    spots, pieces, specs = [], [], []
    col = 0
    for stack in columns:
        first = 0
        for piece in stack:
            count, cols = piece.shape[0] // block, piece.shape[1]
            spots.append((first, count, col, cols))
            pieces.append(piece)

            def at(i, first=first, count=count):
                return (jnp.clip(i - first, 0, count - 1), 0)

            specs.append(pl.BlockSpec((block, cols), at))
            first += count
        col += cols
    return pl.pallas_call(
        lambda *refs: put_kernel(spots, *refs),
        grid=(first,),
        in_specs=specs,
        out_specs=pl.BlockSpec((block, col), lambda i: (i, 0)),
        out_shape=jax.ShapeDtypeStruct((first * block, col), BF),
        cost_estimate=pl.CostEstimate(
            flops=0, bytes_accessed=4 * first * block * col, transcendentals=0
        ),
        **PARAMS,
    )(*pieces)


def stacked(layer):
    def join(cols, *came):
        pieces = [cols[layer]]
        for k in range(len(came[0])):
            pieces += [c[k] for c in came]
        return pieces

    return join


def crossed(pieces):
    return [hop(p, "pipe", 1) for p in pieces]


def pack_attention(w_query, key_matrix, value_matrix, w_output, cores):
    wd = lax.axis_size("wd")
    rows = w_query.shape[0]
    cut = [
        m.reshape(rows, wd, cores, -1) for m in (w_query, key_matrix, value_matrix, w_output.T)
    ]
    return jnp.concatenate(cut, axis=-1).reshape(rows, -1)


def core_order(own, other, axis):
    core = lax.axis_index("pipe")
    return jnp.where(
        core == 0,
        jnp.concatenate([own, other], axis=axis),
        jnp.concatenate([other, own], axis=axis),
    )


def unpack_attention(own, other, widths):
    query_w, kv_w, out_w = widths
    cuts = (query_w, query_w + kv_w, query_w + 2 * kv_w)

    def split(m):
        return (m[:, : cuts[0]], m[:, cuts[0] : cuts[1]], m[:, cuts[1] : cuts[2]], m[:, cuts[2] :])

    q0, k0, v0, o0 = split(own)
    q1, k1, v1, o1 = split(other)
    return (
        jnp.concatenate([q0, q1], axis=1),
        core_order(k0, k1, 1),
        core_order(v0, v1, 1),
        jnp.concatenate([o0, o1], axis=1),
    )


def core_halves(grad):
    half = grad.shape[1] // 2
    core = lax.axis_index("pipe")
    low, high = grad[:, :half], grad[:, half:]
    return (jnp.where(core == 0, low, high), jnp.where(core == 0, high, low))


def grad_pair(own, came):
    total = own + came.astype(F32)
    return total.reshape((lax.axis_size("grp"), -1) + total.shape[1:])


def grad_home(*parts):
    wd = lax.axis_size("wd")
    me = lax.axis_index("wd")
    blocks = jnp.concatenate(parts, axis=0)
    blocks = blocks.reshape((wd, -1) + blocks.shape[1:])
    pieces = [lax.dynamic_index_in_dim(blocks, me, 0, keepdims=False)]
    for k in range(1, wd):
        pieces.append(hop(lax.dynamic_index_in_dim(blocks, me ^ k, 0, keepdims=False), "wd", k))
    return jnp.stack(pieces)


def place_kernel(turned, at_ref, keep_ref, got_ref, out_ref):
    mine = pl.program_id(1) == at_ref[1]

    def put(ref):
        block = ref[0].astype(F32)
        out_ref[...] = block.T if turned else block

    @pl.when(mine)
    def _():
        put(keep_ref)

    @pl.when(jnp.logical_not(mine))
    def _():
        put(got_ref)


def place(keep, got, turned):
    wd, rows, cols = keep.shape
    at = jnp.stack([lax.axis_index("wd"), lax.axis_index("pipe")]).astype(jnp.int32)
    cores = lax.axis_size("pipe")
    source = pl.BlockSpec((1, rows, cols), lambda w, c, at_ref: (w ^ at_ref[0], 0, 0))
    if turned:
        shape, target = (wd * cores * cols, rows), (cols, rows)
        out = pl.BlockSpec(target, lambda w, c, at_ref: (w * cores + c, 0))
    else:
        shape, target = (rows, wd * cores * cols), (rows, cols)
        out = pl.BlockSpec(target, lambda w, c, at_ref: (0, w * cores + c))
    return pl.pallas_call(
        lambda *refs: place_kernel(turned, *refs),
        grid_spec=pltpu.PrefetchScalarGridSpec(
            num_scalar_prefetch=1, grid=(wd, cores), in_specs=[source, source], out_specs=out
        ),
        out_shape=jax.ShapeDtypeStruct(shape, F32),
        cost_estimate=pl.CostEstimate(
            flops=keep.size, bytes_accessed=12 * keep.size, transcendentals=0
        ),
    )(at, keep, got)


def layer_forward(stages, layer, x_rows, gains, where, jobs):
    held = stages.held
    cosine, sine, q_place, q_start, k_place = where
    normed = apply_norm(x_rows, gains[0]).astype(BF)
    rows_a = gather_rows(stages, normed, jobs[0])
    w_q, w_k, w_v, w_ot = held["attn", layer]
    tok = rows_a.shape[0]

    def project(rows):
        key = rotary_apply(mm(rows, w_k).reshape(tok, 1, HEAD_SIZE), cosine, sine).astype(BF)[:, 0]
        value = mm(rows, w_v).astype(BF)
        return jnp.concatenate([key, value], axis=1)

    def queries(rows):
        query = rotary_apply(mm(rows, w_q).reshape(tok, -1, HEAD_SIZE), cosine, sine).astype(BF)
        return query.transpose(1, 0, 2)

    held["rows_a"] = rows_a
    kv_all = stages.run(
        project(rows_a),
        lambda kv: jnp.concatenate(others(kv, "grp"), axis=0),
        [("query", queries, ("rows_a",))] + jobs[1],
    )
    query = held["query"]
    keys, values = kv_all[:, :HEAD_SIZE], kv_all[:, HEAD_SIZE:]

    def attention(q):
        context = attend(q, keys, values, q_place, q_start, k_place)
        context = context.transpose(1, 0, 2).reshape(tok, -1)
        return context, mm_t(context, w_ot).astype(BF)

    context, partial = stages.run(query, attention, jobs[2])
    mid = x_rows + sum_rows(stages, partial, jobs[3])
    rows_b = gather_rows(stages, apply_norm(mid, gains[1]).astype(BF), jobs[4])
    for more in jobs[5:-1]:
        rows_b = stages.run(rows_b, lambda r: r, more)
    w_gu = held["gu", layer]

    def ahead(rows):
        both = mm(rows, w_gu)
        half = both.shape[1] // 2
        gate, up = both[:, :half], both[:, half:]
        return gate, up, (jax.nn.silu(gate) * up).astype(BF)

    gate, up, hidden = stages.run(rows_b, ahead, jobs[-1])
    return x_rows, rows_a, query, keys, values, context, mid, rows_b, gate, up, hidden


def layer_backward(stages, layer, grad_out, grad_mlp, gains, where, kept, jobs):
    held = stages.held
    cosine, sine, q_place, q_start, k_place = where
    x_rows, rows_a, query, keys, values, context, mid, rows_b, gate, up, hidden = kept
    w_q, w_k, w_v, w_ot = held["attn", layer]
    w_gu, w_dt = held["gu", layer], held["down", layer]
    tok = rows_a.shape[0]
    held["rows_b"], held["hidden"], held["grad_mlp"] = rows_b, hidden, grad_mlp

    def feed_back(rows):
        grad_hidden = mm(rows, w_dt)
        sig = jax.nn.sigmoid(gate)
        grad_gate = (grad_hidden * up * sig * (1.0 + gate * (1.0 - sig))).astype(BF)
        grad_up = (grad_hidden * gate * sig).astype(BF)
        return grad_gate, grad_up

    def rows_back(pair):
        return mm_t(jnp.concatenate(pair, axis=1), w_gu).astype(BF)

    pair = stages.run(grad_mlp, feed_back, jobs[0][0])
    held["grad_gate"], held["grad_up"] = pair
    partial = stages.run(pair, rows_back, jobs[0][1])
    for more in jobs[0][2:]:
        partial = stages.run(partial, lambda p: p, more)
    grad_b = sum_rows(stages, partial, jobs[1])
    grad_mid, gain_b = norm_back(mid, gains[1], grad_b)
    grad_mid = grad_mid + grad_out
    grad_attn = gather_rows(stages, grad_mid.astype(BF), jobs[2])

    def attention_back(rows):
        grad_context = mm(rows, w_ot).astype(BF)
        grad_context = grad_context.reshape(tok, -1, HEAD_SIZE).transpose(1, 0, 2)
        return attend_back(query, grad_context, keys, values, q_place, q_start, k_place)

    def keys_back(grads):
        kv = jnp.concatenate(grads, axis=1)
        kv = kv.reshape((-1, tok) + kv.shape[1:])
        return sum_others([kv[k] for k in range(kv.shape[0])], "grp").astype(BF)

    def queries_back(grad_q):
        grad_q = grad_q.transpose(1, 0, 2).astype(F32)
        grad_q = rotary_apply(grad_q, cosine, -sine).astype(BF).reshape(tok, -1)
        return grad_q, mm_t(grad_q, w_q)

    held["grad_q"], *grads = stages.run(grad_attn, attention_back, jobs[3])
    own_kv = stages.run(grads, keys_back, [("g_q", queries_back, ("grad_q",))] + jobs[4])
    grad_q, partial = held["g_q"]
    grad_k = own_kv[:, :HEAD_SIZE].astype(F32)
    grad_k = rotary_apply(grad_k[:, None, :], cosine, -sine).astype(BF)[:, 0]
    grad_v = own_kv[:, HEAD_SIZE:]
    partial = (partial + mm_t(grad_k, w_k) + mm_t(grad_v, w_v)).astype(BF)

    held["g_q"] = grad_q
    held["g_kv"] = core_halves(grad_k), core_halves(grad_v)
    held["g_rows"] = rows_a, grad_attn, context

    def term(which):
        def make(g_q, g_kv, rows):
            half_q = g_q.shape[1] // 2
            cut = slice(half_q * which, half_q * (which + 1))
            right = jnp.concatenate([g_q[:, cut], g_kv[0][which], g_kv[1][which]], axis=1)
            left = [mm_tl(rows[0], right), mm_tl(rows[1], rows[2][:, cut])]
            return jnp.concatenate(left, axis=1)

        return make

    grad_a = sum_rows(stages, partial, jobs[5](term))
    grad_in, gain_a = norm_back(x_rows, gains[0], grad_a)
    return grad_mid + grad_in, jnp.stack([gain_a, gain_b])


def own_layer(first, second):
    core = lax.axis_index("pipe")
    keep = jnp.where(core == 0, first, second)
    return keep, hop(jnp.where(core == 0, second, first), "pipe", 1)


def body(
    block_input,
    cotangent,
    segments,
    norm_gains,
    w_query,
    key_matrix,
    value_matrix,
    w_output,
    w_gate,
    w_up,
    w_down,
):
    core = lax.axis_index("pipe")
    grp = lax.axis_index("grp")
    wd = lax.axis_size("wd")
    groups = lax.axis_size("grp")
    cores = lax.axis_size("pipe")
    tok = block_input.shape[1] * lax.axis_size(CUBE)

    stages = Stages()
    held = stages.held
    packed = pack_attention(w_query[0], key_matrix[0], value_matrix[0], w_output[0], cores)
    attn_cols = columns_out(to_blocks(packed, cores))
    held["attn"], first_gains = lax.optimization_barrier((attn_cols, norm_gains[0]))
    gains = spread_gains(first_gains)
    held["gate_out"] = to_blocks(w_gate[0], cores)
    held["up_out"] = to_blocks(w_up[0], cores)
    held["down_out"] = to_blocks(w_down[0].T, cores)
    widths = tuple(n // (wd * cores) for n in (w_query.shape[2], key_matrix.shape[2], w_output.shape[1]))

    flow = Bulk(
        [
            (name, layer, 4 if name == "attn" else 8)
            for name, layer in (("attn", 0), ("attn", 1))
            + tuple((name, layer) for layer in range(2) for name in ("gate", "up", "down"))
        ],
        weight_unit,
    )

    def move(name):
        return (name, columns_out, (name + "_out",), "later")

    def attn_ready(layer):
        def ready(*values):
            own = stacked(layer)(*values)
            there = crossed(own)
            return unpack_attention(
                jnp.concatenate(own, axis=0), jnp.concatenate(there, axis=0), widths
            )

        return (("attn", layer), ready, ("attn",) + flow.parts("attn", layer))

    def cross(name, layer):
        def ready(*values):
            own = stacked(layer)(*values)
            return own, crossed(own)

        return (("cross", name, layer), ready, (name,) + flow.parts(name, layer))

    def gate_up_ready(layer):
        def ready(gate, up):
            return put_together([gate[0], gate[1], up[0], up[1]])

        return (("gu", layer), ready, (("cross", "gate", layer), ("cross", "up", layer)))

    def down_ready(layer):
        return (("down", layer), lambda d: put_together([d[0], d[1]]), (("cross", "down", layer),))

    seg_row = lax.dynamic_index_in_dim(segments, core, 0, keepdims=False)
    starts = doc_starts(seg_row)
    rows_own = tok // lax.axis_size(CUBE)

    def in_row_order(values):
        values = relative(values, 0, CUBE)
        return jnp.concatenate(
            [values[j * rows_own : (j + 1) * rows_own] for j in ROW_ORDER], axis=0
        )

    local = in_row_order(jnp.arange(tok, dtype=jnp.int32))
    q_place = grp * tok + local
    q_start = in_row_order(lax.dynamic_slice_in_dim(starts, grp * tok, tok))
    cosine, sine = rope_tables(q_place - q_start)
    k_place = jnp.concatenate([(grp ^ k) * tok + local for k in range(groups)])
    where = (cosine, sine, q_place[:, None], q_start[:, None], k_place[None, :])

    rows = relative(lax.dynamic_index_in_dim(block_input, core, 0, keepdims=False), 1, "grp")
    grad = relative(lax.dynamic_index_in_dim(cotangent, core, 0, keepdims=False), 1, "grp")
    held["cotangent"] = grad
    take = flow.take
    [(key, job, _)] = take(4)
    held[key] = job(held["attn"])
    rows, held[key], gains = lax.optimization_barrier((rows, held[key], gains))
    held["gate_out"], _ = lax.optimization_barrier((held["gate_out"], gains))
    held["gate"] = columns_out(held["gate_out"])
    kept = [None, None]
    outs = [None, None]
    kept[0] = layer_forward(
        stages,
        0,
        rows.astype(F32),
        gains[0],
        where,
        (
            (take(1), take(1) + [attn_ready(0)], take(2)),
            take(5) + [move("up")],
            take(3),
            (take(3), [move("down")] + take(1), take(2)),
            (take(1), take(2) + [cross("gate", 0)], take(3)),
            take(2) + [cross("up", 0)],
            take(2) + [gate_up_ready(0)],
            take(2),
        ),
    )
    hidden = stages.run(kept[0][-1], lambda h: h, take(2) + [cross("down", 0)])
    hidden = stages.run(hidden, lambda h: h, take(2) + [down_ready(0)])

    def close(layer, hidden, jobs):
        partial = stages.run(hidden, lambda h: mm_t(h, held["down", layer]).astype(BF), [])
        return (kept[layer][6] + sum_rows(stages, partial, jobs)).astype(BF)

    outs[0] = close(0, hidden, (take(2), take(1), take(1)))
    kept[1] = layer_forward(
        stages,
        1,
        outs[0].astype(F32),
        gains[1],
        where,
        (
            (take(1), take(1) + [attn_ready(1)], take(2)),
            take(4) + [("last_1", gather_far, ("cotangent",))],
            take(2) + [("last_2", gather_across, ("last_1",))],
            (take(2), take(1), take(1) + [cross("gate", 1)]),
            (take(1) + [cross("up", 1)], take(1), take(2) + [cross("down", 1)]),
            take(1) + [gate_up_ready(1), ("last", gather_last, ("last_2",))],
            take(1) + [down_ready(1)],
        ),
    )

    backs = Bulk(
        [
            (name, layer, 4 if name == "attn" else 8)
            for layer in (1, 0)
            for name in (("down", "gate", "up", "attn") if layer else ("down", "gate", "up", "attn"))
        ],
        grad_unit,
    )
    back = backs.take
    sources = {
        "down": ("grad_mlp", "hidden"),
        "gate": ("rows_b", "grad_gate"),
        "up": ("rows_b", "grad_up"),
    }

    def half_of(which):
        def make(left, right):
            half = right.shape[1] // 2
            return mm_tl(left, right[:, half * which : half * (which + 1)])

        return make

    def grad_steps(name, layer, half=None):
        names = sources[name] if half is None else ("g_q", "g_kv", "g_rows")
        half = half or half_of
        out, came = ("out", name, layer), ("came", name, layer)
        return (
            (out, lambda *ins: half(1)(*ins).astype(BF), names),
            (came, lambda x: hop(x, "pipe", 1), (out,)),
            (
                ("pair", name, layer),
                lambda x, *ins: grad_pair(half(0)(*ins), x),
                (came,) + names,
            ),
        )

    def home(name, layer):
        return (("home", name, layer), grad_home, backs.parts(name, layer))

    def final(name, turned):
        def ready(first, second):
            return place(*own_layer(first, second), turned)

        return (("final", name), ready, (("home", name, 0), ("home", name, 1)))

    held["hidden"], held["grad_mlp"] = kept[1][-1], held["last"]
    one, two, three = grad_steps("down", 1)

    grads_in = [None, None]
    gain_grads = [None, None]
    hidden, last = stages.run((kept[1][-1], held["last"]), lambda h: h, [one])
    more = grad_steps("gate", 1), grad_steps("up", 1)
    grad_in, gain_grads[1] = layer_backward(
        stages,
        1,
        grad.astype(F32),
        last,
        gains[1],
        where,
        kept[1][:-1] + (hidden,),
        (
            ([two], [three]),
            (back(3) + [more[0][0]], back(1) + [more[0][1]], back(2) + [more[0][2]]),
            (back(1) + [more[1][0]], back(2) + [more[1][1]], back(3) + [more[1][2]]),
            back(3),
            back(3) + [home("down", 1)],
            lambda term: tuple(
                back(n) + [step] for n, step in zip((3, 1, 2), grad_steps("attn", 1, term))
            ),
        ),
    )
    grads_in[1] = grad_in.astype(BF)
    grad_mlp = gather_rows(stages, grads_in[1], (back(1), back(1), back(2)))
    outs[1] = close(1, hidden, ([], [], []))
    held["hidden"], held["grad_mlp"] = kept[0][-1], grad_mlp
    one, two, three = grad_steps("down", 0)
    more = grad_steps("gate", 0), grad_steps("up", 0)
    grad_in, gain_grads[0] = layer_backward(
        stages,
        0,
        grads_in[1].astype(F32),
        grad_mlp,
        gains[0],
        where,
        kept[0],
        (
            ([one, home("gate", 1)], [two, home("up", 1)], [three]),
            (back(3) + [more[0][0]], back(1) + [more[0][1]], back(2) + [more[0][2]]),
            (back(1) + [more[1][0]], back(2) + [more[1][1]], back(3) + [more[1][2]]),
            back(3),
            back(4) + [home("attn", 1), home("down", 0)],
            lambda term: tuple(
                back(n) + [step] for n, step in zip((3, 1, 1), grad_steps("attn", 0, term))
            ),
        ),
    )
    grads_in[0] = grad_in.astype(BF)
    tail = grads_in[0]
    rest = back(12)
    for jobs in (
        rest + [home("gate", 0), final("down", True)],
        [home("attn", 0), home("up", 0), final("gate", False)],
    ):
        tail = stages.run(tail, lambda t: t, jobs)

    def by_batch(pair):
        own, other = own_layer(pair[0], pair[1])
        both = jnp.where(core == 0, jnp.stack([own, other]), jnp.stack([other, own]))
        return relative(both, 2, "grp")[None]

    layer_out = by_batch(outs)
    input_grad = by_batch(grads_in)

    grad_norm_gains = sum_gains(gain_grads)[None]

    def both(name):
        return own_layer(held["home", name, 0], held["home", name, 1])

    keep, got = both("attn")
    cuts = (0, widths[0], widths[0] + widths[1], widths[0] + 2 * widths[1], keep.shape[2])
    q_pair, k_pair, v_pair, o_pair = (
        (keep[..., lo:hi], got[..., lo:hi]) for lo, hi in zip(cuts[:-1], cuts[1:])
    )

    def small(pair):
        order = jnp.where(core == 0, jnp.stack(pair), jnp.stack(pair[::-1]))
        order = relative(order, 1, "wd").transpose(2, 1, 0, 3).astype(F32)
        return order.reshape(order.shape[0], -1)[None]

    grad_wq = place(*q_pair, False)[None]
    grad_wk = small(k_pair)
    grad_wv = small(v_pair)
    grad_wo = place(*o_pair, True)[None]
    grad_wg = held["final", "gate"][None]
    grad_wu = place(*both("up"), False)[None]
    grad_wd = held["final", "down"][None]
    return (
        layer_out,
        input_grad,
        grad_norm_gains,
        grad_wq,
        grad_wk,
        grad_wv,
        grad_wo,
        grad_wg,
        grad_wu,
        grad_wd,
    )


def solution(mesh):
    sizes = dict(mesh.shape)
    wd = KV_HEADS // sizes["tensor"]
    fine = Mesh(
        mesh.devices.reshape(sizes["pipe"], sizes["dp"] // wd, wd, sizes["tensor"]),
        ("pipe", "grp", "wd", "tensor"),
    )
    dp = ("grp", "wd")
    tokens = P(None, dp + ("tensor",), None)
    outs = P("pipe", None, dp + ("tensor",), None)
    gains = P("pipe", None, dp + ("tensor",))
    tall = P("pipe", dp, "tensor")
    wide = P("pipe", "tensor", dp)
    weights = (tall, tall, tall, wide, tall, tall, wide)
    return jax.shard_map(
        body,
        mesh=fine,
        in_specs=(tokens, tokens, P(), gains) + weights,
        out_specs=(outs, outs, gains) + weights,
        check_vma=False,
    )
```

```python
import jax
import jax.numpy as jnp
from jax import lax
from jax.experimental import pallas as pl
from jax.experimental.pallas import tpu as pltpu
from jax.sharding import Mesh, PartitionSpec as P

HEAD_SIZE = 64
KV_HEADS = 8
EPS = 1e-05
ROPE_BASE = 500000.0
NEG_FILL = -1e30
BF = jnp.bfloat16
F32 = jnp.float32
CUBE = ("wd", "tensor")


def rms_scale(row_values):
    return lax.rsqrt(jnp.mean(row_values * row_values, axis=-1, keepdims=True) + EPS)


def apply_norm(row_values, gain_vector):
    return row_values * rms_scale(row_values) * gain_vector


def norm_back(row_values, gain_vector, grad_normed):
    _, pullback = jax.vjp(apply_norm, row_values, gain_vector)
    return pullback(grad_normed)


def doc_starts(seg_row):
    places = jnp.arange(seg_row.shape[0], dtype=jnp.int32)
    before = jnp.concatenate([seg_row[:1] - 1, seg_row[:-1]])
    return lax.cummax(jnp.where(seg_row != before, places, 0), axis=0)


def rope_tables(positions):
    half_dim = HEAD_SIZE // 2
    freqs = ROPE_BASE ** (-(jnp.arange(half_dim, dtype=F32) * 2.0 / HEAD_SIZE))
    angles = positions.astype(F32)[:, None] * freqs[None, :]
    return (jnp.cos(angles), jnp.sin(angles))


def rotary_apply(head_values, cosine_table, sine_values):
    half_dim = head_values.shape[-1] // 2
    first_half = head_values[..., :half_dim]
    second_half = head_values[..., half_dim:]
    cos_rows = cosine_table[:, None, :]
    sin_rows = sine_values[:, None, :]
    return jnp.concatenate(
        [
            first_half * cos_rows - second_half * sin_rows,
            second_half * cos_rows + first_half * sin_rows,
        ],
        axis=-1,
    )


def mm(left, right):
    return jnp.dot(left, right, preferred_element_type=F32)


def mm_t(left, right):
    return lax.dot_general(left, right, (((1,), (1,)), ((), ())), preferred_element_type=F32)


def mm_tl(left, right):
    return lax.dot_general(left, right, (((0,), (0,)), ((), ())), preferred_element_type=F32)


def trade(blocks, axes):
    return lax.all_to_all(blocks, axes, 0, 0, tiled=True)


def hop(block, axis, step):
    size = lax.axis_size(axis)
    return lax.ppermute(block, axis, [(i, i ^ step) for i in range(size)])


def tie(*values):
    return lax.optimization_barrier(values)


def link_steps():
    steps = []
    step = 1
    while step < lax.axis_size(CUBE):
        steps.append(step)
        step *= 2
    return steps


FAR, NEAR, SIDE = 4, 2, 1
ROW_ORDER = (0, FAR, NEAR, FAR | NEAR, SIDE, FAR | SIDE, NEAR | SIDE, FAR | NEAR | SIDE)


def cube(block, step):
    return hop(block, CUBE, step)


def join_kernel(left_ref, left_came_ref, right_ref, right_came_ref, out_ref):
    half = left_ref.shape[1]
    block = pl.program_id(0)

    @pl.when(block < 2)
    def _():
        out_ref[:, :half] = left_ref[...]

    @pl.when(block >= 2)
    def _():
        out_ref[:, :half] = left_came_ref[...]

    @pl.when(block % 2 == 0)
    def _():
        out_ref[:, half:] = right_ref[...]

    @pl.when(block % 2 == 1)
    def _():
        out_ref[:, half:] = right_came_ref[...]


def join_halves(left, left_came, right, right_came):
    rows, half = left.shape[0] // 2, left.shape[1]

    def spec(place):
        return pl.BlockSpec((rows, half), lambda i: (place(i), 0))

    return pl.pallas_call(
        join_kernel,
        grid=(4,),
        in_specs=[
            spec(lambda i: jnp.minimum(i, 1)),
            spec(lambda i: jnp.maximum(i - 2, 0)),
            spec(lambda i: i // 2),
            spec(lambda i: i // 2),
        ],
        out_specs=pl.BlockSpec((rows, 2 * half), lambda i: (i, 0)),
        out_shape=jax.ShapeDtypeStruct((4 * rows, 2 * half), left.dtype),
        cost_estimate=pl.CostEstimate(
            flops=0, bytes_accessed=32 * rows * half, transcendentals=0
        ),
    )(left, left_came, right, right_came)


def gather_rows(rows):
    two = jnp.concatenate([rows, cube(rows, FAR)], axis=0)
    half = two.shape[1] // 2
    left, right = two[:, :half], two[:, half:]
    left_came, right_came = cube(left, NEAR), cube(right, SIDE)
    left = jnp.concatenate([left, left_came], axis=0)
    right = jnp.concatenate([right, right_came], axis=0)
    return join_halves(left, cube(left, SIDE), right, cube(right, NEAR))


def sum_rows(partial):
    partial = partial.astype(BF)
    n, half = partial.shape[0] // 4, partial.shape[1] // 2
    left, right = partial[:, :half], partial[:, half:]
    left_came = cube(left[2 * n :], SIDE)
    right_came = cube(jnp.concatenate([right[n : 2 * n], right[3 * n :]], axis=0), NEAR)
    left = left[: 2 * n].astype(F32) + left_came.astype(F32)
    right_came = right_came.astype(F32)
    low = right[:n].astype(F32) + right_came[:n]
    high = right[2 * n : 3 * n].astype(F32) + right_came[n:]
    left_came = cube(left[n:].astype(BF), NEAR)
    right_came = cube(high.astype(BF), SIDE)
    left = left[:n] + left_came.astype(F32)
    right = low + right_came.astype(F32)
    both = jnp.concatenate([left, right], axis=1)
    rows = n // 2
    return both[:rows] + cube(both[rows:].astype(BF), FAR).astype(F32)


class Stages:
    def __init__(self):
        self.held = {}

    def run(self, value, step, jobs):
        needed = [[self.held[name] for name in names] for _, _, names in jobs]
        value, needed = lax.optimization_barrier((value, needed))
        out = step(value)
        made = [job(*inputs) for (_, job, _), inputs in zip(jobs, needed)]
        out, made = lax.optimization_barrier((out, made))
        self.held.update((key, result) for (key, _, _), result in zip(jobs, made))
        return out


def others(block, axis):
    return [block] + [hop(block, axis, k) for k in range(1, lax.axis_size(axis))]


def sum_others(blocks, axis):
    total = blocks[0].astype(F32)
    for k in range(1, lax.axis_size(axis)):
        total = total + hop(blocks[k].astype(BF), axis, k).astype(F32)
    return total


def relative(values, dim, axis):
    count = lax.axis_size(axis)
    me = lax.axis_index(axis)
    step = 1
    while step < count:
        shape = values.shape
        cut = shape[:dim] + (count // (2 * step), 2, step * (shape[dim] // count)) + shape[dim + 1 :]
        view = values.reshape(cut)
        swapped = jnp.concatenate(
            [lax.slice_in_dim(view, 1, 2, axis=dim + 1), lax.slice_in_dim(view, 0, 1, axis=dim + 1)],
            axis=dim + 1,
        )
        values = jnp.where((me & step) != 0, swapped.reshape(shape), values)
        step *= 2
    return values


def spread_gains(norm_gains):
    me = lax.axis_index(CUBE)
    gain = norm_gains
    for step in link_steps():
        came = hop(gain, CUBE, step)
        gain = jnp.where(
            (me & step) != 0,
            jnp.concatenate([came, gain], axis=1),
            jnp.concatenate([gain, came], axis=1),
        )
    gain = jnp.concatenate(others(gain, "grp"), axis=1)
    other = hop(gain, "pipe", 1)
    core = lax.axis_index("pipe")
    return [jnp.where(core == 0, gain, other), jnp.where(core == 0, other, gain)]


def sum_gains(grads):
    me = lax.axis_index(CUBE)
    keep, extra = own_layer(grads[0], grads[1])
    total = (keep + extra).reshape(2, lax.axis_size("grp"), -1)
    mine = total[:, 0]
    for k in range(1, total.shape[1]):
        mine = mine + hop(total[:, k], "grp", k)
    for step in link_steps()[::-1]:
        half = mine.shape[1] // 2
        low, high = mine[:, :half], mine[:, half:]
        odd = (me & step) != 0
        mine = jnp.where(odd, high, low) + hop(jnp.where(odd, low, high), CUBE, step)
    return mine


def masked_probs(q, k, q_place, q_start, k_place):
    scores = lax.dot_general(q, k, (((1,), (1,)), ((), ())), preferred_element_type=F32)
    scores = scores * HEAD_SIZE ** (-0.5)
    allowed = (k_place <= q_place) & (k_place >= q_start)
    masked = jnp.where(allowed, scores, NEG_FILL)
    exps = jnp.exp(masked - jnp.max(masked, axis=-1, keepdims=True))
    return exps / jnp.sum(exps, axis=-1, keepdims=True)


def attend_kernel(q_ref, k_ref, v_ref, qp_ref, qs_ref, kp_ref, o_ref):
    probs = masked_probs(q_ref[0], k_ref[...], qp_ref[...], qs_ref[...], kp_ref[...])
    o_ref[0] = jnp.dot(probs.astype(BF), v_ref[...], preferred_element_type=F32).astype(BF)


def attend_back_kernel(q_ref, do_ref, k_ref, v_ref, qp_ref, qs_ref, kp_ref, dq_ref, dk_ref, dv_ref):
    @pl.when((pl.program_id(0) == 0) & (pl.program_id(1) == 0))
    def _():
        dk_ref[...] = jnp.zeros_like(dk_ref)
        dv_ref[...] = jnp.zeros_like(dv_ref)

    q = q_ref[0]
    do = do_ref[0]
    k = k_ref[...]
    probs = masked_probs(q, k, qp_ref[...], qs_ref[...], kp_ref[...])
    grad_probs = lax.dot_general(do, v_ref[...], (((1,), (1,)), ((), ())), preferred_element_type=F32)
    delta = jnp.sum(probs * grad_probs, axis=-1, keepdims=True)
    grad_scores = (probs * (grad_probs - delta) * HEAD_SIZE ** (-0.5)).astype(BF)
    dq_ref[0] = jnp.dot(grad_scores, k, preferred_element_type=F32).astype(BF)
    dk_ref[...] += lax.dot_general(
        grad_scores, q, (((0,), (0,)), ((), ())), preferred_element_type=F32
    )
    dv_ref[...] += lax.dot_general(
        probs.astype(BF), do, (((0,), (0,)), ((), ())), preferred_element_type=F32
    )


def attention_specs(heads, rows, keys):
    rows_blk = max(16, min(rows, (512 * 1024) // keys))
    per_head = pl.BlockSpec((1, rows_blk, HEAD_SIZE), lambda b, h: (h, b, 0))
    full = pl.BlockSpec((keys, HEAD_SIZE), lambda b, h: (0, 0))
    row_info = pl.BlockSpec((rows_blk, 1), lambda b, h: (b, 0))
    key_info = pl.BlockSpec((1, keys), lambda b, h: (0, 0))
    return ((rows // rows_blk, heads), per_head, full, row_info, key_info)


PARAMS = dict(
    compiler_params=pltpu.CompilerParams(vmem_limit_bytes=50 * 1024 * 1024),
)


def attend(q, k, v, q_place, q_start, k_place):
    heads, rows, _ = q.shape
    keys = k.shape[0]
    grid, per_head, full, row_info, key_info = attention_specs(heads, rows, keys)
    return pl.pallas_call(
        attend_kernel,
        grid=grid,
        in_specs=[per_head, full, full, row_info, row_info, key_info],
        out_specs=per_head,
        out_shape=jax.ShapeDtypeStruct(q.shape, BF),
        cost_estimate=pl.CostEstimate(
            flops=4 * heads * rows * keys * HEAD_SIZE,
            bytes_accessed=4 * q.size + 4 * k.size,
            transcendentals=heads * rows * keys,
        ),
        **PARAMS,
    )(q, k, v, q_place, q_start, k_place)


def attend_back(q, do, k, v, q_place, q_start, k_place):
    heads, rows, _ = q.shape
    keys = k.shape[0]
    grid, per_head, full, row_info, key_info = attention_specs(heads, rows, keys)
    return pl.pallas_call(
        attend_back_kernel,
        grid=grid,
        in_specs=[per_head, per_head, full, full, row_info, row_info, key_info],
        out_specs=[per_head, full, full],
        out_shape=[
            jax.ShapeDtypeStruct(q.shape, BF),
            jax.ShapeDtypeStruct(k.shape, F32),
            jax.ShapeDtypeStruct(k.shape, F32),
        ],
        cost_estimate=pl.CostEstimate(
            flops=10 * heads * rows * keys * HEAD_SIZE,
            bytes_accessed=6 * q.size + 12 * k.size,
            transcendentals=heads * rows * keys,
        ),
        **PARAMS,
    )(q, do, k, v, q_place, q_start, k_place)


def to_blocks(weight, cores):
    wd = lax.axis_size("wd")
    rows = weight.shape[0]
    cut = weight.reshape(rows, wd, cores, -1).transpose(2, 1, 0, 3)
    return cut.reshape((cores * wd, rows) + cut.shape[3:])


def columns_out(blocks):
    moved = trade(blocks, ("pipe", "wd"))
    return moved.reshape((2, -1) + moved.shape[2:])


def exchange(piece):
    return [hop(piece, "grp", k) for k in range(1, lax.axis_size("grp"))]


def piece_of(layer, part=None):
    def take(cols):
        rows = cols.shape[1] // 2
        if part is None:
            own = cols[layer]
        else:
            own = cols[layer, part * rows : (part + 1) * rows]
        came = exchange(own)
        return [own] + came, crossed([own] + came)

    return take


def put_kernel(spots, *refs):
    pieces, out = refs[: len(spots)], refs[len(spots)]
    block = pl.program_id(0)
    for piece, (first, count, col, cols) in zip(pieces, spots):

        def put(piece=piece, col=col, cols=cols):
            out[:, col : col + cols] = piece[...]

        pl.when((block >= first) & (block < first + count))(put)


def put_together(columns):
    block = min([256] + [piece.shape[0] for stack in columns for piece in stack])
    spots, pieces, specs = [], [], []
    col = 0
    for stack in columns:
        first = 0
        for piece in stack:
            count, cols = piece.shape[0] // block, piece.shape[1]
            spots.append((first, count, col, cols))
            pieces.append(piece)

            def at(i, first=first, count=count):
                return (jnp.clip(i - first, 0, count - 1), 0)

            specs.append(pl.BlockSpec((block, cols), at))
            first += count
        col += cols
    return pl.pallas_call(
        lambda *refs: put_kernel(spots, *refs),
        grid=(first,),
        in_specs=specs,
        out_specs=pl.BlockSpec((block, col), lambda i: (i, 0)),
        out_shape=jax.ShapeDtypeStruct((first * block, col), BF),
        cost_estimate=pl.CostEstimate(
            flops=0, bytes_accessed=4 * first * block * col, transcendentals=0
        ),
        **PARAMS,
    )(*pieces)


def stacked(parts):
    count = len(parts[0][0])
    return tuple([p[side][k] for k in range(count) for p in parts] for side in range(2))


def crossed(pieces):
    return [hop(p, "pipe", 1) for p in pieces]


def pack_attention(w_query, key_matrix, value_matrix, w_output, cores):
    wd = lax.axis_size("wd")
    rows = w_query.shape[0]
    cut = [
        m.reshape(rows, wd, cores, -1) for m in (w_query, key_matrix, value_matrix, w_output.T)
    ]
    return jnp.concatenate(cut, axis=-1).reshape(rows, -1)


def core_order(own, other, axis):
    core = lax.axis_index("pipe")
    return jnp.where(
        core == 0,
        jnp.concatenate([own, other], axis=axis),
        jnp.concatenate([other, own], axis=axis),
    )


def unpack_attention(own, other, widths):
    query_w, kv_w, out_w = widths
    cuts = (query_w, query_w + kv_w, query_w + 2 * kv_w)

    def split(m):
        return (m[:, : cuts[0]], m[:, cuts[0] : cuts[1]], m[:, cuts[1] : cuts[2]], m[:, cuts[2] :])

    q0, k0, v0, o0 = split(own)
    q1, k1, v1, o1 = split(other)
    return (
        jnp.concatenate([q0, q1], axis=1),
        core_order(k0, k1, 1),
        core_order(v0, v1, 1),
        jnp.concatenate([o0, o1], axis=1),
    )


def core_halves(grad):
    half = grad.shape[1] // 2
    core = lax.axis_index("pipe")
    low, high = grad[:, :half], grad[:, half:]
    return (jnp.where(core == 0, low, high), jnp.where(core == 0, high, low))


def grad_pair(own, other):
    total = own + hop(other.astype(BF), "pipe", 1).astype(F32)
    return total.reshape((lax.axis_size("grp"), -1) + total.shape[1:])


def mlp_pair(left, right):
    half = right.shape[1] // 2
    return grad_pair(mm_tl(left, right[:, :half]), mm_tl(left, right[:, half:]))


def grad_part(part):
    def add(blocks):
        cols = blocks.shape[2] // 2
        cut = blocks[:, :, part * cols : (part + 1) * cols]
        total = cut[0]
        for k in range(1, blocks.shape[0]):
            total = total + hop(cut[k].astype(BF), "grp", k).astype(F32)
        wd = lax.axis_size("wd")
        me = lax.axis_index("wd")
        total = total.astype(BF).reshape((wd, -1) + total.shape[1:])
        pieces = [lax.dynamic_index_in_dim(total, me, 0, keepdims=False)]
        for k in range(1, wd):
            sent = lax.dynamic_index_in_dim(total, me ^ k, 0, keepdims=False)
            pieces.append(hop(sent, "wd", k))
        return jnp.stack(pieces)

    return add


def place_kernel(turned, at_ref, *refs):
    out_ref = refs[-1]
    parts = (len(refs) - 1) // 2
    mine = pl.program_id(1) == at_ref[1]

    def put(sources):
        cols = sources[0].shape[2]
        for i, ref in enumerate(sources):
            block = ref[0].astype(F32)
            if turned:
                out_ref[i * cols : (i + 1) * cols, :] = block.T
            else:
                out_ref[:, i * cols : (i + 1) * cols] = block

    @pl.when(mine)
    def _():
        put(refs[:parts])

    @pl.when(jnp.logical_not(mine))
    def _():
        put(refs[parts:-1])


def place(keep, got, turned):
    wd, rows, cols = keep[0].shape
    at = jnp.stack([lax.axis_index("wd"), lax.axis_index("pipe")]).astype(jnp.int32)
    cores = lax.axis_size("pipe")
    source = pl.BlockSpec((1, rows, cols), lambda w, c, at_ref: (w ^ at_ref[0], 0, 0))
    wide = cols * len(keep)
    if turned:
        shape, target = (wd * cores * wide, rows), (wide, rows)
        out = pl.BlockSpec(target, lambda w, c, at_ref: (w * cores + c, 0))
    else:
        shape, target = (rows, wd * cores * wide), (rows, wide)
        out = pl.BlockSpec(target, lambda w, c, at_ref: (0, w * cores + c))
    return pl.pallas_call(
        lambda *refs: place_kernel(turned, *refs),
        grid_spec=pltpu.PrefetchScalarGridSpec(
            num_scalar_prefetch=1,
            grid=(wd, cores),
            in_specs=[source] * (2 * len(keep)),
            out_specs=out,
        ),
        out_shape=jax.ShapeDtypeStruct(shape, F32),
        cost_estimate=pl.CostEstimate(
            flops=wd * rows * wide, bytes_accessed=12 * wd * rows * wide, transcendentals=0
        ),
    )(at, *keep, *got)


def layer_forward(stages, layer, x_rows, gains, where, jobs):
    held = stages.held
    cosine, sine, q_place, q_start, k_place = where
    normed = apply_norm(x_rows, gains[0]).astype(BF)
    rows_a = stages.run(normed, gather_rows, jobs[0])
    w_q, w_k, w_v, w_ot = held["attn", layer]
    tok = rows_a.shape[0]

    def project(rows):
        key = rotary_apply(mm(rows, w_k).reshape(tok, 1, HEAD_SIZE), cosine, sine).astype(BF)[:, 0]
        value = mm(rows, w_v).astype(BF)
        return jnp.concatenate([key, value], axis=1)

    def queries(rows):
        query = rotary_apply(mm(rows, w_q).reshape(tok, -1, HEAD_SIZE), cosine, sine).astype(BF)
        return query.transpose(1, 0, 2)

    held["rows_a"] = rows_a
    kv_all = stages.run(
        project(rows_a),
        lambda kv: jnp.concatenate(others(kv, "grp"), axis=0),
        [("query", queries, ("rows_a",))] + jobs[1],
    )
    query = held["query"]
    keys, values = kv_all[:, :HEAD_SIZE], kv_all[:, HEAD_SIZE:]

    def attention(q):
        context = attend(q, keys, values, q_place, q_start, k_place)
        context = context.transpose(1, 0, 2).reshape(tok, -1)
        return context, mm_t(context, w_ot).astype(BF)

    context, partial = stages.run(query, attention, jobs[2])
    mid = stages.run(partial, lambda p: x_rows + sum_rows(p), jobs[3])
    rows_b = stages.run(
        mid, lambda m: gather_rows(apply_norm(m, gains[1]).astype(BF)), jobs[4]
    )
    rows_b = stages.run(rows_b, lambda r: r, jobs[5])
    w_gu = held["gu", layer]

    def ahead(rows):
        both = mm(rows, w_gu)
        half = both.shape[1] // 2
        gate, up = both[:, :half], both[:, half:]
        return gate, up, (jax.nn.silu(gate) * up).astype(BF)

    gate, up, hidden = stages.run(rows_b, ahead, jobs[6])
    return x_rows, rows_a, query, keys, values, context, mid, rows_b, gate, up, hidden


def layer_backward(stages, layer, grad_out, grad_mlp, gains, where, kept, also, jobs):
    held = stages.held
    cosine, sine, q_place, q_start, k_place = where
    x_rows, rows_a, query, keys, values, context, mid, rows_b, gate, up, hidden = kept
    w_q, w_k, w_v, w_ot = held["attn", layer]
    w_gu, w_dt = held["gu", layer], held["down", layer]
    tok = rows_a.shape[0]
    held["rows_b"], held["hidden"], held["grad_mlp"] = rows_b, hidden, grad_mlp

    def feed_back(rows):
        grad_hidden = mm(rows, w_dt)
        sig = jax.nn.sigmoid(gate)
        grad_gate = (grad_hidden * up * sig * (1.0 + gate * (1.0 - sig))).astype(BF)
        grad_up = (grad_hidden * gate * sig).astype(BF)
        both = jnp.concatenate([grad_gate, grad_up], axis=1)
        return grad_gate, grad_up, mm_t(both, w_gu).astype(BF), also(hidden)

    grad_gate, grad_up, partial, extra = stages.run(grad_mlp, feed_back, jobs[0])
    held["grad_gate"], held["grad_up"] = grad_gate, grad_up
    grad_b = stages.run(partial, sum_rows, jobs[1])
    grad_mid, gain_b = norm_back(mid, gains[1], grad_b)
    grad_mid = grad_mid + grad_out
    grad_attn = stages.run(grad_mid.astype(BF), gather_rows, jobs[2])

    def attention_back(rows):
        grad_context = mm(rows, w_ot).astype(BF)
        grad_context = grad_context.reshape(tok, -1, HEAD_SIZE).transpose(1, 0, 2)
        return attend_back(query, grad_context, keys, values, q_place, q_start, k_place)

    def keys_back(grads):
        kv = jnp.concatenate(grads, axis=1)
        kv = kv.reshape((-1, tok) + kv.shape[1:])
        return sum_others([kv[k] for k in range(kv.shape[0])], "grp").astype(BF)

    def queries_back(grad_q):
        grad_q = grad_q.transpose(1, 0, 2).astype(F32)
        grad_q = rotary_apply(grad_q, cosine, -sine).astype(BF).reshape(tok, -1)
        return grad_q, mm_t(grad_q, w_q)

    held["grad_q"], *grads = stages.run(grad_attn, attention_back, jobs[3])
    own_kv = stages.run(grads, keys_back, [("g_q", queries_back, ("grad_q",))] + jobs[4])
    grad_q, partial = held["g_q"]
    grad_k = own_kv[:, :HEAD_SIZE].astype(F32)
    grad_k = rotary_apply(grad_k[:, None, :], cosine, -sine).astype(BF)[:, 0]
    grad_v = own_kv[:, HEAD_SIZE:]
    partial = (partial + mm_t(grad_k, w_k) + mm_t(grad_v, w_v)).astype(BF)

    def attn_pair(g_q, g_k, g_v):
        half_q = g_q.shape[1] // 2
        kv_0, kv_1 = core_halves(g_k)
        v_0, v_1 = core_halves(g_v)

        def term(q_half, k_half, v_half, o_half):
            right = jnp.concatenate([q_half, k_half, v_half], axis=1)
            return jnp.concatenate([mm_tl(rows_a, right), mm_tl(grad_attn, o_half)], axis=1)

        return grad_pair(
            term(g_q[:, :half_q], kv_0, v_0, context[:, :half_q]),
            term(g_q[:, half_q:], kv_1, v_1, context[:, half_q:]),
        )

    held["g_q"], held["g_k"], held["g_v"] = grad_q, grad_k, grad_v
    grad_a = stages.run(partial, sum_rows, jobs[5](attn_pair))
    grad_in, gain_a = norm_back(x_rows, gains[0], grad_a)
    return grad_mid + grad_in, jnp.stack([gain_a, gain_b]), extra


def own_layer(first, second):
    core = lax.axis_index("pipe")
    keep = jnp.where(core == 0, first, second)
    return keep, hop(jnp.where(core == 0, second, first), "pipe", 1)


def body(
    block_input,
    cotangent,
    segments,
    norm_gains,
    w_query,
    key_matrix,
    value_matrix,
    w_output,
    w_gate,
    w_up,
    w_down,
):
    core = lax.axis_index("pipe")
    grp = lax.axis_index("grp")
    wd = lax.axis_size("wd")
    groups = lax.axis_size("grp")
    cores = lax.axis_size("pipe")
    tok = block_input.shape[1] * lax.axis_size(CUBE)

    stages = Stages()
    held = stages.held
    packed = pack_attention(w_query[0], key_matrix[0], value_matrix[0], w_output[0], cores)
    attn_cols = columns_out(to_blocks(packed, cores))
    held["attn"], first_gains = lax.optimization_barrier((attn_cols, norm_gains[0]))
    gains = spread_gains(first_gains)
    held["gate_out"] = to_blocks(w_gate[0], cores)
    held["up_out"] = to_blocks(w_up[0], cores)
    held["down_out"] = to_blocks(w_down[0].T, cores)
    widths = tuple(n // (wd * cores) for n in (w_query.shape[2], key_matrix.shape[2], w_output.shape[1]))

    def move(name):
        return (name, columns_out, (name + "_out",))

    def swap(name, layer, part=None):
        return ((name, layer, part), piece_of(layer, part), (name,))

    def parts(name, layer):
        if name == "attn":
            return ((name, layer, None),)
        return ((name, layer, 0), (name, layer, 1))

    def attn_ready(layer):
        def ready(*values):
            own, there = stacked(values)
            return unpack_attention(
                jnp.concatenate(own, axis=0), jnp.concatenate(there, axis=0), widths
            )

        return (("attn", layer), ready, parts("attn", layer))

    def gate_up_ready(layer):
        def ready(*values):
            gate, up = stacked(values[:2]), stacked(values[2:])
            return put_together([gate[0], gate[1], up[0], up[1]])

        return (("gu", layer), ready, parts("gate", layer) + parts("up", layer))

    def down_ready(layer):
        return (
            ("down", layer),
            lambda *values: put_together(stacked(values)),
            parts("down", layer),
        )

    seg_row = lax.dynamic_index_in_dim(segments, core, 0, keepdims=False)
    starts = doc_starts(seg_row)
    rows_own = tok // lax.axis_size(CUBE)

    def in_row_order(values):
        values = relative(values, 0, CUBE)
        return jnp.concatenate(
            [values[j * rows_own : (j + 1) * rows_own] for j in ROW_ORDER], axis=0
        )

    local = in_row_order(jnp.arange(tok, dtype=jnp.int32))
    q_place = grp * tok + local
    q_start = in_row_order(lax.dynamic_slice_in_dim(starts, grp * tok, tok))
    cosine, sine = rope_tables(q_place - q_start)
    k_place = jnp.concatenate([(grp ^ k) * tok + local for k in range(groups)])
    where = (cosine, sine, q_place[:, None], q_start[:, None], k_place[None, :])

    rows = relative(lax.dynamic_index_in_dim(block_input, core, 0, keepdims=False), 1, "grp")
    grad = relative(lax.dynamic_index_in_dim(cotangent, core, 0, keepdims=False), 1, "grp")
    held["cotangent"] = grad
    key, job, names = swap("attn", 0)
    held[key] = job(held["attn"])
    rows, held[key], gains = lax.optimization_barrier((rows, held[key], gains))
    kept = [None, None]
    outs = [None, None]
    kept[0] = layer_forward(
        stages,
        0,
        rows.astype(F32),
        gains[0],
        where,
        (
            [attn_ready(0), swap("attn", 1), move("gate")],
            [swap("gate", 0, 0), move("up")],
            [swap("gate", 0, 1), move("down")],
            [swap("up", 0, 0), swap("up", 0, 1)],
            [swap("down", 0, 0)],
            [swap("down", 0, 1), gate_up_ready(0)],
            [],
        ),
    )

    def close(hidden, layer):
        return (kept[layer][6] + sum_rows(mm_t(hidden, held["down", layer]))).astype(BF)

    hidden = kept[0][-1]
    hidden = stages.run(hidden, lambda h: h, [down_ready(0)])
    outs[0] = stages.run(hidden, lambda h: close(h, 0), [swap("gate", 1, 0)])
    kept[1] = layer_forward(
        stages,
        1,
        outs[0].astype(F32),
        gains[1],
        where,
        (
            [swap("gate", 1, 1), attn_ready(1)],
            [swap("up", 1, 0)],
            [swap("up", 1, 1), ("last", gather_rows, ("cotangent",))],
            [swap("down", 1, 0)],
            [swap("down", 1, 1)],
            [gate_up_ready(1)],
            [],
        ),
    )

    def grad_of(name, layer):
        sources = {
            "down": ("grad_mlp", "hidden"),
            "gate": ("rows_b", "grad_gate"),
            "up": ("rows_b", "grad_up"),
        }[name]
        return (("pair", name, layer), mlp_pair, sources)

    def grad_swap(name, layer, part):
        return (("part", name, layer, part), grad_part(part), (("pair", name, layer),))

    def attn_grad(layer):
        return lambda pair: (("pair", "attn", layer), pair, ("g_q", "g_k", "g_v"))

    def both(firsts, seconds):
        pairs = [own_layer(first, second) for first, second in zip(firsts, seconds)]
        return [p[0] for p in pairs], [p[1] for p in pairs]

    def final(name, turned):
        def ready(*values):
            return place(*both(values[:2], values[2:]), turned)

        names = tuple(("part", name, layer, part) for layer in range(2) for part in range(2))
        return (("final", name), ready, names)

    held["hidden"], held["grad_mlp"] = kept[1][-1], held["last"]
    hidden = stages.run(kept[1][-1], lambda h: h, [down_ready(1), grad_of("down", 1)])

    grads_in = [None, None]
    gain_grads = [None, None]
    grad_in, gain_grads[1], outs[1] = layer_backward(
        stages,
        1,
        grad.astype(F32),
        held["last"],
        gains[1],
        where,
        kept[1][:-1] + (hidden,),
        lambda h: close(h, 1),
        (
            [grad_swap("down", 1, 0)],
            [grad_swap("down", 1, 1), grad_of("gate", 1)],
            [grad_of("up", 1)],
            [grad_swap("gate", 1, 0)],
            [grad_swap("gate", 1, 1)],
            lambda pair: [grad_swap("up", 1, 0), attn_grad(1)(pair)],
        ),
    )
    grads_in[1] = grad_in.astype(BF)
    grad_mlp = stages.run(grads_in[1], gather_rows, [grad_swap("up", 1, 1)])
    grad_in, gain_grads[0], _ = layer_backward(
        stages,
        0,
        grads_in[1].astype(F32),
        grad_mlp,
        gains[0],
        where,
        kept[0],
        lambda h: (),
        (
            [grad_of("down", 0), grad_swap("attn", 1, 0), grad_swap("attn", 1, 1)],
            [grad_swap("down", 0, 0), grad_of("gate", 0)],
            [grad_swap("down", 0, 1), grad_of("up", 0)],
            [grad_swap("gate", 0, 0)],
            [grad_swap("gate", 0, 1)],
            lambda pair: [grad_swap("up", 0, 0), attn_grad(0)(pair), final("down", True)],
        ),
    )
    grads_in[0] = grad_in.astype(BF)
    tail = grads_in[0]
    for jobs in (
        [grad_swap("attn", 0, 0), grad_swap("attn", 0, 1)],
        [grad_swap("up", 0, 1), final("gate", False)],
    ):
        tail = stages.run(tail, lambda t: t, jobs)

    def by_batch(pair):
        own, other = own_layer(pair[0], pair[1])
        both = jnp.where(core == 0, jnp.stack([own, other]), jnp.stack([other, own]))
        return relative(both, 2, "grp")[None]

    layer_out = by_batch(outs)
    input_grad = by_batch(grads_in)

    grad_norm_gains = sum_gains(gain_grads)[None]

    halves = [[held["part", "attn", layer, part] for part in range(2)] for layer in range(2)]
    keep, got = both([jnp.concatenate(halves[0], axis=2)], [jnp.concatenate(halves[1], axis=2)])
    keep, got = keep[0], got[0]
    cuts = (0, widths[0], widths[0] + widths[1], widths[0] + 2 * widths[1], keep.shape[2])
    q_pair, k_pair, v_pair, o_pair = (
        (keep[..., lo:hi], got[..., lo:hi]) for lo, hi in zip(cuts[:-1], cuts[1:])
    )

    def small(pair):
        order = jnp.where(core == 0, jnp.stack(pair), jnp.stack(pair[::-1]))
        order = relative(order, 1, "wd").transpose(2, 1, 0, 3).astype(F32)
        return order.reshape(order.shape[0], -1)[None]

    grad_wq = place([q_pair[0]], [q_pair[1]], False)[None]
    grad_wk = small(k_pair)
    grad_wv = small(v_pair)
    grad_wo = place([o_pair[0]], [o_pair[1]], True)[None]
    grad_wg = held["final", "gate"][None]
    key, job, names = final("up", False)
    grad_wu = job(*[held[name] for name in names])[None]
    grad_wd = held["final", "down"][None]
    return (
        layer_out,
        input_grad,
        grad_norm_gains,
        grad_wq,
        grad_wk,
        grad_wv,
        grad_wo,
        grad_wg,
        grad_wu,
        grad_wd,
    )


def solution(mesh):
    sizes = dict(mesh.shape)
    wd = KV_HEADS // sizes["tensor"]
    fine = Mesh(
        mesh.devices.reshape(sizes["pipe"], sizes["dp"] // wd, wd, sizes["tensor"]),
        ("pipe", "grp", "wd", "tensor"),
    )
    dp = ("grp", "wd")
    tokens = P(None, dp + ("tensor",), None)
    outs = P("pipe", None, dp + ("tensor",), None)
    gains = P("pipe", None, dp + ("tensor",))
    tall = P("pipe", dp, "tensor")
    wide = P("pipe", "tensor", dp)
    weights = (tall, tall, tall, wide, tall, tall, wide)
    return jax.shard_map(
        body,
        mesh=fine,
        in_specs=(tokens, tokens, P(), gains) + weights,
        out_specs=(outs, outs, gains) + weights,
        check_vma=False,
    )
```

```python
import jax
import jax.numpy as jnp
from jax import lax
from jax.experimental import pallas as pl
from jax.experimental.pallas import tpu as pltpu
from jax.sharding import Mesh, PartitionSpec as P

HEAD_SIZE = 64
KV_HEADS = 8
EPS = 1e-05
ROPE_BASE = 500000.0
NEG_FILL = -1e30
BF = jnp.bfloat16
F32 = jnp.float32
CUBE = ("wd", "tensor")


def rms_scale(row_values):
    return lax.rsqrt(jnp.mean(row_values * row_values, axis=-1, keepdims=True) + EPS)


def apply_norm(row_values, gain_vector):
    return row_values * rms_scale(row_values) * gain_vector


def norm_back(row_values, gain_vector, grad_normed):
    _, pullback = jax.vjp(apply_norm, row_values, gain_vector)
    return pullback(grad_normed)


def doc_starts(seg_row):
    places = jnp.arange(seg_row.shape[0], dtype=jnp.int32)
    before = jnp.concatenate([seg_row[:1] - 1, seg_row[:-1]])
    return lax.cummax(jnp.where(seg_row != before, places, 0), axis=0)


def rope_tables(positions):
    half_dim = HEAD_SIZE // 2
    freqs = ROPE_BASE ** (-(jnp.arange(half_dim, dtype=F32) * 2.0 / HEAD_SIZE))
    angles = positions.astype(F32)[:, None] * freqs[None, :]
    return (jnp.cos(angles), jnp.sin(angles))


def rotary_apply(head_values, cosine_table, sine_values):
    half_dim = head_values.shape[-1] // 2
    first_half = head_values[..., :half_dim]
    second_half = head_values[..., half_dim:]
    cos_rows = cosine_table[:, None, :]
    sin_rows = sine_values[:, None, :]
    return jnp.concatenate(
        [
            first_half * cos_rows - second_half * sin_rows,
            second_half * cos_rows + first_half * sin_rows,
        ],
        axis=-1,
    )


def mm(left, right):
    return jnp.dot(left, right, preferred_element_type=F32)


def mm_t(left, right):
    return lax.dot_general(left, right, (((1,), (1,)), ((), ())), preferred_element_type=F32)


def mm_tl(left, right):
    return lax.dot_general(left, right, (((0,), (0,)), ((), ())), preferred_element_type=F32)


def trade(blocks, axes):
    return lax.all_to_all(blocks, axes, 0, 0, tiled=True)


def hop(block, axis, step):
    size = lax.axis_size(axis)
    return lax.ppermute(block, axis, [(i, i ^ step) for i in range(size)])


def tie(*values):
    return lax.optimization_barrier(values)


def link_steps():
    steps = []
    step = 1
    while step < lax.axis_size(CUBE):
        steps.append(step)
        step *= 2
    return steps


FAR, NEAR, SIDE = 4, 2, 1
ROW_ORDER = (0, FAR, NEAR, FAR | NEAR, SIDE, FAR | SIDE, NEAR | SIDE, FAR | NEAR | SIDE)


def cube(block, step):
    return hop(block, CUBE, step)


def join_kernel(left_ref, left_came_ref, right_ref, right_came_ref, out_ref):
    half = left_ref.shape[1]
    block = pl.program_id(0)

    @pl.when(block < 2)
    def _():
        out_ref[:, :half] = left_ref[...]

    @pl.when(block >= 2)
    def _():
        out_ref[:, :half] = left_came_ref[...]

    @pl.when(block % 2 == 0)
    def _():
        out_ref[:, half:] = right_ref[...]

    @pl.when(block % 2 == 1)
    def _():
        out_ref[:, half:] = right_came_ref[...]


def join_halves(left, left_came, right, right_came):
    rows, half = left.shape[0] // 2, left.shape[1]

    def spec(place):
        return pl.BlockSpec((rows, half), lambda i: (place(i), 0))

    return pl.pallas_call(
        join_kernel,
        grid=(4,),
        in_specs=[
            spec(lambda i: jnp.minimum(i, 1)),
            spec(lambda i: jnp.maximum(i - 2, 0)),
            spec(lambda i: i // 2),
            spec(lambda i: i // 2),
        ],
        out_specs=pl.BlockSpec((rows, 2 * half), lambda i: (i, 0)),
        out_shape=jax.ShapeDtypeStruct((4 * rows, 2 * half), left.dtype),
        cost_estimate=pl.CostEstimate(
            flops=0, bytes_accessed=32 * rows * half, transcendentals=0
        ),
    )(left, left_came, right, right_came)


def gather_rows(rows):
    two = jnp.concatenate([rows, cube(rows, FAR)], axis=0)
    half = two.shape[1] // 2
    left, right = two[:, :half], two[:, half:]
    left_came, right_came = cube(left, NEAR), cube(right, SIDE)
    left = jnp.concatenate([left, left_came], axis=0)
    right = jnp.concatenate([right, right_came], axis=0)
    return join_halves(left, cube(left, SIDE), right, cube(right, NEAR))


def sum_rows(partial):
    partial = partial.astype(BF)
    n, half = partial.shape[0] // 4, partial.shape[1] // 2
    left, right = partial[:, :half], partial[:, half:]
    left_came = cube(left[2 * n :], SIDE)
    right_came = cube(jnp.concatenate([right[n : 2 * n], right[3 * n :]], axis=0), NEAR)
    left = left[: 2 * n].astype(F32) + left_came.astype(F32)
    right_came = right_came.astype(F32)
    low = right[:n].astype(F32) + right_came[:n]
    high = right[2 * n : 3 * n].astype(F32) + right_came[n:]
    left_came = cube(left[n:].astype(BF), NEAR)
    right_came = cube(high.astype(BF), SIDE)
    left = left[:n] + left_came.astype(F32)
    right = low + right_came.astype(F32)
    both = jnp.concatenate([left, right], axis=1)
    rows = n // 2
    return both[:rows] + cube(both[rows:].astype(BF), FAR).astype(F32)


class Stages:
    def __init__(self):
        self.held = {}

    def run(self, value, step, jobs):
        needed = [[self.held[name] for name in job[2]] for job in jobs]
        value, needed = lax.optimization_barrier((value, needed))
        out = step(value)
        made = [job[1](*inputs) for job, inputs in zip(jobs, needed)]
        due = [m for m, job in zip(made, jobs) if len(job) == 3]
        out, due = lax.optimization_barrier((out, due))
        for job, result in zip(jobs, made):
            self.held[job[0]] = due.pop(0) if len(job) == 3 else result
        return out


def others(block, axis):
    return [block] + [hop(block, axis, k) for k in range(1, lax.axis_size(axis))]


def sum_others(blocks, axis):
    total = blocks[0].astype(F32)
    for k in range(1, lax.axis_size(axis)):
        total = total + hop(blocks[k].astype(BF), axis, k).astype(F32)
    return total


def relative(values, dim, axis):
    count = lax.axis_size(axis)
    me = lax.axis_index(axis)
    step = 1
    while step < count:
        shape = values.shape
        cut = shape[:dim] + (count // (2 * step), 2, step * (shape[dim] // count)) + shape[dim + 1 :]
        view = values.reshape(cut)
        swapped = jnp.concatenate(
            [lax.slice_in_dim(view, 1, 2, axis=dim + 1), lax.slice_in_dim(view, 0, 1, axis=dim + 1)],
            axis=dim + 1,
        )
        values = jnp.where((me & step) != 0, swapped.reshape(shape), values)
        step *= 2
    return values


def spread_gains(norm_gains):
    me = lax.axis_index(CUBE)
    gain = norm_gains
    for step in link_steps():
        came = hop(gain, CUBE, step)
        gain = jnp.where(
            (me & step) != 0,
            jnp.concatenate([came, gain], axis=1),
            jnp.concatenate([gain, came], axis=1),
        )
    gain = relative(jnp.concatenate(others(gain, "grp"), axis=1), 1, "grp")
    other = hop(gain, "pipe", 1)
    core = lax.axis_index("pipe")
    return [jnp.where(core == 0, gain, other), jnp.where(core == 0, other, gain)]


def sum_gains(grads):
    me = lax.axis_index(CUBE)
    keep, extra = own_layer(grads[0], grads[1])
    count = lax.axis_size("grp")
    total = relative((keep + extra).reshape(2, count, -1), 1, "grp")
    mine = total[:, 0]
    for k in range(1, count):
        mine = mine + hop(total[:, k], "grp", k)
    for step in link_steps()[::-1]:
        half = mine.shape[1] // 2
        low, high = mine[:, :half], mine[:, half:]
        odd = (me & step) != 0
        mine = jnp.where(odd, high, low) + hop(jnp.where(odd, low, high), CUBE, step)
    return mine


def masked_probs(q, k, q_place, q_start, k_place):
    scores = lax.dot_general(q, k, (((1,), (1,)), ((), ())), preferred_element_type=F32)
    scores = scores * HEAD_SIZE ** (-0.5)
    allowed = (k_place <= q_place) & (k_place >= q_start)
    masked = jnp.where(allowed, scores, NEG_FILL)
    exps = jnp.exp(masked - jnp.max(masked, axis=-1, keepdims=True))
    return exps / jnp.sum(exps, axis=-1, keepdims=True)


def attend_kernel(q_ref, k_ref, v_ref, qp_ref, qs_ref, kp_ref, o_ref):
    probs = masked_probs(q_ref[0], k_ref[...], qp_ref[...], qs_ref[...], kp_ref[...])
    o_ref[0] = jnp.dot(probs.astype(BF), v_ref[...], preferred_element_type=F32).astype(BF)


def attend_back_kernel(q_ref, do_ref, k_ref, v_ref, qp_ref, qs_ref, kp_ref, dq_ref, dk_ref, dv_ref):
    @pl.when((pl.program_id(0) == 0) & (pl.program_id(1) == 0))
    def _():
        dk_ref[...] = jnp.zeros_like(dk_ref)
        dv_ref[...] = jnp.zeros_like(dv_ref)

    q = q_ref[0]
    do = do_ref[0]
    k = k_ref[...]
    probs = masked_probs(q, k, qp_ref[...], qs_ref[...], kp_ref[...])
    grad_probs = lax.dot_general(do, v_ref[...], (((1,), (1,)), ((), ())), preferred_element_type=F32)
    delta = jnp.sum(probs * grad_probs, axis=-1, keepdims=True)
    grad_scores = (probs * (grad_probs - delta) * HEAD_SIZE ** (-0.5)).astype(BF)
    dq_ref[0] = jnp.dot(grad_scores, k, preferred_element_type=F32).astype(BF)
    dk_ref[...] += lax.dot_general(
        grad_scores, q, (((0,), (0,)), ((), ())), preferred_element_type=F32
    )
    dv_ref[...] += lax.dot_general(
        probs.astype(BF), do, (((0,), (0,)), ((), ())), preferred_element_type=F32
    )


def attention_specs(heads, rows, keys):
    rows_blk = max(16, min(rows, (512 * 1024) // keys))
    per_head = pl.BlockSpec((1, rows_blk, HEAD_SIZE), lambda b, h: (h, b, 0))
    full = pl.BlockSpec((keys, HEAD_SIZE), lambda b, h: (0, 0))
    row_info = pl.BlockSpec((rows_blk, 1), lambda b, h: (b, 0))
    key_info = pl.BlockSpec((1, keys), lambda b, h: (0, 0))
    return ((rows // rows_blk, heads), per_head, full, row_info, key_info)


PARAMS = dict(
    compiler_params=pltpu.CompilerParams(vmem_limit_bytes=50 * 1024 * 1024),
)


def attend(q, k, v, q_place, q_start, k_place):
    heads, rows, _ = q.shape
    keys = k.shape[0]
    grid, per_head, full, row_info, key_info = attention_specs(heads, rows, keys)
    return pl.pallas_call(
        attend_kernel,
        grid=grid,
        in_specs=[per_head, full, full, row_info, row_info, key_info],
        out_specs=per_head,
        out_shape=jax.ShapeDtypeStruct(q.shape, BF),
        cost_estimate=pl.CostEstimate(
            flops=4 * heads * rows * keys * HEAD_SIZE,
            bytes_accessed=4 * q.size + 4 * k.size,
            transcendentals=heads * rows * keys,
        ),
        **PARAMS,
    )(q, k, v, q_place, q_start, k_place)


def attend_back(q, do, k, v, q_place, q_start, k_place):
    heads, rows, _ = q.shape
    keys = k.shape[0]
    grid, per_head, full, row_info, key_info = attention_specs(heads, rows, keys)
    return pl.pallas_call(
        attend_back_kernel,
        grid=grid,
        in_specs=[per_head, per_head, full, full, row_info, row_info, key_info],
        out_specs=[per_head, full, full],
        out_shape=[
            jax.ShapeDtypeStruct(q.shape, BF),
            jax.ShapeDtypeStruct(k.shape, F32),
            jax.ShapeDtypeStruct(k.shape, F32),
        ],
        cost_estimate=pl.CostEstimate(
            flops=10 * heads * rows * keys * HEAD_SIZE,
            bytes_accessed=6 * q.size + 12 * k.size,
            transcendentals=heads * rows * keys,
        ),
        **PARAMS,
    )(q, do, k, v, q_place, q_start, k_place)


def to_blocks(weight, cores):
    wd = lax.axis_size("wd")
    rows = weight.shape[0]
    cut = weight.reshape(rows, wd, cores, -1).transpose(2, 1, 0, 3)
    return cut.reshape((cores * wd, rows) + cut.shape[3:])


def columns_out(blocks):
    moved = trade(blocks, ("pipe", "wd"))
    return moved.reshape((2, -1) + moved.shape[2:])


def put_kernel(spots, *refs):
    pieces, out = refs[: len(spots)], refs[len(spots)]
    block = pl.program_id(0)
    for piece, (first, count, col, cols) in zip(pieces, spots):

        def put(piece=piece, col=col, cols=cols):
            out[:, col : col + cols] = piece[...]

        pl.when((block >= first) & (block < first + count))(put)


def put_together(columns):
    block = min([256] + [piece.shape[0] for stack in columns for piece in stack])
    spots, pieces, specs = [], [], []
    col = 0
    for stack in columns:
        first = 0
        for piece in stack:
            count, cols = piece.shape[0] // block, piece.shape[1]
            spots.append((first, count, col, cols))
            pieces.append(piece)

            def at(i, first=first, count=count):
                return (jnp.clip(i - first, 0, count - 1), 0)

            specs.append(pl.BlockSpec((block, cols), at))
            first += count
        col += cols
    return pl.pallas_call(
        lambda *refs: put_kernel(spots, *refs),
        grid=(first,),
        in_specs=specs,
        out_specs=pl.BlockSpec((block, col), lambda i: (i, 0)),
        out_shape=jax.ShapeDtypeStruct((first * block, col), BF),
        cost_estimate=pl.CostEstimate(
            flops=0, bytes_accessed=4 * first * block * col, transcendentals=0
        ),
        **PARAMS,
    )(*pieces)


def all_rows(cols):
    own = lax.all_gather(cols, "grp", axis=0, tiled=True)
    return own, hop(own, "pipe", 1)


def pack_attention(w_query, key_matrix, value_matrix, w_output, cores):
    wd = lax.axis_size("wd")
    rows = w_query.shape[0]
    cut = [
        m.reshape(rows, wd, cores, -1) for m in (w_query, key_matrix, value_matrix, w_output.T)
    ]
    return jnp.concatenate(cut, axis=-1).reshape(rows, -1)


def core_order(own, other, axis):
    core = lax.axis_index("pipe")
    return jnp.where(
        core == 0,
        jnp.concatenate([own, other], axis=axis),
        jnp.concatenate([other, own], axis=axis),
    )


def unpack_attention(own, other, widths):
    query_w, kv_w, out_w = widths
    cuts = (query_w, query_w + kv_w, query_w + 2 * kv_w)

    def split(m):
        return (m[:, : cuts[0]], m[:, cuts[0] : cuts[1]], m[:, cuts[1] : cuts[2]], m[:, cuts[2] :])

    q0, k0, v0, o0 = split(own)
    q1, k1, v1, o1 = split(other)
    return (
        jnp.concatenate([q0, q1], axis=1),
        core_order(k0, k1, 1),
        core_order(v0, v1, 1),
        jnp.concatenate([o0, o1], axis=1),
    )


def core_halves(grad):
    half = grad.shape[1] // 2
    core = lax.axis_index("pipe")
    low, high = grad[:, :half], grad[:, half:]
    return (jnp.where(core == 0, low, high), jnp.where(core == 0, high, low))


def grad_pair(own, other):
    return (own + hop(other.astype(BF), "pipe", 1).astype(F32)).astype(BF)


def mlp_pair(left, right):
    half = right.shape[1] // 2
    return grad_pair(mm_tl(left, right[:, :half]), mm_tl(left, right[:, half:]))


def grad_group(total):
    return lax.psum_scatter(total, "grp", scatter_dimension=0, tiled=True)


def grad_home(total):
    wd = lax.axis_size("wd")
    me = lax.axis_index("wd")
    blocks = total.reshape((wd, -1) + total.shape[1:])
    pieces = [lax.dynamic_index_in_dim(blocks, me, 0, keepdims=False)]
    for k in range(1, wd):
        pieces.append(hop(lax.dynamic_index_in_dim(blocks, me ^ k, 0, keepdims=False), "wd", k))
    return jnp.stack(pieces)


def place_kernel(turned, at_ref, keep_ref, got_ref, out_ref):
    mine = pl.program_id(1) == at_ref[1]

    def put(ref):
        block = ref[0].astype(F32)
        out_ref[...] = block.T if turned else block

    @pl.when(mine)
    def _():
        put(keep_ref)

    @pl.when(jnp.logical_not(mine))
    def _():
        put(got_ref)


def place(keep, got, turned):
    wd, rows, cols = keep.shape
    at = jnp.stack([lax.axis_index("wd"), lax.axis_index("pipe")]).astype(jnp.int32)
    cores = lax.axis_size("pipe")
    source = pl.BlockSpec((1, rows, cols), lambda w, c, at_ref: (w ^ at_ref[0], 0, 0))
    if turned:
        shape, target = (wd * cores * cols, rows), (cols, rows)
        out = pl.BlockSpec(target, lambda w, c, at_ref: (w * cores + c, 0))
    else:
        shape, target = (rows, wd * cores * cols), (rows, cols)
        out = pl.BlockSpec(target, lambda w, c, at_ref: (0, w * cores + c))
    return pl.pallas_call(
        lambda *refs: place_kernel(turned, *refs),
        grid_spec=pltpu.PrefetchScalarGridSpec(
            num_scalar_prefetch=1, grid=(wd, cores), in_specs=[source, source], out_specs=out
        ),
        out_shape=jax.ShapeDtypeStruct(shape, F32),
        cost_estimate=pl.CostEstimate(
            flops=keep.size, bytes_accessed=12 * keep.size, transcendentals=0
        ),
    )(at, keep, got)


def layer_forward(stages, layer, x_rows, gains, where, jobs):
    held = stages.held
    cosine, sine, q_place, q_start, k_place = where
    normed = apply_norm(x_rows, gains[0]).astype(BF)
    rows_a = stages.run(normed, gather_rows, jobs[0])
    w_q, w_k, w_v, w_ot = held["attn", layer]
    tok = rows_a.shape[0]

    def project(rows):
        key = rotary_apply(mm(rows, w_k).reshape(tok, 1, HEAD_SIZE), cosine, sine).astype(BF)[:, 0]
        value = mm(rows, w_v).astype(BF)
        return jnp.concatenate([key, value], axis=1)

    def queries(rows):
        query = rotary_apply(mm(rows, w_q).reshape(tok, -1, HEAD_SIZE), cosine, sine).astype(BF)
        return query.transpose(1, 0, 2)

    held["rows_a"] = rows_a
    kv_all = stages.run(
        project(rows_a),
        lambda kv: jnp.concatenate(others(kv, "grp"), axis=0),
        [("query", queries, ("rows_a",))] + jobs[1],
    )
    query = held["query"]
    keys, values = kv_all[:, :HEAD_SIZE], kv_all[:, HEAD_SIZE:]

    def attention(q):
        context = attend(q, keys, values, q_place, q_start, k_place)
        context = context.transpose(1, 0, 2).reshape(tok, -1)
        return context, mm_t(context, w_ot).astype(BF)

    context, partial = stages.run(query, attention, jobs[2])
    mid = stages.run(partial, lambda p: x_rows + sum_rows(p), jobs[3])
    rows_b = stages.run(
        mid, lambda m: gather_rows(apply_norm(m, gains[1]).astype(BF)), jobs[4]
    )
    rows_b = stages.run(rows_b, lambda r: r, jobs[5])
    w_gu = held["gu", layer]

    def ahead(rows):
        both = mm(rows, w_gu)
        half = both.shape[1] // 2
        gate, up = both[:, :half], both[:, half:]
        return gate, up, (jax.nn.silu(gate) * up).astype(BF)

    gate, up, hidden = stages.run(rows_b, ahead, jobs[6])
    return x_rows, rows_a, query, keys, values, context, mid, rows_b, gate, up, hidden


def layer_backward(stages, layer, grad_out, grad_mlp, gains, where, kept, also, jobs):
    held = stages.held
    cosine, sine, q_place, q_start, k_place = where
    x_rows, rows_a, query, keys, values, context, mid, rows_b, gate, up, hidden = kept
    w_q, w_k, w_v, w_ot = held["attn", layer]
    w_gu, w_dt = held["gu", layer], held["down", layer]
    tok = rows_a.shape[0]
    held["rows_b"], held["hidden"], held["grad_mlp"] = rows_b, hidden, grad_mlp

    def feed_back(rows):
        grad_hidden = mm(rows, w_dt)
        sig = jax.nn.sigmoid(gate)
        grad_gate = (grad_hidden * up * sig * (1.0 + gate * (1.0 - sig))).astype(BF)
        grad_up = (grad_hidden * gate * sig).astype(BF)
        both = jnp.concatenate([grad_gate, grad_up], axis=1)
        return grad_gate, grad_up, mm_t(both, w_gu).astype(BF), also(hidden)

    grad_gate, grad_up, partial, extra = stages.run(grad_mlp, feed_back, jobs[0])
    held["grad_gate"], held["grad_up"] = grad_gate, grad_up
    grad_b = stages.run(partial, sum_rows, jobs[1])
    grad_mid, gain_b = norm_back(mid, gains[1], grad_b)
    grad_mid = grad_mid + grad_out
    grad_attn = stages.run(grad_mid.astype(BF), gather_rows, jobs[2])

    def attention_back(rows):
        grad_context = mm(rows, w_ot).astype(BF)
        grad_context = grad_context.reshape(tok, -1, HEAD_SIZE).transpose(1, 0, 2)
        return attend_back(query, grad_context, keys, values, q_place, q_start, k_place)

    def keys_back(grads):
        kv = jnp.concatenate(grads, axis=1)
        kv = kv.reshape((-1, tok) + kv.shape[1:])
        return sum_others([kv[k] for k in range(kv.shape[0])], "grp").astype(BF)

    def queries_back(grad_q):
        grad_q = grad_q.transpose(1, 0, 2).astype(F32)
        grad_q = rotary_apply(grad_q, cosine, -sine).astype(BF).reshape(tok, -1)
        return grad_q, mm_t(grad_q, w_q)

    held["grad_q"], *grads = stages.run(grad_attn, attention_back, jobs[3])
    own_kv = stages.run(grads, keys_back, [("g_q", queries_back, ("grad_q",))] + jobs[4])
    grad_q, partial = held["g_q"]
    grad_k = own_kv[:, :HEAD_SIZE].astype(F32)
    grad_k = rotary_apply(grad_k[:, None, :], cosine, -sine).astype(BF)[:, 0]
    grad_v = own_kv[:, HEAD_SIZE:]
    partial = (partial + mm_t(grad_k, w_k) + mm_t(grad_v, w_v)).astype(BF)

    def attn_pair(g_q, g_k, g_v):
        half_q = g_q.shape[1] // 2
        kv_0, kv_1 = core_halves(g_k)
        v_0, v_1 = core_halves(g_v)

        def term(q_half, k_half, v_half, o_half):
            right = jnp.concatenate([q_half, k_half, v_half], axis=1)
            return jnp.concatenate([mm_tl(rows_a, right), mm_tl(grad_attn, o_half)], axis=1)

        return grad_pair(
            term(g_q[:, :half_q], kv_0, v_0, context[:, :half_q]),
            term(g_q[:, half_q:], kv_1, v_1, context[:, half_q:]),
        )

    held["g_q"], held["g_k"], held["g_v"] = grad_q, grad_k, grad_v
    grad_a = stages.run(partial, sum_rows, jobs[5](attn_pair))
    grad_in, gain_a = norm_back(x_rows, gains[0], grad_a)
    return grad_mid + grad_in, jnp.stack([gain_a, gain_b]), extra


def own_layer(first, second):
    core = lax.axis_index("pipe")
    keep = jnp.where(core == 0, first, second)
    return keep, hop(jnp.where(core == 0, second, first), "pipe", 1)


def body(
    block_input,
    cotangent,
    segments,
    norm_gains,
    w_query,
    key_matrix,
    value_matrix,
    w_output,
    w_gate,
    w_up,
    w_down,
):
    core = lax.axis_index("pipe")
    grp = lax.axis_index("grp")
    wd = lax.axis_size("wd")
    groups = lax.axis_size("grp")
    cores = lax.axis_size("pipe")
    tok = block_input.shape[1] * lax.axis_size(CUBE)

    stages = Stages()
    held = stages.held
    packed = pack_attention(w_query[0], key_matrix[0], value_matrix[0], w_output[0], cores)
    attn_cols = columns_out(to_blocks(packed, cores))
    attn_cols, first_gains = lax.optimization_barrier((attn_cols, norm_gains[0]))
    gains = spread_gains(first_gains)
    held["gate_out"] = to_blocks(w_gate[0], cores)
    held["up_out"] = to_blocks(w_up[0], cores)
    held["down_out"] = to_blocks(w_down[0].T, cores)
    widths = tuple(n // (wd * cores) for n in (w_query.shape[2], key_matrix.shape[2], w_output.shape[1]))

    held["gate_out"], gains = lax.optimization_barrier((held["gate_out"], gains))
    gate_cols = columns_out(held["gate_out"])
    up_cols = columns_out(held["up_out"])
    down_cols = columns_out(held["down_out"])
    for layer in range(2):
        held["attn", layer] = unpack_attention(*all_rows(attn_cols[layer]), widths)
        gate, up, down = (all_rows(m[layer]) for m in (gate_cols, up_cols, down_cols))
        held["gu", layer] = put_together([[m] for m in gate + up])
        held["down", layer] = put_together([[m] for m in down])

    seg_row = lax.dynamic_index_in_dim(segments, core, 0, keepdims=False)
    starts = doc_starts(seg_row)
    rows_own = tok // lax.axis_size(CUBE)

    def in_row_order(values):
        values = relative(values, 0, CUBE)
        return jnp.concatenate(
            [values[j * rows_own : (j + 1) * rows_own] for j in ROW_ORDER], axis=0
        )

    local = in_row_order(jnp.arange(tok, dtype=jnp.int32))
    q_place = grp * tok + local
    q_start = in_row_order(lax.dynamic_slice_in_dim(starts, grp * tok, tok))
    cosine, sine = rope_tables(q_place - q_start)
    k_place = jnp.concatenate([(grp ^ k) * tok + local for k in range(groups)])
    where = (cosine, sine, q_place[:, None], q_start[:, None], k_place[None, :])

    rows = lax.dynamic_index_in_dim(block_input, core, 0, keepdims=False)
    grad = lax.dynamic_index_in_dim(cotangent, core, 0, keepdims=False)
    held["cotangent"] = grad
    kept = [None, None]
    outs = [None, None]
    kept[0] = layer_forward(
        stages,
        0,
        rows.astype(F32),
        gains[0],
        where,
        [[]] * 7,
    )

    def close(hidden, layer):
        return (kept[layer][6] + sum_rows(mm_t(hidden, held["down", layer]))).astype(BF)

    outs[0] = close(kept[0][-1], 0)
    kept[1] = layer_forward(
        stages,
        1,
        outs[0].astype(F32),
        gains[1],
        where,
        [[], [], [("last", gather_rows, ("cotangent",))], [], [], [], []],
    )

    def grad_of(name, layer):
        sources = {
            "down": ("grad_mlp", "hidden"),
            "gate": ("rows_b", "grad_gate"),
            "up": ("rows_b", "grad_up"),
        }[name]
        return (("pair", name, layer), mlp_pair, sources)

    def group_sum(name, layer):
        return (("sum", name, layer), grad_group, (("pair", name, layer),), "later")

    def home(name, layer):
        return (("home", name, layer), grad_home, (("sum", name, layer),))

    def attn_grad(layer):
        return lambda pair: (("pair", "attn", layer), pair, ("g_q", "g_k", "g_v"))

    def final(name, turned):
        def ready(first, second):
            return place(*own_layer(first, second), turned)

        return (("final", name), ready, (("home", name, 0), ("home", name, 1)))

    held["hidden"], held["grad_mlp"] = kept[1][-1], held["last"]
    hidden = stages.run(kept[1][-1], lambda h: h, [grad_of("down", 1)])

    grads_in = [None, None]
    gain_grads = [None, None]
    grad_in, gain_grads[1], outs[1] = layer_backward(
        stages,
        1,
        grad.astype(F32),
        held["last"],
        gains[1],
        where,
        kept[1][:-1] + (hidden,),
        lambda h: close(h, 1),
        (
            [],
            [group_sum("down", 1), grad_of("gate", 1)],
            [group_sum("gate", 1), grad_of("up", 1)],
            [group_sum("up", 1)],
            [home("down", 1)],
            lambda pair: [attn_grad(1)(pair)],
        ),
    )
    grads_in[1] = grad_in.astype(BF)
    grad_mlp = stages.run(grads_in[1], gather_rows, [group_sum("attn", 1)])
    grad_in, gain_grads[0], _ = layer_backward(
        stages,
        0,
        grads_in[1].astype(F32),
        grad_mlp,
        gains[0],
        where,
        kept[0],
        lambda h: (),
        (
            [grad_of("down", 0), home("gate", 1)],
            [group_sum("down", 0), grad_of("gate", 0)],
            [group_sum("gate", 0), grad_of("up", 0), home("up", 1)],
            [group_sum("up", 0)],
            [home("attn", 1), home("down", 0)],
            lambda pair: [attn_grad(0)(pair), final("down", True), home("gate", 0)],
        ),
    )
    grads_in[0] = grad_in.astype(BF)
    for key, job, names, *_ in (
        group_sum("attn", 0),
        home("up", 0),
        final("gate", False),
        home("attn", 0),
    ):
        held[key] = job(*[held[name] for name in names])

    def by_batch(pair):
        own, other = own_layer(pair[0], pair[1])
        both = jnp.where(core == 0, jnp.stack([own, other]), jnp.stack([other, own]))
        return both[None]

    layer_out = by_batch(outs)
    input_grad = by_batch(grads_in)

    grad_norm_gains = sum_gains(gain_grads)[None]

    def both(name):
        return own_layer(held["home", name, 0], held["home", name, 1])

    keep, got = both("attn")
    cuts = (0, widths[0], widths[0] + widths[1], widths[0] + 2 * widths[1], keep.shape[2])
    q_pair, k_pair, v_pair, o_pair = (
        (keep[..., lo:hi], got[..., lo:hi]) for lo, hi in zip(cuts[:-1], cuts[1:])
    )

    def small(pair):
        order = jnp.where(core == 0, jnp.stack(pair), jnp.stack(pair[::-1]))
        order = relative(order, 1, "wd").transpose(2, 1, 0, 3).astype(F32)
        return order.reshape(order.shape[0], -1)[None]

    grad_wq = place(*q_pair, False)[None]
    grad_wk = small(k_pair)
    grad_wv = small(v_pair)
    grad_wo = place(*o_pair, True)[None]
    grad_wg = held["final", "gate"][None]
    grad_wu = place(*both("up"), False)[None]
    grad_wd = held["final", "down"][None]
    return (
        layer_out,
        input_grad,
        grad_norm_gains,
        grad_wq,
        grad_wk,
        grad_wv,
        grad_wo,
        grad_wg,
        grad_wu,
        grad_wd,
    )


def solution(mesh):
    sizes = dict(mesh.shape)
    wd = KV_HEADS // sizes["tensor"]
    fine = Mesh(
        mesh.devices.reshape(sizes["pipe"], sizes["dp"] // wd, wd, sizes["tensor"]),
        ("pipe", "grp", "wd", "tensor"),
    )
    dp = ("grp", "wd")
    tokens = P(None, dp + ("tensor",), None)
    outs = P("pipe", None, dp + ("tensor",), None)
    gains = P("pipe", None, dp + ("tensor",))
    tall = P("pipe", dp, "tensor")
    wide = P("pipe", "tensor", dp)
    weights = (tall, tall, tall, wide, tall, tall, wide)
    return jax.shard_map(
        body,
        mesh=fine,
        in_specs=(tokens, tokens, P(), gains) + weights,
        out_specs=(outs, outs, gains) + weights,
        check_vma=False,
    )
```

```python
import jax
import jax.numpy as jnp
from jax import lax
from jax.experimental import pallas as pl
from jax.experimental.pallas import tpu as pltpu
from jax.sharding import Mesh, PartitionSpec as P

HEAD_SIZE = 64
KV_HEADS = 8
EPS = 1e-05
ROPE_BASE = 500000.0
NEG_FILL = -1e30
BF = jnp.bfloat16
F32 = jnp.float32
CUBE = ("wd", "tensor")


def rms_scale(row_values):
    return lax.rsqrt(jnp.mean(row_values * row_values, axis=-1, keepdims=True) + EPS)


def apply_norm(row_values, gain_vector):
    return row_values * rms_scale(row_values) * gain_vector


def norm_back(row_values, gain_vector, grad_normed):
    _, pullback = jax.vjp(apply_norm, row_values, gain_vector)
    return pullback(grad_normed)


def doc_starts(seg_row):
    places = jnp.arange(seg_row.shape[0], dtype=jnp.int32)
    before = jnp.concatenate([seg_row[:1] - 1, seg_row[:-1]])
    return lax.cummax(jnp.where(seg_row != before, places, 0), axis=0)


def rope_tables(positions):
    half_dim = HEAD_SIZE // 2
    freqs = ROPE_BASE ** (-(jnp.arange(half_dim, dtype=F32) * 2.0 / HEAD_SIZE))
    angles = positions.astype(F32)[:, None] * freqs[None, :]
    return (jnp.cos(angles), jnp.sin(angles))


def rotary_apply(head_values, cosine_table, sine_values):
    half_dim = head_values.shape[-1] // 2
    first_half = head_values[..., :half_dim]
    second_half = head_values[..., half_dim:]
    cos_rows = cosine_table[:, None, :]
    sin_rows = sine_values[:, None, :]
    return jnp.concatenate(
        [
            first_half * cos_rows - second_half * sin_rows,
            second_half * cos_rows + first_half * sin_rows,
        ],
        axis=-1,
    )


def mm(left, right):
    return jnp.dot(left, right, preferred_element_type=F32)


def mm_t(left, right):
    return lax.dot_general(left, right, (((1,), (1,)), ((), ())), preferred_element_type=F32)


def mm_tl(left, right):
    return lax.dot_general(left, right, (((0,), (0,)), ((), ())), preferred_element_type=F32)


def trade(blocks, axes):
    return lax.all_to_all(blocks, axes, 0, 0, tiled=True)


def hop(block, axis, step):
    size = lax.axis_size(axis)
    return lax.ppermute(block, axis, [(i, i ^ step) for i in range(size)])


def tie(*values):
    return lax.optimization_barrier(values)


def link_steps():
    steps = []
    step = 1
    while step < lax.axis_size(CUBE):
        steps.append(step)
        step *= 2
    return steps


FAR, NEAR, SIDE = 4, 2, 1
ROW_ORDER = (0, FAR, NEAR, FAR | NEAR, SIDE, FAR | SIDE, NEAR | SIDE, FAR | NEAR | SIDE)


def cube(block, step):
    return hop(block, CUBE, step)


def join_kernel(left_ref, left_came_ref, right_ref, right_came_ref, out_ref):
    half = left_ref.shape[1]
    block = pl.program_id(0)

    @pl.when(block < 2)
    def _():
        out_ref[:, :half] = left_ref[...]

    @pl.when(block >= 2)
    def _():
        out_ref[:, :half] = left_came_ref[...]

    @pl.when(block % 2 == 0)
    def _():
        out_ref[:, half:] = right_ref[...]

    @pl.when(block % 2 == 1)
    def _():
        out_ref[:, half:] = right_came_ref[...]


def join_halves(left, left_came, right, right_came):
    rows, half = left.shape[0] // 2, left.shape[1]

    def spec(place):
        return pl.BlockSpec((rows, half), lambda i: (place(i), 0))

    return pl.pallas_call(
        join_kernel,
        grid=(4,),
        in_specs=[
            spec(lambda i: jnp.minimum(i, 1)),
            spec(lambda i: jnp.maximum(i - 2, 0)),
            spec(lambda i: i // 2),
            spec(lambda i: i // 2),
        ],
        out_specs=pl.BlockSpec((rows, 2 * half), lambda i: (i, 0)),
        out_shape=jax.ShapeDtypeStruct((4 * rows, 2 * half), left.dtype),
        cost_estimate=pl.CostEstimate(
            flops=0, bytes_accessed=32 * rows * half, transcendentals=0
        ),
    )(left, left_came, right, right_came)


def gather_rows(rows):
    two = jnp.concatenate([rows, cube(rows, FAR)], axis=0)
    half = two.shape[1] // 2
    left, right = two[:, :half], two[:, half:]
    left_came, right_came = cube(left, NEAR), cube(right, SIDE)
    left = jnp.concatenate([left, left_came], axis=0)
    right = jnp.concatenate([right, right_came], axis=0)
    return join_halves(left, cube(left, SIDE), right, cube(right, NEAR))


def sum_rows(partial):
    partial = partial.astype(BF)
    n, half = partial.shape[0] // 4, partial.shape[1] // 2
    left, right = partial[:, :half], partial[:, half:]
    left_came = cube(left[2 * n :], SIDE)
    right_came = cube(jnp.concatenate([right[n : 2 * n], right[3 * n :]], axis=0), NEAR)
    left = left[: 2 * n].astype(F32) + left_came.astype(F32)
    right_came = right_came.astype(F32)
    low = right[:n].astype(F32) + right_came[:n]
    high = right[2 * n : 3 * n].astype(F32) + right_came[n:]
    left_came = cube(left[n:].astype(BF), NEAR)
    right_came = cube(high.astype(BF), SIDE)
    left = left[:n] + left_came.astype(F32)
    right = low + right_came.astype(F32)
    both = jnp.concatenate([left, right], axis=1)
    rows = n // 2
    return both[:rows] + cube(both[rows:].astype(BF), FAR).astype(F32)


class Stages:
    def __init__(self):
        self.held = {}
        self.then = {}

    def run(self, value, step, jobs, settle=()):
        needed = [[self.held[name] for name in job[2]] for job in jobs]
        value, needed = lax.optimization_barrier((value, needed))
        out = step(value)
        made = [job[1](*inputs) for job, inputs in zip(jobs, needed)]
        due = [m for m, job in zip(made, jobs) if len(job) == 3]
        ready = [self.held[key] for key in settle]
        out, due, ready = lax.optimization_barrier((out, due, ready))
        self.held.update(zip(settle, ready))
        for job, result in zip(jobs, made):
            self.held[job[0]] = due.pop(0) if len(job) == 3 else result
            if job[0] in self.then:
                self.then[job[0]](job[0])
        return out


def others(block, axis):
    return [block] + [hop(block, axis, k) for k in range(1, lax.axis_size(axis))]


def sum_others(blocks, axis):
    total = blocks[0].astype(F32)
    for k in range(1, lax.axis_size(axis)):
        total = total + hop(blocks[k].astype(BF), axis, k).astype(F32)
    return total


def relative(values, dim, axis):
    count = lax.axis_size(axis)
    me = lax.axis_index(axis)
    step = 1
    while step < count:
        shape = values.shape
        cut = shape[:dim] + (count // (2 * step), 2, step * (shape[dim] // count)) + shape[dim + 1 :]
        view = values.reshape(cut)
        swapped = jnp.concatenate(
            [lax.slice_in_dim(view, 1, 2, axis=dim + 1), lax.slice_in_dim(view, 0, 1, axis=dim + 1)],
            axis=dim + 1,
        )
        values = jnp.where((me & step) != 0, swapped.reshape(shape), values)
        step *= 2
    return values


def spread_gains(norm_gains):
    me = lax.axis_index(CUBE)
    gain = norm_gains
    for step in link_steps():
        came = hop(gain, CUBE, step)
        gain = jnp.where(
            (me & step) != 0,
            jnp.concatenate([came, gain], axis=1),
            jnp.concatenate([gain, came], axis=1),
        )
    gain = relative(jnp.concatenate(others(gain, "grp"), axis=1), 1, "grp")
    other = hop(gain, "pipe", 1)
    core = lax.axis_index("pipe")
    return [jnp.where(core == 0, gain, other), jnp.where(core == 0, other, gain)]


def sum_gains(grads):
    me = lax.axis_index(CUBE)
    keep, extra = own_layer(grads[0], grads[1])
    count = lax.axis_size("grp")
    total = relative((keep + extra).reshape(2, count, -1), 1, "grp")
    mine = total[:, 0]
    for k in range(1, count):
        mine = mine + hop(total[:, k], "grp", k)
    for step in link_steps()[::-1]:
        half = mine.shape[1] // 2
        low, high = mine[:, :half], mine[:, half:]
        odd = (me & step) != 0
        mine = jnp.where(odd, high, low) + hop(jnp.where(odd, low, high), CUBE, step)
    return mine


def masked_probs(q, k, q_place, q_start, k_place):
    scores = lax.dot_general(q, k, (((1,), (1,)), ((), ())), preferred_element_type=F32)
    scores = scores * HEAD_SIZE ** (-0.5)
    allowed = (k_place <= q_place) & (k_place >= q_start)
    masked = jnp.where(allowed, scores, NEG_FILL)
    exps = jnp.exp(masked - jnp.max(masked, axis=-1, keepdims=True))
    return exps / jnp.sum(exps, axis=-1, keepdims=True)


def attend_kernel(q_ref, k_ref, v_ref, qp_ref, qs_ref, kp_ref, o_ref):
    probs = masked_probs(q_ref[0], k_ref[...], qp_ref[...], qs_ref[...], kp_ref[...])
    o_ref[0] = jnp.dot(probs.astype(BF), v_ref[...], preferred_element_type=F32).astype(BF)


def attend_back_kernel(q_ref, do_ref, k_ref, v_ref, qp_ref, qs_ref, kp_ref, dq_ref, dk_ref, dv_ref):
    @pl.when((pl.program_id(0) == 0) & (pl.program_id(1) == 0))
    def _():
        dk_ref[...] = jnp.zeros_like(dk_ref)
        dv_ref[...] = jnp.zeros_like(dv_ref)

    q = q_ref[0]
    do = do_ref[0]
    k = k_ref[...]
    probs = masked_probs(q, k, qp_ref[...], qs_ref[...], kp_ref[...])
    grad_probs = lax.dot_general(do, v_ref[...], (((1,), (1,)), ((), ())), preferred_element_type=F32)
    delta = jnp.sum(probs * grad_probs, axis=-1, keepdims=True)
    grad_scores = (probs * (grad_probs - delta) * HEAD_SIZE ** (-0.5)).astype(BF)
    dq_ref[0] = jnp.dot(grad_scores, k, preferred_element_type=F32).astype(BF)
    dk_ref[...] += lax.dot_general(
        grad_scores, q, (((0,), (0,)), ((), ())), preferred_element_type=F32
    )
    dv_ref[...] += lax.dot_general(
        probs.astype(BF), do, (((0,), (0,)), ((), ())), preferred_element_type=F32
    )


def attention_specs(heads, rows, keys):
    rows_blk = max(16, min(rows, (512 * 1024) // keys))
    per_head = pl.BlockSpec((1, rows_blk, HEAD_SIZE), lambda b, h: (h, b, 0))
    full = pl.BlockSpec((keys, HEAD_SIZE), lambda b, h: (0, 0))
    row_info = pl.BlockSpec((rows_blk, 1), lambda b, h: (b, 0))
    key_info = pl.BlockSpec((1, keys), lambda b, h: (0, 0))
    return ((rows // rows_blk, heads), per_head, full, row_info, key_info)


PARAMS = dict(
    compiler_params=pltpu.CompilerParams(vmem_limit_bytes=50 * 1024 * 1024),
)


def attend(q, k, v, q_place, q_start, k_place):
    heads, rows, _ = q.shape
    keys = k.shape[0]
    grid, per_head, full, row_info, key_info = attention_specs(heads, rows, keys)
    return pl.pallas_call(
        attend_kernel,
        grid=grid,
        in_specs=[per_head, full, full, row_info, row_info, key_info],
        out_specs=per_head,
        out_shape=jax.ShapeDtypeStruct(q.shape, BF),
        cost_estimate=pl.CostEstimate(
            flops=4 * heads * rows * keys * HEAD_SIZE,
            bytes_accessed=4 * q.size + 4 * k.size,
            transcendentals=heads * rows * keys,
        ),
        **PARAMS,
    )(q, k, v, q_place, q_start, k_place)


def attend_back(q, do, k, v, q_place, q_start, k_place):
    heads, rows, _ = q.shape
    keys = k.shape[0]
    grid, per_head, full, row_info, key_info = attention_specs(heads, rows, keys)
    return pl.pallas_call(
        attend_back_kernel,
        grid=grid,
        in_specs=[per_head, per_head, full, full, row_info, row_info, key_info],
        out_specs=[per_head, full, full],
        out_shape=[
            jax.ShapeDtypeStruct(q.shape, BF),
            jax.ShapeDtypeStruct(k.shape, F32),
            jax.ShapeDtypeStruct(k.shape, F32),
        ],
        cost_estimate=pl.CostEstimate(
            flops=10 * heads * rows * keys * HEAD_SIZE,
            bytes_accessed=6 * q.size + 12 * k.size,
            transcendentals=heads * rows * keys,
        ),
        **PARAMS,
    )(q, do, k, v, q_place, q_start, k_place)


def to_blocks(weight, cores):
    wd = lax.axis_size("wd")
    rows = weight.shape[0]
    cut = weight.reshape(rows, wd, cores, -1).transpose(2, 1, 0, 3)
    return cut.reshape((cores * wd, rows) + cut.shape[3:])


def columns_out(blocks):
    moved = trade(blocks, ("pipe", "wd"))
    return moved.reshape((2, -1) + moved.shape[2:])


def put_kernel(spots, *refs):
    pieces, out = refs[: len(spots)], refs[len(spots)]
    block = pl.program_id(0)
    for piece, (first, count, col, cols) in zip(pieces, spots):

        def put(piece=piece, col=col, cols=cols):
            out[:, col : col + cols] = piece[...]

        pl.when((block >= first) & (block < first + count))(put)


def put_together(columns):
    block = min([256] + [piece.shape[0] for stack in columns for piece in stack])
    spots, pieces, specs = [], [], []
    col = 0
    for stack in columns:
        first = 0
        for piece in stack:
            count, cols = piece.shape[0] // block, piece.shape[1]
            spots.append((first, count, col, cols))
            pieces.append(piece)

            def at(i, first=first, count=count):
                return (jnp.clip(i - first, 0, count - 1), 0)

            specs.append(pl.BlockSpec((block, cols), at))
            first += count
        col += cols
    return pl.pallas_call(
        lambda *refs: put_kernel(spots, *refs),
        grid=(first,),
        in_specs=specs,
        out_specs=pl.BlockSpec((block, col), lambda i: (i, 0)),
        out_shape=jax.ShapeDtypeStruct((first * block, col), BF),
        cost_estimate=pl.CostEstimate(
            flops=0, bytes_accessed=4 * first * block * col, transcendentals=0
        ),
        **PARAMS,
    )(*pieces)


def pack_attention(w_query, key_matrix, value_matrix, w_output, cores):
    wd = lax.axis_size("wd")
    rows = w_query.shape[0]
    cut = [w_query.reshape(rows, wd, cores, -1)]
    for m in (key_matrix, value_matrix):
        m = m.reshape(rows, wd, 1, -1)
        cut.append(jnp.broadcast_to(m, (rows, wd, cores, m.shape[3])))
    cut.append(w_output.T.reshape(rows, wd, cores, -1))
    return jnp.concatenate(cut, axis=-1).reshape(rows, -1)


def unpack_attention(own, widths):
    other = hop(own, "pipe", 1)
    query_w, kv_w, out_w = widths
    cuts = (query_w, query_w + kv_w, query_w + 2 * kv_w)
    return (
        jnp.concatenate([own[:, : cuts[0]], other[:, : cuts[0]]], axis=1),
        own[:, cuts[0] : cuts[1]],
        own[:, cuts[1] : cuts[2]],
        jnp.concatenate([own[:, cuts[2] :], other[:, cuts[2] :]], axis=1),
    )


def grad_pair(own, other):
    return (own + hop(other.astype(BF), "pipe", 1).astype(F32)).astype(BF)


def mlp_pair(left, right):
    half = right.shape[1] // 2
    return grad_pair(mm_tl(left, right[:, :half]), mm_tl(left, right[:, half:]))


def grad_group(total):
    return lax.psum_scatter(total, "grp", scatter_dimension=0, tiled=True)


def grad_home(total):
    wd = lax.axis_size("wd")
    me = lax.axis_index("wd")
    blocks = total.reshape((wd, -1) + total.shape[1:])
    pieces = [lax.dynamic_index_in_dim(blocks, me, 0, keepdims=False)]
    for k in range(1, wd):
        pieces.append(hop(lax.dynamic_index_in_dim(blocks, me ^ k, 0, keepdims=False), "wd", k))
    return jnp.stack(pieces)


def place_kernel(turned, at_ref, keep_ref, got_ref, out_ref):
    mine = pl.program_id(1) == at_ref[1]

    def put(ref):
        block = ref[0].astype(F32)
        out_ref[...] = block.T if turned else block

    @pl.when(mine)
    def _():
        put(keep_ref)

    @pl.when(jnp.logical_not(mine))
    def _():
        put(got_ref)


def place(keep, got, turned):
    wd, rows, cols = keep.shape
    at = jnp.stack([lax.axis_index("wd"), lax.axis_index("pipe")]).astype(jnp.int32)
    cores = lax.axis_size("pipe")
    source = pl.BlockSpec((1, rows, cols), lambda w, c, at_ref: (w ^ at_ref[0], 0, 0))
    if turned:
        shape, target = (wd * cores * cols, rows), (cols, rows)
        out = pl.BlockSpec(target, lambda w, c, at_ref: (w * cores + c, 0))
    else:
        shape, target = (rows, wd * cores * cols), (rows, cols)
        out = pl.BlockSpec(target, lambda w, c, at_ref: (0, w * cores + c))
    return pl.pallas_call(
        lambda *refs: place_kernel(turned, *refs),
        grid_spec=pltpu.PrefetchScalarGridSpec(
            num_scalar_prefetch=1, grid=(wd, cores), in_specs=[source, source], out_specs=out
        ),
        out_shape=jax.ShapeDtypeStruct(shape, F32),
        cost_estimate=pl.CostEstimate(
            flops=keep.size, bytes_accessed=12 * keep.size, transcendentals=0
        ),
    )(at, keep, got)


def layer_forward(stages, layer, x_rows, gains, where, build, jobs, settle):
    held = stages.held
    cosine, sine, q_place, q_start, k_place = where
    normed = apply_norm(x_rows, gains[0]).astype(BF)
    rows_a = stages.run(normed, gather_rows, jobs[0], settle[0])
    held["attn", layer] = build("attn", layer)
    w_q, w_k, w_v, w_ot = held["attn", layer]
    tok = rows_a.shape[0]

    def project(rows):
        key = rotary_apply(mm(rows, w_k).reshape(tok, 1, HEAD_SIZE), cosine, sine).astype(BF)[:, 0]
        value = mm(rows, w_v).astype(BF)
        return jnp.concatenate([key, value], axis=1)

    def queries(rows):
        query = rotary_apply(mm(rows, w_q).reshape(tok, -1, HEAD_SIZE), cosine, sine).astype(BF)
        return query.transpose(1, 0, 2)

    held["rows_a"] = rows_a
    kv_all = stages.run(
        project(rows_a),
        lambda kv: jnp.concatenate(others(kv, "grp"), axis=0),
        [("query", queries, ("rows_a",))] + jobs[1],
        settle[1],
    )
    query = held["query"]
    keys, values = kv_all[:, :HEAD_SIZE], kv_all[:, HEAD_SIZE:]

    def attention(q):
        context = attend(q, keys, values, q_place, q_start, k_place)
        context = context.transpose(1, 0, 2).reshape(tok, -1)
        return context, mm_t(context, w_ot).astype(BF)

    context, partial = stages.run(query, attention, jobs[2], settle[2])
    mid = stages.run(partial, lambda p: x_rows + sum_rows(p), jobs[3], settle[3])
    rows_b = stages.run(
        mid, lambda m: gather_rows(apply_norm(m, gains[1]).astype(BF)), jobs[4], settle[4]
    )
    held["gu", layer] = w_gu = build("gu", layer)

    def ahead(rows):
        both = mm(rows, w_gu)
        half = both.shape[1] // 2
        gate, up = both[:, :half], both[:, half:]
        return gate, up, (jax.nn.silu(gate) * up).astype(BF)

    gate, up, hidden = stages.run(rows_b, ahead, jobs[5], settle[5])
    held["down", layer] = build("down", layer)
    return x_rows, rows_a, query, keys, values, context, mid, rows_b, gate, up, hidden


def layer_backward(
    stages, layer, grad_out, grad_mlp, gains, where, kept, also, jobs, settle
):
    held = stages.held
    cosine, sine, q_place, q_start, k_place = where
    x_rows, rows_a, query, keys, values, context, mid, rows_b, gate, up, hidden = kept
    w_q, w_k, w_v, w_ot = held["attn", layer]
    w_gu, w_dt = held["gu", layer], held["down", layer]
    tok = rows_a.shape[0]
    held["rows_b"], held["hidden"], held["grad_mlp"] = rows_b, hidden, grad_mlp

    def feed_back(rows):
        grad_hidden = mm(rows, w_dt)
        sig = jax.nn.sigmoid(gate)
        grad_gate = (grad_hidden * up * sig * (1.0 + gate * (1.0 - sig))).astype(BF)
        grad_up = (grad_hidden * gate * sig).astype(BF)
        both = jnp.concatenate([grad_gate, grad_up], axis=1)
        return grad_gate, grad_up, mm_t(both, w_gu).astype(BF), also(hidden)

    grad_gate, grad_up, partial, extra = stages.run(grad_mlp, feed_back, jobs[0], settle[0])
    held["grad_gate"], held["grad_up"] = grad_gate, grad_up
    grad_b = stages.run(partial, sum_rows, jobs[1], settle[1])
    grad_mid, gain_b = norm_back(mid, gains[1], grad_b)
    grad_mid = grad_mid + grad_out
    grad_attn = stages.run(grad_mid.astype(BF), gather_rows, jobs[2], settle[2])

    def attention_back(rows):
        grad_context = mm(rows, w_ot).astype(BF)
        grad_context = grad_context.reshape(tok, -1, HEAD_SIZE).transpose(1, 0, 2)
        return attend_back(query, grad_context, keys, values, q_place, q_start, k_place)

    def keys_back(grads):
        kv = jnp.concatenate(grads, axis=1)
        kv = kv.reshape((-1, tok) + kv.shape[1:])
        return sum_others([kv[k] for k in range(kv.shape[0])], "grp").astype(BF)

    def queries_back(grad_q):
        grad_q = grad_q.transpose(1, 0, 2).astype(F32)
        grad_q = rotary_apply(grad_q, cosine, -sine).astype(BF).reshape(tok, -1)
        return grad_q, mm_t(grad_q, w_q)

    held["grad_q"], *grads = stages.run(grad_attn, attention_back, jobs[3])
    own_kv = stages.run(
        grads, keys_back, [("g_q", queries_back, ("grad_q",))] + jobs[4], settle[4]
    )
    grad_q, partial = held["g_q"]
    grad_k = own_kv[:, :HEAD_SIZE].astype(F32)
    grad_k = rotary_apply(grad_k[:, None, :], cosine, -sine).astype(BF)[:, 0]
    grad_v = own_kv[:, HEAD_SIZE:]
    partial = (partial + mm_t(grad_k, w_k) + mm_t(grad_v, w_v)).astype(BF)

    def attn_pair(g_q, g_k, g_v):
        half_q = g_q.shape[1] // 2

        def term(cut):
            right = jnp.concatenate([g_q[:, cut], g_k, g_v], axis=1)
            left = [mm_tl(rows_a, right), mm_tl(grad_attn, context[:, cut])]
            return jnp.concatenate(left, axis=1)

        return grad_pair(term(slice(0, half_q)), term(slice(half_q, None)))

    held["g_q"], held["g_k"], held["g_v"] = grad_q, grad_k, grad_v
    grad_a = stages.run(partial, sum_rows, jobs[5](attn_pair), settle[5])
    grad_in, gain_a = norm_back(x_rows, gains[0], grad_a)
    return grad_mid + grad_in, jnp.stack([gain_a, gain_b]), extra


def own_layer(first, second):
    core = lax.axis_index("pipe")
    keep = jnp.where(core == 0, first, second)
    return keep, hop(jnp.where(core == 0, second, first), "pipe", 1)


def body(
    block_input,
    cotangent,
    segments,
    norm_gains,
    w_query,
    key_matrix,
    value_matrix,
    w_output,
    w_gate,
    w_up,
    w_down,
):
    core = lax.axis_index("pipe")
    grp = lax.axis_index("grp")
    wd = lax.axis_size("wd")
    groups = lax.axis_size("grp")
    cores = lax.axis_size("pipe")
    tok = block_input.shape[1] * lax.axis_size(CUBE)

    stages = Stages()
    held = stages.held
    packed = pack_attention(w_query[0], key_matrix[0], value_matrix[0], w_output[0], cores)
    attn_cols = columns_out(to_blocks(packed, cores))
    attn_cols, first_gains = lax.optimization_barrier((attn_cols, norm_gains[0]))
    gains = spread_gains(first_gains)
    held["gate_out"] = to_blocks(w_gate[0], cores)
    held["up_out"] = to_blocks(w_up[0], cores)
    held["down_out"] = to_blocks(w_down[0].T, cores)
    query_w, out_w = w_query.shape[2] // (wd * cores), w_output.shape[1] // (wd * cores)
    widths = (query_w, key_matrix.shape[2] // wd, out_w)

    held["gate_out"], gains = lax.optimization_barrier((held["gate_out"], gains))
    held["gate"] = columns_out(held["gate_out"])

    def move(name):
        return (name, columns_out, (name + "_out",), "later")

    def rows_of(name, layer):
        return lax.all_gather(held[name][layer], "grp", axis=0, tiled=True)

    def put(*names):
        return put_together([[m] for n in names for m in (held[n], hop(held[n], "pipe", 1))])

    def build(kind, layer):
        if kind == "attn":
            return unpack_attention(held["own", "attn", layer], widths)
        if kind == "gu":
            return put(("own", "gate", layer), ("own", "up", layer))
        return put(("own", "down", layer))

    held["attn"] = attn_cols
    for name, layer in (("attn", 0), ("gate", 0), ("attn", 1), ("gate", 1)):
        held["own", name, layer] = rows_of(name, layer)

    def start(name):
        for layer in range(2):
            held["own", name, layer] = rows_of(name, layer)

    stages.then.update(up=start, down=start)

    seg_row = lax.dynamic_index_in_dim(segments, core, 0, keepdims=False)
    starts = doc_starts(seg_row)
    rows_own = tok // lax.axis_size(CUBE)

    def in_row_order(values):
        values = relative(values, 0, CUBE)
        return jnp.concatenate(
            [values[j * rows_own : (j + 1) * rows_own] for j in ROW_ORDER], axis=0
        )

    local = in_row_order(jnp.arange(tok, dtype=jnp.int32))
    q_place = grp * tok + local
    q_start = in_row_order(lax.dynamic_slice_in_dim(starts, grp * tok, tok))
    cosine, sine = rope_tables(q_place - q_start)
    k_place = jnp.concatenate([(grp ^ k) * tok + local for k in range(groups)])
    where = (cosine, sine, q_place[:, None], q_start[:, None], k_place[None, :])

    rows = lax.dynamic_index_in_dim(block_input, core, 0, keepdims=False)
    grad = lax.dynamic_index_in_dim(cotangent, core, 0, keepdims=False)
    held["cotangent"] = grad
    kept = [None, None]
    outs = [None, None]
    kept[0] = layer_forward(
        stages,
        0,
        rows.astype(F32),
        gains[0],
        where,
        build,
        [[], [move("up")], [move("down")], [], [], []],
        [(), (), (("own", "gate", 0),), (("own", "attn", 1),), (("own", "up", 0),), ()],
    )

    def close(hidden, layer):
        return (kept[layer][6] + sum_rows(mm_t(hidden, held["down", layer]))).astype(BF)

    outs[0] = stages.run(
        kept[0][-1], lambda h: close(h, 0), [], (("own", "gate", 1),)
    )
    kept[1] = layer_forward(
        stages,
        1,
        outs[0].astype(F32),
        gains[1],
        where,
        build,
        [[], [], [("last", gather_rows, ("cotangent",))], [], [], []],
        [(), (("own", "up", 1),), (), (("own", "down", 1),), (), ()],
    )

    def grad_of(name, layer):
        sources = {
            "down": ("grad_mlp", "hidden"),
            "gate": ("rows_b", "grad_gate"),
            "up": ("rows_b", "grad_up"),
        }[name]
        return (("pair", name, layer), mlp_pair, sources)

    def group_sum(name, layer):
        return (("sum", name, layer), grad_group, (("pair", name, layer),), "later")

    def home(name, layer):
        return (("home", name, layer), grad_home, (("sum", name, layer),))

    def attn_grad(layer):
        return lambda pair: (("pair", "attn", layer), pair, ("g_q", "g_k", "g_v"))

    def final(name, turned):
        def ready(first, second):
            return place(*own_layer(first, second), turned)

        return (("final", name), ready, (("home", name, 0), ("home", name, 1)))

    held["hidden"], held["grad_mlp"] = kept[1][-1], held["last"]
    hidden = stages.run(kept[1][-1], lambda h: h, [grad_of("down", 1)])

    grads_in = [None, None]
    gain_grads = [None, None]
    grad_in, gain_grads[1], outs[1] = layer_backward(
        stages,
        1,
        grad.astype(F32),
        held["last"],
        gains[1],
        where,
        kept[1][:-1] + (hidden,),
        lambda h: close(h, 1),
        (
            [],
            [group_sum("down", 1), grad_of("gate", 1)],
            [group_sum("gate", 1), grad_of("up", 1)],
            [group_sum("up", 1)],
            [home("down", 1)],
            lambda pair: [attn_grad(1)(pair)],
        ),
        [(), (), (), (), (), (("sum", "gate", 1),)],
    )
    grads_in[1] = grad_in.astype(BF)
    grad_mlp = stages.run(grads_in[1], gather_rows, [group_sum("attn", 1)], (("sum", "up", 1),))
    grad_in, gain_grads[0], _ = layer_backward(
        stages,
        0,
        grads_in[1].astype(F32),
        grad_mlp,
        gains[0],
        where,
        kept[0],
        lambda h: (),
        (
            [grad_of("down", 0), home("gate", 1)],
            [group_sum("down", 0), grad_of("gate", 0)],
            [group_sum("gate", 0), grad_of("up", 0)],
            [group_sum("up", 0)],
            [home("up", 1)],
            lambda pair: [attn_grad(0)(pair)],
        ),
        [
            (),
            (("sum", "attn", 1),),
            (("sum", "down", 0),),
            (),
            (("sum", "gate", 0),),
            (("sum", "up", 0),),
        ],
    )
    grads_in[0] = grad_in.astype(BF)
    for key, job, names, *_ in (
        group_sum("attn", 0),
        home("down", 0),
        final("down", True),
        home("gate", 0),
        final("gate", False),
        home("up", 0),
        home("attn", 1),
        home("attn", 0),
    ):
        held[key] = job(*[held[name] for name in names])

    def by_batch(pair):
        own, other = own_layer(pair[0], pair[1])
        both = jnp.where(core == 0, jnp.stack([own, other]), jnp.stack([other, own]))
        return both[None]

    layer_out = by_batch(outs)
    input_grad = by_batch(grads_in)

    grad_norm_gains = sum_gains(gain_grads)[None]

    def both(name):
        return own_layer(held["home", name, 0], held["home", name, 1])

    keep, got = both("attn")
    cuts = (0, widths[0], widths[0] + widths[1], widths[0] + 2 * widths[1], keep.shape[2])
    q_pair, k_pair, v_pair, o_pair = (
        (keep[..., lo:hi], got[..., lo:hi]) for lo, hi in zip(cuts[:-1], cuts[1:])
    )

    def small(pair):
        order = relative(pair[0], 0, "wd").transpose(1, 0, 2).astype(F32)
        return order.reshape(order.shape[0], -1)[None]

    grad_wq = place(*q_pair, False)[None]
    grad_wk = small(k_pair)
    grad_wv = small(v_pair)
    grad_wo = place(*o_pair, True)[None]
    grad_wg = held["final", "gate"][None]
    grad_wu = place(*both("up"), False)[None]
    grad_wd = held["final", "down"][None]
    return (
        layer_out,
        input_grad,
        grad_norm_gains,
        grad_wq,
        grad_wk,
        grad_wv,
        grad_wo,
        grad_wg,
        grad_wu,
        grad_wd,
    )


def solution(mesh):
    sizes = dict(mesh.shape)
    wd = KV_HEADS // sizes["tensor"]
    fine = Mesh(
        mesh.devices.reshape(sizes["pipe"], sizes["dp"] // wd, wd, sizes["tensor"]),
        ("pipe", "grp", "wd", "tensor"),
    )
    dp = ("grp", "wd")
    tokens = P(None, dp + ("tensor",), None)
    outs = P("pipe", None, dp + ("tensor",), None)
    gains = P("pipe", None, dp + ("tensor",))
    tall = P("pipe", dp, "tensor")
    wide = P("pipe", "tensor", dp)
    weights = (tall, tall, tall, wide, tall, tall, wide)
    return jax.shard_map(
        body,
        mesh=fine,
        in_specs=(tokens, tokens, P(), gains) + weights,
        out_specs=(outs, outs, gains) + weights,
        check_vma=False,
    )
```

```python
import jax
import jax.numpy as jnp
from jax import lax
from jax.experimental import pallas as pl
from jax.experimental.pallas import tpu as pltpu
from jax.sharding import Mesh, PartitionSpec as P

HEAD_SIZE = 64
KV_HEADS = 8
EPS = 1e-05
ROPE_BASE = 500000.0
NEG_FILL = -1e30
BF = jnp.bfloat16
F32 = jnp.float32
CUBE = ("wd", "tensor")


def rms_scale(row_values):
    return lax.rsqrt(jnp.mean(row_values * row_values, axis=-1, keepdims=True) + EPS)


def apply_norm(row_values, gain_vector):
    return row_values * rms_scale(row_values) * gain_vector


def norm_back(row_values, gain_vector, grad_normed):
    _, pullback = jax.vjp(apply_norm, row_values, gain_vector)
    return pullback(grad_normed)


def doc_starts(seg_row):
    places = jnp.arange(seg_row.shape[0], dtype=jnp.int32)
    before = jnp.concatenate([seg_row[:1] - 1, seg_row[:-1]])
    return lax.cummax(jnp.where(seg_row != before, places, 0), axis=0)


def rope_tables(positions):
    half_dim = HEAD_SIZE // 2
    freqs = ROPE_BASE ** (-(jnp.arange(half_dim, dtype=F32) * 2.0 / HEAD_SIZE))
    angles = positions.astype(F32)[:, None] * freqs[None, :]
    return (jnp.cos(angles), jnp.sin(angles))


def rotary_apply(head_values, cosine_table, sine_values):
    half_dim = head_values.shape[-1] // 2
    first_half = head_values[..., :half_dim]
    second_half = head_values[..., half_dim:]
    cos_rows = cosine_table[:, None, :]
    sin_rows = sine_values[:, None, :]
    return jnp.concatenate(
        [
            first_half * cos_rows - second_half * sin_rows,
            second_half * cos_rows + first_half * sin_rows,
        ],
        axis=-1,
    )


def mm(left, right):
    return jnp.dot(left, right, preferred_element_type=F32)


def mm_t(left, right):
    return lax.dot_general(left, right, (((1,), (1,)), ((), ())), preferred_element_type=F32)


def mm_tl(left, right):
    return lax.dot_general(left, right, (((0,), (0,)), ((), ())), preferred_element_type=F32)


def trade(blocks, axes):
    return lax.all_to_all(blocks, axes, 0, 0, tiled=True)


def hop(block, axis, step):
    size = lax.axis_size(axis)
    return lax.ppermute(block, axis, [(i, i ^ step) for i in range(size)])


def tie(*values):
    return lax.optimization_barrier(values)


def link_steps():
    steps = []
    step = 1
    while step < lax.axis_size(CUBE):
        steps.append(step)
        step *= 2
    return steps


FAR, NEAR, SIDE = 4, 2, 1
ROW_ORDER = (0, FAR, NEAR, FAR | NEAR, SIDE, FAR | SIDE, NEAR | SIDE, FAR | NEAR | SIDE)


def cube(block, step):
    return hop(block, CUBE, step)


def join_kernel(left_ref, left_came_ref, right_ref, right_came_ref, out_ref):
    half = left_ref.shape[1]
    block = pl.program_id(0)

    @pl.when(block < 2)
    def _():
        out_ref[:, :half] = left_ref[...]

    @pl.when(block >= 2)
    def _():
        out_ref[:, :half] = left_came_ref[...]

    @pl.when(block % 2 == 0)
    def _():
        out_ref[:, half:] = right_ref[...]

    @pl.when(block % 2 == 1)
    def _():
        out_ref[:, half:] = right_came_ref[...]


def join_halves(left, left_came, right, right_came):
    rows, half = left.shape[0] // 2, left.shape[1]

    def spec(place):
        return pl.BlockSpec((rows, half), lambda i: (place(i), 0))

    return pl.pallas_call(
        join_kernel,
        grid=(4,),
        in_specs=[
            spec(lambda i: jnp.minimum(i, 1)),
            spec(lambda i: jnp.maximum(i - 2, 0)),
            spec(lambda i: i // 2),
            spec(lambda i: i // 2),
        ],
        out_specs=pl.BlockSpec((rows, 2 * half), lambda i: (i, 0)),
        out_shape=jax.ShapeDtypeStruct((4 * rows, 2 * half), left.dtype),
        cost_estimate=pl.CostEstimate(
            flops=0, bytes_accessed=32 * rows * half, transcendentals=0
        ),
    )(left, left_came, right, right_came)


def gather_rows(rows):
    two = jnp.concatenate([rows, cube(rows, FAR)], axis=0)
    half = two.shape[1] // 2
    left, right = two[:, :half], two[:, half:]
    left_came, right_came = cube(left, NEAR), cube(right, SIDE)
    left = jnp.concatenate([left, left_came], axis=0)
    right = jnp.concatenate([right, right_came], axis=0)
    return join_halves(left, cube(left, SIDE), right, cube(right, NEAR))


def sum_rows(partial):
    partial = partial.astype(BF)
    n, half = partial.shape[0] // 4, partial.shape[1] // 2
    left, right = partial[:, :half], partial[:, half:]
    left_came = cube(left[2 * n :], SIDE)
    right_came = cube(jnp.concatenate([right[n : 2 * n], right[3 * n :]], axis=0), NEAR)
    left = left[: 2 * n].astype(F32) + left_came.astype(F32)
    right_came = right_came.astype(F32)
    low = right[:n].astype(F32) + right_came[:n]
    high = right[2 * n : 3 * n].astype(F32) + right_came[n:]
    left_came = cube(left[n:].astype(BF), NEAR)
    right_came = cube(high.astype(BF), SIDE)
    left = left[:n] + left_came.astype(F32)
    right = low + right_came.astype(F32)
    both = jnp.concatenate([left, right], axis=1)
    rows = n // 2
    return both[:rows] + cube(both[rows:].astype(BF), FAR).astype(F32)


class Stages:
    def __init__(self):
        self.held = {}
        self.then = {}

    def run(self, value, step, jobs, settle=()):
        needed = [[self.held[name] for name in job[2]] for job in jobs]
        value, needed = lax.optimization_barrier((value, needed))
        out = step(value)
        made = [job[1](*inputs) for job, inputs in zip(jobs, needed)]
        due = [m for m, job in zip(made, jobs) if len(job) == 3]
        ready = [self.held[key] for key in settle]
        out, due, ready = lax.optimization_barrier((out, due, ready))
        self.held.update(zip(settle, ready))
        for job, result in zip(jobs, made):
            self.held[job[0]] = due.pop(0) if len(job) == 3 else result
            if job[0] in self.then:
                self.then[job[0]](job[0])
        return out


def others(block, axis):
    return [block] + [hop(block, axis, k) for k in range(1, lax.axis_size(axis))]


def sum_others(blocks, axis):
    total = blocks[0].astype(F32)
    for k in range(1, lax.axis_size(axis)):
        total = total + hop(blocks[k].astype(BF), axis, k).astype(F32)
    return total


def relative(values, dim, axis):
    count = lax.axis_size(axis)
    me = lax.axis_index(axis)
    step = 1
    while step < count:
        shape = values.shape
        cut = shape[:dim] + (count // (2 * step), 2, step * (shape[dim] // count)) + shape[dim + 1 :]
        view = values.reshape(cut)
        swapped = jnp.concatenate(
            [lax.slice_in_dim(view, 1, 2, axis=dim + 1), lax.slice_in_dim(view, 0, 1, axis=dim + 1)],
            axis=dim + 1,
        )
        values = jnp.where((me & step) != 0, swapped.reshape(shape), values)
        step *= 2
    return values


def spread_gains(norm_gains):
    me = lax.axis_index(CUBE)
    gain = norm_gains
    for step in link_steps():
        came = hop(gain, CUBE, step)
        gain = jnp.where(
            (me & step) != 0,
            jnp.concatenate([came, gain], axis=1),
            jnp.concatenate([gain, came], axis=1),
        )
    gain = relative(jnp.concatenate(others(gain, "grp"), axis=1), 1, "grp")
    other = hop(gain, "pipe", 1)
    core = lax.axis_index("pipe")
    return [jnp.where(core == 0, gain, other), jnp.where(core == 0, other, gain)]


def sum_gains(grads):
    me = lax.axis_index(CUBE)
    keep, extra = own_layer(grads[0], grads[1])
    count = lax.axis_size("grp")
    total = relative((keep + extra).reshape(2, count, -1), 1, "grp")
    mine = total[:, 0]
    for k in range(1, count):
        mine = mine + hop(total[:, k], "grp", k)
    for step in link_steps()[::-1]:
        half = mine.shape[1] // 2
        low, high = mine[:, :half], mine[:, half:]
        odd = (me & step) != 0
        mine = jnp.where(odd, high, low) + hop(jnp.where(odd, low, high), CUBE, step)
    return mine


def masked_probs(q, k, q_place, q_start, k_place):
    scores = lax.dot_general(q, k, (((1,), (1,)), ((), ())), preferred_element_type=F32)
    scores = scores * HEAD_SIZE ** (-0.5)
    allowed = (k_place <= q_place) & (k_place >= q_start)
    masked = jnp.where(allowed, scores, NEG_FILL)
    exps = jnp.exp(masked - jnp.max(masked, axis=-1, keepdims=True))
    return exps / jnp.sum(exps, axis=-1, keepdims=True)


def attend_kernel(q_ref, k_ref, v_ref, qp_ref, qs_ref, kp_ref, o_ref):
    probs = masked_probs(q_ref[0], k_ref[...], qp_ref[...], qs_ref[...], kp_ref[...])
    o_ref[0] = jnp.dot(probs.astype(BF), v_ref[...], preferred_element_type=F32).astype(BF)


def attend_back_kernel(q_ref, do_ref, k_ref, v_ref, qp_ref, qs_ref, kp_ref, dq_ref, dk_ref, dv_ref):
    @pl.when((pl.program_id(0) == 0) & (pl.program_id(1) == 0))
    def _():
        dk_ref[...] = jnp.zeros_like(dk_ref)
        dv_ref[...] = jnp.zeros_like(dv_ref)

    q = q_ref[0]
    do = do_ref[0]
    k = k_ref[...]
    probs = masked_probs(q, k, qp_ref[...], qs_ref[...], kp_ref[...])
    grad_probs = lax.dot_general(do, v_ref[...], (((1,), (1,)), ((), ())), preferred_element_type=F32)
    delta = jnp.sum(probs * grad_probs, axis=-1, keepdims=True)
    grad_scores = (probs * (grad_probs - delta) * HEAD_SIZE ** (-0.5)).astype(BF)
    dq_ref[0] = jnp.dot(grad_scores, k, preferred_element_type=F32).astype(BF)
    dk_ref[...] += lax.dot_general(
        grad_scores, q, (((0,), (0,)), ((), ())), preferred_element_type=F32
    )
    dv_ref[...] += lax.dot_general(
        probs.astype(BF), do, (((0,), (0,)), ((), ())), preferred_element_type=F32
    )


def attention_specs(heads, rows, keys):
    rows_blk = max(16, min(rows, (512 * 1024) // keys))
    per_head = pl.BlockSpec((1, rows_blk, HEAD_SIZE), lambda b, h: (h, b, 0))
    full = pl.BlockSpec((keys, HEAD_SIZE), lambda b, h: (0, 0))
    row_info = pl.BlockSpec((rows_blk, 1), lambda b, h: (b, 0))
    key_info = pl.BlockSpec((1, keys), lambda b, h: (0, 0))
    return ((rows // rows_blk, heads), per_head, full, row_info, key_info)


PARAMS = dict(
    compiler_params=pltpu.CompilerParams(vmem_limit_bytes=50 * 1024 * 1024),
)


def attend(q, k, v, q_place, q_start, k_place):
    heads, rows, _ = q.shape
    keys = k.shape[0]
    grid, per_head, full, row_info, key_info = attention_specs(heads, rows, keys)
    return pl.pallas_call(
        attend_kernel,
        grid=grid,
        in_specs=[per_head, full, full, row_info, row_info, key_info],
        out_specs=per_head,
        out_shape=jax.ShapeDtypeStruct(q.shape, BF),
        cost_estimate=pl.CostEstimate(
            flops=4 * heads * rows * keys * HEAD_SIZE,
            bytes_accessed=4 * q.size + 4 * k.size,
            transcendentals=heads * rows * keys,
        ),
        **PARAMS,
    )(q, k, v, q_place, q_start, k_place)


def attend_back(q, do, k, v, q_place, q_start, k_place):
    heads, rows, _ = q.shape
    keys = k.shape[0]
    grid, per_head, full, row_info, key_info = attention_specs(heads, rows, keys)
    return pl.pallas_call(
        attend_back_kernel,
        grid=grid,
        in_specs=[per_head, per_head, full, full, row_info, row_info, key_info],
        out_specs=[per_head, full, full],
        out_shape=[
            jax.ShapeDtypeStruct(q.shape, BF),
            jax.ShapeDtypeStruct(k.shape, F32),
            jax.ShapeDtypeStruct(k.shape, F32),
        ],
        cost_estimate=pl.CostEstimate(
            flops=10 * heads * rows * keys * HEAD_SIZE,
            bytes_accessed=6 * q.size + 12 * k.size,
            transcendentals=heads * rows * keys,
        ),
        **PARAMS,
    )(q, do, k, v, q_place, q_start, k_place)


def to_blocks(weight, cores):
    wd = lax.axis_size("wd")
    rows = weight.shape[0]
    cut = weight.reshape(rows, wd, cores, -1).transpose(2, 1, 0, 3)
    return cut.reshape((cores * wd, rows) + cut.shape[3:])


def columns_out(blocks):
    moved = trade(blocks, ("pipe", "wd"))
    return moved.reshape((2, -1) + moved.shape[2:])


def put_kernel(spots, *refs):
    pieces, out = refs[: len(spots)], refs[len(spots)]
    block = pl.program_id(0)
    for piece, (first, count, col, cols) in zip(pieces, spots):

        def put(piece=piece, col=col, cols=cols):
            out[:, col : col + cols] = piece[...]

        pl.when((block >= first) & (block < first + count))(put)


def put_together(columns):
    block = min([256] + [piece.shape[0] for stack in columns for piece in stack])
    spots, pieces, specs = [], [], []
    col = 0
    for stack in columns:
        first = 0
        for piece in stack:
            count, cols = piece.shape[0] // block, piece.shape[1]
            spots.append((first, count, col, cols))
            pieces.append(piece)

            def at(i, first=first, count=count):
                return (jnp.clip(i - first, 0, count - 1), 0)

            specs.append(pl.BlockSpec((block, cols), at))
            first += count
        col += cols
    return pl.pallas_call(
        lambda *refs: put_kernel(spots, *refs),
        grid=(first,),
        in_specs=specs,
        out_specs=pl.BlockSpec((block, col), lambda i: (i, 0)),
        out_shape=jax.ShapeDtypeStruct((first * block, col), BF),
        cost_estimate=pl.CostEstimate(
            flops=0, bytes_accessed=4 * first * block * col, transcendentals=0
        ),
        **PARAMS,
    )(*pieces)


def pack_attention(w_query, key_matrix, value_matrix, w_output, cores):
    wd = lax.axis_size("wd")
    rows = w_query.shape[0]
    cut = [w_query.reshape(rows, wd, cores, -1)]
    for m in (key_matrix, value_matrix):
        m = m.reshape(rows, wd, 1, -1)
        cut.append(jnp.broadcast_to(m, (rows, wd, cores, m.shape[3])))
    cut.append(w_output.T.reshape(rows, wd, cores, -1))
    return jnp.concatenate(cut, axis=-1).reshape(rows, -1)


def unpack_attention(own, widths):
    other = hop(own, "pipe", 1)
    query_w, kv_w, out_w = widths
    cuts = (query_w, query_w + kv_w, query_w + 2 * kv_w)
    return (
        jnp.concatenate([own[:, : cuts[0]], other[:, : cuts[0]]], axis=1),
        own[:, cuts[0] : cuts[1]],
        own[:, cuts[1] : cuts[2]],
        jnp.concatenate([own[:, cuts[2] :], other[:, cuts[2] :]], axis=1),
    )


def grad_pair(own, other):
    return (own + hop(other.astype(BF), "pipe", 1).astype(F32)).astype(BF)


def mlp_pair(left, right):
    half = right.shape[1] // 2
    return grad_pair(mm_tl(left, right[:, :half]), mm_tl(left, right[:, half:]))


def grad_group(total):
    return lax.psum_scatter(total, "grp", scatter_dimension=0, tiled=True)


def grad_home(total):
    return trade(total.reshape((lax.axis_size("wd"), -1) + total.shape[1:]), "wd")


def place_kernel(turned, at_ref, keep_ref, got_ref, out_ref):
    mine = pl.program_id(1) == at_ref[0]

    def put(ref):
        block = ref[0].astype(F32)
        out_ref[...] = block.T if turned else block

    @pl.when(mine)
    def _():
        put(keep_ref)

    @pl.when(jnp.logical_not(mine))
    def _():
        put(got_ref)


def place(keep, got, turned):
    wd, rows, cols = keep.shape
    at = lax.axis_index("pipe").astype(jnp.int32)[None]
    cores = lax.axis_size("pipe")
    source = pl.BlockSpec((1, rows, cols), lambda w, c, at_ref: (w, 0, 0))
    if turned:
        shape, target = (wd * cores * cols, rows), (cols, rows)
        out = pl.BlockSpec(target, lambda w, c, at_ref: (w * cores + c, 0))
    else:
        shape, target = (rows, wd * cores * cols), (rows, cols)
        out = pl.BlockSpec(target, lambda w, c, at_ref: (0, w * cores + c))
    return pl.pallas_call(
        lambda *refs: place_kernel(turned, *refs),
        grid_spec=pltpu.PrefetchScalarGridSpec(
            num_scalar_prefetch=1, grid=(wd, cores), in_specs=[source, source], out_specs=out
        ),
        out_shape=jax.ShapeDtypeStruct(shape, F32),
        cost_estimate=pl.CostEstimate(
            flops=keep.size, bytes_accessed=12 * keep.size, transcendentals=0
        ),
    )(at, keep, got)


def layer_forward(stages, layer, x_rows, gains, where, build, jobs, settle):
    held = stages.held
    cosine, sine, q_place, q_start, k_place = where
    normed = apply_norm(x_rows, gains[0]).astype(BF)
    rows_a = stages.run(normed, gather_rows, jobs[0], settle[0])
    held["attn", layer] = build("attn", layer)
    w_q, w_k, w_v, w_ot = held["attn", layer]
    tok = rows_a.shape[0]

    def project(rows):
        key = rotary_apply(mm(rows, w_k).reshape(tok, 1, HEAD_SIZE), cosine, sine).astype(BF)[:, 0]
        value = mm(rows, w_v).astype(BF)
        return jnp.concatenate([key, value], axis=1)

    def queries(rows):
        query = rotary_apply(mm(rows, w_q).reshape(tok, -1, HEAD_SIZE), cosine, sine).astype(BF)
        return query.transpose(1, 0, 2)

    held["rows_a"] = rows_a
    kv_all = stages.run(
        project(rows_a),
        lambda kv: jnp.concatenate(others(kv, "grp"), axis=0),
        [("query", queries, ("rows_a",))] + jobs[1],
        settle[1],
    )
    query = held["query"]
    keys, values = kv_all[:, :HEAD_SIZE], kv_all[:, HEAD_SIZE:]

    def attention(q):
        context = attend(q, keys, values, q_place, q_start, k_place)
        context = context.transpose(1, 0, 2).reshape(tok, -1)
        return context, mm_t(context, w_ot).astype(BF)

    context, partial = stages.run(query, attention, jobs[2], settle[2])
    mid = stages.run(partial, lambda p: x_rows + sum_rows(p), jobs[3], settle[3])
    rows_b = stages.run(
        mid, lambda m: gather_rows(apply_norm(m, gains[1]).astype(BF)), jobs[4], settle[4]
    )
    held["gu", layer] = w_gu = build("gu", layer)

    def ahead(rows):
        both = mm(rows, w_gu)
        half = both.shape[1] // 2
        gate, up = both[:, :half], both[:, half:]
        return gate, up, (jax.nn.silu(gate) * up).astype(BF)

    gate, up, hidden = stages.run(rows_b, ahead, jobs[5], settle[5])
    held["down", layer] = build("down", layer)
    return x_rows, rows_a, query, keys, values, context, mid, rows_b, gate, up, hidden


def layer_backward(
    stages, layer, grad_out, grad_mlp, gains, where, kept, also, jobs, settle
):
    held = stages.held
    cosine, sine, q_place, q_start, k_place = where
    x_rows, rows_a, query, keys, values, context, mid, rows_b, gate, up, hidden = kept
    w_q, w_k, w_v, w_ot = held["attn", layer]
    w_gu, w_dt = held["gu", layer], held["down", layer]
    tok = rows_a.shape[0]
    held["rows_b"], held["hidden"], held["grad_mlp"] = rows_b, hidden, grad_mlp

    def feed_back(rows):
        grad_hidden = mm(rows, w_dt)
        sig = jax.nn.sigmoid(gate)
        grad_gate = (grad_hidden * up * sig * (1.0 + gate * (1.0 - sig))).astype(BF)
        grad_up = (grad_hidden * gate * sig).astype(BF)
        both = jnp.concatenate([grad_gate, grad_up], axis=1)
        return grad_gate, grad_up, mm_t(both, w_gu).astype(BF), also(hidden)

    grad_gate, grad_up, partial, extra = stages.run(grad_mlp, feed_back, jobs[0], settle[0])
    held["grad_gate"], held["grad_up"] = grad_gate, grad_up
    grad_b = stages.run(partial, sum_rows, jobs[1], settle[1])
    grad_mid, gain_b = norm_back(mid, gains[1], grad_b)
    grad_mid = grad_mid + grad_out
    grad_attn = stages.run(grad_mid.astype(BF), gather_rows, jobs[2], settle[2])

    def attention_back(rows):
        grad_context = mm(rows, w_ot).astype(BF)
        grad_context = grad_context.reshape(tok, -1, HEAD_SIZE).transpose(1, 0, 2)
        return attend_back(query, grad_context, keys, values, q_place, q_start, k_place)

    def keys_back(grads):
        kv = jnp.concatenate(grads, axis=1)
        kv = kv.reshape((-1, tok) + kv.shape[1:])
        return sum_others([kv[k] for k in range(kv.shape[0])], "grp").astype(BF)

    def queries_back(grad_q):
        grad_q = grad_q.transpose(1, 0, 2).astype(F32)
        grad_q = rotary_apply(grad_q, cosine, -sine).astype(BF).reshape(tok, -1)
        return grad_q, mm_t(grad_q, w_q)

    held["grad_q"], *grads = stages.run(grad_attn, attention_back, jobs[3])
    own_kv = stages.run(
        grads, keys_back, [("g_q", queries_back, ("grad_q",))] + jobs[4], settle[4]
    )
    grad_q, partial = held["g_q"]
    grad_k = own_kv[:, :HEAD_SIZE].astype(F32)
    grad_k = rotary_apply(grad_k[:, None, :], cosine, -sine).astype(BF)[:, 0]
    grad_v = own_kv[:, HEAD_SIZE:]
    partial = (partial + mm_t(grad_k, w_k) + mm_t(grad_v, w_v)).astype(BF)

    def attn_pair(g_q, g_k, g_v):
        half_q = g_q.shape[1] // 2

        def term(cut):
            right = jnp.concatenate([g_q[:, cut], g_k, g_v], axis=1)
            left = [mm_tl(rows_a, right), mm_tl(grad_attn, context[:, cut])]
            return jnp.concatenate(left, axis=1)

        return grad_pair(term(slice(0, half_q)), term(slice(half_q, None)))

    held["g_q"], held["g_k"], held["g_v"] = grad_q, grad_k, grad_v
    grad_a = stages.run(partial, sum_rows, jobs[5](attn_pair), settle[5])
    grad_in, gain_a = norm_back(x_rows, gains[0], grad_a)
    return grad_mid + grad_in, jnp.stack([gain_a, gain_b]), extra


def own_layer(first, second):
    core = lax.axis_index("pipe")
    keep = jnp.where(core == 0, first, second)
    return keep, hop(jnp.where(core == 0, second, first), "pipe", 1)


def body(
    block_input,
    cotangent,
    segments,
    norm_gains,
    w_query,
    key_matrix,
    value_matrix,
    w_output,
    w_gate,
    w_up,
    w_down,
):
    core = lax.axis_index("pipe")
    grp = lax.axis_index("grp")
    wd = lax.axis_size("wd")
    groups = lax.axis_size("grp")
    cores = lax.axis_size("pipe")
    tok = block_input.shape[1] * lax.axis_size(CUBE)

    stages = Stages()
    held = stages.held
    packed = pack_attention(w_query[0], key_matrix[0], value_matrix[0], w_output[0], cores)
    gains = spread_gains(norm_gains[0])
    packed, gains = lax.optimization_barrier((packed, gains))
    attn_cols = columns_out(to_blocks(packed, cores))
    held["gate_out"] = to_blocks(w_gate[0], cores)
    held["up_out"] = to_blocks(w_up[0], cores)
    held["down_out"] = to_blocks(w_down[0].T, cores)
    query_w, out_w = w_query.shape[2] // (wd * cores), w_output.shape[1] // (wd * cores)
    widths = (query_w, key_matrix.shape[2] // wd, out_w)

    def move(name):
        return (name, columns_out, (name + "_out",), "later")

    def rows_of(name, layer):
        return lax.all_gather(held[name][layer], "grp", axis=0, tiled=True)

    def put(*names):
        return put_together([[m] for n in names for m in (held[n], hop(held[n], "pipe", 1))])

    def build(kind, layer):
        if kind == "attn":
            return unpack_attention(held["own", "attn", layer], widths)
        if kind == "gu":
            return put(("own", "gate", layer), ("own", "up", layer))
        return put(("own", "down", layer))

    held["attn"] = attn_cols
    for layer in range(2):
        held["own", "attn", layer] = rows_of("attn", layer)

    def start(name):
        for layer in range(2):
            held["own", name, layer] = rows_of(name, layer)

    stages.then.update(gate=start, up=start, down=start)

    seg_row = lax.dynamic_index_in_dim(segments, core, 0, keepdims=False)
    starts = doc_starts(seg_row)
    rows_own = tok // lax.axis_size(CUBE)

    def in_row_order(values):
        values = relative(values, 0, CUBE)
        return jnp.concatenate(
            [values[j * rows_own : (j + 1) * rows_own] for j in ROW_ORDER], axis=0
        )

    local = in_row_order(jnp.arange(tok, dtype=jnp.int32))
    q_place = grp * tok + local
    q_start = in_row_order(lax.dynamic_slice_in_dim(starts, grp * tok, tok))
    cosine, sine = rope_tables(q_place - q_start)
    k_place = jnp.concatenate([(grp ^ k) * tok + local for k in range(groups)])
    where = (cosine, sine, q_place[:, None], q_start[:, None], k_place[None, :])

    rows = lax.dynamic_index_in_dim(block_input, core, 0, keepdims=False)
    grad = lax.dynamic_index_in_dim(cotangent, core, 0, keepdims=False)
    held["cotangent"] = grad
    kept = [None, None]
    outs = [None, None]
    kept[0] = layer_forward(
        stages,
        0,
        rows.astype(F32),
        gains[0],
        where,
        build,
        [[], [move("gate")], [move("up")], [move("down")], [], []],
        [(), (), (("own", "attn", 1),), (("own", "gate", 0),), (("own", "up", 0),), ()],
    )

    def close(hidden, layer):
        return (kept[layer][6] + sum_rows(mm_t(hidden, held["down", layer]))).astype(BF)

    outs[0] = stages.run(
        kept[0][-1], lambda h: close(h, 0), [], (("own", "gate", 1),)
    )
    kept[1] = layer_forward(
        stages,
        1,
        outs[0].astype(F32),
        gains[1],
        where,
        build,
        [[], [], [("last", gather_rows, ("cotangent",))], [], [], []],
        [(), (("own", "up", 1),), (), (("own", "down", 1),), (), ()],
    )

    def grad_of(name, layer):
        sources = {
            "down": ("grad_mlp", "hidden"),
            "gate": ("rows_b", "grad_gate"),
            "up": ("rows_b", "grad_up"),
        }[name]
        return (("pair", name, layer), mlp_pair, sources)

    def group_sum(name, layer):
        return (("sum", name, layer), grad_group, (("pair", name, layer),), "later")

    def home(name, layer):
        return (("home", name, layer), grad_home, (("sum", name, layer),))

    def attn_grad(layer):
        return lambda pair: (("pair", "attn", layer), pair, ("g_q", "g_k", "g_v"))

    def final(name, turned):
        def ready(first, second):
            return place(*own_layer(first, second), turned)

        return (("final", name), ready, (("home", name, 0), ("home", name, 1)))

    held["hidden"], held["grad_mlp"] = kept[1][-1], held["last"]
    hidden = stages.run(kept[1][-1], lambda h: h, [grad_of("down", 1)])

    grads_in = [None, None]
    gain_grads = [None, None]
    grad_in, gain_grads[1], outs[1] = layer_backward(
        stages,
        1,
        grad.astype(F32),
        held["last"],
        gains[1],
        where,
        kept[1][:-1] + (hidden,),
        lambda h: close(h, 1),
        (
            [],
            [group_sum("down", 1), grad_of("gate", 1)],
            [group_sum("gate", 1), grad_of("up", 1)],
            [group_sum("up", 1)],
            [home("down", 1)],
            lambda pair: [attn_grad(1)(pair)],
        ),
        [(), (), (), (), (), (("sum", "gate", 1),)],
    )
    grads_in[1] = grad_in.astype(BF)
    grad_mlp = stages.run(grads_in[1], gather_rows, [group_sum("attn", 1)], (("sum", "up", 1),))
    grad_in, gain_grads[0], _ = layer_backward(
        stages,
        0,
        grads_in[1].astype(F32),
        grad_mlp,
        gains[0],
        where,
        kept[0],
        lambda h: (),
        (
            [grad_of("down", 0), home("gate", 1)],
            [group_sum("down", 0), grad_of("gate", 0)],
            [group_sum("gate", 0), grad_of("up", 0)],
            [group_sum("up", 0)],
            [],
            lambda pair: [attn_grad(0)(pair)],
        ),
        [
            (),
            (("sum", "attn", 1),),
            (("sum", "down", 0),),
            (),
            (("sum", "gate", 0),),
            (("sum", "up", 0),),
        ],
    )
    grads_in[0] = grad_in.astype(BF)
    for key, job, names, *_ in (
        group_sum("attn", 0),
        home("up", 1),
        home("down", 0),
        final("down", True),
        home("gate", 0),
        final("gate", False),
        home("up", 0),
        home("attn", 1),
        home("attn", 0),
    ):
        held[key] = job(*[held[name] for name in names])

    def by_batch(pair):
        own, other = own_layer(pair[0], pair[1])
        both = jnp.where(core == 0, jnp.stack([own, other]), jnp.stack([other, own]))
        return both[None]

    layer_out = by_batch(outs)
    input_grad = by_batch(grads_in)

    grad_norm_gains = sum_gains(gain_grads)[None]

    def both(name):
        return own_layer(held["home", name, 0], held["home", name, 1])

    keep, got = both("attn")
    cuts = (0, widths[0], widths[0] + widths[1], widths[0] + 2 * widths[1], keep.shape[2])
    q_pair, k_pair, v_pair, o_pair = (
        (keep[..., lo:hi], got[..., lo:hi]) for lo, hi in zip(cuts[:-1], cuts[1:])
    )

    def small(pair):
        order = pair[0].transpose(1, 0, 2).astype(F32)
        return order.reshape(order.shape[0], -1)[None]

    grad_wq = place(*q_pair, False)[None]
    grad_wk = small(k_pair)
    grad_wv = small(v_pair)
    grad_wo = place(*o_pair, True)[None]
    grad_wg = held["final", "gate"][None]
    grad_wu = place(*both("up"), False)[None]
    grad_wd = held["final", "down"][None]
    return (
        layer_out,
        input_grad,
        grad_norm_gains,
        grad_wq,
        grad_wk,
        grad_wv,
        grad_wo,
        grad_wg,
        grad_wu,
        grad_wd,
    )


def solution(mesh):
    sizes = dict(mesh.shape)
    wd = KV_HEADS // sizes["tensor"]
    fine = Mesh(
        mesh.devices.reshape(sizes["pipe"], sizes["dp"] // wd, wd, sizes["tensor"]),
        ("pipe", "grp", "wd", "tensor"),
    )
    dp = ("grp", "wd")
    tokens = P(None, dp + ("tensor",), None)
    outs = P("pipe", None, dp + ("tensor",), None)
    gains = P("pipe", None, dp + ("tensor",))
    tall = P("pipe", dp, "tensor")
    wide = P("pipe", "tensor", dp)
    weights = (tall, tall, tall, wide, tall, tall, wide)
    return jax.shard_map(
        body,
        mesh=fine,
        in_specs=(tokens, tokens, P(), gains) + weights,
        out_specs=(outs, outs, gains) + weights,
        check_vma=False,
    )
```

```python
import jax
import jax.numpy as jnp
from jax import lax
from jax.experimental import pallas as pl
from jax.experimental.pallas import tpu as pltpu
from jax.sharding import Mesh, PartitionSpec as P

HEAD_SIZE = 64
KV_HEADS = 8
EPS = 1e-05
ROPE_BASE = 500000.0
NEG_FILL = -1e30
BF = jnp.bfloat16
F32 = jnp.float32
CUBE = ("wd", "tensor")


def rms_scale(row_values):
    return lax.rsqrt(jnp.mean(row_values * row_values, axis=-1, keepdims=True) + EPS)


def apply_norm(row_values, gain_vector):
    return row_values * rms_scale(row_values) * gain_vector


def norm_back(row_values, gain_vector, grad_normed):
    _, pullback = jax.vjp(apply_norm, row_values, gain_vector)
    return pullback(grad_normed)


def doc_starts(seg_row):
    places = jnp.arange(seg_row.shape[0], dtype=jnp.int32)
    before = jnp.concatenate([seg_row[:1] - 1, seg_row[:-1]])
    return lax.cummax(jnp.where(seg_row != before, places, 0), axis=0)


def rope_tables(positions):
    half_dim = HEAD_SIZE // 2
    freqs = ROPE_BASE ** (-(jnp.arange(half_dim, dtype=F32) * 2.0 / HEAD_SIZE))
    angles = positions.astype(F32)[:, None] * freqs[None, :]
    return (jnp.cos(angles), jnp.sin(angles))


def rotary_apply(head_values, cosine_table, sine_values):
    half_dim = head_values.shape[-1] // 2
    first_half = head_values[..., :half_dim]
    second_half = head_values[..., half_dim:]
    cos_rows = cosine_table[:, None, :]
    sin_rows = sine_values[:, None, :]
    return jnp.concatenate(
        [
            first_half * cos_rows - second_half * sin_rows,
            second_half * cos_rows + first_half * sin_rows,
        ],
        axis=-1,
    )


def mm(left, right):
    return jnp.dot(left, right, preferred_element_type=F32)


def mm_t(left, right):
    return lax.dot_general(left, right, (((1,), (1,)), ((), ())), preferred_element_type=F32)


def mm_tl(left, right):
    return lax.dot_general(left, right, (((0,), (0,)), ((), ())), preferred_element_type=F32)


def trade(blocks, axes):
    return lax.all_to_all(blocks, axes, 0, 0, tiled=True)


def hop(block, axis, step):
    size = lax.axis_size(axis)
    return lax.ppermute(block, axis, [(i, i ^ step) for i in range(size)])


def tie(*values):
    return lax.optimization_barrier(values)


def link_steps():
    steps = []
    step = 1
    while step < lax.axis_size(CUBE):
        steps.append(step)
        step *= 2
    return steps


FAR, NEAR, SIDE = 4, 2, 1
ROW_ORDER = (0, FAR, NEAR, FAR | NEAR, SIDE, FAR | SIDE, NEAR | SIDE, FAR | NEAR | SIDE)


def cube(block, step):
    return hop(block, CUBE, step)


def join_kernel(left_ref, left_came_ref, right_ref, right_came_ref, out_ref):
    half = left_ref.shape[1]
    block = pl.program_id(0)

    @pl.when(block < 2)
    def _():
        out_ref[:, :half] = left_ref[...]

    @pl.when(block >= 2)
    def _():
        out_ref[:, :half] = left_came_ref[...]

    @pl.when(block % 2 == 0)
    def _():
        out_ref[:, half:] = right_ref[...]

    @pl.when(block % 2 == 1)
    def _():
        out_ref[:, half:] = right_came_ref[...]


def join_halves(left, left_came, right, right_came):
    rows, half = left.shape[0] // 2, left.shape[1]

    def spec(place):
        return pl.BlockSpec((rows, half), lambda i: (place(i), 0))

    return pl.pallas_call(
        join_kernel,
        grid=(4,),
        in_specs=[
            spec(lambda i: jnp.minimum(i, 1)),
            spec(lambda i: jnp.maximum(i - 2, 0)),
            spec(lambda i: i // 2),
            spec(lambda i: i // 2),
        ],
        out_specs=pl.BlockSpec((rows, 2 * half), lambda i: (i, 0)),
        out_shape=jax.ShapeDtypeStruct((4 * rows, 2 * half), left.dtype),
        cost_estimate=pl.CostEstimate(
            flops=0, bytes_accessed=32 * rows * half, transcendentals=0
        ),
    )(left, left_came, right, right_came)


def gather_rows(rows):
    two = jnp.concatenate([rows, cube(rows, FAR)], axis=0)
    half = two.shape[1] // 2
    left, right = two[:, :half], two[:, half:]
    left_came, right_came = cube(left, NEAR), cube(right, SIDE)
    left = jnp.concatenate([left, left_came], axis=0)
    right = jnp.concatenate([right, right_came], axis=0)
    return join_halves(left, cube(left, SIDE), right, cube(right, NEAR))


def sum_rows(partial):
    partial = partial.astype(BF)
    n, half = partial.shape[0] // 4, partial.shape[1] // 2
    left, right = partial[:, :half], partial[:, half:]
    left_came = cube(left[2 * n :], SIDE)
    right_came = cube(jnp.concatenate([right[n : 2 * n], right[3 * n :]], axis=0), NEAR)
    left = left[: 2 * n].astype(F32) + left_came.astype(F32)
    right_came = right_came.astype(F32)
    low = right[:n].astype(F32) + right_came[:n]
    high = right[2 * n : 3 * n].astype(F32) + right_came[n:]
    left_came = cube(left[n:].astype(BF), NEAR)
    right_came = cube(high.astype(BF), SIDE)
    left = left[:n] + left_came.astype(F32)
    right = low + right_came.astype(F32)
    both = jnp.concatenate([left, right], axis=1)
    rows = n // 2
    return both[:rows] + cube(both[rows:].astype(BF), FAR).astype(F32)


class Stages:
    def __init__(self):
        self.held = {}
        self.then = {}

    def run(self, value, step, jobs, settle=()):
        needed = [[self.held[name] for name in job[2]] for job in jobs]
        value, needed = lax.optimization_barrier((value, needed))
        out = step(value)
        made = [job[1](*inputs) for job, inputs in zip(jobs, needed)]
        due = [m for m, job in zip(made, jobs) if len(job) == 3]
        ready = [self.held[key] for key in settle]
        out, due, ready = lax.optimization_barrier((out, due, ready))
        self.held.update(zip(settle, ready))
        for job, result in zip(jobs, made):
            self.held[job[0]] = due.pop(0) if len(job) == 3 else result
            if job[0] in self.then:
                self.then[job[0]](job[0])
        return out


def others(block, axis):
    return [block] + [hop(block, axis, k) for k in range(1, lax.axis_size(axis))]


def sum_others(blocks, axis):
    total = blocks[0].astype(F32)
    for k in range(1, lax.axis_size(axis)):
        total = total + hop(blocks[k].astype(BF), axis, k).astype(F32)
    return total


def relative(values, dim, axis):
    count = lax.axis_size(axis)
    me = lax.axis_index(axis)
    step = 1
    while step < count:
        shape = values.shape
        cut = shape[:dim] + (count // (2 * step), 2, step * (shape[dim] // count)) + shape[dim + 1 :]
        view = values.reshape(cut)
        swapped = jnp.concatenate(
            [lax.slice_in_dim(view, 1, 2, axis=dim + 1), lax.slice_in_dim(view, 0, 1, axis=dim + 1)],
            axis=dim + 1,
        )
        values = jnp.where((me & step) != 0, swapped.reshape(shape), values)
        step *= 2
    return values


def spread_gains(norm_gains):
    me = lax.axis_index(CUBE)
    gain = norm_gains
    for step in link_steps():
        came = hop(gain, CUBE, step)
        gain = jnp.where(
            (me & step) != 0,
            jnp.concatenate([came, gain], axis=1),
            jnp.concatenate([gain, came], axis=1),
        )
    gain = relative(jnp.concatenate(others(gain, "grp"), axis=1), 1, "grp")
    other = hop(gain, "pipe", 1)
    core = lax.axis_index("pipe")
    return [jnp.where(core == 0, gain, other), jnp.where(core == 0, other, gain)]


def sum_gains(grads):
    me = lax.axis_index(CUBE)
    keep, extra = own_layer(grads[0], grads[1])
    count = lax.axis_size("grp")
    total = relative((keep + extra).reshape(2, count, -1), 1, "grp")
    mine = total[:, 0]
    for k in range(1, count):
        mine = mine + hop(total[:, k], "grp", k)
    for step in link_steps()[::-1]:
        half = mine.shape[1] // 2
        low, high = mine[:, :half], mine[:, half:]
        odd = (me & step) != 0
        mine = jnp.where(odd, high, low) + hop(jnp.where(odd, low, high), CUBE, step)
    return mine


def masked_probs(q, k, q_place, q_start, k_place):
    scores = lax.dot_general(q, k, (((1,), (1,)), ((), ())), preferred_element_type=F32)
    scores = scores * HEAD_SIZE ** (-0.5)
    allowed = (k_place <= q_place) & (k_place >= q_start)
    masked = jnp.where(allowed, scores, NEG_FILL)
    exps = jnp.exp(masked - jnp.max(masked, axis=-1, keepdims=True))
    return exps / jnp.sum(exps, axis=-1, keepdims=True)


def attend_kernel(q_ref, k_ref, v_ref, qp_ref, qs_ref, kp_ref, o_ref):
    probs = masked_probs(q_ref[0], k_ref[...], qp_ref[...], qs_ref[...], kp_ref[...])
    o_ref[0] = jnp.dot(probs.astype(BF), v_ref[...], preferred_element_type=F32).astype(BF)


def attend_back_kernel(q_ref, do_ref, k_ref, v_ref, qp_ref, qs_ref, kp_ref, dq_ref, dk_ref, dv_ref):
    @pl.when((pl.program_id(0) == 0) & (pl.program_id(1) == 0))
    def _():
        dk_ref[...] = jnp.zeros_like(dk_ref)
        dv_ref[...] = jnp.zeros_like(dv_ref)

    q = q_ref[0]
    do = do_ref[0]
    k = k_ref[...]
    probs = masked_probs(q, k, qp_ref[...], qs_ref[...], kp_ref[...])
    grad_probs = lax.dot_general(do, v_ref[...], (((1,), (1,)), ((), ())), preferred_element_type=F32)
    delta = jnp.sum(probs * grad_probs, axis=-1, keepdims=True)
    grad_scores = (probs * (grad_probs - delta) * HEAD_SIZE ** (-0.5)).astype(BF)
    dq_ref[0] = jnp.dot(grad_scores, k, preferred_element_type=F32).astype(BF)
    dk_ref[...] += lax.dot_general(
        grad_scores, q, (((0,), (0,)), ((), ())), preferred_element_type=F32
    )
    dv_ref[...] += lax.dot_general(
        probs.astype(BF), do, (((0,), (0,)), ((), ())), preferred_element_type=F32
    )


def attention_specs(heads, rows, keys):
    rows_blk = max(16, min(rows, (512 * 1024) // keys))
    per_head = pl.BlockSpec((1, rows_blk, HEAD_SIZE), lambda b, h: (h, b, 0))
    full = pl.BlockSpec((keys, HEAD_SIZE), lambda b, h: (0, 0))
    row_info = pl.BlockSpec((rows_blk, 1), lambda b, h: (b, 0))
    key_info = pl.BlockSpec((1, keys), lambda b, h: (0, 0))
    return ((rows // rows_blk, heads), per_head, full, row_info, key_info)


PARAMS = dict(
    compiler_params=pltpu.CompilerParams(vmem_limit_bytes=50 * 1024 * 1024),
)


def attend(q, k, v, q_place, q_start, k_place):
    heads, rows, _ = q.shape
    keys = k.shape[0]
    grid, per_head, full, row_info, key_info = attention_specs(heads, rows, keys)
    return pl.pallas_call(
        attend_kernel,
        grid=grid,
        in_specs=[per_head, full, full, row_info, row_info, key_info],
        out_specs=per_head,
        out_shape=jax.ShapeDtypeStruct(q.shape, BF),
        cost_estimate=pl.CostEstimate(
            flops=4 * heads * rows * keys * HEAD_SIZE,
            bytes_accessed=4 * q.size + 4 * k.size,
            transcendentals=heads * rows * keys,
        ),
        **PARAMS,
    )(q, k, v, q_place, q_start, k_place)


def attend_back(q, do, k, v, q_place, q_start, k_place):
    heads, rows, _ = q.shape
    keys = k.shape[0]
    grid, per_head, full, row_info, key_info = attention_specs(heads, rows, keys)
    return pl.pallas_call(
        attend_back_kernel,
        grid=grid,
        in_specs=[per_head, per_head, full, full, row_info, row_info, key_info],
        out_specs=[per_head, full, full],
        out_shape=[
            jax.ShapeDtypeStruct(q.shape, BF),
            jax.ShapeDtypeStruct(k.shape, F32),
            jax.ShapeDtypeStruct(k.shape, F32),
        ],
        cost_estimate=pl.CostEstimate(
            flops=10 * heads * rows * keys * HEAD_SIZE,
            bytes_accessed=6 * q.size + 12 * k.size,
            transcendentals=heads * rows * keys,
        ),
        **PARAMS,
    )(q, do, k, v, q_place, q_start, k_place)


def to_blocks(weight, cores):
    wd = lax.axis_size("wd")
    rows = weight.shape[0]
    cut = weight.reshape(rows, wd, cores, -1).transpose(2, 1, 0, 3)
    return cut.reshape((cores * wd, rows) + cut.shape[3:])


def columns_out(blocks):
    moved = trade(blocks, ("pipe", "wd"))
    return moved.reshape((2, -1) + moved.shape[2:])


def put_kernel(spots, *refs):
    pieces, out = refs[: len(spots)], refs[len(spots)]
    block = pl.program_id(0)
    for piece, (first, count, col, cols) in zip(pieces, spots):

        def put(piece=piece, col=col, cols=cols):
            out[:, col : col + cols] = piece[...]

        pl.when((block >= first) & (block < first + count))(put)


def put_together(columns):
    block = min([256] + [piece.shape[0] for stack in columns for piece in stack])
    spots, pieces, specs = [], [], []
    col = 0
    for stack in columns:
        first = 0
        for piece in stack:
            count, cols = piece.shape[0] // block, piece.shape[1]
            spots.append((first, count, col, cols))
            pieces.append(piece)

            def at(i, first=first, count=count):
                return (jnp.clip(i - first, 0, count - 1), 0)

            specs.append(pl.BlockSpec((block, cols), at))
            first += count
        col += cols
    return pl.pallas_call(
        lambda *refs: put_kernel(spots, *refs),
        grid=(first,),
        in_specs=specs,
        out_specs=pl.BlockSpec((block, col), lambda i: (i, 0)),
        out_shape=jax.ShapeDtypeStruct((first * block, col), BF),
        cost_estimate=pl.CostEstimate(
            flops=0, bytes_accessed=4 * first * block * col, transcendentals=0
        ),
        **PARAMS,
    )(*pieces)


def pack_attention(w_query, key_matrix, value_matrix, w_output, cores):
    wd = lax.axis_size("wd")
    rows = w_query.shape[0]
    cut = [w_query.reshape(rows, wd, cores, -1)]
    for m in (key_matrix, value_matrix):
        m = m.reshape(rows, wd, 1, -1)
        cut.append(jnp.broadcast_to(m, (rows, wd, cores, m.shape[3])))
    cut.append(w_output.T.reshape(rows, wd, cores, -1))
    return jnp.concatenate(cut, axis=-1).reshape(rows, -1)


def unpack_attention(own, widths):
    other = hop(own, "pipe", 1)
    query_w, kv_w, out_w = widths
    cuts = (query_w, query_w + kv_w, query_w + 2 * kv_w)
    return (
        jnp.concatenate([own[:, : cuts[0]], other[:, : cuts[0]]], axis=1),
        own[:, cuts[0] : cuts[1]],
        own[:, cuts[1] : cuts[2]],
        jnp.concatenate([own[:, cuts[2] :], other[:, cuts[2] :]], axis=1),
    )


def grad_pair(own, other):
    return (own + hop(other.astype(BF), "pipe", 1).astype(F32)).astype(BF)


def mlp_pair(left, right):
    half = right.shape[1] // 2
    return grad_pair(mm_tl(left, right[:, :half]), mm_tl(left, right[:, half:]))


def grad_group(total):
    return lax.psum_scatter(total, "grp", scatter_dimension=0, tiled=True)


def grad_home(total):
    return trade(total.reshape((lax.axis_size("wd"), -1) + total.shape[1:]), "wd")


def place_kernel(turned, at_ref, keep_ref, got_ref, out_ref):
    mine = pl.program_id(1) == at_ref[0]

    def put(ref):
        block = ref[0].astype(F32)
        out_ref[...] = block.T if turned else block

    @pl.when(mine)
    def _():
        put(keep_ref)

    @pl.when(jnp.logical_not(mine))
    def _():
        put(got_ref)


def place(keep, got, turned):
    wd, rows, cols = keep.shape
    at = lax.axis_index("pipe").astype(jnp.int32)[None]
    cores = lax.axis_size("pipe")
    source = pl.BlockSpec((1, rows, cols), lambda w, c, at_ref: (w, 0, 0))
    if turned:
        shape, target = (wd * cores * cols, rows), (cols, rows)
        out = pl.BlockSpec(target, lambda w, c, at_ref: (w * cores + c, 0))
    else:
        shape, target = (rows, wd * cores * cols), (rows, cols)
        out = pl.BlockSpec(target, lambda w, c, at_ref: (0, w * cores + c))
    return pl.pallas_call(
        lambda *refs: place_kernel(turned, *refs),
        grid_spec=pltpu.PrefetchScalarGridSpec(
            num_scalar_prefetch=1, grid=(wd, cores), in_specs=[source, source], out_specs=out
        ),
        out_shape=jax.ShapeDtypeStruct(shape, F32),
        cost_estimate=pl.CostEstimate(
            flops=keep.size, bytes_accessed=12 * keep.size, transcendentals=0
        ),
    )(at, keep, got)


def layer_forward(stages, layer, x_rows, gains, where, build, jobs, settle):
    held = stages.held
    cosine, sine, q_place, q_start, k_place = where
    normed = apply_norm(x_rows, gains[0]).astype(BF)
    rows_a = stages.run(normed, gather_rows, jobs[0], settle[0])
    held["attn", layer] = build("attn", layer)
    w_q, w_k, w_v, w_ot = held["attn", layer]
    tok = rows_a.shape[0]

    def project(rows):
        key = rotary_apply(mm(rows, w_k).reshape(tok, 1, HEAD_SIZE), cosine, sine).astype(BF)[:, 0]
        value = mm(rows, w_v).astype(BF)
        return jnp.concatenate([key, value], axis=1)

    def queries(rows):
        query = rotary_apply(mm(rows, w_q).reshape(tok, -1, HEAD_SIZE), cosine, sine).astype(BF)
        return query.transpose(1, 0, 2)

    held["rows_a"] = rows_a
    kv_all = stages.run(
        project(rows_a),
        lambda kv: jnp.concatenate(others(kv, "grp"), axis=0),
        [("query", queries, ("rows_a",))] + jobs[1],
        settle[1],
    )
    query = held["query"]
    keys, values = kv_all[:, :HEAD_SIZE], kv_all[:, HEAD_SIZE:]

    def attention(q):
        context = attend(q, keys, values, q_place, q_start, k_place)
        context = context.transpose(1, 0, 2).reshape(tok, -1)
        return context, mm_t(context, w_ot).astype(BF)

    context, partial = stages.run(query, attention, jobs[2], settle[2])
    mid = stages.run(partial, lambda p: x_rows + sum_rows(p), jobs[3], settle[3])
    rows_b = stages.run(
        mid, lambda m: gather_rows(apply_norm(m, gains[1]).astype(BF)), jobs[4], settle[4]
    )
    held["gu", layer] = w_gu = build("gu", layer)

    def ahead(rows):
        both = mm(rows, w_gu)
        half = both.shape[1] // 2
        gate, up = both[:, :half], both[:, half:]
        return gate, up, (jax.nn.silu(gate) * up).astype(BF)

    gate, up, hidden = stages.run(rows_b, ahead, jobs[5], settle[5])
    held["down", layer] = build("down", layer)
    return x_rows, rows_a, query, keys, values, context, mid, rows_b, gate, up, hidden


def layer_backward(
    stages, layer, grad_out, grad_mlp, gains, where, kept, also, jobs, settle
):
    held = stages.held
    cosine, sine, q_place, q_start, k_place = where
    x_rows, rows_a, query, keys, values, context, mid, rows_b, gate, up, hidden = kept
    w_q, w_k, w_v, w_ot = held["attn", layer]
    w_gu, w_dt = held["gu", layer], held["down", layer]
    tok = rows_a.shape[0]
    held["rows_b"], held["hidden"], held["grad_mlp"] = rows_b, hidden, grad_mlp

    def feed_back(rows):
        grad_hidden = mm(rows, w_dt)
        sig = jax.nn.sigmoid(gate)
        grad_gate = (grad_hidden * up * sig * (1.0 + gate * (1.0 - sig))).astype(BF)
        grad_up = (grad_hidden * gate * sig).astype(BF)
        both = jnp.concatenate([grad_gate, grad_up], axis=1)
        return grad_gate, grad_up, mm_t(both, w_gu).astype(BF), also(hidden)

    grad_gate, grad_up, partial, extra = stages.run(grad_mlp, feed_back, jobs[0], settle[0])
    held["grad_gate"], held["grad_up"] = grad_gate, grad_up
    grad_b = stages.run(partial, sum_rows, jobs[1], settle[1])
    grad_mid, gain_b = norm_back(mid, gains[1], grad_b)
    grad_mid = grad_mid + grad_out
    grad_attn = stages.run(grad_mid.astype(BF), gather_rows, jobs[2], settle[2])

    def attention_back(rows):
        grad_context = mm(rows, w_ot).astype(BF)
        grad_context = grad_context.reshape(tok, -1, HEAD_SIZE).transpose(1, 0, 2)
        return attend_back(query, grad_context, keys, values, q_place, q_start, k_place)

    def keys_back(grads):
        kv = jnp.concatenate(grads, axis=1)
        kv = kv.reshape((-1, tok) + kv.shape[1:])
        return sum_others([kv[k] for k in range(kv.shape[0])], "grp").astype(BF)

    def queries_back(grad_q):
        grad_q = grad_q.transpose(1, 0, 2).astype(F32)
        grad_q = rotary_apply(grad_q, cosine, -sine).astype(BF).reshape(tok, -1)
        return grad_q, mm_t(grad_q, w_q)

    held["grad_q"], *grads = stages.run(grad_attn, attention_back, jobs[3])
    own_kv = stages.run(
        grads, keys_back, [("g_q", queries_back, ("grad_q",))] + jobs[4], settle[4]
    )
    grad_q, partial = held["g_q"]
    grad_k = own_kv[:, :HEAD_SIZE].astype(F32)
    grad_k = rotary_apply(grad_k[:, None, :], cosine, -sine).astype(BF)[:, 0]
    grad_v = own_kv[:, HEAD_SIZE:]
    partial = (partial + mm_t(grad_k, w_k) + mm_t(grad_v, w_v)).astype(BF)

    def attn_pair(g_q, g_k, g_v):
        half_q = g_q.shape[1] // 2

        def term(cut):
            right = jnp.concatenate([g_q[:, cut], g_k, g_v], axis=1)
            left = [mm_tl(rows_a, right), mm_tl(grad_attn, context[:, cut])]
            return jnp.concatenate(left, axis=1)

        return grad_pair(term(slice(0, half_q)), term(slice(half_q, None)))

    held["g_q"], held["g_k"], held["g_v"] = grad_q, grad_k, grad_v
    grad_a = stages.run(partial, sum_rows, jobs[5](attn_pair), settle[5])
    grad_in, gain_a = norm_back(x_rows, gains[0], grad_a)
    return grad_mid + grad_in, jnp.stack([gain_a, gain_b]), extra


def own_layer(first, second):
    core = lax.axis_index("pipe")
    keep = jnp.where(core == 0, first, second)
    return keep, hop(jnp.where(core == 0, second, first), "pipe", 1)


def body(
    block_input,
    cotangent,
    segments,
    norm_gains,
    w_query,
    key_matrix,
    value_matrix,
    w_output,
    w_gate,
    w_up,
    w_down,
):
    core = lax.axis_index("pipe")
    grp = lax.axis_index("grp")
    wd = lax.axis_size("wd")
    groups = lax.axis_size("grp")
    cores = lax.axis_size("pipe")
    tok = block_input.shape[1] * lax.axis_size(CUBE)

    stages = Stages()
    held = stages.held
    packed = pack_attention(w_query[0], key_matrix[0], value_matrix[0], w_output[0], cores)
    gains = spread_gains(norm_gains[0])
    packed, gains = lax.optimization_barrier((packed, gains))
    attn_cols = columns_out(to_blocks(packed, cores))
    held["gate_out"] = to_blocks(w_gate[0], cores)
    held["up_out"] = to_blocks(w_up[0], cores)
    held["down_out"] = to_blocks(w_down[0].T, cores)
    query_w, out_w = w_query.shape[2] // (wd * cores), w_output.shape[1] // (wd * cores)
    widths = (query_w, key_matrix.shape[2] // wd, out_w)

    def move(name):
        return (name, columns_out, (name + "_out",), "later")

    def rows_of(name, layer):
        return lax.all_gather(held[name][layer], "grp", axis=0, tiled=True)

    def put(*names):
        return put_together([[m] for n in names for m in (held[n], hop(held[n], "pipe", 1))])

    def build(kind, layer):
        if kind == "attn":
            return unpack_attention(held["own", "attn", layer], widths)
        if kind == "gu":
            return put(("own", "gate", layer), ("own", "up", layer))
        return put(("own", "down", layer))

    held["attn"] = attn_cols
    for layer in range(2):
        held["own", "attn", layer] = rows_of("attn", layer)

    def start(name):
        for layer in range(2):
            held["own", name, layer] = rows_of(name, layer)

    stages.then.update(gate=start, up=start, down=start)

    seg_row = lax.dynamic_index_in_dim(segments, core, 0, keepdims=False)
    starts = doc_starts(seg_row)
    rows_own = tok // lax.axis_size(CUBE)

    def in_row_order(values):
        values = relative(values, 0, CUBE)
        return jnp.concatenate(
            [values[j * rows_own : (j + 1) * rows_own] for j in ROW_ORDER], axis=0
        )

    local = in_row_order(jnp.arange(tok, dtype=jnp.int32))
    q_place = grp * tok + local
    q_start = in_row_order(lax.dynamic_slice_in_dim(starts, grp * tok, tok))
    cosine, sine = rope_tables(q_place - q_start)
    k_place = jnp.concatenate([(grp ^ k) * tok + local for k in range(groups)])
    where = (cosine, sine, q_place[:, None], q_start[:, None], k_place[None, :])

    rows = lax.dynamic_index_in_dim(block_input, core, 0, keepdims=False)
    grad = lax.dynamic_index_in_dim(cotangent, core, 0, keepdims=False)
    held["cotangent"] = grad
    kept = [None, None]
    outs = [None, None]
    kept[0] = layer_forward(
        stages,
        0,
        rows.astype(F32),
        gains[0],
        where,
        build,
        [[move("gate")], [move("up")], [move("down")], [], [], []],
        [(), (), (("own", "gate", 0),), (("own", "attn", 1),), (("own", "up", 0),), ()],
    )

    def close(hidden, layer):
        return (kept[layer][6] + sum_rows(mm_t(hidden, held["down", layer]))).astype(BF)

    outs[0] = stages.run(
        kept[0][-1], lambda h: close(h, 0), [], (("own", "gate", 1),)
    )
    kept[1] = layer_forward(
        stages,
        1,
        outs[0].astype(F32),
        gains[1],
        where,
        build,
        [[], [], [("last", gather_rows, ("cotangent",))], [], [], []],
        [(("own", "up", 1),), (), (("own", "down", 1),), (), (), ()],
    )

    def grad_of(name, layer):
        sources = {
            "down": ("grad_mlp", "hidden"),
            "gate": ("rows_b", "grad_gate"),
            "up": ("rows_b", "grad_up"),
        }[name]
        return (("pair", name, layer), mlp_pair, sources)

    def group_sum(name, layer):
        return (("sum", name, layer), grad_group, (("pair", name, layer),), "later")

    def home(name, layer):
        return (("home", name, layer), grad_home, (("sum", name, layer),), "later")

    def attn_grad(layer):
        return lambda pair: (("pair", "attn", layer), pair, ("g_q", "g_k", "g_v"))

    def final(name, turned):
        def ready(first, second):
            return place(*own_layer(first, second), turned)

        return (("final", name), ready, (("home", name, 0), ("home", name, 1)))

    held["hidden"], held["grad_mlp"] = kept[1][-1], held["last"]
    hidden = stages.run(kept[1][-1], lambda h: h, [grad_of("down", 1)])

    grads_in = [None, None]
    gain_grads = [None, None]
    grad_in, gain_grads[1], outs[1] = layer_backward(
        stages,
        1,
        grad.astype(F32),
        held["last"],
        gains[1],
        where,
        kept[1][:-1] + (hidden,),
        lambda h: close(h, 1),
        (
            [],
            [group_sum("down", 1), grad_of("gate", 1)],
            [group_sum("gate", 1), grad_of("up", 1)],
            [group_sum("up", 1)],
            [home("down", 1)],
            lambda pair: [attn_grad(1)(pair)],
        ),
        [(), (), (), (), (), (("sum", "gate", 1), ("home", "down", 1))],
    )
    grads_in[1] = grad_in.astype(BF)
    grad_mlp = stages.run(grads_in[1], gather_rows, [group_sum("attn", 1)], (("sum", "up", 1),))
    grad_in, gain_grads[0], _ = layer_backward(
        stages,
        0,
        grads_in[1].astype(F32),
        grad_mlp,
        gains[0],
        where,
        kept[0],
        lambda h: (),
        (
            [grad_of("down", 0), home("gate", 1)],
            [group_sum("down", 0), grad_of("gate", 0), home("up", 1)],
            [group_sum("gate", 0), grad_of("up", 0), home("attn", 1)],
            [group_sum("up", 0)],
            [home("down", 0)],
            lambda pair: [attn_grad(0)(pair)],
        ),
        [
            (),
            (("sum", "attn", 1), ("home", "gate", 1)),
            (("sum", "down", 0), ("home", "up", 1)),
            (),
            (("sum", "gate", 0), ("home", "attn", 1)),
            (("sum", "up", 0), ("home", "down", 0)),
        ],
    )
    grads_in[0] = grad_in.astype(BF)
    for key, job, names, *_ in (
        group_sum("attn", 0),
        final("down", True),
        home("gate", 0),
        final("gate", False),
        home("up", 0),
        home("attn", 0),
    ):
        held[key] = job(*[held[name] for name in names])

    def by_batch(pair):
        own, other = own_layer(pair[0], pair[1])
        both = jnp.where(core == 0, jnp.stack([own, other]), jnp.stack([other, own]))
        return both[None]

    layer_out = by_batch(outs)
    input_grad = by_batch(grads_in)

    grad_norm_gains = sum_gains(gain_grads)[None]

    def both(name):
        return own_layer(held["home", name, 0], held["home", name, 1])

    keep, got = both("attn")
    cuts = (0, widths[0], widths[0] + widths[1], widths[0] + 2 * widths[1], keep.shape[2])
    q_pair, k_pair, v_pair, o_pair = (
        (keep[..., lo:hi], got[..., lo:hi]) for lo, hi in zip(cuts[:-1], cuts[1:])
    )

    def small(pair):
        order = pair[0].transpose(1, 0, 2).astype(F32)
        return order.reshape(order.shape[0], -1)[None]

    grad_wq = place(*q_pair, False)[None]
    grad_wk = small(k_pair)
    grad_wv = small(v_pair)
    grad_wo = place(*o_pair, True)[None]
    grad_wg = held["final", "gate"][None]
    grad_wu = place(*both("up"), False)[None]
    grad_wd = held["final", "down"][None]
    return (
        layer_out,
        input_grad,
        grad_norm_gains,
        grad_wq,
        grad_wk,
        grad_wv,
        grad_wo,
        grad_wg,
        grad_wu,
        grad_wd,
    )


def solution(mesh):
    sizes = dict(mesh.shape)
    wd = KV_HEADS // sizes["tensor"]
    fine = Mesh(
        mesh.devices.reshape(sizes["pipe"], sizes["dp"] // wd, wd, sizes["tensor"]),
        ("pipe", "grp", "wd", "tensor"),
    )
    dp = ("grp", "wd")
    tokens = P(None, dp + ("tensor",), None)
    outs = P("pipe", None, dp + ("tensor",), None)
    gains = P("pipe", None, dp + ("tensor",))
    tall = P("pipe", dp, "tensor")
    wide = P("pipe", "tensor", dp)
    weights = (tall, tall, tall, wide, tall, tall, wide)
    return jax.shard_map(
        body,
        mesh=fine,
        in_specs=(tokens, tokens, P(), gains) + weights,
        out_specs=(outs, outs, gains) + weights,
        check_vma=False,
    )
```

```python
import jax
import jax.numpy as jnp
from jax import lax
from jax.experimental import pallas as pl
from jax.experimental.pallas import tpu as pltpu
from jax.sharding import Mesh, PartitionSpec as P

HEAD_SIZE = 64
KV_HEADS = 8
EPS = 1e-05
ROPE_BASE = 500000.0
NEG_FILL = -1e30
BF = jnp.bfloat16
F32 = jnp.float32
CUBE = ("wd", "tensor")


def rms_scale(row_values):
    return lax.rsqrt(jnp.mean(row_values * row_values, axis=-1, keepdims=True) + EPS)


def apply_norm(row_values, gain_vector):
    return row_values * rms_scale(row_values) * gain_vector


def norm_back(row_values, gain_vector, grad_normed):
    _, pullback = jax.vjp(apply_norm, row_values, gain_vector)
    return pullback(grad_normed)


def doc_starts(seg_row):
    places = jnp.arange(seg_row.shape[0], dtype=jnp.int32)
    before = jnp.concatenate([seg_row[:1] - 1, seg_row[:-1]])
    return lax.cummax(jnp.where(seg_row != before, places, 0), axis=0)


def rope_tables(positions):
    half_dim = HEAD_SIZE // 2
    freqs = ROPE_BASE ** (-(jnp.arange(half_dim, dtype=F32) * 2.0 / HEAD_SIZE))
    angles = positions.astype(F32)[:, None] * freqs[None, :]
    return (jnp.cos(angles), jnp.sin(angles))


def rotary_apply(head_values, cosine_table, sine_values):
    half_dim = head_values.shape[-1] // 2
    first_half = head_values[..., :half_dim]
    second_half = head_values[..., half_dim:]
    cos_rows = cosine_table[:, None, :]
    sin_rows = sine_values[:, None, :]
    return jnp.concatenate(
        [
            first_half * cos_rows - second_half * sin_rows,
            second_half * cos_rows + first_half * sin_rows,
        ],
        axis=-1,
    )


def mm(left, right):
    return jnp.dot(left, right, preferred_element_type=F32)


def mm_t(left, right):
    return lax.dot_general(left, right, (((1,), (1,)), ((), ())), preferred_element_type=F32)


def mm_tl(left, right):
    return lax.dot_general(left, right, (((0,), (0,)), ((), ())), preferred_element_type=F32)


def trade(blocks, axes):
    return lax.all_to_all(blocks, axes, 0, 0, tiled=True)


def hop(block, axis, step):
    size = lax.axis_size(axis)
    return lax.ppermute(block, axis, [(i, i ^ step) for i in range(size)])


def tie(*values):
    return lax.optimization_barrier(values)


def link_steps():
    steps = []
    step = 1
    while step < lax.axis_size(CUBE):
        steps.append(step)
        step *= 2
    return steps


FAR, NEAR, SIDE = 4, 2, 1
ROW_ORDER = (0, FAR, NEAR, FAR | NEAR, SIDE, FAR | SIDE, NEAR | SIDE, FAR | NEAR | SIDE)


def cube(block, step):
    return hop(block, CUBE, step)


def join_kernel(left_ref, left_came_ref, right_ref, right_came_ref, out_ref):
    half = left_ref.shape[1]
    block = pl.program_id(0)

    @pl.when(block < 2)
    def _():
        out_ref[:, :half] = left_ref[...]

    @pl.when(block >= 2)
    def _():
        out_ref[:, :half] = left_came_ref[...]

    @pl.when(block % 2 == 0)
    def _():
        out_ref[:, half:] = right_ref[...]

    @pl.when(block % 2 == 1)
    def _():
        out_ref[:, half:] = right_came_ref[...]


def join_halves(left, left_came, right, right_came):
    rows, half = left.shape[0] // 2, left.shape[1]

    def spec(place):
        return pl.BlockSpec((rows, half), lambda i: (place(i), 0))

    return pl.pallas_call(
        join_kernel,
        grid=(4,),
        in_specs=[
            spec(lambda i: jnp.minimum(i, 1)),
            spec(lambda i: jnp.maximum(i - 2, 0)),
            spec(lambda i: i // 2),
            spec(lambda i: i // 2),
        ],
        out_specs=pl.BlockSpec((rows, 2 * half), lambda i: (i, 0)),
        out_shape=jax.ShapeDtypeStruct((4 * rows, 2 * half), left.dtype),
        cost_estimate=pl.CostEstimate(
            flops=0, bytes_accessed=32 * rows * half, transcendentals=0
        ),
    )(left, left_came, right, right_came)


def gather_rows(rows):
    two = jnp.concatenate([rows, cube(rows, FAR)], axis=0)
    half = two.shape[1] // 2
    left, right = two[:, :half], two[:, half:]
    left_came, right_came = cube(left, NEAR), cube(right, SIDE)
    left = jnp.concatenate([left, left_came], axis=0)
    right = jnp.concatenate([right, right_came], axis=0)
    return join_halves(left, cube(left, SIDE), right, cube(right, NEAR))


def sum_rows(partial):
    partial = partial.astype(BF)
    n, half = partial.shape[0] // 4, partial.shape[1] // 2
    left, right = partial[:, :half], partial[:, half:]
    left_came = cube(left[2 * n :], SIDE)
    right_came = cube(jnp.concatenate([right[n : 2 * n], right[3 * n :]], axis=0), NEAR)
    left = left[: 2 * n].astype(F32) + left_came.astype(F32)
    right_came = right_came.astype(F32)
    low = right[:n].astype(F32) + right_came[:n]
    high = right[2 * n : 3 * n].astype(F32) + right_came[n:]
    left_came = cube(left[n:].astype(BF), NEAR)
    right_came = cube(high.astype(BF), SIDE)
    left = left[:n] + left_came.astype(F32)
    right = low + right_came.astype(F32)
    both = jnp.concatenate([left, right], axis=1)
    rows = n // 2
    return both[:rows] + cube(both[rows:].astype(BF), FAR).astype(F32)


class Stages:
    def __init__(self):
        self.held = {}
        self.then = {}

    def run(self, value, step, jobs, settle=()):
        needed = [[self.held[name] for name in job[2]] for job in jobs]
        value, needed = lax.optimization_barrier((value, needed))
        out = step(value)
        made = [job[1](*inputs) for job, inputs in zip(jobs, needed)]
        due = [m for m, job in zip(made, jobs) if len(job) == 3]
        ready = [self.held[key] for key in settle]
        out, due, ready = lax.optimization_barrier((out, due, ready))
        self.held.update(zip(settle, ready))
        for job, result in zip(jobs, made):
            self.held[job[0]] = due.pop(0) if len(job) == 3 else result
            if job[0] in self.then:
                self.then[job[0]](job[0])
        return out


def others(block, axis):
    return [block] + [hop(block, axis, k) for k in range(1, lax.axis_size(axis))]


def sum_others(blocks, axis):
    total = blocks[0].astype(F32)
    for k in range(1, lax.axis_size(axis)):
        total = total + hop(blocks[k].astype(BF), axis, k).astype(F32)
    return total


def relative(values, dim, axis):
    count = lax.axis_size(axis)
    me = lax.axis_index(axis)
    step = 1
    while step < count:
        shape = values.shape
        cut = shape[:dim] + (count // (2 * step), 2, step * (shape[dim] // count)) + shape[dim + 1 :]
        view = values.reshape(cut)
        swapped = jnp.concatenate(
            [lax.slice_in_dim(view, 1, 2, axis=dim + 1), lax.slice_in_dim(view, 0, 1, axis=dim + 1)],
            axis=dim + 1,
        )
        values = jnp.where((me & step) != 0, swapped.reshape(shape), values)
        step *= 2
    return values


def spread_gains(norm_gains):
    me = lax.axis_index(CUBE)
    gain = norm_gains
    for step in link_steps():
        came = hop(gain, CUBE, step)
        gain = jnp.where(
            (me & step) != 0,
            jnp.concatenate([came, gain], axis=1),
            jnp.concatenate([gain, came], axis=1),
        )
    gain = relative(jnp.concatenate(others(gain, "grp"), axis=1), 1, "grp")
    other = hop(gain, "pipe", 1)
    core = lax.axis_index("pipe")
    return [jnp.where(core == 0, gain, other), jnp.where(core == 0, other, gain)]


def sum_gains(grads):
    me = lax.axis_index(CUBE)
    keep, extra = own_layer(grads[0], grads[1])
    count = lax.axis_size("grp")
    total = relative((keep + extra).reshape(2, count, -1), 1, "grp")
    mine = total[:, 0]
    for k in range(1, count):
        mine = mine + hop(total[:, k], "grp", k)
    for step in link_steps()[::-1]:
        half = mine.shape[1] // 2
        low, high = mine[:, :half], mine[:, half:]
        odd = (me & step) != 0
        mine = jnp.where(odd, high, low) + hop(jnp.where(odd, low, high), CUBE, step)
    return mine


def masked_probs(q, k, q_place, q_start, k_place):
    scores = lax.dot_general(q, k, (((1,), (1,)), ((), ())), preferred_element_type=F32)
    scores = scores * HEAD_SIZE ** (-0.5)
    allowed = (k_place <= q_place) & (k_place >= q_start)
    masked = jnp.where(allowed, scores, NEG_FILL)
    exps = jnp.exp(masked - jnp.max(masked, axis=-1, keepdims=True))
    return exps / jnp.sum(exps, axis=-1, keepdims=True)


def attend_kernel(q_ref, k_ref, v_ref, qp_ref, qs_ref, kp_ref, o_ref):
    probs = masked_probs(q_ref[0], k_ref[...], qp_ref[...], qs_ref[...], kp_ref[...])
    o_ref[0] = jnp.dot(probs.astype(BF), v_ref[...], preferred_element_type=F32).astype(BF)


def attend_back_kernel(q_ref, do_ref, k_ref, v_ref, qp_ref, qs_ref, kp_ref, dq_ref, dk_ref, dv_ref):
    @pl.when((pl.program_id(0) == 0) & (pl.program_id(1) == 0))
    def _():
        dk_ref[...] = jnp.zeros_like(dk_ref)
        dv_ref[...] = jnp.zeros_like(dv_ref)

    q = q_ref[0]
    do = do_ref[0]
    k = k_ref[...]
    probs = masked_probs(q, k, qp_ref[...], qs_ref[...], kp_ref[...])
    grad_probs = lax.dot_general(do, v_ref[...], (((1,), (1,)), ((), ())), preferred_element_type=F32)
    delta = jnp.sum(probs * grad_probs, axis=-1, keepdims=True)
    grad_scores = (probs * (grad_probs - delta) * HEAD_SIZE ** (-0.5)).astype(BF)
    dq_ref[0] = jnp.dot(grad_scores, k, preferred_element_type=F32).astype(BF)
    dk_ref[...] += lax.dot_general(
        grad_scores, q, (((0,), (0,)), ((), ())), preferred_element_type=F32
    )
    dv_ref[...] += lax.dot_general(
        probs.astype(BF), do, (((0,), (0,)), ((), ())), preferred_element_type=F32
    )


def attention_specs(heads, rows, keys):
    rows_blk = max(16, min(rows, (512 * 1024) // keys))
    per_head = pl.BlockSpec((1, rows_blk, HEAD_SIZE), lambda b, h: (h, b, 0))
    full = pl.BlockSpec((keys, HEAD_SIZE), lambda b, h: (0, 0))
    row_info = pl.BlockSpec((rows_blk, 1), lambda b, h: (b, 0))
    key_info = pl.BlockSpec((1, keys), lambda b, h: (0, 0))
    return ((rows // rows_blk, heads), per_head, full, row_info, key_info)


PARAMS = dict(
    compiler_params=pltpu.CompilerParams(vmem_limit_bytes=50 * 1024 * 1024),
)


def attend(q, k, v, q_place, q_start, k_place):
    heads, rows, _ = q.shape
    keys = k.shape[0]
    grid, per_head, full, row_info, key_info = attention_specs(heads, rows, keys)
    return pl.pallas_call(
        attend_kernel,
        grid=grid,
        in_specs=[per_head, full, full, row_info, row_info, key_info],
        out_specs=per_head,
        out_shape=jax.ShapeDtypeStruct(q.shape, BF),
        cost_estimate=pl.CostEstimate(
            flops=4 * heads * rows * keys * HEAD_SIZE,
            bytes_accessed=4 * q.size + 4 * k.size,
            transcendentals=heads * rows * keys,
        ),
        **PARAMS,
    )(q, k, v, q_place, q_start, k_place)


def attend_back(q, do, k, v, q_place, q_start, k_place):
    heads, rows, _ = q.shape
    keys = k.shape[0]
    grid, per_head, full, row_info, key_info = attention_specs(heads, rows, keys)
    return pl.pallas_call(
        attend_back_kernel,
        grid=grid,
        in_specs=[per_head, per_head, full, full, row_info, row_info, key_info],
        out_specs=[per_head, full, full],
        out_shape=[
            jax.ShapeDtypeStruct(q.shape, BF),
            jax.ShapeDtypeStruct(k.shape, F32),
            jax.ShapeDtypeStruct(k.shape, F32),
        ],
        cost_estimate=pl.CostEstimate(
            flops=10 * heads * rows * keys * HEAD_SIZE,
            bytes_accessed=6 * q.size + 12 * k.size,
            transcendentals=heads * rows * keys,
        ),
        **PARAMS,
    )(q, do, k, v, q_place, q_start, k_place)


def to_blocks(weight, cores):
    wd = lax.axis_size("wd")
    rows = weight.shape[0]
    cut = weight.reshape(rows, wd, cores, -1).transpose(2, 1, 0, 3)
    return cut.reshape((cores * wd, rows) + cut.shape[3:])


def columns_out(blocks):
    moved = trade(blocks, ("pipe", "wd"))
    return moved.reshape((2, -1) + moved.shape[2:])


def put_kernel(spots, *refs):
    pieces, out = refs[: len(spots)], refs[len(spots)]
    block = pl.program_id(0)
    for piece, (first, count, col, cols) in zip(pieces, spots):

        def put(piece=piece, col=col, cols=cols):
            out[:, col : col + cols] = piece[...]

        pl.when((block >= first) & (block < first + count))(put)


def put_together(columns):
    block = min([256] + [piece.shape[0] for stack in columns for piece in stack])
    spots, pieces, specs = [], [], []
    col = 0
    for stack in columns:
        first = 0
        for piece in stack:
            count, cols = piece.shape[0] // block, piece.shape[1]
            spots.append((first, count, col, cols))
            pieces.append(piece)

            def at(i, first=first, count=count):
                return (jnp.clip(i - first, 0, count - 1), 0)

            specs.append(pl.BlockSpec((block, cols), at))
            first += count
        col += cols
    return pl.pallas_call(
        lambda *refs: put_kernel(spots, *refs),
        grid=(first,),
        in_specs=specs,
        out_specs=pl.BlockSpec((block, col), lambda i: (i, 0)),
        out_shape=jax.ShapeDtypeStruct((first * block, col), BF),
        cost_estimate=pl.CostEstimate(
            flops=0, bytes_accessed=4 * first * block * col, transcendentals=0
        ),
        **PARAMS,
    )(*pieces)


def pack_attention(w_query, key_matrix, value_matrix, w_output, cores):
    wd = lax.axis_size("wd")
    rows = w_query.shape[0]
    cut = [w_query.reshape(rows, wd, cores, -1)]
    for m in (key_matrix, value_matrix):
        m = m.reshape(rows, wd, 1, -1)
        cut.append(jnp.broadcast_to(m, (rows, wd, cores, m.shape[3])))
    cut.append(w_output.T.reshape(rows, wd, cores, -1))
    return jnp.concatenate(cut, axis=-1).reshape(rows, -1)


def unpack_attention(own, widths):
    other = hop(own, "pipe", 1)
    query_w, kv_w, out_w = widths
    cuts = (query_w, query_w + kv_w, query_w + 2 * kv_w)
    return (
        jnp.concatenate([own[:, : cuts[0]], other[:, : cuts[0]]], axis=1),
        own[:, cuts[0] : cuts[1]],
        own[:, cuts[1] : cuts[2]],
        jnp.concatenate([own[:, cuts[2] :], other[:, cuts[2] :]], axis=1),
    )


def grad_pair(own, other):
    return (own + hop(other.astype(BF), "pipe", 1).astype(F32)).astype(BF)


def mlp_pair(left, right):
    half = right.shape[1] // 2
    return grad_pair(mm_tl(left, right[:, :half]), mm_tl(left, right[:, half:]))


def grad_group(total):
    return lax.psum_scatter(total, "grp", scatter_dimension=0, tiled=True)


def grad_home(total):
    return trade(total.reshape((lax.axis_size("wd"), -1) + total.shape[1:]), "wd")


def place_kernel(turned, at_ref, keep_ref, got_ref, out_ref):
    mine = pl.program_id(1) == at_ref[0]

    def put(ref):
        block = ref[0].astype(F32)
        out_ref[...] = block.T if turned else block

    @pl.when(mine)
    def _():
        put(keep_ref)

    @pl.when(jnp.logical_not(mine))
    def _():
        put(got_ref)


def place(keep, got, turned):
    wd, rows, cols = keep.shape
    at = lax.axis_index("pipe").astype(jnp.int32)[None]
    cores = lax.axis_size("pipe")
    source = pl.BlockSpec((1, rows, cols), lambda w, c, at_ref: (w, 0, 0))
    if turned:
        shape, target = (wd * cores * cols, rows), (cols, rows)
        out = pl.BlockSpec(target, lambda w, c, at_ref: (w * cores + c, 0))
    else:
        shape, target = (rows, wd * cores * cols), (rows, cols)
        out = pl.BlockSpec(target, lambda w, c, at_ref: (0, w * cores + c))
    return pl.pallas_call(
        lambda *refs: place_kernel(turned, *refs),
        grid_spec=pltpu.PrefetchScalarGridSpec(
            num_scalar_prefetch=1, grid=(wd, cores), in_specs=[source, source], out_specs=out
        ),
        out_shape=jax.ShapeDtypeStruct(shape, F32),
        cost_estimate=pl.CostEstimate(
            flops=keep.size, bytes_accessed=12 * keep.size, transcendentals=0
        ),
    )(at, keep, got)


def layer_forward(stages, layer, x_rows, gains, where, build, jobs, settle):
    held = stages.held
    cosine, sine, q_place, q_start, k_place = where
    normed = apply_norm(x_rows, gains[0]).astype(BF)
    rows_a = stages.run(normed, gather_rows, jobs[0], settle[0])
    held["attn", layer] = build("attn", layer)
    w_q, w_k, w_v, w_ot = held["attn", layer]
    tok = rows_a.shape[0]

    def project(rows):
        key = rotary_apply(mm(rows, w_k).reshape(tok, 1, HEAD_SIZE), cosine, sine).astype(BF)[:, 0]
        value = mm(rows, w_v).astype(BF)
        return jnp.concatenate([key, value], axis=1)

    def queries(rows):
        query = rotary_apply(mm(rows, w_q).reshape(tok, -1, HEAD_SIZE), cosine, sine).astype(BF)
        return query.transpose(1, 0, 2)

    held["rows_a"] = rows_a
    kv_all = stages.run(
        project(rows_a),
        lambda kv: jnp.concatenate(others(kv, "grp"), axis=0),
        [("query", queries, ("rows_a",))] + jobs[1],
        settle[1],
    )
    query = held["query"]
    keys, values = kv_all[:, :HEAD_SIZE], kv_all[:, HEAD_SIZE:]

    def attention(q):
        context = attend(q, keys, values, q_place, q_start, k_place)
        context = context.transpose(1, 0, 2).reshape(tok, -1)
        return context, mm_t(context, w_ot).astype(BF)

    context, partial = stages.run(query, attention, jobs[2], settle[2])
    mid = stages.run(partial, lambda p: x_rows + sum_rows(p), jobs[3], settle[3])
    rows_b = stages.run(
        mid, lambda m: gather_rows(apply_norm(m, gains[1]).astype(BF)), jobs[4], settle[4]
    )
    held["gu", layer] = w_gu = build("gu", layer)

    def ahead(rows):
        both = mm(rows, w_gu)
        half = both.shape[1] // 2
        gate, up = both[:, :half], both[:, half:]
        return gate, up, (jax.nn.silu(gate) * up).astype(BF)

    gate, up, hidden = stages.run(rows_b, ahead, jobs[5], settle[5])
    held["down", layer] = build("down", layer)
    return x_rows, rows_a, query, keys, values, context, mid, rows_b, gate, up, hidden


def layer_backward(
    stages, layer, grad_out, grad_mlp, gains, where, kept, also, jobs, settle
):
    held = stages.held
    cosine, sine, q_place, q_start, k_place = where
    x_rows, rows_a, query, keys, values, context, mid, rows_b, gate, up, hidden = kept
    w_q, w_k, w_v, w_ot = held["attn", layer]
    w_gu, w_dt = held["gu", layer], held["down", layer]
    tok = rows_a.shape[0]
    held["rows_b"], held["hidden"], held["grad_mlp"] = rows_b, hidden, grad_mlp

    def feed_back(rows):
        grad_hidden = mm(rows, w_dt)
        sig = jax.nn.sigmoid(gate)
        grad_gate = (grad_hidden * up * sig * (1.0 + gate * (1.0 - sig))).astype(BF)
        grad_up = (grad_hidden * gate * sig).astype(BF)
        both = jnp.concatenate([grad_gate, grad_up], axis=1)
        return grad_gate, grad_up, mm_t(both, w_gu).astype(BF), also(hidden)

    grad_gate, grad_up, partial, extra = stages.run(grad_mlp, feed_back, jobs[0], settle[0])
    held["grad_gate"], held["grad_up"] = grad_gate, grad_up
    grad_b = stages.run(partial, sum_rows, jobs[1], settle[1])
    grad_mid, gain_b = norm_back(mid, gains[1], grad_b)
    grad_mid = grad_mid + grad_out
    grad_attn = stages.run(grad_mid.astype(BF), gather_rows, jobs[2], settle[2])

    def attention_back(rows):
        grad_context = mm(rows, w_ot).astype(BF)
        grad_context = grad_context.reshape(tok, -1, HEAD_SIZE).transpose(1, 0, 2)
        return attend_back(query, grad_context, keys, values, q_place, q_start, k_place)

    def keys_back(grads):
        kv = jnp.concatenate(grads, axis=1)
        kv = kv.reshape((-1, tok) + kv.shape[1:])
        return sum_others([kv[k] for k in range(kv.shape[0])], "grp").astype(BF)

    def queries_back(grad_q):
        grad_q = grad_q.transpose(1, 0, 2).astype(F32)
        grad_q = rotary_apply(grad_q, cosine, -sine).astype(BF).reshape(tok, -1)
        return grad_q, mm_t(grad_q, w_q)

    held["grad_q"], *grads = stages.run(grad_attn, attention_back, jobs[3])
    own_kv = stages.run(
        grads, keys_back, [("g_q", queries_back, ("grad_q",))] + jobs[4], settle[4]
    )
    grad_q, partial = held["g_q"]
    grad_k = own_kv[:, :HEAD_SIZE].astype(F32)
    grad_k = rotary_apply(grad_k[:, None, :], cosine, -sine).astype(BF)[:, 0]
    grad_v = own_kv[:, HEAD_SIZE:]
    partial = (partial + mm_t(grad_k, w_k) + mm_t(grad_v, w_v)).astype(BF)

    def attn_pair(g_q, g_k, g_v):
        half_q = g_q.shape[1] // 2

        def term(cut):
            right = jnp.concatenate([g_q[:, cut], g_k, g_v], axis=1)
            left = [mm_tl(rows_a, right), mm_tl(grad_attn, context[:, cut])]
            return jnp.concatenate(left, axis=1)

        return grad_pair(term(slice(0, half_q)), term(slice(half_q, None)))

    held["g_q"], held["g_k"], held["g_v"] = grad_q, grad_k, grad_v
    grad_a = stages.run(partial, sum_rows, jobs[5](attn_pair), settle[5])
    grad_in, gain_a = norm_back(x_rows, gains[0], grad_a)
    return grad_mid + grad_in, jnp.stack([gain_a, gain_b]), extra


def own_layer(first, second):
    core = lax.axis_index("pipe")
    keep = jnp.where(core == 0, first, second)
    return keep, hop(jnp.where(core == 0, second, first), "pipe", 1)


def body(
    block_input,
    cotangent,
    segments,
    norm_gains,
    w_query,
    key_matrix,
    value_matrix,
    w_output,
    w_gate,
    w_up,
    w_down,
):
    core = lax.axis_index("pipe")
    grp = lax.axis_index("grp")
    wd = lax.axis_size("wd")
    groups = lax.axis_size("grp")
    cores = lax.axis_size("pipe")
    tok = block_input.shape[1] * lax.axis_size(CUBE)

    stages = Stages()
    held = stages.held
    packed = pack_attention(w_query[0], key_matrix[0], value_matrix[0], w_output[0], cores)
    gains = spread_gains(norm_gains[0])
    packed, gains = lax.optimization_barrier((packed, gains))
    attn_cols = columns_out(to_blocks(packed, cores))
    held["gate_out"] = to_blocks(w_gate[0], cores)
    held["up_out"] = to_blocks(w_up[0], cores)
    held["down_out"] = to_blocks(w_down[0].T, cores)
    query_w, out_w = w_query.shape[2] // (wd * cores), w_output.shape[1] // (wd * cores)
    widths = (query_w, key_matrix.shape[2] // wd, out_w)

    def move(name):
        return (name, columns_out, (name + "_out",), "later")

    def rows_of(name, layer):
        return lax.all_gather(held[name][layer], "grp", axis=0, tiled=True)

    def put(*names):
        return put_together([[m] for n in names for m in (held[n], hop(held[n], "pipe", 1))])

    def build(kind, layer):
        if kind == "attn":
            return unpack_attention(held["own", "attn", layer], widths)
        if kind == "gu":
            return put(("own", "gate", layer), ("own", "up", layer))
        return put(("own", "down", layer))

    held["attn"] = attn_cols
    for layer in range(2):
        held["own", "attn", layer] = rows_of("attn", layer)

    def start(name):
        for layer in range(2):
            held["own", name, layer] = rows_of(name, layer)

    stages.then.update(gate=start, up=start, down=start)

    seg_row = lax.dynamic_index_in_dim(segments, core, 0, keepdims=False)
    starts = doc_starts(seg_row)
    rows_own = tok // lax.axis_size(CUBE)

    def in_row_order(values):
        values = relative(values, 0, CUBE)
        return jnp.concatenate(
            [values[j * rows_own : (j + 1) * rows_own] for j in ROW_ORDER], axis=0
        )

    local = in_row_order(jnp.arange(tok, dtype=jnp.int32))
    q_place = grp * tok + local
    q_start = in_row_order(lax.dynamic_slice_in_dim(starts, grp * tok, tok))
    cosine, sine = rope_tables(q_place - q_start)
    k_place = jnp.concatenate([(grp ^ k) * tok + local for k in range(groups)])
    where = (cosine, sine, q_place[:, None], q_start[:, None], k_place[None, :])

    rows = lax.dynamic_index_in_dim(block_input, core, 0, keepdims=False)
    grad = lax.dynamic_index_in_dim(cotangent, core, 0, keepdims=False)
    held["cotangent"] = grad
    kept = [None, None]
    outs = [None, None]
    kept[0] = layer_forward(
        stages,
        0,
        rows.astype(F32),
        gains[0],
        where,
        build,
        [[], [move("gate")], [move("up")], [move("down")], [], []],
        [
            (),
            (("own", "attn", 1),),
            (("own", "gate", 0),),
            (("own", "up", 0),),
            (("own", "down", 0),),
            (),
        ],
    )

    def close(hidden, layer):
        return (kept[layer][6] + sum_rows(mm_t(hidden, held["down", layer]))).astype(BF)

    outs[0] = stages.run(
        kept[0][-1], lambda h: close(h, 0), [], (("own", "gate", 1),)
    )
    kept[1] = layer_forward(
        stages,
        1,
        outs[0].astype(F32),
        gains[1],
        where,
        build,
        [[], [], [("last", gather_rows, ("cotangent",))], [], [], []],
        [(("own", "up", 1),), (), (("own", "down", 1),), (), (), ()],
    )

    def grad_of(name, layer):
        sources = {
            "down": ("grad_mlp", "hidden"),
            "gate": ("rows_b", "grad_gate"),
            "up": ("rows_b", "grad_up"),
        }[name]
        return (("pair", name, layer), mlp_pair, sources)

    def group_sum(name, layer):
        return (("sum", name, layer), grad_group, (("pair", name, layer),), "later")

    def home(name, layer):
        return (("home", name, layer), grad_home, (("sum", name, layer),), "later")

    def attn_grad(layer):
        return lambda pair: (("pair", "attn", layer), pair, ("g_q", "g_k", "g_v"))

    def final(name, turned):
        def ready(first, second):
            return place(*own_layer(first, second), turned)

        return (("final", name), ready, (("home", name, 0), ("home", name, 1)))

    held["hidden"], held["grad_mlp"] = kept[1][-1], held["last"]
    hidden = stages.run(kept[1][-1], lambda h: h, [grad_of("down", 1)])

    grads_in = [None, None]
    gain_grads = [None, None]
    grad_in, gain_grads[1], outs[1] = layer_backward(
        stages,
        1,
        grad.astype(F32),
        held["last"],
        gains[1],
        where,
        kept[1][:-1] + (hidden,),
        lambda h: close(h, 1),
        (
            [],
            [group_sum("down", 1), grad_of("gate", 1)],
            [group_sum("gate", 1), grad_of("up", 1)],
            [group_sum("up", 1)],
            [home("down", 1)],
            lambda pair: [attn_grad(1)(pair)],
        ),
        [(), (), (), (), (), (("sum", "gate", 1), ("home", "down", 1))],
    )
    grads_in[1] = grad_in.astype(BF)
    grad_mlp = stages.run(grads_in[1], gather_rows, [group_sum("attn", 1)], (("sum", "up", 1),))
    grad_in, gain_grads[0], _ = layer_backward(
        stages,
        0,
        grads_in[1].astype(F32),
        grad_mlp,
        gains[0],
        where,
        kept[0],
        lambda h: (),
        (
            [grad_of("down", 0), home("gate", 1)],
            [group_sum("down", 0), grad_of("gate", 0), home("up", 1)],
            [group_sum("gate", 0), grad_of("up", 0), home("attn", 1)],
            [group_sum("up", 0)],
            [home("down", 0)],
            lambda pair: [attn_grad(0)(pair)],
        ),
        [
            (),
            (("sum", "attn", 1), ("home", "gate", 1)),
            (("sum", "down", 0), ("home", "up", 1)),
            (),
            (("sum", "gate", 0), ("home", "attn", 1)),
            (("sum", "up", 0), ("home", "down", 0)),
        ],
    )
    grads_in[0] = grad_in.astype(BF)
    for key, job, names, *_ in (
        group_sum("attn", 0),
        home("gate", 0),
        final("down", True),
        final("gate", False),
        home("up", 0),
        final("up", False),
    ):
        held[key] = job(*[held[name] for name in names])
    keys = (("sum", "attn", 0),) + tuple(("final", name) for name in ("down", "gate", "up"))
    held.update(zip(keys, lax.optimization_barrier([held[key] for key in keys])))
    key, job, *_ = home("attn", 0)
    held[key] = job(held["sum", "attn", 0])

    def by_batch(pair):
        own, other = own_layer(pair[0], pair[1])
        both = jnp.where(core == 0, jnp.stack([own, other]), jnp.stack([other, own]))
        return both[None]

    layer_out = by_batch(outs)
    input_grad = by_batch(grads_in)

    grad_norm_gains = sum_gains(gain_grads)[None]

    def both(name):
        return own_layer(held["home", name, 0], held["home", name, 1])

    keep, got = both("attn")
    cuts = (0, widths[0], widths[0] + widths[1], widths[0] + 2 * widths[1], keep.shape[2])
    q_pair, k_pair, v_pair, o_pair = (
        (keep[..., lo:hi], got[..., lo:hi]) for lo, hi in zip(cuts[:-1], cuts[1:])
    )

    def small(pair):
        order = pair[0].transpose(1, 0, 2).astype(F32)
        return order.reshape(order.shape[0], -1)[None]

    grad_wq = place(*q_pair, False)[None]
    grad_wk = small(k_pair)
    grad_wv = small(v_pair)
    grad_wo = place(*o_pair, True)[None]
    grad_wg = held["final", "gate"][None]
    grad_wu = held["final", "up"][None]
    grad_wd = held["final", "down"][None]
    return (
        layer_out,
        input_grad,
        grad_norm_gains,
        grad_wq,
        grad_wk,
        grad_wv,
        grad_wo,
        grad_wg,
        grad_wu,
        grad_wd,
    )


def solution(mesh):
    sizes = dict(mesh.shape)
    wd = KV_HEADS // sizes["tensor"]
    fine = Mesh(
        mesh.devices.reshape(sizes["pipe"], sizes["dp"] // wd, wd, sizes["tensor"]),
        ("pipe", "grp", "wd", "tensor"),
    )
    dp = ("grp", "wd")
    tokens = P(None, dp + ("tensor",), None)
    outs = P("pipe", None, dp + ("tensor",), None)
    gains = P("pipe", None, dp + ("tensor",))
    tall = P("pipe", dp, "tensor")
    wide = P("pipe", "tensor", dp)
    weights = (tall, tall, tall, wide, tall, tall, wide)
    return jax.shard_map(
        body,
        mesh=fine,
        in_specs=(tokens, tokens, P(), gains) + weights,
        out_specs=(outs, outs, gains) + weights,
        check_vma=False,
    )
```

```python
import jax
import jax.numpy as jnp
from jax import lax
from jax.experimental import pallas as pl
from jax.experimental.pallas import tpu as pltpu
from jax.sharding import Mesh, PartitionSpec as P

HEAD_SIZE = 64
KV_HEADS = 8
EPS = 1e-05
ROPE_BASE = 500000.0
NEG_FILL = -1e30
BF = jnp.bfloat16
F32 = jnp.float32
CUBE = ("wd", "tensor")


def rms_scale(row_values):
    return lax.rsqrt(jnp.mean(row_values * row_values, axis=-1, keepdims=True) + EPS)


def apply_norm(row_values, gain_vector):
    return row_values * rms_scale(row_values) * gain_vector


def norm_back(row_values, gain_vector, grad_normed):
    _, pullback = jax.vjp(apply_norm, row_values, gain_vector)
    return pullback(grad_normed)


def doc_starts(seg_row):
    places = jnp.arange(seg_row.shape[0], dtype=jnp.int32)
    before = jnp.concatenate([seg_row[:1] - 1, seg_row[:-1]])
    return lax.cummax(jnp.where(seg_row != before, places, 0), axis=0)


def rope_tables(positions):
    half_dim = HEAD_SIZE // 2
    freqs = ROPE_BASE ** (-(jnp.arange(half_dim, dtype=F32) * 2.0 / HEAD_SIZE))
    angles = positions.astype(F32)[:, None] * freqs[None, :]
    return (jnp.cos(angles), jnp.sin(angles))


def rotary_apply(head_values, cosine_table, sine_values):
    half_dim = head_values.shape[-1] // 2
    first_half = head_values[..., :half_dim]
    second_half = head_values[..., half_dim:]
    cos_rows = cosine_table[:, None, :]
    sin_rows = sine_values[:, None, :]
    return jnp.concatenate(
        [
            first_half * cos_rows - second_half * sin_rows,
            second_half * cos_rows + first_half * sin_rows,
        ],
        axis=-1,
    )


def mm(left, right):
    return jnp.dot(left, right, preferred_element_type=F32)


def mm_t(left, right):
    return lax.dot_general(left, right, (((1,), (1,)), ((), ())), preferred_element_type=F32)


def mm_tl(left, right):
    return lax.dot_general(left, right, (((0,), (0,)), ((), ())), preferred_element_type=F32)


def trade(blocks, axes):
    return lax.all_to_all(blocks, axes, 0, 0, tiled=True)


def hop(block, axis, step):
    size = lax.axis_size(axis)
    return lax.ppermute(block, axis, [(i, i ^ step) for i in range(size)])


def tie(*values):
    return lax.optimization_barrier(values)


def link_steps():
    steps = []
    step = 1
    while step < lax.axis_size(CUBE):
        steps.append(step)
        step *= 2
    return steps


FAR, NEAR, SIDE = 4, 2, 1
ROW_ORDER = (0, FAR, NEAR, FAR | NEAR, SIDE, FAR | SIDE, NEAR | SIDE, FAR | NEAR | SIDE)


def cube(block, step):
    return hop(block, CUBE, step)


def join_kernel(left_ref, left_came_ref, right_ref, right_came_ref, out_ref):
    half = left_ref.shape[1]
    block = pl.program_id(0)

    @pl.when(block < 2)
    def _():
        out_ref[:, :half] = left_ref[...]

    @pl.when(block >= 2)
    def _():
        out_ref[:, :half] = left_came_ref[...]

    @pl.when(block % 2 == 0)
    def _():
        out_ref[:, half:] = right_ref[...]

    @pl.when(block % 2 == 1)
    def _():
        out_ref[:, half:] = right_came_ref[...]


def join_halves(left, left_came, right, right_came):
    rows, half = left.shape[0] // 2, left.shape[1]

    def spec(place):
        return pl.BlockSpec((rows, half), lambda i: (place(i), 0))

    return pl.pallas_call(
        join_kernel,
        grid=(4,),
        in_specs=[
            spec(lambda i: jnp.minimum(i, 1)),
            spec(lambda i: jnp.maximum(i - 2, 0)),
            spec(lambda i: i // 2),
            spec(lambda i: i // 2),
        ],
        out_specs=pl.BlockSpec((rows, 2 * half), lambda i: (i, 0)),
        out_shape=jax.ShapeDtypeStruct((4 * rows, 2 * half), left.dtype),
        cost_estimate=pl.CostEstimate(
            flops=0, bytes_accessed=32 * rows * half, transcendentals=0
        ),
    )(left, left_came, right, right_came)


def gather_rows(rows):
    two = jnp.concatenate([rows, cube(rows, FAR)], axis=0)
    half = two.shape[1] // 2
    left, right = two[:, :half], two[:, half:]
    left_came, right_came = cube(left, NEAR), cube(right, SIDE)
    left = jnp.concatenate([left, left_came], axis=0)
    right = jnp.concatenate([right, right_came], axis=0)
    return join_halves(left, cube(left, SIDE), right, cube(right, NEAR))


def sum_rows(partial):
    partial = partial.astype(BF)
    n, half = partial.shape[0] // 4, partial.shape[1] // 2
    left, right = partial[:, :half], partial[:, half:]
    left_came = cube(left[2 * n :], SIDE)
    right_came = cube(jnp.concatenate([right[n : 2 * n], right[3 * n :]], axis=0), NEAR)
    left = left[: 2 * n].astype(F32) + left_came.astype(F32)
    right_came = right_came.astype(F32)
    low = right[:n].astype(F32) + right_came[:n]
    high = right[2 * n : 3 * n].astype(F32) + right_came[n:]
    left_came = cube(left[n:].astype(BF), NEAR)
    right_came = cube(high.astype(BF), SIDE)
    left = left[:n] + left_came.astype(F32)
    right = low + right_came.astype(F32)
    both = jnp.concatenate([left, right], axis=1)
    rows = n // 2
    return both[:rows] + cube(both[rows:].astype(BF), FAR).astype(F32)


class Stages:
    def __init__(self):
        self.held = {}
        self.then = {}

    def run(self, value, step, jobs, settle=()):
        needed = [[self.held[name] for name in job[2]] for job in jobs]
        value, needed = lax.optimization_barrier((value, needed))
        out = step(value)
        made = [job[1](*inputs) for job, inputs in zip(jobs, needed)]
        due = [m for m, job in zip(made, jobs) if len(job) == 3]
        ready = [self.held[key] for key in settle]
        out, due, ready = lax.optimization_barrier((out, due, ready))
        self.held.update(zip(settle, ready))
        for job, result in zip(jobs, made):
            self.held[job[0]] = due.pop(0) if len(job) == 3 else result
            if job[0] in self.then:
                self.then[job[0]](job[0])
        return out


def others(block, axis):
    return [block] + [hop(block, axis, k) for k in range(1, lax.axis_size(axis))]


def sum_others(blocks, axis):
    total = blocks[0].astype(F32)
    for k in range(1, lax.axis_size(axis)):
        total = total + hop(blocks[k].astype(BF), axis, k).astype(F32)
    return total


def relative(values, dim, axis):
    count = lax.axis_size(axis)
    me = lax.axis_index(axis)
    step = 1
    while step < count:
        shape = values.shape
        cut = shape[:dim] + (count // (2 * step), 2, step * (shape[dim] // count)) + shape[dim + 1 :]
        view = values.reshape(cut)
        swapped = jnp.concatenate(
            [lax.slice_in_dim(view, 1, 2, axis=dim + 1), lax.slice_in_dim(view, 0, 1, axis=dim + 1)],
            axis=dim + 1,
        )
        values = jnp.where((me & step) != 0, swapped.reshape(shape), values)
        step *= 2
    return values


def spread_gains(norm_gains):
    me = lax.axis_index(CUBE)
    gain = norm_gains
    for step in link_steps():
        came = hop(gain, CUBE, step)
        gain = jnp.where(
            (me & step) != 0,
            jnp.concatenate([came, gain], axis=1),
            jnp.concatenate([gain, came], axis=1),
        )
    gain = relative(jnp.concatenate(others(gain, "grp"), axis=1), 1, "grp")
    other = hop(gain, "pipe", 1)
    core = lax.axis_index("pipe")
    return [jnp.where(core == 0, gain, other), jnp.where(core == 0, other, gain)]


def sum_gains(grads):
    me = lax.axis_index(CUBE)
    keep, extra = own_layer(grads[0], grads[1])
    count = lax.axis_size("grp")
    total = relative((keep + extra).reshape(2, count, -1), 1, "grp")
    mine = total[:, 0]
    for k in range(1, count):
        mine = mine + hop(total[:, k], "grp", k)
    for step in link_steps()[::-1]:
        half = mine.shape[1] // 2
        low, high = mine[:, :half], mine[:, half:]
        odd = (me & step) != 0
        mine = jnp.where(odd, high, low) + hop(jnp.where(odd, low, high), CUBE, step)
    return mine


def masked_probs(q, k, q_place, q_start, k_place):
    scores = lax.dot_general(q, k, (((1,), (1,)), ((), ())), preferred_element_type=F32)
    scores = scores * HEAD_SIZE ** (-0.5)
    allowed = (k_place <= q_place) & (k_place >= q_start)
    masked = jnp.where(allowed, scores, NEG_FILL)
    exps = jnp.exp(masked - jnp.max(masked, axis=-1, keepdims=True))
    return exps / jnp.sum(exps, axis=-1, keepdims=True)


def attend_kernel(q_ref, k_ref, v_ref, qp_ref, qs_ref, kp_ref, o_ref):
    probs = masked_probs(q_ref[0], k_ref[...], qp_ref[...], qs_ref[...], kp_ref[...])
    o_ref[0] = jnp.dot(probs.astype(BF), v_ref[...], preferred_element_type=F32).astype(BF)


def attend_back_kernel(q_ref, do_ref, k_ref, v_ref, qp_ref, qs_ref, kp_ref, dq_ref, dk_ref, dv_ref):
    @pl.when((pl.program_id(0) == 0) & (pl.program_id(1) == 0))
    def _():
        dk_ref[...] = jnp.zeros_like(dk_ref)
        dv_ref[...] = jnp.zeros_like(dv_ref)

    q = q_ref[0]
    do = do_ref[0]
    k = k_ref[...]
    probs = masked_probs(q, k, qp_ref[...], qs_ref[...], kp_ref[...])
    grad_probs = lax.dot_general(do, v_ref[...], (((1,), (1,)), ((), ())), preferred_element_type=F32)
    delta = jnp.sum(probs * grad_probs, axis=-1, keepdims=True)
    grad_scores = (probs * (grad_probs - delta) * HEAD_SIZE ** (-0.5)).astype(BF)
    dq_ref[0] = jnp.dot(grad_scores, k, preferred_element_type=F32).astype(BF)
    dk_ref[...] += lax.dot_general(
        grad_scores, q, (((0,), (0,)), ((), ())), preferred_element_type=F32
    )
    dv_ref[...] += lax.dot_general(
        probs.astype(BF), do, (((0,), (0,)), ((), ())), preferred_element_type=F32
    )


def attention_specs(heads, rows, keys):
    rows_blk = max(16, min(rows, (512 * 1024) // keys))
    per_head = pl.BlockSpec((1, rows_blk, HEAD_SIZE), lambda b, h: (h, b, 0))
    full = pl.BlockSpec((keys, HEAD_SIZE), lambda b, h: (0, 0))
    row_info = pl.BlockSpec((rows_blk, 1), lambda b, h: (b, 0))
    key_info = pl.BlockSpec((1, keys), lambda b, h: (0, 0))
    return ((rows // rows_blk, heads), per_head, full, row_info, key_info)


PARAMS = dict(
    compiler_params=pltpu.CompilerParams(vmem_limit_bytes=50 * 1024 * 1024),
)


def attend(q, k, v, q_place, q_start, k_place):
    heads, rows, _ = q.shape
    keys = k.shape[0]
    grid, per_head, full, row_info, key_info = attention_specs(heads, rows, keys)
    return pl.pallas_call(
        attend_kernel,
        grid=grid,
        in_specs=[per_head, full, full, row_info, row_info, key_info],
        out_specs=per_head,
        out_shape=jax.ShapeDtypeStruct(q.shape, BF),
        cost_estimate=pl.CostEstimate(
            flops=4 * heads * rows * keys * HEAD_SIZE,
            bytes_accessed=4 * q.size + 4 * k.size,
            transcendentals=heads * rows * keys,
        ),
        **PARAMS,
    )(q, k, v, q_place, q_start, k_place)


def attend_back(q, do, k, v, q_place, q_start, k_place):
    heads, rows, _ = q.shape
    keys = k.shape[0]
    grid, per_head, full, row_info, key_info = attention_specs(heads, rows, keys)
    return pl.pallas_call(
        attend_back_kernel,
        grid=grid,
        in_specs=[per_head, per_head, full, full, row_info, row_info, key_info],
        out_specs=[per_head, full, full],
        out_shape=[
            jax.ShapeDtypeStruct(q.shape, BF),
            jax.ShapeDtypeStruct(k.shape, F32),
            jax.ShapeDtypeStruct(k.shape, F32),
        ],
        cost_estimate=pl.CostEstimate(
            flops=10 * heads * rows * keys * HEAD_SIZE,
            bytes_accessed=6 * q.size + 12 * k.size,
            transcendentals=heads * rows * keys,
        ),
        **PARAMS,
    )(q, do, k, v, q_place, q_start, k_place)


def to_blocks(weight, cores):
    wd = lax.axis_size("wd")
    rows = weight.shape[0]
    cut = weight.reshape(rows, wd, cores, -1).transpose(2, 1, 0, 3)
    return cut.reshape((cores * wd, rows) + cut.shape[3:])


def columns_out(blocks):
    moved = trade(blocks, ("pipe", "wd"))
    return moved.reshape((2, -1) + moved.shape[2:])


def put_kernel(spots, *refs):
    pieces, out = refs[: len(spots)], refs[len(spots)]
    block = pl.program_id(0)
    for piece, (first, count, col, cols) in zip(pieces, spots):

        def put(piece=piece, col=col, cols=cols):
            out[:, col : col + cols] = piece[...]

        pl.when((block >= first) & (block < first + count))(put)


def put_together(columns):
    block = min([256] + [piece.shape[0] for stack in columns for piece in stack])
    spots, pieces, specs = [], [], []
    col = 0
    for stack in columns:
        first = 0
        for piece in stack:
            count, cols = piece.shape[0] // block, piece.shape[1]
            spots.append((first, count, col, cols))
            pieces.append(piece)

            def at(i, first=first, count=count):
                return (jnp.clip(i - first, 0, count - 1), 0)

            specs.append(pl.BlockSpec((block, cols), at))
            first += count
        col += cols
    return pl.pallas_call(
        lambda *refs: put_kernel(spots, *refs),
        grid=(first,),
        in_specs=specs,
        out_specs=pl.BlockSpec((block, col), lambda i: (i, 0)),
        out_shape=jax.ShapeDtypeStruct((first * block, col), BF),
        cost_estimate=pl.CostEstimate(
            flops=0, bytes_accessed=4 * first * block * col, transcendentals=0
        ),
        **PARAMS,
    )(*pieces)


def pack_attention(w_query, key_matrix, value_matrix, w_output, cores):
    wd = lax.axis_size("wd")
    rows = w_query.shape[0]
    cut = [w_query.reshape(rows, wd, cores, -1)]
    for m in (key_matrix, value_matrix):
        m = m.reshape(rows, wd, 1, -1)
        cut.append(jnp.broadcast_to(m, (rows, wd, cores, m.shape[3])))
    cut.append(w_output.T.reshape(rows, wd, cores, -1))
    return jnp.concatenate(cut, axis=-1).reshape(rows, -1)


def unpack_attention(own, widths):
    other = hop(own, "pipe", 1)
    query_w, kv_w, out_w = widths
    cuts = (query_w, query_w + kv_w, query_w + 2 * kv_w)
    return (
        jnp.concatenate([own[:, : cuts[0]], other[:, : cuts[0]]], axis=1),
        own[:, cuts[0] : cuts[1]],
        own[:, cuts[1] : cuts[2]],
        jnp.concatenate([own[:, cuts[2] :], other[:, cuts[2] :]], axis=1),
    )


def grad_pair(own, other):
    return (own + hop(other.astype(BF), "pipe", 1).astype(F32)).astype(BF)


def mlp_pair(left, right):
    half = right.shape[1] // 2
    return grad_pair(mm_tl(left, right[:, :half]), mm_tl(left, right[:, half:]))


def grad_group(total):
    return lax.psum_scatter(total, "grp", scatter_dimension=0, tiled=True)


def grad_home(total):
    return trade(total.reshape((lax.axis_size("wd"), -1) + total.shape[1:]), "wd")


def place_kernel(turned, at_ref, keep_ref, got_ref, out_ref):
    mine = pl.program_id(1) == at_ref[0]

    def put(ref):
        block = ref[0].astype(F32)
        out_ref[...] = block.T if turned else block

    @pl.when(mine)
    def _():
        put(keep_ref)

    @pl.when(jnp.logical_not(mine))
    def _():
        put(got_ref)


def place(keep, got, turned):
    wd, rows, cols = keep.shape
    at = lax.axis_index("pipe").astype(jnp.int32)[None]
    cores = lax.axis_size("pipe")
    source = pl.BlockSpec((1, rows, cols), lambda w, c, at_ref: (w, 0, 0))
    if turned:
        shape, target = (wd * cores * cols, rows), (cols, rows)
        out = pl.BlockSpec(target, lambda w, c, at_ref: (w * cores + c, 0))
    else:
        shape, target = (rows, wd * cores * cols), (rows, cols)
        out = pl.BlockSpec(target, lambda w, c, at_ref: (0, w * cores + c))
    return pl.pallas_call(
        lambda *refs: place_kernel(turned, *refs),
        grid_spec=pltpu.PrefetchScalarGridSpec(
            num_scalar_prefetch=1, grid=(wd, cores), in_specs=[source, source], out_specs=out
        ),
        out_shape=jax.ShapeDtypeStruct(shape, F32),
        cost_estimate=pl.CostEstimate(
            flops=keep.size, bytes_accessed=12 * keep.size, transcendentals=0
        ),
    )(at, keep, got)


def layer_forward(stages, layer, x_rows, gains, where, build, jobs, settle):
    held = stages.held
    cosine, sine, q_place, q_start, k_place = where
    normed = apply_norm(x_rows, gains[0]).astype(BF)
    rows_a = stages.run(normed, gather_rows, jobs[0], settle[0])
    held["attn", layer] = build("attn", layer)
    w_q, w_k, w_v, w_ot = held["attn", layer]
    tok = rows_a.shape[0]

    def project(rows):
        key = rotary_apply(mm(rows, w_k).reshape(tok, 1, HEAD_SIZE), cosine, sine).astype(BF)[:, 0]
        value = mm(rows, w_v).astype(BF)
        return jnp.concatenate([key, value], axis=1)

    def queries(rows):
        query = rotary_apply(mm(rows, w_q).reshape(tok, -1, HEAD_SIZE), cosine, sine).astype(BF)
        return query.transpose(1, 0, 2)

    held["rows_a"] = rows_a
    kv_all = stages.run(
        project(rows_a),
        lambda kv: jnp.concatenate(others(kv, "grp"), axis=0),
        [("query", queries, ("rows_a",))] + jobs[1],
        settle[1],
    )
    query = held["query"]
    keys, values = kv_all[:, :HEAD_SIZE], kv_all[:, HEAD_SIZE:]

    def attention(q):
        context = attend(q, keys, values, q_place, q_start, k_place)
        context = context.transpose(1, 0, 2).reshape(tok, -1)
        return context, mm_t(context, w_ot).astype(BF)

    context, partial = stages.run(query, attention, jobs[2], settle[2])
    mid = stages.run(partial, lambda p: x_rows + sum_rows(p), jobs[3], settle[3])
    rows_b = stages.run(
        mid, lambda m: gather_rows(apply_norm(m, gains[1]).astype(BF)), jobs[4], settle[4]
    )
    held["gu", layer] = w_gu = build("gu", layer)

    def ahead(rows):
        both = mm(rows, w_gu)
        half = both.shape[1] // 2
        gate, up = both[:, :half], both[:, half:]
        return gate, up, (jax.nn.silu(gate) * up).astype(BF)

    gate, up, hidden = stages.run(rows_b, ahead, jobs[5], settle[5])
    held["down", layer] = build("down", layer)
    return x_rows, rows_a, query, keys, values, context, mid, rows_b, gate, up, hidden


def layer_backward(
    stages, layer, grad_out, grad_mlp, gains, where, kept, also, jobs, settle
):
    held = stages.held
    cosine, sine, q_place, q_start, k_place = where
    x_rows, rows_a, query, keys, values, context, mid, rows_b, gate, up, hidden = kept
    w_q, w_k, w_v, w_ot = held["attn", layer]
    w_gu, w_dt = held["gu", layer], held["down", layer]
    tok = rows_a.shape[0]
    held["rows_b"], held["hidden"], held["grad_mlp"] = rows_b, hidden, grad_mlp

    def feed_back(rows):
        grad_hidden = mm(rows, w_dt)
        sig = jax.nn.sigmoid(gate)
        grad_gate = (grad_hidden * up * sig * (1.0 + gate * (1.0 - sig))).astype(BF)
        grad_up = (grad_hidden * gate * sig).astype(BF)
        both = jnp.concatenate([grad_gate, grad_up], axis=1)
        return grad_gate, grad_up, mm_t(both, w_gu).astype(BF), also(hidden)

    grad_gate, grad_up, partial, extra = stages.run(grad_mlp, feed_back, jobs[0], settle[0])
    held["grad_gate"], held["grad_up"] = grad_gate, grad_up
    grad_b = stages.run(partial, sum_rows, jobs[1], settle[1])
    grad_mid, gain_b = norm_back(mid, gains[1], grad_b)
    grad_mid = grad_mid + grad_out
    grad_attn = stages.run(grad_mid.astype(BF), gather_rows, jobs[2], settle[2])

    def attention_back(rows):
        grad_context = mm(rows, w_ot).astype(BF)
        grad_context = grad_context.reshape(tok, -1, HEAD_SIZE).transpose(1, 0, 2)
        return attend_back(query, grad_context, keys, values, q_place, q_start, k_place)

    def keys_back(grads):
        kv = jnp.concatenate(grads, axis=1)
        kv = kv.reshape((-1, tok) + kv.shape[1:])
        return sum_others([kv[k] for k in range(kv.shape[0])], "grp").astype(BF)

    def queries_back(grad_q):
        grad_q = grad_q.transpose(1, 0, 2).astype(F32)
        grad_q = rotary_apply(grad_q, cosine, -sine).astype(BF).reshape(tok, -1)
        return grad_q, mm_t(grad_q, w_q)

    held["grad_q"], *grads = stages.run(grad_attn, attention_back, jobs[3])
    own_kv = stages.run(
        grads, keys_back, [("g_q", queries_back, ("grad_q",))] + jobs[4], settle[4]
    )
    grad_q, partial = held["g_q"]
    grad_k = own_kv[:, :HEAD_SIZE].astype(F32)
    grad_k = rotary_apply(grad_k[:, None, :], cosine, -sine).astype(BF)[:, 0]
    grad_v = own_kv[:, HEAD_SIZE:]
    partial = (partial + mm_t(grad_k, w_k) + mm_t(grad_v, w_v)).astype(BF)

    def attn_pair(g_q, g_k, g_v):
        half_q = g_q.shape[1] // 2

        def term(cut):
            right = jnp.concatenate([g_q[:, cut], g_k, g_v], axis=1)
            left = [mm_tl(rows_a, right), mm_tl(grad_attn, context[:, cut])]
            return jnp.concatenate(left, axis=1)

        return grad_pair(term(slice(0, half_q)), term(slice(half_q, None)))

    held["g_q"], held["g_k"], held["g_v"] = grad_q, grad_k, grad_v
    grad_a = stages.run(partial, sum_rows, jobs[5](attn_pair), settle[5])
    grad_in, gain_a = norm_back(x_rows, gains[0], grad_a)
    return grad_mid + grad_in, jnp.stack([gain_a, gain_b]), extra


def own_layer(first, second):
    core = lax.axis_index("pipe")
    keep = jnp.where(core == 0, first, second)
    return keep, hop(jnp.where(core == 0, second, first), "pipe", 1)


def body(
    block_input,
    cotangent,
    segments,
    norm_gains,
    w_query,
    key_matrix,
    value_matrix,
    w_output,
    w_gate,
    w_up,
    w_down,
):
    core = lax.axis_index("pipe")
    grp = lax.axis_index("grp")
    wd = lax.axis_size("wd")
    groups = lax.axis_size("grp")
    cores = lax.axis_size("pipe")
    tok = block_input.shape[1] * lax.axis_size(CUBE)

    stages = Stages()
    held = stages.held
    packed = pack_attention(w_query[0], key_matrix[0], value_matrix[0], w_output[0], cores)
    gains = spread_gains(norm_gains[0])
    packed, gains = lax.optimization_barrier((packed, gains))
    attn_cols = columns_out(to_blocks(packed, cores))
    held["gate_out"] = to_blocks(w_gate[0], cores)
    held["up_out"] = to_blocks(w_up[0], cores)
    held["down_out"] = to_blocks(w_down[0].T, cores)
    query_w, out_w = w_query.shape[2] // (wd * cores), w_output.shape[1] // (wd * cores)
    widths = (query_w, key_matrix.shape[2] // wd, out_w)

    def move(name):
        return (name, columns_out, (name + "_out",), "later")

    def rows_of(name, layer):
        return lax.all_gather(held[name][layer], "grp", axis=0, tiled=True)

    def put(*names):
        return put_together([[m] for n in names for m in (held[n], hop(held[n], "pipe", 1))])

    def build(kind, layer):
        if kind == "attn":
            return unpack_attention(held["own", "attn", layer], widths)
        if kind == "gu":
            return put(("own", "gate", layer), ("own", "up", layer))
        return put(("own", "down", layer))

    attn_rows = lax.all_gather(attn_cols, "grp", axis=1, tiled=True)
    for layer in range(2):
        held["own", "attn", layer] = attn_rows[layer]

    def start(name):
        for layer in range(2):
            held["own", name, layer] = rows_of(name, layer)

    stages.then.update(gate=start, up=start, down=start)

    seg_row = lax.dynamic_index_in_dim(segments, core, 0, keepdims=False)
    starts = doc_starts(seg_row)
    rows_own = tok // lax.axis_size(CUBE)

    def in_row_order(values):
        values = relative(values, 0, CUBE)
        return jnp.concatenate(
            [values[j * rows_own : (j + 1) * rows_own] for j in ROW_ORDER], axis=0
        )

    local = in_row_order(jnp.arange(tok, dtype=jnp.int32))
    q_place = grp * tok + local
    q_start = in_row_order(lax.dynamic_slice_in_dim(starts, grp * tok, tok))
    cosine, sine = rope_tables(q_place - q_start)
    k_place = jnp.concatenate([(grp ^ k) * tok + local for k in range(groups)])
    where = (cosine, sine, q_place[:, None], q_start[:, None], k_place[None, :])

    rows = lax.dynamic_index_in_dim(block_input, core, 0, keepdims=False)
    grad = lax.dynamic_index_in_dim(cotangent, core, 0, keepdims=False)
    held["cotangent"] = grad
    kept = [None, None]
    outs = [None, None]
    kept[0] = layer_forward(
        stages,
        0,
        rows.astype(F32),
        gains[0],
        where,
        build,
        [
            [],
            [move("gate"), ("last", gather_rows, ("cotangent",))],
            [move("up")],
            [move("down")],
            [],
            [],
        ],
        [
            (),
            (),
            (("own", "gate", 0),),
            (("own", "up", 0),),
            (("own", "down", 0),),
            (),
        ],
    )

    def close(hidden, layer):
        return (kept[layer][6] + sum_rows(mm_t(hidden, held["down", layer]))).astype(BF)

    outs[0] = stages.run(
        kept[0][-1], lambda h: close(h, 0), [], (("own", "gate", 1),)
    )
    kept[1] = layer_forward(
        stages,
        1,
        outs[0].astype(F32),
        gains[1],
        where,
        build,
        [[]] * 6,
        [(("own", "up", 1),), (), (("own", "down", 1),), (), (), ()],
    )

    def grad_of(name, layer):
        sources = {
            "down": ("grad_mlp", "hidden"),
            "gate": ("rows_b", "grad_gate"),
            "up": ("rows_b", "grad_up"),
        }[name]
        return (("pair", name, layer), mlp_pair, sources)

    def group_sum(name, layer):
        return (("sum", name, layer), grad_group, (("pair", name, layer),), "later")

    def home(name, layer):
        return (("home", name, layer), grad_home, (("sum", name, layer),), "later")

    def attn_grad(layer):
        return lambda pair: (("pair", "attn", layer), pair, ("g_q", "g_k", "g_v"))

    def final(name, turned):
        def ready(first, second):
            return place(*own_layer(first, second), turned)

        return (("final", name), ready, (("home", name, 0), ("home", name, 1)))

    held["hidden"], held["grad_mlp"] = kept[1][-1], held["last"]
    hidden = stages.run(kept[1][-1], lambda h: h, [grad_of("down", 1)])

    grads_in = [None, None]
    gain_grads = [None, None]
    grad_in, gain_grads[1], outs[1] = layer_backward(
        stages,
        1,
        grad.astype(F32),
        held["last"],
        gains[1],
        where,
        kept[1][:-1] + (hidden,),
        lambda h: close(h, 1),
        (
            [],
            [group_sum("down", 1), grad_of("gate", 1)],
            [group_sum("gate", 1), grad_of("up", 1)],
            [group_sum("up", 1)],
            [home("down", 1)],
            lambda pair: [attn_grad(1)(pair)],
        ),
        [(), (), (), (), (), (("sum", "gate", 1), ("home", "down", 1))],
    )
    grads_in[1] = grad_in.astype(BF)
    grad_mlp = stages.run(grads_in[1], gather_rows, [group_sum("attn", 1)], (("sum", "up", 1),))
    grad_in, gain_grads[0], _ = layer_backward(
        stages,
        0,
        grads_in[1].astype(F32),
        grad_mlp,
        gains[0],
        where,
        kept[0],
        lambda h: (),
        (
            [grad_of("down", 0), home("gate", 1)],
            [group_sum("down", 0), grad_of("gate", 0), home("up", 1)],
            [group_sum("gate", 0), grad_of("up", 0), home("attn", 1)],
            [group_sum("up", 0)],
            [home("down", 0)],
            lambda pair: [attn_grad(0)(pair)],
        ),
        [
            (),
            (("sum", "attn", 1), ("home", "gate", 1)),
            (("sum", "down", 0), ("home", "up", 1)),
            (),
            (("sum", "gate", 0), ("home", "attn", 1)),
            (("sum", "up", 0), ("home", "down", 0)),
        ],
    )
    grads_in[0] = grad_in.astype(BF)
    for key, job, names, *_ in (
        group_sum("attn", 0),
        home("gate", 0),
        final("down", True),
        final("gate", False),
        home("up", 0),
        final("up", False),
    ):
        held[key] = job(*[held[name] for name in names])
    keys = (("sum", "attn", 0),) + tuple(("final", name) for name in ("down", "gate", "up"))
    held.update(zip(keys, lax.optimization_barrier([held[key] for key in keys])))
    key, job, *_ = home("attn", 0)
    held[key] = job(held["sum", "attn", 0])

    def by_batch(pair):
        own, other = own_layer(pair[0], pair[1])
        both = jnp.where(core == 0, jnp.stack([own, other]), jnp.stack([other, own]))
        return both[None]

    layer_out = by_batch(outs)
    input_grad = by_batch(grads_in)

    grad_norm_gains = sum_gains(gain_grads)[None]

    def both(name):
        return own_layer(held["home", name, 0], held["home", name, 1])

    keep, got = both("attn")
    cuts = (0, widths[0], widths[0] + widths[1], widths[0] + 2 * widths[1], keep.shape[2])
    q_pair, k_pair, v_pair, o_pair = (
        (keep[..., lo:hi], got[..., lo:hi]) for lo, hi in zip(cuts[:-1], cuts[1:])
    )

    def small(pair):
        order = pair[0].transpose(1, 0, 2).astype(F32)
        return order.reshape(order.shape[0], -1)[None]

    grad_wq = place(*q_pair, False)[None]
    grad_wk = small(k_pair)
    grad_wv = small(v_pair)
    grad_wo = place(*o_pair, True)[None]
    grad_wg = held["final", "gate"][None]
    grad_wu = held["final", "up"][None]
    grad_wd = held["final", "down"][None]
    return (
        layer_out,
        input_grad,
        grad_norm_gains,
        grad_wq,
        grad_wk,
        grad_wv,
        grad_wo,
        grad_wg,
        grad_wu,
        grad_wd,
    )


def solution(mesh):
    sizes = dict(mesh.shape)
    wd = KV_HEADS // sizes["tensor"]
    fine = Mesh(
        mesh.devices.reshape(sizes["pipe"], sizes["dp"] // wd, wd, sizes["tensor"]),
        ("pipe", "grp", "wd", "tensor"),
    )
    dp = ("grp", "wd")
    tokens = P(None, dp + ("tensor",), None)
    outs = P("pipe", None, dp + ("tensor",), None)
    gains = P("pipe", None, dp + ("tensor",))
    tall = P("pipe", dp, "tensor")
    wide = P("pipe", "tensor", dp)
    weights = (tall, tall, tall, wide, tall, tall, wide)
    return jax.shard_map(
        body,
        mesh=fine,
        in_specs=(tokens, tokens, P(), gains) + weights,
        out_specs=(outs, outs, gains) + weights,
        check_vma=False,
    )
```

```python
import jax
import jax.numpy as jnp
from jax import lax
from jax.experimental import pallas as pl
from jax.experimental.pallas import tpu as pltpu
from jax.sharding import Mesh, PartitionSpec as P

HEAD_SIZE = 64
KV_HEADS = 8
EPS = 1e-05
ROPE_BASE = 500000.0
NEG_FILL = -1e30
BF = jnp.bfloat16
F32 = jnp.float32
CUBE = ("wd", "tensor")


def rms_scale(row_values):
    return lax.rsqrt(jnp.mean(row_values * row_values, axis=-1, keepdims=True) + EPS)


def apply_norm(row_values, gain_vector):
    return row_values * rms_scale(row_values) * gain_vector


def norm_back(row_values, gain_vector, grad_normed):
    _, pullback = jax.vjp(apply_norm, row_values, gain_vector)
    return pullback(grad_normed)


def doc_starts(seg_row):
    places = jnp.arange(seg_row.shape[0], dtype=jnp.int32)
    before = jnp.concatenate([seg_row[:1] - 1, seg_row[:-1]])
    return lax.cummax(jnp.where(seg_row != before, places, 0), axis=0)


def rope_tables(positions):
    half_dim = HEAD_SIZE // 2
    freqs = ROPE_BASE ** (-(jnp.arange(half_dim, dtype=F32) * 2.0 / HEAD_SIZE))
    angles = positions.astype(F32)[:, None] * freqs[None, :]
    return (jnp.cos(angles), jnp.sin(angles))


def rotary_apply(head_values, cosine_table, sine_values):
    half_dim = head_values.shape[-1] // 2
    first_half = head_values[..., :half_dim]
    second_half = head_values[..., half_dim:]
    cos_rows = cosine_table[:, None, :]
    sin_rows = sine_values[:, None, :]
    return jnp.concatenate(
        [
            first_half * cos_rows - second_half * sin_rows,
            second_half * cos_rows + first_half * sin_rows,
        ],
        axis=-1,
    )


def mm(left, right):
    return jnp.dot(left, right, preferred_element_type=F32)


def mm_t(left, right):
    return lax.dot_general(left, right, (((1,), (1,)), ((), ())), preferred_element_type=F32)


def mm_tl(left, right):
    return lax.dot_general(left, right, (((0,), (0,)), ((), ())), preferred_element_type=F32)


def trade(blocks, axes):
    return lax.all_to_all(blocks, axes, 0, 0, tiled=True)


def hop(block, axis, step):
    size = lax.axis_size(axis)
    return lax.ppermute(block, axis, [(i, i ^ step) for i in range(size)])


def tie(*values):
    return lax.optimization_barrier(values)


def link_steps():
    steps = []
    step = 1
    while step < lax.axis_size(CUBE):
        steps.append(step)
        step *= 2
    return steps


FAR, NEAR, SIDE = 4, 2, 1
ROW_ORDER = (0, FAR, NEAR, FAR | NEAR, SIDE, FAR | SIDE, NEAR | SIDE, FAR | NEAR | SIDE)


def cube(block, step):
    return hop(block, CUBE, step)


def join_kernel(left_ref, left_came_ref, right_ref, right_came_ref, out_ref):
    half = left_ref.shape[1]
    block = pl.program_id(0)

    @pl.when(block < 2)
    def _():
        out_ref[:, :half] = left_ref[...]

    @pl.when(block >= 2)
    def _():
        out_ref[:, :half] = left_came_ref[...]

    @pl.when(block % 2 == 0)
    def _():
        out_ref[:, half:] = right_ref[...]

    @pl.when(block % 2 == 1)
    def _():
        out_ref[:, half:] = right_came_ref[...]


def join_halves(left, left_came, right, right_came):
    rows, half = left.shape[0] // 2, left.shape[1]

    def spec(place):
        return pl.BlockSpec((rows, half), lambda i: (place(i), 0))

    return pl.pallas_call(
        join_kernel,
        grid=(4,),
        in_specs=[
            spec(lambda i: jnp.minimum(i, 1)),
            spec(lambda i: jnp.maximum(i - 2, 0)),
            spec(lambda i: i // 2),
            spec(lambda i: i // 2),
        ],
        out_specs=pl.BlockSpec((rows, 2 * half), lambda i: (i, 0)),
        out_shape=jax.ShapeDtypeStruct((4 * rows, 2 * half), left.dtype),
        cost_estimate=pl.CostEstimate(
            flops=0, bytes_accessed=32 * rows * half, transcendentals=0
        ),
    )(left, left_came, right, right_came)


def gather_rows(rows):
    two = jnp.concatenate([rows, cube(rows, FAR)], axis=0)
    half = two.shape[1] // 2
    left, right = two[:, :half], two[:, half:]
    left_came, right_came = cube(left, NEAR), cube(right, SIDE)
    left = jnp.concatenate([left, left_came], axis=0)
    right = jnp.concatenate([right, right_came], axis=0)
    return join_halves(left, cube(left, SIDE), right, cube(right, NEAR))


def sum_rows(partial):
    partial = partial.astype(BF)
    n, half = partial.shape[0] // 4, partial.shape[1] // 2
    left, right = partial[:, :half], partial[:, half:]
    left_came = cube(left[2 * n :], SIDE)
    right_came = cube(jnp.concatenate([right[n : 2 * n], right[3 * n :]], axis=0), NEAR)
    left = left[: 2 * n].astype(F32) + left_came.astype(F32)
    right_came = right_came.astype(F32)
    low = right[:n].astype(F32) + right_came[:n]
    high = right[2 * n : 3 * n].astype(F32) + right_came[n:]
    left_came = cube(left[n:].astype(BF), NEAR)
    right_came = cube(high.astype(BF), SIDE)
    left = left[:n] + left_came.astype(F32)
    right = low + right_came.astype(F32)
    both = jnp.concatenate([left, right], axis=1)
    rows = n // 2
    return both[:rows] + cube(both[rows:].astype(BF), FAR).astype(F32)


class Stages:
    def __init__(self):
        self.held = {}
        self.then = {}

    def run(self, value, step, jobs, settle=()):
        needed = [[self.held[name] for name in job[2]] for job in jobs]
        value, needed = lax.optimization_barrier((value, needed))
        out = step(value)
        made = [job[1](*inputs) for job, inputs in zip(jobs, needed)]
        due = [m for m, job in zip(made, jobs) if len(job) == 3]
        ready = [self.held[key] for key in settle]
        out, due, ready = lax.optimization_barrier((out, due, ready))
        self.held.update(zip(settle, ready))
        for job, result in zip(jobs, made):
            self.held[job[0]] = due.pop(0) if len(job) == 3 else result
            if job[0] in self.then:
                self.then[job[0]](job[0])
        return out


def others(block, axis):
    return [block] + [hop(block, axis, k) for k in range(1, lax.axis_size(axis))]


def sum_others(blocks, axis):
    total = blocks[0].astype(F32)
    for k in range(1, lax.axis_size(axis)):
        total = total + hop(blocks[k].astype(BF), axis, k).astype(F32)
    return total


def relative(values, dim, axis):
    count = lax.axis_size(axis)
    me = lax.axis_index(axis)
    step = 1
    while step < count:
        shape = values.shape
        cut = shape[:dim] + (count // (2 * step), 2, step * (shape[dim] // count)) + shape[dim + 1 :]
        view = values.reshape(cut)
        swapped = jnp.concatenate(
            [lax.slice_in_dim(view, 1, 2, axis=dim + 1), lax.slice_in_dim(view, 0, 1, axis=dim + 1)],
            axis=dim + 1,
        )
        values = jnp.where((me & step) != 0, swapped.reshape(shape), values)
        step *= 2
    return values


def spread_gains(norm_gains):
    me = lax.axis_index(CUBE)
    gain = norm_gains
    for step in link_steps():
        came = hop(gain, CUBE, step)
        gain = jnp.where(
            (me & step) != 0,
            jnp.concatenate([came, gain], axis=1),
            jnp.concatenate([gain, came], axis=1),
        )
    gain = relative(jnp.concatenate(others(gain, "grp"), axis=1), 1, "grp")
    other = hop(gain, "pipe", 1)
    core = lax.axis_index("pipe")
    return [jnp.where(core == 0, gain, other), jnp.where(core == 0, other, gain)]


def sum_gains(grads):
    me = lax.axis_index(CUBE)
    keep, extra = own_layer(grads[0], grads[1])
    count = lax.axis_size("grp")
    total = relative((keep + extra).reshape(2, count, -1), 1, "grp")
    mine = total[:, 0]
    for k in range(1, count):
        mine = mine + hop(total[:, k], "grp", k)
    for step in link_steps()[::-1]:
        half = mine.shape[1] // 2
        low, high = mine[:, :half], mine[:, half:]
        odd = (me & step) != 0
        mine = jnp.where(odd, high, low) + hop(jnp.where(odd, low, high), CUBE, step)
    return mine


def masked_probs(q, k, q_place, q_start, k_place):
    scores = lax.dot_general(q, k, (((1,), (1,)), ((), ())), preferred_element_type=F32)
    scores = scores * HEAD_SIZE ** (-0.5)
    allowed = (k_place <= q_place) & (k_place >= q_start)
    masked = jnp.where(allowed, scores, NEG_FILL)
    exps = jnp.exp(masked - jnp.max(masked, axis=-1, keepdims=True))
    return exps / jnp.sum(exps, axis=-1, keepdims=True)


def attend_kernel(q_ref, k_ref, v_ref, qp_ref, qs_ref, kp_ref, o_ref):
    probs = masked_probs(q_ref[0], k_ref[...], qp_ref[...], qs_ref[...], kp_ref[...])
    o_ref[0] = jnp.dot(probs.astype(BF), v_ref[...], preferred_element_type=F32).astype(BF)


def attend_back_kernel(q_ref, do_ref, k_ref, v_ref, qp_ref, qs_ref, kp_ref, dq_ref, dk_ref, dv_ref):
    @pl.when((pl.program_id(0) == 0) & (pl.program_id(1) == 0))
    def _():
        dk_ref[...] = jnp.zeros_like(dk_ref)
        dv_ref[...] = jnp.zeros_like(dv_ref)

    q = q_ref[0]
    do = do_ref[0]
    k = k_ref[...]
    probs = masked_probs(q, k, qp_ref[...], qs_ref[...], kp_ref[...])
    grad_probs = lax.dot_general(do, v_ref[...], (((1,), (1,)), ((), ())), preferred_element_type=F32)
    delta = jnp.sum(probs * grad_probs, axis=-1, keepdims=True)
    grad_scores = (probs * (grad_probs - delta) * HEAD_SIZE ** (-0.5)).astype(BF)
    dq_ref[0] = jnp.dot(grad_scores, k, preferred_element_type=F32).astype(BF)
    dk_ref[...] += lax.dot_general(
        grad_scores, q, (((0,), (0,)), ((), ())), preferred_element_type=F32
    )
    dv_ref[...] += lax.dot_general(
        probs.astype(BF), do, (((0,), (0,)), ((), ())), preferred_element_type=F32
    )


def attention_specs(heads, rows, keys):
    rows_blk = max(16, min(rows, (512 * 1024) // keys))
    per_head = pl.BlockSpec((1, rows_blk, HEAD_SIZE), lambda b, h: (h, b, 0))
    full = pl.BlockSpec((keys, HEAD_SIZE), lambda b, h: (0, 0))
    row_info = pl.BlockSpec((rows_blk, 1), lambda b, h: (b, 0))
    key_info = pl.BlockSpec((1, keys), lambda b, h: (0, 0))
    return ((rows // rows_blk, heads), per_head, full, row_info, key_info)


PARAMS = dict(
    compiler_params=pltpu.CompilerParams(vmem_limit_bytes=50 * 1024 * 1024),
)


def attend(q, k, v, q_place, q_start, k_place):
    heads, rows, _ = q.shape
    keys = k.shape[0]
    grid, per_head, full, row_info, key_info = attention_specs(heads, rows, keys)
    return pl.pallas_call(
        attend_kernel,
        grid=grid,
        in_specs=[per_head, full, full, row_info, row_info, key_info],
        out_specs=per_head,
        out_shape=jax.ShapeDtypeStruct(q.shape, BF),
        cost_estimate=pl.CostEstimate(
            flops=4 * heads * rows * keys * HEAD_SIZE,
            bytes_accessed=4 * q.size + 4 * k.size,
            transcendentals=heads * rows * keys,
        ),
        **PARAMS,
    )(q, k, v, q_place, q_start, k_place)


def attend_back(q, do, k, v, q_place, q_start, k_place):
    heads, rows, _ = q.shape
    keys = k.shape[0]
    grid, per_head, full, row_info, key_info = attention_specs(heads, rows, keys)
    return pl.pallas_call(
        attend_back_kernel,
        grid=grid,
        in_specs=[per_head, per_head, full, full, row_info, row_info, key_info],
        out_specs=[per_head, full, full],
        out_shape=[
            jax.ShapeDtypeStruct(q.shape, BF),
            jax.ShapeDtypeStruct(k.shape, F32),
            jax.ShapeDtypeStruct(k.shape, F32),
        ],
        cost_estimate=pl.CostEstimate(
            flops=10 * heads * rows * keys * HEAD_SIZE,
            bytes_accessed=6 * q.size + 12 * k.size,
            transcendentals=heads * rows * keys,
        ),
        **PARAMS,
    )(q, do, k, v, q_place, q_start, k_place)


def to_blocks(weight, cores):
    wd = lax.axis_size("wd")
    rows = weight.shape[0]
    cut = weight.reshape(rows, wd, cores, -1).transpose(2, 1, 0, 3)
    return cut.reshape((cores * wd, rows) + cut.shape[3:])


def columns_out(blocks):
    moved = trade(blocks, ("pipe", "wd"))
    return moved.reshape((2, -1) + moved.shape[2:])


def put_kernel(spots, *refs):
    pieces, out = refs[: len(spots)], refs[len(spots)]
    block = pl.program_id(0)
    for piece, (first, count, col, cols) in zip(pieces, spots):

        def put(piece=piece, col=col, cols=cols):
            out[:, col : col + cols] = piece[...]

        pl.when((block >= first) & (block < first + count))(put)


def put_together(columns):
    block = min([256] + [piece.shape[0] for stack in columns for piece in stack])
    spots, pieces, specs = [], [], []
    col = 0
    for stack in columns:
        first = 0
        for piece in stack:
            count, cols = piece.shape[0] // block, piece.shape[1]
            spots.append((first, count, col, cols))
            pieces.append(piece)

            def at(i, first=first, count=count):
                return (jnp.clip(i - first, 0, count - 1), 0)

            specs.append(pl.BlockSpec((block, cols), at))
            first += count
        col += cols
    return pl.pallas_call(
        lambda *refs: put_kernel(spots, *refs),
        grid=(first,),
        in_specs=specs,
        out_specs=pl.BlockSpec((block, col), lambda i: (i, 0)),
        out_shape=jax.ShapeDtypeStruct((first * block, col), BF),
        cost_estimate=pl.CostEstimate(
            flops=0, bytes_accessed=4 * first * block * col, transcendentals=0
        ),
        **PARAMS,
    )(*pieces)


def pack_attention(w_query, key_matrix, value_matrix, w_output, cores):
    wd = lax.axis_size("wd")
    rows = w_query.shape[0]
    cut = [w_query.reshape(rows, wd, cores, -1)]
    for m in (key_matrix, value_matrix):
        m = m.reshape(rows, wd, 1, -1)
        cut.append(jnp.broadcast_to(m, (rows, wd, cores, m.shape[3])))
    cut.append(w_output.T.reshape(rows, wd, cores, -1))
    return jnp.concatenate(cut, axis=-1).reshape(rows, -1)


def unpack_attention(own, widths):
    other = hop(own, "pipe", 1)
    query_w, kv_w, out_w = widths
    cuts = (query_w, query_w + kv_w, query_w + 2 * kv_w)
    return (
        jnp.concatenate([own[:, : cuts[0]], other[:, : cuts[0]]], axis=1),
        own[:, cuts[0] : cuts[1]],
        own[:, cuts[1] : cuts[2]],
        jnp.concatenate([own[:, cuts[2] :], other[:, cuts[2] :]], axis=1),
    )


def grad_pair(own, other):
    return (own + hop(other.astype(BF), "pipe", 1).astype(F32)).astype(BF)


def mlp_pair(left, right):
    half = right.shape[1] // 2
    return grad_pair(mm_tl(left, right[:, :half]), mm_tl(left, right[:, half:]))


def grad_group(total):
    return lax.psum_scatter(total, "grp", scatter_dimension=0, tiled=True)


def grad_home(total):
    return trade(total.reshape((lax.axis_size("wd"), -1) + total.shape[1:]), "wd")


def place_kernel(turned, at_ref, keep_ref, got_ref, out_ref):
    mine = pl.program_id(1) == at_ref[0]

    def put(ref):
        block = ref[0].astype(F32)
        out_ref[...] = block.T if turned else block

    @pl.when(mine)
    def _():
        put(keep_ref)

    @pl.when(jnp.logical_not(mine))
    def _():
        put(got_ref)


def place(keep, got, turned):
    wd, rows, cols = keep.shape
    at = lax.axis_index("pipe").astype(jnp.int32)[None]
    cores = lax.axis_size("pipe")
    source = pl.BlockSpec((1, rows, cols), lambda w, c, at_ref: (w, 0, 0))
    if turned:
        shape, target = (wd * cores * cols, rows), (cols, rows)
        out = pl.BlockSpec(target, lambda w, c, at_ref: (w * cores + c, 0))
    else:
        shape, target = (rows, wd * cores * cols), (rows, cols)
        out = pl.BlockSpec(target, lambda w, c, at_ref: (0, w * cores + c))
    return pl.pallas_call(
        lambda *refs: place_kernel(turned, *refs),
        grid_spec=pltpu.PrefetchScalarGridSpec(
            num_scalar_prefetch=1, grid=(wd, cores), in_specs=[source, source], out_specs=out
        ),
        out_shape=jax.ShapeDtypeStruct(shape, F32),
        cost_estimate=pl.CostEstimate(
            flops=keep.size, bytes_accessed=12 * keep.size, transcendentals=0
        ),
    )(at, keep, got)


def layer_forward(stages, layer, x_rows, gains, where, build, jobs, settle):
    held = stages.held
    cosine, sine, q_place, q_start, k_place = where
    normed = apply_norm(x_rows, gains[0]).astype(BF)
    rows_a = stages.run(normed, gather_rows, jobs[0], settle[0])
    held["attn", layer] = build("attn", layer)
    w_q, w_k, w_v, w_ot = held["attn", layer]
    tok = rows_a.shape[0]

    def project(rows):
        key = rotary_apply(mm(rows, w_k).reshape(tok, 1, HEAD_SIZE), cosine, sine).astype(BF)[:, 0]
        value = mm(rows, w_v).astype(BF)
        return jnp.concatenate([key, value], axis=1)

    def queries(rows):
        query = rotary_apply(mm(rows, w_q).reshape(tok, -1, HEAD_SIZE), cosine, sine).astype(BF)
        return query.transpose(1, 0, 2)

    held["rows_a"] = rows_a
    kv_all = stages.run(
        project(rows_a),
        lambda kv: jnp.concatenate(others(kv, "grp"), axis=0),
        [("query", queries, ("rows_a",))] + jobs[1],
        settle[1],
    )
    query = held["query"]
    keys, values = kv_all[:, :HEAD_SIZE], kv_all[:, HEAD_SIZE:]

    def attention(q):
        context = attend(q, keys, values, q_place, q_start, k_place)
        context = context.transpose(1, 0, 2).reshape(tok, -1)
        return context, mm_t(context, w_ot).astype(BF)

    context, partial = stages.run(query, attention, jobs[2], settle[2])
    mid = stages.run(partial, lambda p: x_rows + sum_rows(p), jobs[3], settle[3])
    rows_b = stages.run(
        mid, lambda m: gather_rows(apply_norm(m, gains[1]).astype(BF)), jobs[4], settle[4]
    )
    held["gu", layer] = w_gu = build("gu", layer)

    def ahead(rows):
        both = mm(rows, w_gu)
        half = both.shape[1] // 2
        gate, up = both[:, :half], both[:, half:]
        return gate, up, (jax.nn.silu(gate) * up).astype(BF)

    gate, up, hidden = stages.run(rows_b, ahead, jobs[5], settle[5])
    held["down", layer] = build("down", layer)
    return x_rows, rows_a, query, keys, values, context, mid, rows_b, gate, up, hidden


def layer_backward(
    stages, layer, grad_out, grad_mlp, gains, where, kept, also, jobs, settle
):
    held = stages.held
    cosine, sine, q_place, q_start, k_place = where
    x_rows, rows_a, query, keys, values, context, mid, rows_b, gate, up, hidden = kept
    w_q, w_k, w_v, w_ot = held["attn", layer]
    w_gu, w_dt = held["gu", layer], held["down", layer]
    tok = rows_a.shape[0]
    held["rows_b"], held["hidden"], held["grad_mlp"] = rows_b, hidden, grad_mlp

    def feed_back(rows):
        grad_hidden = mm(rows, w_dt)
        sig = jax.nn.sigmoid(gate)
        grad_gate = (grad_hidden * up * sig * (1.0 + gate * (1.0 - sig))).astype(BF)
        grad_up = (grad_hidden * gate * sig).astype(BF)
        both = jnp.concatenate([grad_gate, grad_up], axis=1)
        return grad_gate, grad_up, mm_t(both, w_gu).astype(BF), also(hidden)

    grad_gate, grad_up, partial, extra = stages.run(grad_mlp, feed_back, jobs[0], settle[0])
    held["grad_gate"], held["grad_up"] = grad_gate, grad_up
    grad_b = stages.run(partial, sum_rows, jobs[1], settle[1])
    grad_mid, gain_b = norm_back(mid, gains[1], grad_b)
    grad_mid = grad_mid + grad_out
    grad_attn = stages.run(grad_mid.astype(BF), gather_rows, jobs[2], settle[2])

    def attention_back(rows):
        grad_context = mm(rows, w_ot).astype(BF)
        grad_context = grad_context.reshape(tok, -1, HEAD_SIZE).transpose(1, 0, 2)
        return attend_back(query, grad_context, keys, values, q_place, q_start, k_place)

    def keys_back(grads):
        kv = jnp.concatenate(grads, axis=1)
        kv = kv.reshape((-1, tok) + kv.shape[1:])
        return sum_others([kv[k] for k in range(kv.shape[0])], "grp").astype(BF)

    def queries_back(grad_q):
        grad_q = grad_q.transpose(1, 0, 2).astype(F32)
        grad_q = rotary_apply(grad_q, cosine, -sine).astype(BF).reshape(tok, -1)
        return grad_q, mm_t(grad_q, w_q)

    held["grad_q"], *grads = stages.run(grad_attn, attention_back, jobs[3])
    own_kv = stages.run(
        grads, keys_back, [("g_q", queries_back, ("grad_q",))] + jobs[4], settle[4]
    )
    grad_q, partial = held["g_q"]
    grad_k = own_kv[:, :HEAD_SIZE].astype(F32)
    grad_k = rotary_apply(grad_k[:, None, :], cosine, -sine).astype(BF)[:, 0]
    grad_v = own_kv[:, HEAD_SIZE:]
    partial = (partial + mm_t(grad_k, w_k) + mm_t(grad_v, w_v)).astype(BF)

    def attn_pair(g_q, g_k, g_v):
        half_q = g_q.shape[1] // 2

        def term(cut):
            right = jnp.concatenate([g_q[:, cut], g_k, g_v], axis=1)
            left = [mm_tl(rows_a, right), mm_tl(grad_attn, context[:, cut])]
            return jnp.concatenate(left, axis=1)

        return grad_pair(term(slice(0, half_q)), term(slice(half_q, None)))

    held["g_q"], held["g_k"], held["g_v"] = grad_q, grad_k, grad_v
    grad_a = stages.run(partial, sum_rows, jobs[5](attn_pair), settle[5])
    grad_in, gain_a = norm_back(x_rows, gains[0], grad_a)
    return grad_mid + grad_in, jnp.stack([gain_a, gain_b]), extra


def own_layer(first, second):
    core = lax.axis_index("pipe")
    keep = jnp.where(core == 0, first, second)
    return keep, hop(jnp.where(core == 0, second, first), "pipe", 1)


def body(
    block_input,
    cotangent,
    segments,
    norm_gains,
    w_query,
    key_matrix,
    value_matrix,
    w_output,
    w_gate,
    w_up,
    w_down,
):
    core = lax.axis_index("pipe")
    grp = lax.axis_index("grp")
    wd = lax.axis_size("wd")
    groups = lax.axis_size("grp")
    cores = lax.axis_size("pipe")
    tok = block_input.shape[1] * lax.axis_size(CUBE)

    stages = Stages()
    held = stages.held
    packed = pack_attention(w_query[0], key_matrix[0], value_matrix[0], w_output[0], cores)
    gains = spread_gains(norm_gains[0])
    packed, gains = lax.optimization_barrier((packed, gains))
    attn_cols = columns_out(to_blocks(packed, cores))
    held["gate_out"] = to_blocks(w_gate[0], cores)
    held["up_out"] = to_blocks(w_up[0], cores)
    held["down_out"] = to_blocks(w_down[0].T, cores)
    query_w, out_w = w_query.shape[2] // (wd * cores), w_output.shape[1] // (wd * cores)
    widths = (query_w, key_matrix.shape[2] // wd, out_w)

    def move(name):
        return (name, columns_out, (name + "_out",), "later")

    def rows_of(name, layer):
        return lax.all_gather(held[name][layer], "grp", axis=0, tiled=True)

    def put(*names):
        return put_together([[m] for n in names for m in (held[n], hop(held[n], "pipe", 1))])

    def build(kind, layer):
        if kind == "attn":
            return unpack_attention(held["own", "attn", layer], widths)
        if kind == "gu":
            return put(("own", "gate", layer), ("own", "up", layer))
        return put(("own", "down", layer))

    held["attn"] = attn_cols
    for layer in range(2):
        held["own", "attn", layer] = rows_of("attn", layer)

    def start(name):
        for layer in range(2):
            held["own", name, layer] = rows_of(name, layer)

    stages.then.update(gate=start, up=start, down=start)

    seg_row = lax.dynamic_index_in_dim(segments, core, 0, keepdims=False)
    starts = doc_starts(seg_row)
    rows_own = tok // lax.axis_size(CUBE)

    def in_row_order(values):
        values = relative(values, 0, CUBE)
        return jnp.concatenate(
            [values[j * rows_own : (j + 1) * rows_own] for j in ROW_ORDER], axis=0
        )

    local = in_row_order(jnp.arange(tok, dtype=jnp.int32))
    q_place = grp * tok + local
    q_start = in_row_order(lax.dynamic_slice_in_dim(starts, grp * tok, tok))
    cosine, sine = rope_tables(q_place - q_start)
    k_place = jnp.concatenate([(grp ^ k) * tok + local for k in range(groups)])
    where = (cosine, sine, q_place[:, None], q_start[:, None], k_place[None, :])

    rows = lax.dynamic_index_in_dim(block_input, core, 0, keepdims=False)
    grad = lax.dynamic_index_in_dim(cotangent, core, 0, keepdims=False)
    held["cotangent"] = grad
    kept = [None, None]
    outs = [None, None]
    kept[0] = layer_forward(
        stages,
        0,
        rows.astype(F32),
        gains[0],
        where,
        build,
        [
            [],
            [move("gate")],
            [move("up"), ("last", gather_rows, ("cotangent",))],
            [move("down")],
            [],
            [],
        ],
        [
            (),
            (("own", "attn", 1),),
            (("own", "gate", 0),),
            (("own", "up", 0),),
            (("own", "down", 0),),
            (),
        ],
    )

    def close(hidden, layer):
        return (kept[layer][6] + sum_rows(mm_t(hidden, held["down", layer]))).astype(BF)

    outs[0] = stages.run(
        kept[0][-1], lambda h: close(h, 0), [], (("own", "gate", 1),)
    )
    kept[1] = layer_forward(
        stages,
        1,
        outs[0].astype(F32),
        gains[1],
        where,
        build,
        [[]] * 6,
        [(("own", "up", 1),), (), (("own", "down", 1),), (), (), ()],
    )

    def grad_of(name, layer):
        sources = {
            "down": ("grad_mlp", "hidden"),
            "gate": ("rows_b", "grad_gate"),
            "up": ("rows_b", "grad_up"),
        }[name]
        return (("pair", name, layer), mlp_pair, sources)

    def group_sum(name, layer):
        return (("sum", name, layer), grad_group, (("pair", name, layer),), "later")

    def home(name, layer):
        return (("home", name, layer), grad_home, (("sum", name, layer),), "later")

    def attn_grad(layer):
        return lambda pair: (("pair", "attn", layer), pair, ("g_q", "g_k", "g_v"))

    def final(name, turned):
        def ready(first, second):
            return place(*own_layer(first, second), turned)

        return (("final", name), ready, (("home", name, 0), ("home", name, 1)))

    held["hidden"], held["grad_mlp"] = kept[1][-1], held["last"]
    hidden = stages.run(kept[1][-1], lambda h: h, [grad_of("down", 1)])

    grads_in = [None, None]
    gain_grads = [None, None]
    grad_in, gain_grads[1], outs[1] = layer_backward(
        stages,
        1,
        grad.astype(F32),
        held["last"],
        gains[1],
        where,
        kept[1][:-1] + (hidden,),
        lambda h: close(h, 1),
        (
            [],
            [group_sum("down", 1), grad_of("gate", 1)],
            [group_sum("gate", 1), grad_of("up", 1)],
            [group_sum("up", 1)],
            [home("down", 1)],
            lambda pair: [attn_grad(1)(pair)],
        ),
        [(), (), (), (), (), (("sum", "gate", 1), ("home", "down", 1))],
    )
    grads_in[1] = grad_in.astype(BF)
    grad_mlp = stages.run(grads_in[1], gather_rows, [group_sum("attn", 1)], (("sum", "up", 1),))
    grad_in, gain_grads[0], _ = layer_backward(
        stages,
        0,
        grads_in[1].astype(F32),
        grad_mlp,
        gains[0],
        where,
        kept[0],
        lambda h: (),
        (
            [grad_of("down", 0), home("gate", 1)],
            [group_sum("down", 0), grad_of("gate", 0), home("up", 1)],
            [group_sum("gate", 0), grad_of("up", 0), home("attn", 1)],
            [group_sum("up", 0)],
            [home("down", 0)],
            lambda pair: [attn_grad(0)(pair)],
        ),
        [
            (),
            (("sum", "attn", 1), ("home", "gate", 1)),
            (("sum", "down", 0), ("home", "up", 1)),
            (),
            (("sum", "gate", 0), ("home", "attn", 1)),
            (("sum", "up", 0), ("home", "down", 0)),
        ],
    )
    grads_in[0] = grad_in.astype(BF)
    for key, job, names, *_ in (
        group_sum("attn", 0),
        home("gate", 0),
        final("down", True),
        final("gate", False),
        home("up", 0),
        final("up", False),
    ):
        held[key] = job(*[held[name] for name in names])
    keys = (("sum", "attn", 0),) + tuple(("final", name) for name in ("down", "gate", "up"))
    held.update(zip(keys, lax.optimization_barrier([held[key] for key in keys])))
    key, job, *_ = home("attn", 0)
    held[key] = job(held["sum", "attn", 0])

    def by_batch(pair):
        own, other = own_layer(pair[0], pair[1])
        both = jnp.where(core == 0, jnp.stack([own, other]), jnp.stack([other, own]))
        return both[None]

    layer_out = by_batch(outs)
    input_grad = by_batch(grads_in)

    grad_norm_gains = sum_gains(gain_grads)[None]

    def both(name):
        return own_layer(held["home", name, 0], held["home", name, 1])

    keep, got = both("attn")
    cuts = (0, widths[0], widths[0] + widths[1], widths[0] + 2 * widths[1], keep.shape[2])
    q_pair, k_pair, v_pair, o_pair = (
        (keep[..., lo:hi], got[..., lo:hi]) for lo, hi in zip(cuts[:-1], cuts[1:])
    )

    def small(pair):
        order = pair[0].transpose(1, 0, 2).astype(F32)
        return order.reshape(order.shape[0], -1)[None]

    grad_wq = place(*q_pair, False)[None]
    grad_wk = small(k_pair)
    grad_wv = small(v_pair)
    grad_wo = place(*o_pair, True)[None]
    grad_wg = held["final", "gate"][None]
    grad_wu = held["final", "up"][None]
    grad_wd = held["final", "down"][None]
    return (
        layer_out,
        input_grad,
        grad_norm_gains,
        grad_wq,
        grad_wk,
        grad_wv,
        grad_wo,
        grad_wg,
        grad_wu,
        grad_wd,
    )


def solution(mesh):
    sizes = dict(mesh.shape)
    wd = KV_HEADS // sizes["tensor"]
    fine = Mesh(
        mesh.devices.reshape(sizes["pipe"], sizes["dp"] // wd, wd, sizes["tensor"]),
        ("pipe", "grp", "wd", "tensor"),
    )
    dp = ("grp", "wd")
    tokens = P(None, dp + ("tensor",), None)
    outs = P("pipe", None, dp + ("tensor",), None)
    gains = P("pipe", None, dp + ("tensor",))
    tall = P("pipe", dp, "tensor")
    wide = P("pipe", "tensor", dp)
    weights = (tall, tall, tall, wide, tall, tall, wide)
    return jax.shard_map(
        body,
        mesh=fine,
        in_specs=(tokens, tokens, P(), gains) + weights,
        out_specs=(outs, outs, gains) + weights,
        check_vma=False,
    )
```

```python
import jax
import jax.numpy as jnp
from jax import lax
from jax.experimental import pallas as pl
from jax.experimental.pallas import tpu as pltpu
from jax.sharding import Mesh, PartitionSpec as P

HEAD_SIZE = 64
KV_HEADS = 8
EPS = 1e-05
ROPE_BASE = 500000.0
NEG_FILL = -1e30
BF = jnp.bfloat16
F32 = jnp.float32
CUBE = ("wd", "tensor")


def rms_scale(row_values):
    return lax.rsqrt(jnp.mean(row_values * row_values, axis=-1, keepdims=True) + EPS)


def apply_norm(row_values, gain_vector):
    return row_values * rms_scale(row_values) * gain_vector


def norm_back(row_values, gain_vector, grad_normed):
    _, pullback = jax.vjp(apply_norm, row_values, gain_vector)
    return pullback(grad_normed)


def doc_starts(seg_row):
    places = jnp.arange(seg_row.shape[0], dtype=jnp.int32)
    before = jnp.concatenate([seg_row[:1] - 1, seg_row[:-1]])
    return lax.cummax(jnp.where(seg_row != before, places, 0), axis=0)


def rope_tables(positions):
    half_dim = HEAD_SIZE // 2
    freqs = ROPE_BASE ** (-(jnp.arange(half_dim, dtype=F32) * 2.0 / HEAD_SIZE))
    angles = positions.astype(F32)[:, None] * freqs[None, :]
    return (jnp.cos(angles), jnp.sin(angles))


def rotary_apply(head_values, cosine_table, sine_values):
    half_dim = head_values.shape[-1] // 2
    first_half = head_values[..., :half_dim]
    second_half = head_values[..., half_dim:]
    cos_rows = cosine_table[:, None, :]
    sin_rows = sine_values[:, None, :]
    return jnp.concatenate(
        [
            first_half * cos_rows - second_half * sin_rows,
            second_half * cos_rows + first_half * sin_rows,
        ],
        axis=-1,
    )


def mm(left, right):
    return jnp.dot(left, right, preferred_element_type=F32)


def mm_t(left, right):
    return lax.dot_general(left, right, (((1,), (1,)), ((), ())), preferred_element_type=F32)


def mm_tl(left, right):
    return lax.dot_general(left, right, (((0,), (0,)), ((), ())), preferred_element_type=F32)


def trade(blocks, axes):
    return lax.all_to_all(blocks, axes, 0, 0, tiled=True)


def hop(block, axis, step):
    size = lax.axis_size(axis)
    return lax.ppermute(block, axis, [(i, i ^ step) for i in range(size)])


def tie(*values):
    return lax.optimization_barrier(values)


def link_steps():
    steps = []
    step = 1
    while step < lax.axis_size(CUBE):
        steps.append(step)
        step *= 2
    return steps


FAR, NEAR, SIDE = 4, 2, 1
ROW_ORDER = (0, FAR, NEAR, FAR | NEAR, SIDE, FAR | SIDE, NEAR | SIDE, FAR | NEAR | SIDE)


def cube(block, step):
    return hop(block, CUBE, step)


def join_kernel(left_ref, left_came_ref, right_ref, right_came_ref, out_ref):
    half = left_ref.shape[1]
    block = pl.program_id(0)

    @pl.when(block < 2)
    def _():
        out_ref[:, :half] = left_ref[...]

    @pl.when(block >= 2)
    def _():
        out_ref[:, :half] = left_came_ref[...]

    @pl.when(block % 2 == 0)
    def _():
        out_ref[:, half:] = right_ref[...]

    @pl.when(block % 2 == 1)
    def _():
        out_ref[:, half:] = right_came_ref[...]


def join_halves(left, left_came, right, right_came):
    rows, half = left.shape[0] // 2, left.shape[1]

    def spec(place):
        return pl.BlockSpec((rows, half), lambda i: (place(i), 0))

    return pl.pallas_call(
        join_kernel,
        grid=(4,),
        in_specs=[
            spec(lambda i: jnp.minimum(i, 1)),
            spec(lambda i: jnp.maximum(i - 2, 0)),
            spec(lambda i: i // 2),
            spec(lambda i: i // 2),
        ],
        out_specs=pl.BlockSpec((rows, 2 * half), lambda i: (i, 0)),
        out_shape=jax.ShapeDtypeStruct((4 * rows, 2 * half), left.dtype),
        cost_estimate=pl.CostEstimate(
            flops=0, bytes_accessed=32 * rows * half, transcendentals=0
        ),
    )(left, left_came, right, right_came)


def gather_rows(rows):
    two = jnp.concatenate([rows, cube(rows, FAR)], axis=0)
    half = two.shape[1] // 2
    left, right = two[:, :half], two[:, half:]
    left_came, right_came = cube(left, NEAR), cube(right, SIDE)
    left = jnp.concatenate([left, left_came], axis=0)
    right = jnp.concatenate([right, right_came], axis=0)
    return join_halves(left, cube(left, SIDE), right, cube(right, NEAR))


def sum_rows(partial):
    partial = partial.astype(BF)
    n, half = partial.shape[0] // 4, partial.shape[1] // 2
    left, right = partial[:, :half], partial[:, half:]
    left_came = cube(left[2 * n :], SIDE)
    right_came = cube(jnp.concatenate([right[n : 2 * n], right[3 * n :]], axis=0), NEAR)
    left = left[: 2 * n].astype(F32) + left_came.astype(F32)
    right_came = right_came.astype(F32)
    low = right[:n].astype(F32) + right_came[:n]
    high = right[2 * n : 3 * n].astype(F32) + right_came[n:]
    left_came = cube(left[n:].astype(BF), NEAR)
    right_came = cube(high.astype(BF), SIDE)
    left = left[:n] + left_came.astype(F32)
    right = low + right_came.astype(F32)
    both = jnp.concatenate([left, right], axis=1)
    rows = n // 2
    return both[:rows] + cube(both[rows:].astype(BF), FAR).astype(F32)


class Stages:
    def __init__(self):
        self.held = {}
        self.then = {}

    def run(self, value, step, jobs, settle=()):
        needed = [[self.held[name] for name in job[2]] for job in jobs]
        value, needed = lax.optimization_barrier((value, needed))
        out = step(value)
        made = [job[1](*inputs) for job, inputs in zip(jobs, needed)]
        due = [m for m, job in zip(made, jobs) if len(job) == 3]
        ready = [self.held[key] for key in settle]
        out, due, ready = lax.optimization_barrier((out, due, ready))
        self.held.update(zip(settle, ready))
        for job, result in zip(jobs, made):
            self.held[job[0]] = due.pop(0) if len(job) == 3 else result
            if job[0] in self.then:
                self.then[job[0]](job[0])
        return out


def others(block, axis):
    return [block] + [hop(block, axis, k) for k in range(1, lax.axis_size(axis))]


def sum_others(blocks, axis):
    total = blocks[0].astype(F32)
    for k in range(1, lax.axis_size(axis)):
        total = total + hop(blocks[k].astype(BF), axis, k).astype(F32)
    return total


def relative(values, dim, axis):
    count = lax.axis_size(axis)
    me = lax.axis_index(axis)
    step = 1
    while step < count:
        shape = values.shape
        cut = shape[:dim] + (count // (2 * step), 2, step * (shape[dim] // count)) + shape[dim + 1 :]
        view = values.reshape(cut)
        swapped = jnp.concatenate(
            [lax.slice_in_dim(view, 1, 2, axis=dim + 1), lax.slice_in_dim(view, 0, 1, axis=dim + 1)],
            axis=dim + 1,
        )
        values = jnp.where((me & step) != 0, swapped.reshape(shape), values)
        step *= 2
    return values


def spread_gains(norm_gains):
    me = lax.axis_index(CUBE)
    gain = norm_gains
    for step in link_steps():
        came = hop(gain, CUBE, step)
        gain = jnp.where(
            (me & step) != 0,
            jnp.concatenate([came, gain], axis=1),
            jnp.concatenate([gain, came], axis=1),
        )
    gain = relative(jnp.concatenate(others(gain, "grp"), axis=1), 1, "grp")
    other = hop(gain, "pipe", 1)
    core = lax.axis_index("pipe")
    return [jnp.where(core == 0, gain, other), jnp.where(core == 0, other, gain)]


def sum_gains(grads):
    me = lax.axis_index(CUBE)
    keep, extra = own_layer(grads[0], grads[1])
    count = lax.axis_size("grp")
    total = relative((keep + extra).reshape(2, count, -1), 1, "grp")
    mine = total[:, 0]
    for k in range(1, count):
        mine = mine + hop(total[:, k], "grp", k)
    for step in link_steps()[::-1]:
        half = mine.shape[1] // 2
        low, high = mine[:, :half], mine[:, half:]
        odd = (me & step) != 0
        mine = jnp.where(odd, high, low) + hop(jnp.where(odd, low, high), CUBE, step)
    return mine


def masked_probs(q, k, q_place, q_start, k_place):
    scores = lax.dot_general(q, k, (((1,), (1,)), ((), ())), preferred_element_type=F32)
    scores = scores * HEAD_SIZE ** (-0.5)
    allowed = (k_place <= q_place) & (k_place >= q_start)
    masked = jnp.where(allowed, scores, NEG_FILL)
    exps = jnp.exp(masked - jnp.max(masked, axis=-1, keepdims=True))
    return exps / jnp.sum(exps, axis=-1, keepdims=True)


def attend_kernel(q_ref, k_ref, v_ref, qp_ref, qs_ref, kp_ref, o_ref):
    probs = masked_probs(q_ref[0], k_ref[...], qp_ref[...], qs_ref[...], kp_ref[...])
    o_ref[0] = jnp.dot(probs.astype(BF), v_ref[...], preferred_element_type=F32).astype(BF)


def attend_back_kernel(q_ref, do_ref, k_ref, v_ref, qp_ref, qs_ref, kp_ref, dq_ref, dk_ref, dv_ref):
    @pl.when((pl.program_id(0) == 0) & (pl.program_id(1) == 0))
    def _():
        dk_ref[...] = jnp.zeros_like(dk_ref)
        dv_ref[...] = jnp.zeros_like(dv_ref)

    q = q_ref[0]
    do = do_ref[0]
    k = k_ref[...]
    probs = masked_probs(q, k, qp_ref[...], qs_ref[...], kp_ref[...])
    grad_probs = lax.dot_general(do, v_ref[...], (((1,), (1,)), ((), ())), preferred_element_type=F32)
    delta = jnp.sum(probs * grad_probs, axis=-1, keepdims=True)
    grad_scores = (probs * (grad_probs - delta) * HEAD_SIZE ** (-0.5)).astype(BF)
    dq_ref[0] = jnp.dot(grad_scores, k, preferred_element_type=F32).astype(BF)
    dk_ref[...] += lax.dot_general(
        grad_scores, q, (((0,), (0,)), ((), ())), preferred_element_type=F32
    )
    dv_ref[...] += lax.dot_general(
        probs.astype(BF), do, (((0,), (0,)), ((), ())), preferred_element_type=F32
    )


def attention_specs(heads, rows, keys):
    rows_blk = max(16, min(rows, (512 * 1024) // keys))
    per_head = pl.BlockSpec((1, rows_blk, HEAD_SIZE), lambda b, h: (h, b, 0))
    full = pl.BlockSpec((keys, HEAD_SIZE), lambda b, h: (0, 0))
    row_info = pl.BlockSpec((rows_blk, 1), lambda b, h: (b, 0))
    key_info = pl.BlockSpec((1, keys), lambda b, h: (0, 0))
    return ((rows // rows_blk, heads), per_head, full, row_info, key_info)


PARAMS = dict(
    compiler_params=pltpu.CompilerParams(vmem_limit_bytes=50 * 1024 * 1024),
)


def attend(q, k, v, q_place, q_start, k_place):
    heads, rows, _ = q.shape
    keys = k.shape[0]
    grid, per_head, full, row_info, key_info = attention_specs(heads, rows, keys)
    return pl.pallas_call(
        attend_kernel,
        grid=grid,
        in_specs=[per_head, full, full, row_info, row_info, key_info],
        out_specs=per_head,
        out_shape=jax.ShapeDtypeStruct(q.shape, BF),
        cost_estimate=pl.CostEstimate(
            flops=4 * heads * rows * keys * HEAD_SIZE,
            bytes_accessed=4 * q.size + 4 * k.size,
            transcendentals=heads * rows * keys,
        ),
        **PARAMS,
    )(q, k, v, q_place, q_start, k_place)


def attend_back(q, do, k, v, q_place, q_start, k_place):
    heads, rows, _ = q.shape
    keys = k.shape[0]
    grid, per_head, full, row_info, key_info = attention_specs(heads, rows, keys)
    return pl.pallas_call(
        attend_back_kernel,
        grid=grid,
        in_specs=[per_head, per_head, full, full, row_info, row_info, key_info],
        out_specs=[per_head, full, full],
        out_shape=[
            jax.ShapeDtypeStruct(q.shape, BF),
            jax.ShapeDtypeStruct(k.shape, F32),
            jax.ShapeDtypeStruct(k.shape, F32),
        ],
        cost_estimate=pl.CostEstimate(
            flops=10 * heads * rows * keys * HEAD_SIZE,
            bytes_accessed=6 * q.size + 12 * k.size,
            transcendentals=heads * rows * keys,
        ),
        **PARAMS,
    )(q, do, k, v, q_place, q_start, k_place)


def to_blocks(weight, cores):
    wd = lax.axis_size("wd")
    rows = weight.shape[0]
    cut = weight.reshape(rows, wd, cores, -1).transpose(2, 1, 0, 3)
    return cut.reshape((cores * wd, rows) + cut.shape[3:])


def columns_out(blocks):
    moved = trade(blocks, ("pipe", "wd"))
    return moved.reshape((2, -1) + moved.shape[2:])


def put_kernel(spots, *refs):
    pieces, out = refs[: len(spots)], refs[len(spots)]
    block = pl.program_id(0)
    for piece, (first, count, col, cols) in zip(pieces, spots):

        def put(piece=piece, col=col, cols=cols):
            out[:, col : col + cols] = piece[...]

        pl.when((block >= first) & (block < first + count))(put)


def put_together(columns):
    block = min([256] + [piece.shape[0] for stack in columns for piece in stack])
    spots, pieces, specs = [], [], []
    col = 0
    for stack in columns:
        first = 0
        for piece in stack:
            count, cols = piece.shape[0] // block, piece.shape[1]
            spots.append((first, count, col, cols))
            pieces.append(piece)

            def at(i, first=first, count=count):
                return (jnp.clip(i - first, 0, count - 1), 0)

            specs.append(pl.BlockSpec((block, cols), at))
            first += count
        col += cols
    return pl.pallas_call(
        lambda *refs: put_kernel(spots, *refs),
        grid=(first,),
        in_specs=specs,
        out_specs=pl.BlockSpec((block, col), lambda i: (i, 0)),
        out_shape=jax.ShapeDtypeStruct((first * block, col), BF),
        cost_estimate=pl.CostEstimate(
            flops=0, bytes_accessed=4 * first * block * col, transcendentals=0
        ),
        **PARAMS,
    )(*pieces)


def pack_attention(w_query, key_matrix, value_matrix, w_output, cores):
    wd = lax.axis_size("wd")
    rows = w_query.shape[0]
    cut = [w_query.reshape(rows, wd, cores, -1)]
    for m in (key_matrix, value_matrix):
        m = m.reshape(rows, wd, 1, -1)
        cut.append(jnp.broadcast_to(m, (rows, wd, cores, m.shape[3])))
    cut.append(w_output.T.reshape(rows, wd, cores, -1))
    return jnp.concatenate(cut, axis=-1).reshape(rows, -1)


def unpack_attention(own, widths):
    other = hop(own, "pipe", 1)
    query_w, kv_w, out_w = widths
    cuts = (query_w, query_w + kv_w, query_w + 2 * kv_w)
    return (
        jnp.concatenate([own[:, : cuts[0]], other[:, : cuts[0]]], axis=1),
        own[:, cuts[0] : cuts[1]],
        own[:, cuts[1] : cuts[2]],
        jnp.concatenate([own[:, cuts[2] :], other[:, cuts[2] :]], axis=1),
    )


def grad_pair(own, other):
    return (own + hop(other.astype(BF), "pipe", 1).astype(F32)).astype(BF)


def mlp_pair(left, right):
    half = right.shape[1] // 2
    return grad_pair(mm_tl(left, right[:, :half]), mm_tl(left, right[:, half:]))


def grad_group(total):
    return lax.psum_scatter(total, "grp", scatter_dimension=0, tiled=True)


def grad_home(total):
    return trade(total.reshape((lax.axis_size("wd"), -1) + total.shape[1:]), "wd")


def place_kernel(turned, at_ref, keep_ref, got_ref, out_ref):
    mine = pl.program_id(1) == at_ref[0]

    def put(ref):
        block = ref[0].astype(F32)
        out_ref[...] = block.T if turned else block

    @pl.when(mine)
    def _():
        put(keep_ref)

    @pl.when(jnp.logical_not(mine))
    def _():
        put(got_ref)


def place(keep, got, turned):
    wd, rows, cols = keep.shape
    at = lax.axis_index("pipe").astype(jnp.int32)[None]
    cores = lax.axis_size("pipe")
    source = pl.BlockSpec((1, rows, cols), lambda w, c, at_ref: (w, 0, 0))
    if turned:
        shape, target = (wd * cores * cols, rows), (cols, rows)
        out = pl.BlockSpec(target, lambda w, c, at_ref: (w * cores + c, 0))
    else:
        shape, target = (rows, wd * cores * cols), (rows, cols)
        out = pl.BlockSpec(target, lambda w, c, at_ref: (0, w * cores + c))
    return pl.pallas_call(
        lambda *refs: place_kernel(turned, *refs),
        grid_spec=pltpu.PrefetchScalarGridSpec(
            num_scalar_prefetch=1, grid=(wd, cores), in_specs=[source, source], out_specs=out
        ),
        out_shape=jax.ShapeDtypeStruct(shape, F32),
        cost_estimate=pl.CostEstimate(
            flops=keep.size, bytes_accessed=12 * keep.size, transcendentals=0
        ),
    )(at, keep, got)


def layer_forward(stages, layer, x_rows, gains, where, build, jobs, settle):
    held = stages.held
    cosine, sine, q_place, q_start, k_place = where
    normed = apply_norm(x_rows, gains[0]).astype(BF)
    rows_a = stages.run(normed, gather_rows, jobs[0], settle[0])
    held["attn", layer] = build("attn", layer)
    w_q, w_k, w_v, w_ot = held["attn", layer]
    tok = rows_a.shape[0]

    def project(rows):
        key = rotary_apply(mm(rows, w_k).reshape(tok, 1, HEAD_SIZE), cosine, sine).astype(BF)[:, 0]
        value = mm(rows, w_v).astype(BF)
        return jnp.concatenate([key, value], axis=1)

    def queries(rows):
        query = rotary_apply(mm(rows, w_q).reshape(tok, -1, HEAD_SIZE), cosine, sine).astype(BF)
        return query.transpose(1, 0, 2)

    held["rows_a"] = rows_a
    kv_all = stages.run(
        project(rows_a),
        lambda kv: jnp.concatenate(others(kv, "grp"), axis=0),
        [("query", queries, ("rows_a",))] + jobs[1],
        settle[1],
    )
    query = held["query"]
    keys, values = kv_all[:, :HEAD_SIZE], kv_all[:, HEAD_SIZE:]

    def attention(q):
        context = attend(q, keys, values, q_place, q_start, k_place)
        context = context.transpose(1, 0, 2).reshape(tok, -1)
        return context, mm_t(context, w_ot).astype(BF)

    context, partial = stages.run(query, attention, jobs[2], settle[2])
    mid = stages.run(partial, lambda p: x_rows + sum_rows(p), jobs[3], settle[3])
    rows_b = stages.run(
        mid, lambda m: gather_rows(apply_norm(m, gains[1]).astype(BF)), jobs[4], settle[4]
    )
    held["gu", layer] = w_gu = build("gu", layer)

    def ahead(rows):
        both = mm(rows, w_gu)
        half = both.shape[1] // 2
        gate, up = both[:, :half], both[:, half:]
        return gate, up, (jax.nn.silu(gate) * up).astype(BF)

    gate, up, hidden = stages.run(rows_b, ahead, jobs[5], settle[5])
    held["down", layer] = build("down", layer)
    return x_rows, rows_a, query, keys, values, context, mid, rows_b, gate, up, hidden


def layer_backward(
    stages, layer, grad_out, grad_mlp, gains, where, kept, also, jobs, settle
):
    held = stages.held
    cosine, sine, q_place, q_start, k_place = where
    x_rows, rows_a, query, keys, values, context, mid, rows_b, gate, up, hidden = kept
    w_q, w_k, w_v, w_ot = held["attn", layer]
    w_gu, w_dt = held["gu", layer], held["down", layer]
    tok = rows_a.shape[0]
    held["rows_b"], held["hidden"], held["grad_mlp"] = rows_b, hidden, grad_mlp

    def feed_back(rows):
        grad_hidden = mm(rows, w_dt)
        sig = jax.nn.sigmoid(gate)
        grad_gate = (grad_hidden * up * sig * (1.0 + gate * (1.0 - sig))).astype(BF)
        grad_up = (grad_hidden * gate * sig).astype(BF)
        both = jnp.concatenate([grad_gate, grad_up], axis=1)
        return grad_gate, grad_up, mm_t(both, w_gu).astype(BF), also(hidden)

    grad_gate, grad_up, partial, extra = stages.run(grad_mlp, feed_back, jobs[0], settle[0])
    held["grad_gate"], held["grad_up"] = grad_gate, grad_up
    grad_b = stages.run(partial, sum_rows, jobs[1], settle[1])
    grad_mid, gain_b = norm_back(mid, gains[1], grad_b)
    grad_mid = grad_mid + grad_out
    grad_attn = stages.run(grad_mid.astype(BF), gather_rows, jobs[2], settle[2])

    def attention_back(rows):
        grad_context = mm(rows, w_ot).astype(BF)
        grad_context = grad_context.reshape(tok, -1, HEAD_SIZE).transpose(1, 0, 2)
        return attend_back(query, grad_context, keys, values, q_place, q_start, k_place)

    def keys_back(grads):
        kv = jnp.concatenate(grads, axis=1)
        kv = kv.reshape((-1, tok) + kv.shape[1:])
        return sum_others([kv[k] for k in range(kv.shape[0])], "grp").astype(BF)

    def queries_back(grad_q):
        grad_q = grad_q.transpose(1, 0, 2).astype(F32)
        grad_q = rotary_apply(grad_q, cosine, -sine).astype(BF).reshape(tok, -1)
        return grad_q, mm_t(grad_q, w_q)

    held["grad_q"], *grads = stages.run(grad_attn, attention_back, jobs[3])
    own_kv = stages.run(
        grads, keys_back, [("g_q", queries_back, ("grad_q",))] + jobs[4], settle[4]
    )
    grad_q, partial = held["g_q"]
    grad_k = own_kv[:, :HEAD_SIZE].astype(F32)
    grad_k = rotary_apply(grad_k[:, None, :], cosine, -sine).astype(BF)[:, 0]
    grad_v = own_kv[:, HEAD_SIZE:]
    partial = (partial + mm_t(grad_k, w_k) + mm_t(grad_v, w_v)).astype(BF)

    def attn_pair(g_q, g_k, g_v):
        half_q = g_q.shape[1] // 2

        def term(cut):
            right = jnp.concatenate([g_q[:, cut], g_k, g_v], axis=1)
            left = [mm_tl(rows_a, right), mm_tl(grad_attn, context[:, cut])]
            return jnp.concatenate(left, axis=1)

        return grad_pair(term(slice(0, half_q)), term(slice(half_q, None)))

    held["g_q"], held["g_k"], held["g_v"] = grad_q, grad_k, grad_v
    grad_a = stages.run(partial, sum_rows, jobs[5](attn_pair), settle[5])
    grad_in, gain_a = norm_back(x_rows, gains[0], grad_a)
    return grad_mid + grad_in, jnp.stack([gain_a, gain_b]), extra


def own_layer(first, second):
    core = lax.axis_index("pipe")
    keep = jnp.where(core == 0, first, second)
    return keep, hop(jnp.where(core == 0, second, first), "pipe", 1)


def body(
    block_input,
    cotangent,
    segments,
    norm_gains,
    w_query,
    key_matrix,
    value_matrix,
    w_output,
    w_gate,
    w_up,
    w_down,
):
    core = lax.axis_index("pipe")
    grp = lax.axis_index("grp")
    wd = lax.axis_size("wd")
    groups = lax.axis_size("grp")
    cores = lax.axis_size("pipe")
    tok = block_input.shape[1] * lax.axis_size(CUBE)

    stages = Stages()
    held = stages.held
    packed = pack_attention(w_query[0], key_matrix[0], value_matrix[0], w_output[0], cores)
    gains = spread_gains(norm_gains[0])
    packed, gains = lax.optimization_barrier((packed, gains))
    attn_cols = columns_out(to_blocks(packed, cores))
    held["gate_out"] = to_blocks(w_gate[0], cores)
    held["up_out"] = to_blocks(w_up[0], cores)
    held["down_out"] = to_blocks(w_down[0].T, cores)
    query_w, out_w = w_query.shape[2] // (wd * cores), w_output.shape[1] // (wd * cores)
    widths = (query_w, key_matrix.shape[2] // wd, out_w)

    def move(name):
        return (name, columns_out, (name + "_out",), "later")

    def rows_of(name, layer):
        return lax.all_gather(held[name][layer], "grp", axis=0, tiled=True)

    def put(*names):
        return put_together([[m] for n in names for m in (held[n], hop(held[n], "pipe", 1))])

    def build(kind, layer):
        if kind == "attn":
            return unpack_attention(held["own", "attn", layer], widths)
        if kind == "gu":
            return put(("own", "gate", layer), ("own", "up", layer))
        return put(("own", "down", layer))

    held["attn"] = attn_cols
    for layer in range(2):
        held["own", "attn", layer] = rows_of("attn", layer)

    def start(name):
        for layer in range(2):
            held["own", name, layer] = rows_of(name, layer)

    stages.then.update(gate=start, up=start, down=start)

    seg_row = lax.dynamic_index_in_dim(segments, core, 0, keepdims=False)
    starts = doc_starts(seg_row)
    rows_own = tok // lax.axis_size(CUBE)

    def in_row_order(values):
        values = relative(values, 0, CUBE)
        return jnp.concatenate(
            [values[j * rows_own : (j + 1) * rows_own] for j in ROW_ORDER], axis=0
        )

    local = in_row_order(jnp.arange(tok, dtype=jnp.int32))
    q_place = grp * tok + local
    q_start = in_row_order(lax.dynamic_slice_in_dim(starts, grp * tok, tok))
    cosine, sine = rope_tables(q_place - q_start)
    k_place = jnp.concatenate([(grp ^ k) * tok + local for k in range(groups)])
    where = (cosine, sine, q_place[:, None], q_start[:, None], k_place[None, :])

    rows = lax.dynamic_index_in_dim(block_input, core, 0, keepdims=False)
    grad = lax.dynamic_index_in_dim(cotangent, core, 0, keepdims=False)
    held["cotangent"] = grad
    kept = [None, None]
    outs = [None, None]
    kept[0] = layer_forward(
        stages,
        0,
        rows.astype(F32),
        gains[0],
        where,
        build,
        [
            [],
            [move("gate")],
            [move("up"), ("last", gather_rows, ("cotangent",))],
            [move("down")],
            [],
            [],
        ],
        [
            (),
            (),
            (("own", "gate", 0),),
            (("own", "up", 0),),
            (("own", "down", 0),),
            (),
        ],
    )

    def close(hidden, layer):
        return (kept[layer][6] + sum_rows(mm_t(hidden, held["down", layer]))).astype(BF)

    outs[0] = stages.run(
        kept[0][-1], lambda h: close(h, 0), [], (("own", "attn", 1), ("own", "gate", 1))
    )
    kept[1] = layer_forward(
        stages,
        1,
        outs[0].astype(F32),
        gains[1],
        where,
        build,
        [[]] * 6,
        [(("own", "up", 1),), (), (("own", "down", 1),), (), (), ()],
    )

    def grad_of(name, layer):
        sources = {
            "down": ("grad_mlp", "hidden"),
            "gate": ("rows_b", "grad_gate"),
            "up": ("rows_b", "grad_up"),
        }[name]
        return (("pair", name, layer), mlp_pair, sources)

    def group_sum(name, layer):
        return (("sum", name, layer), grad_group, (("pair", name, layer),), "later")

    def home(name, layer):
        return (("home", name, layer), grad_home, (("sum", name, layer),), "later")

    def attn_grad(layer):
        return lambda pair: (("pair", "attn", layer), pair, ("g_q", "g_k", "g_v"))

    def final(name, turned):
        def ready(first, second):
            return place(*own_layer(first, second), turned)

        return (("final", name), ready, (("home", name, 0), ("home", name, 1)))

    held["hidden"], held["grad_mlp"] = kept[1][-1], held["last"]
    hidden = stages.run(kept[1][-1], lambda h: h, [grad_of("down", 1)])

    grads_in = [None, None]
    gain_grads = [None, None]
    grad_in, gain_grads[1], outs[1] = layer_backward(
        stages,
        1,
        grad.astype(F32),
        held["last"],
        gains[1],
        where,
        kept[1][:-1] + (hidden,),
        lambda h: close(h, 1),
        (
            [],
            [group_sum("down", 1), grad_of("gate", 1)],
            [group_sum("gate", 1), grad_of("up", 1)],
            [group_sum("up", 1)],
            [home("down", 1)],
            lambda pair: [attn_grad(1)(pair)],
        ),
        [(), (), (), (), (), (("sum", "gate", 1), ("home", "down", 1))],
    )
    grads_in[1] = grad_in.astype(BF)
    grad_mlp = stages.run(grads_in[1], gather_rows, [group_sum("attn", 1)], (("sum", "up", 1),))
    grad_in, gain_grads[0], _ = layer_backward(
        stages,
        0,
        grads_in[1].astype(F32),
        grad_mlp,
        gains[0],
        where,
        kept[0],
        lambda h: (),
        (
            [grad_of("down", 0), home("gate", 1)],
            [group_sum("down", 0), grad_of("gate", 0), home("up", 1)],
            [group_sum("gate", 0), grad_of("up", 0), home("attn", 1)],
            [group_sum("up", 0)],
            [home("down", 0)],
            lambda pair: [attn_grad(0)(pair)],
        ),
        [
            (),
            (("sum", "attn", 1), ("home", "gate", 1)),
            (("sum", "down", 0), ("home", "up", 1)),
            (),
            (("sum", "gate", 0), ("home", "attn", 1)),
            (("sum", "up", 0), ("home", "down", 0)),
        ],
    )
    grads_in[0] = grad_in.astype(BF)
    for key, job, names, *_ in (
        group_sum("attn", 0),
        home("gate", 0),
        final("down", True),
        final("gate", False),
        home("up", 0),
        final("up", False),
    ):
        held[key] = job(*[held[name] for name in names])
    keys = (("sum", "attn", 0),) + tuple(("final", name) for name in ("down", "gate", "up"))
    held.update(zip(keys, lax.optimization_barrier([held[key] for key in keys])))
    key, job, *_ = home("attn", 0)
    held[key] = job(held["sum", "attn", 0])

    def by_batch(pair):
        own, other = own_layer(pair[0], pair[1])
        both = jnp.where(core == 0, jnp.stack([own, other]), jnp.stack([other, own]))
        return both[None]

    layer_out = by_batch(outs)
    input_grad = by_batch(grads_in)

    grad_norm_gains = sum_gains(gain_grads)[None]

    def both(name):
        return own_layer(held["home", name, 0], held["home", name, 1])

    keep, got = both("attn")
    cuts = (0, widths[0], widths[0] + widths[1], widths[0] + 2 * widths[1], keep.shape[2])
    q_pair, k_pair, v_pair, o_pair = (
        (keep[..., lo:hi], got[..., lo:hi]) for lo, hi in zip(cuts[:-1], cuts[1:])
    )

    def small(pair):
        order = pair[0].transpose(1, 0, 2).astype(F32)
        return order.reshape(order.shape[0], -1)[None]

    grad_wq = place(*q_pair, False)[None]
    grad_wk = small(k_pair)
    grad_wv = small(v_pair)
    grad_wo = place(*o_pair, True)[None]
    grad_wg = held["final", "gate"][None]
    grad_wu = held["final", "up"][None]
    grad_wd = held["final", "down"][None]
    return (
        layer_out,
        input_grad,
        grad_norm_gains,
        grad_wq,
        grad_wk,
        grad_wv,
        grad_wo,
        grad_wg,
        grad_wu,
        grad_wd,
    )


def solution(mesh):
    sizes = dict(mesh.shape)
    wd = KV_HEADS // sizes["tensor"]
    fine = Mesh(
        mesh.devices.reshape(sizes["pipe"], sizes["dp"] // wd, wd, sizes["tensor"]),
        ("pipe", "grp", "wd", "tensor"),
    )
    dp = ("grp", "wd")
    tokens = P(None, dp + ("tensor",), None)
    outs = P("pipe", None, dp + ("tensor",), None)
    gains = P("pipe", None, dp + ("tensor",))
    tall = P("pipe", dp, "tensor")
    wide = P("pipe", "tensor", dp)
    weights = (tall, tall, tall, wide, tall, tall, wide)
    return jax.shard_map(
        body,
        mesh=fine,
        in_specs=(tokens, tokens, P(), gains) + weights,
        out_specs=(outs, outs, gains) + weights,
        check_vma=False,
    )
```

```python
import jax
import jax.numpy as jnp
from jax import lax
from jax.experimental import pallas as pl
from jax.experimental.pallas import tpu as pltpu
from jax.sharding import Mesh, PartitionSpec as P

HEAD_SIZE = 64
KV_HEADS = 8
EPS = 1e-05
ROPE_BASE = 500000.0
NEG_FILL = -1e30
BF = jnp.bfloat16
F32 = jnp.float32
CUBE = ("wd", "tensor")


def rms_scale(row_values):
    return lax.rsqrt(jnp.mean(row_values * row_values, axis=-1, keepdims=True) + EPS)


def apply_norm(row_values, gain_vector):
    return row_values * rms_scale(row_values) * gain_vector


def norm_back(row_values, gain_vector, grad_normed):
    _, pullback = jax.vjp(apply_norm, row_values, gain_vector)
    return pullback(grad_normed)


def doc_starts(seg_row):
    places = jnp.arange(seg_row.shape[0], dtype=jnp.int32)
    before = jnp.concatenate([seg_row[:1] - 1, seg_row[:-1]])
    return lax.cummax(jnp.where(seg_row != before, places, 0), axis=0)


def rope_tables(positions):
    half_dim = HEAD_SIZE // 2
    freqs = ROPE_BASE ** (-(jnp.arange(half_dim, dtype=F32) * 2.0 / HEAD_SIZE))
    angles = positions.astype(F32)[:, None] * freqs[None, :]
    return (jnp.cos(angles), jnp.sin(angles))


def rotary_apply(head_values, cosine_table, sine_values):
    half_dim = head_values.shape[-1] // 2
    first_half = head_values[..., :half_dim]
    second_half = head_values[..., half_dim:]
    cos_rows = cosine_table[:, None, :]
    sin_rows = sine_values[:, None, :]
    return jnp.concatenate(
        [
            first_half * cos_rows - second_half * sin_rows,
            second_half * cos_rows + first_half * sin_rows,
        ],
        axis=-1,
    )


def mm(left, right):
    return jnp.dot(left, right, preferred_element_type=F32)


def mm_t(left, right):
    return lax.dot_general(left, right, (((1,), (1,)), ((), ())), preferred_element_type=F32)


def mm_tl(left, right):
    return lax.dot_general(left, right, (((0,), (0,)), ((), ())), preferred_element_type=F32)


def trade(blocks, axes):
    return lax.all_to_all(blocks, axes, 0, 0, tiled=True)


def hop(block, axis, step):
    size = lax.axis_size(axis)
    return lax.ppermute(block, axis, [(i, i ^ step) for i in range(size)])


def tie(*values):
    return lax.optimization_barrier(values)


def link_steps():
    steps = []
    step = 1
    while step < lax.axis_size(CUBE):
        steps.append(step)
        step *= 2
    return steps


FAR, NEAR, SIDE = 4, 2, 1
ROW_ORDER = (0, FAR, NEAR, FAR | NEAR, SIDE, FAR | SIDE, NEAR | SIDE, FAR | NEAR | SIDE)


def cube(block, step):
    return hop(block, CUBE, step)


def join_kernel(left_ref, left_came_ref, right_ref, right_came_ref, out_ref):
    half = left_ref.shape[1]
    block = pl.program_id(0)

    @pl.when(block < 2)
    def _():
        out_ref[:, :half] = left_ref[...]

    @pl.when(block >= 2)
    def _():
        out_ref[:, :half] = left_came_ref[...]

    @pl.when(block % 2 == 0)
    def _():
        out_ref[:, half:] = right_ref[...]

    @pl.when(block % 2 == 1)
    def _():
        out_ref[:, half:] = right_came_ref[...]


def join_halves(left, left_came, right, right_came):
    rows, half = left.shape[0] // 2, left.shape[1]

    def spec(place):
        return pl.BlockSpec((rows, half), lambda i: (place(i), 0))

    return pl.pallas_call(
        join_kernel,
        grid=(4,),
        in_specs=[
            spec(lambda i: jnp.minimum(i, 1)),
            spec(lambda i: jnp.maximum(i - 2, 0)),
            spec(lambda i: i // 2),
            spec(lambda i: i // 2),
        ],
        out_specs=pl.BlockSpec((rows, 2 * half), lambda i: (i, 0)),
        out_shape=jax.ShapeDtypeStruct((4 * rows, 2 * half), left.dtype),
        cost_estimate=pl.CostEstimate(
            flops=0, bytes_accessed=32 * rows * half, transcendentals=0
        ),
    )(left, left_came, right, right_came)


def gather_rows(rows):
    two = jnp.concatenate([rows, cube(rows, FAR)], axis=0)
    half = two.shape[1] // 2
    left, right = two[:, :half], two[:, half:]
    left_came, right_came = cube(left, NEAR), cube(right, SIDE)
    left = jnp.concatenate([left, left_came], axis=0)
    right = jnp.concatenate([right, right_came], axis=0)
    return join_halves(left, cube(left, SIDE), right, cube(right, NEAR))


def sum_rows(partial):
    partial = partial.astype(BF)
    n, half = partial.shape[0] // 4, partial.shape[1] // 2
    left, right = partial[:, :half], partial[:, half:]
    left_came = cube(left[2 * n :], SIDE)
    right_came = cube(jnp.concatenate([right[n : 2 * n], right[3 * n :]], axis=0), NEAR)
    left = left[: 2 * n].astype(F32) + left_came.astype(F32)
    right_came = right_came.astype(F32)
    low = right[:n].astype(F32) + right_came[:n]
    high = right[2 * n : 3 * n].astype(F32) + right_came[n:]
    left_came = cube(left[n:].astype(BF), NEAR)
    right_came = cube(high.astype(BF), SIDE)
    left = left[:n] + left_came.astype(F32)
    right = low + right_came.astype(F32)
    both = jnp.concatenate([left, right], axis=1)
    rows = n // 2
    return both[:rows] + cube(both[rows:].astype(BF), FAR).astype(F32)


class Stages:
    def __init__(self):
        self.held = {}
        self.then = {}

    def run(self, value, step, jobs, settle=()):
        needed = [[self.held[name] for name in job[2]] for job in jobs]
        value, needed = lax.optimization_barrier((value, needed))
        out = step(value)
        made = [job[1](*inputs) for job, inputs in zip(jobs, needed)]
        due = [m for m, job in zip(made, jobs) if len(job) == 3]
        ready = [self.held[key] for key in settle]
        out, due, ready = lax.optimization_barrier((out, due, ready))
        self.held.update(zip(settle, ready))
        for job, result in zip(jobs, made):
            self.held[job[0]] = due.pop(0) if len(job) == 3 else result
            if job[0] in self.then:
                self.then[job[0]](job[0])
        return out


def others(block, axis):
    return [block] + [hop(block, axis, k) for k in range(1, lax.axis_size(axis))]


def sum_others(blocks, axis):
    total = blocks[0].astype(F32)
    for k in range(1, lax.axis_size(axis)):
        total = total + hop(blocks[k].astype(BF), axis, k).astype(F32)
    return total


def relative(values, dim, axis):
    count = lax.axis_size(axis)
    me = lax.axis_index(axis)
    step = 1
    while step < count:
        shape = values.shape
        cut = shape[:dim] + (count // (2 * step), 2, step * (shape[dim] // count)) + shape[dim + 1 :]
        view = values.reshape(cut)
        swapped = jnp.concatenate(
            [lax.slice_in_dim(view, 1, 2, axis=dim + 1), lax.slice_in_dim(view, 0, 1, axis=dim + 1)],
            axis=dim + 1,
        )
        values = jnp.where((me & step) != 0, swapped.reshape(shape), values)
        step *= 2
    return values


def spread_gains(norm_gains):
    me = lax.axis_index(CUBE)
    gain = norm_gains
    for step in link_steps():
        came = hop(gain, CUBE, step)
        gain = jnp.where(
            (me & step) != 0,
            jnp.concatenate([came, gain], axis=1),
            jnp.concatenate([gain, came], axis=1),
        )
    gain = relative(jnp.concatenate(others(gain, "grp"), axis=1), 1, "grp")
    other = hop(gain, "pipe", 1)
    core = lax.axis_index("pipe")
    return [jnp.where(core == 0, gain, other), jnp.where(core == 0, other, gain)]


def sum_gains(grads):
    me = lax.axis_index(CUBE)
    keep, extra = own_layer(grads[0], grads[1])
    count = lax.axis_size("grp")
    total = relative((keep + extra).reshape(2, count, -1), 1, "grp")
    mine = total[:, 0]
    for k in range(1, count):
        mine = mine + hop(total[:, k], "grp", k)
    for step in link_steps()[::-1]:
        half = mine.shape[1] // 2
        low, high = mine[:, :half], mine[:, half:]
        odd = (me & step) != 0
        mine = jnp.where(odd, high, low) + hop(jnp.where(odd, low, high), CUBE, step)
    return mine


def masked_probs(q, k, q_place, q_start, k_place):
    scores = lax.dot_general(q, k, (((1,), (1,)), ((), ())), preferred_element_type=F32)
    scores = scores * HEAD_SIZE ** (-0.5)
    allowed = (k_place <= q_place) & (k_place >= q_start)
    masked = jnp.where(allowed, scores, NEG_FILL)
    exps = jnp.exp(masked - jnp.max(masked, axis=-1, keepdims=True))
    return exps / jnp.sum(exps, axis=-1, keepdims=True)


def attend_kernel(q_ref, k_ref, v_ref, qp_ref, qs_ref, kp_ref, o_ref):
    probs = masked_probs(q_ref[0], k_ref[...], qp_ref[...], qs_ref[...], kp_ref[...])
    o_ref[0] = jnp.dot(probs.astype(BF), v_ref[...], preferred_element_type=F32).astype(BF)


def attend_back_kernel(q_ref, do_ref, k_ref, v_ref, qp_ref, qs_ref, kp_ref, dq_ref, dk_ref, dv_ref):
    @pl.when((pl.program_id(0) == 0) & (pl.program_id(1) == 0))
    def _():
        dk_ref[...] = jnp.zeros_like(dk_ref)
        dv_ref[...] = jnp.zeros_like(dv_ref)

    q = q_ref[0]
    do = do_ref[0]
    k = k_ref[...]
    probs = masked_probs(q, k, qp_ref[...], qs_ref[...], kp_ref[...])
    grad_probs = lax.dot_general(do, v_ref[...], (((1,), (1,)), ((), ())), preferred_element_type=F32)
    delta = jnp.sum(probs * grad_probs, axis=-1, keepdims=True)
    grad_scores = (probs * (grad_probs - delta) * HEAD_SIZE ** (-0.5)).astype(BF)
    dq_ref[0] = jnp.dot(grad_scores, k, preferred_element_type=F32).astype(BF)
    dk_ref[...] += lax.dot_general(
        grad_scores, q, (((0,), (0,)), ((), ())), preferred_element_type=F32
    )
    dv_ref[...] += lax.dot_general(
        probs.astype(BF), do, (((0,), (0,)), ((), ())), preferred_element_type=F32
    )


def attention_specs(heads, rows, keys):
    rows_blk = max(16, min(rows, (512 * 1024) // keys))
    per_head = pl.BlockSpec((1, rows_blk, HEAD_SIZE), lambda b, h: (h, b, 0))
    full = pl.BlockSpec((keys, HEAD_SIZE), lambda b, h: (0, 0))
    row_info = pl.BlockSpec((rows_blk, 1), lambda b, h: (b, 0))
    key_info = pl.BlockSpec((1, keys), lambda b, h: (0, 0))
    return ((rows // rows_blk, heads), per_head, full, row_info, key_info)


PARAMS = dict(
    compiler_params=pltpu.CompilerParams(vmem_limit_bytes=50 * 1024 * 1024),
)


def attend(q, k, v, q_place, q_start, k_place):
    heads, rows, _ = q.shape
    keys = k.shape[0]
    grid, per_head, full, row_info, key_info = attention_specs(heads, rows, keys)
    return pl.pallas_call(
        attend_kernel,
        grid=grid,
        in_specs=[per_head, full, full, row_info, row_info, key_info],
        out_specs=per_head,
        out_shape=jax.ShapeDtypeStruct(q.shape, BF),
        cost_estimate=pl.CostEstimate(
            flops=4 * heads * rows * keys * HEAD_SIZE,
            bytes_accessed=4 * q.size + 4 * k.size,
            transcendentals=heads * rows * keys,
        ),
        **PARAMS,
    )(q, k, v, q_place, q_start, k_place)


def attend_back(q, do, k, v, q_place, q_start, k_place):
    heads, rows, _ = q.shape
    keys = k.shape[0]
    grid, per_head, full, row_info, key_info = attention_specs(heads, rows, keys)
    return pl.pallas_call(
        attend_back_kernel,
        grid=grid,
        in_specs=[per_head, per_head, full, full, row_info, row_info, key_info],
        out_specs=[per_head, full, full],
        out_shape=[
            jax.ShapeDtypeStruct(q.shape, BF),
            jax.ShapeDtypeStruct(k.shape, F32),
            jax.ShapeDtypeStruct(k.shape, F32),
        ],
        cost_estimate=pl.CostEstimate(
            flops=10 * heads * rows * keys * HEAD_SIZE,
            bytes_accessed=6 * q.size + 12 * k.size,
            transcendentals=heads * rows * keys,
        ),
        **PARAMS,
    )(q, do, k, v, q_place, q_start, k_place)


def to_blocks(weight, cores):
    wd = lax.axis_size("wd")
    rows = weight.shape[0]
    cut = weight.reshape(rows, wd, cores, -1).transpose(2, 1, 0, 3)
    return cut.reshape((cores * wd, rows) + cut.shape[3:])


def columns_out(blocks):
    moved = trade(blocks, ("pipe", "wd"))
    return moved.reshape((2, -1) + moved.shape[2:])


def put_kernel(spots, *refs):
    pieces, out = refs[: len(spots)], refs[len(spots)]
    block = pl.program_id(0)
    for piece, (first, count, col, cols) in zip(pieces, spots):

        def put(piece=piece, col=col, cols=cols):
            out[:, col : col + cols] = piece[...]

        pl.when((block >= first) & (block < first + count))(put)


def put_together(columns):
    block = min([256] + [piece.shape[0] for stack in columns for piece in stack])
    spots, pieces, specs = [], [], []
    col = 0
    for stack in columns:
        first = 0
        for piece in stack:
            count, cols = piece.shape[0] // block, piece.shape[1]
            spots.append((first, count, col, cols))
            pieces.append(piece)

            def at(i, first=first, count=count):
                return (jnp.clip(i - first, 0, count - 1), 0)

            specs.append(pl.BlockSpec((block, cols), at))
            first += count
        col += cols
    return pl.pallas_call(
        lambda *refs: put_kernel(spots, *refs),
        grid=(first,),
        in_specs=specs,
        out_specs=pl.BlockSpec((block, col), lambda i: (i, 0)),
        out_shape=jax.ShapeDtypeStruct((first * block, col), BF),
        cost_estimate=pl.CostEstimate(
            flops=0, bytes_accessed=4 * first * block * col, transcendentals=0
        ),
        **PARAMS,
    )(*pieces)


def pack_attention(w_query, key_matrix, value_matrix, w_output, cores):
    wd = lax.axis_size("wd")
    rows = w_query.shape[0]
    cut = [w_query.reshape(rows, wd, cores, -1)]
    for m in (key_matrix, value_matrix):
        m = m.reshape(rows, wd, 1, -1)
        cut.append(jnp.broadcast_to(m, (rows, wd, cores, m.shape[3])))
    cut.append(w_output.T.reshape(rows, wd, cores, -1))
    return jnp.concatenate(cut, axis=-1).reshape(rows, -1)


def unpack_attention(own, widths):
    other = hop(own, "pipe", 1)
    query_w, kv_w, out_w = widths
    cuts = (query_w, query_w + kv_w, query_w + 2 * kv_w)
    return (
        jnp.concatenate([own[:, : cuts[0]], other[:, : cuts[0]]], axis=1),
        own[:, cuts[0] : cuts[1]],
        own[:, cuts[1] : cuts[2]],
        jnp.concatenate([own[:, cuts[2] :], other[:, cuts[2] :]], axis=1),
    )


def grad_pair(own, other):
    return (own + hop(other.astype(BF), "pipe", 1).astype(F32)).astype(BF)


def mlp_pair(left, right):
    half = right.shape[1] // 2
    return grad_pair(mm_tl(left, right[:, :half]), mm_tl(left, right[:, half:]))


def grad_group(total):
    return lax.psum_scatter(total, "grp", scatter_dimension=0, tiled=True)


def grad_home(total):
    return trade(total.reshape((lax.axis_size("wd"), -1) + total.shape[1:]), "wd")


def place_kernel(turned, at_ref, keep_ref, got_ref, out_ref):
    mine = pl.program_id(1) == at_ref[0]

    def put(ref):
        block = ref[0].astype(F32)
        out_ref[...] = block.T if turned else block

    @pl.when(mine)
    def _():
        put(keep_ref)

    @pl.when(jnp.logical_not(mine))
    def _():
        put(got_ref)


def place(keep, got, turned):
    wd, rows, cols = keep.shape
    at = lax.axis_index("pipe").astype(jnp.int32)[None]
    cores = lax.axis_size("pipe")
    source = pl.BlockSpec((1, rows, cols), lambda w, c, at_ref: (w, 0, 0))
    if turned:
        shape, target = (wd * cores * cols, rows), (cols, rows)
        out = pl.BlockSpec(target, lambda w, c, at_ref: (w * cores + c, 0))
    else:
        shape, target = (rows, wd * cores * cols), (rows, cols)
        out = pl.BlockSpec(target, lambda w, c, at_ref: (0, w * cores + c))
    return pl.pallas_call(
        lambda *refs: place_kernel(turned, *refs),
        grid_spec=pltpu.PrefetchScalarGridSpec(
            num_scalar_prefetch=1, grid=(wd, cores), in_specs=[source, source], out_specs=out
        ),
        out_shape=jax.ShapeDtypeStruct(shape, F32),
        cost_estimate=pl.CostEstimate(
            flops=keep.size, bytes_accessed=12 * keep.size, transcendentals=0
        ),
    )(at, keep, got)


def layer_forward(stages, layer, x_rows, gains, where, build, jobs, settle):
    held = stages.held
    cosine, sine, q_place, q_start, k_place = where
    normed = apply_norm(x_rows, gains[0]).astype(BF)
    rows_a = stages.run(normed, gather_rows, jobs[0], settle[0])
    held["attn", layer] = build("attn", layer)
    w_q, w_k, w_v, w_ot = held["attn", layer]
    tok = rows_a.shape[0]

    def project(rows):
        key = rotary_apply(mm(rows, w_k).reshape(tok, 1, HEAD_SIZE), cosine, sine).astype(BF)[:, 0]
        value = mm(rows, w_v).astype(BF)
        return jnp.concatenate([key, value], axis=1)

    def queries(rows):
        query = rotary_apply(mm(rows, w_q).reshape(tok, -1, HEAD_SIZE), cosine, sine).astype(BF)
        return query.transpose(1, 0, 2)

    held["rows_a"] = rows_a
    kv_all = stages.run(
        project(rows_a),
        lambda kv: jnp.concatenate(others(kv, "grp"), axis=0),
        [("query", queries, ("rows_a",))] + jobs[1],
        settle[1],
    )
    query = held["query"]
    keys, values = kv_all[:, :HEAD_SIZE], kv_all[:, HEAD_SIZE:]

    def attention(q):
        context = attend(q, keys, values, q_place, q_start, k_place)
        context = context.transpose(1, 0, 2).reshape(tok, -1)
        return context, mm_t(context, w_ot).astype(BF)

    context, partial = stages.run(query, attention, jobs[2], settle[2])
    mid = stages.run(partial, lambda p: x_rows + sum_rows(p), jobs[3], settle[3])
    rows_b = stages.run(
        mid, lambda m: gather_rows(apply_norm(m, gains[1]).astype(BF)), jobs[4], settle[4]
    )
    held["gu", layer] = w_gu = build("gu", layer)

    def ahead(rows):
        both = mm(rows, w_gu)
        half = both.shape[1] // 2
        gate, up = both[:, :half], both[:, half:]
        return gate, up, (jax.nn.silu(gate) * up).astype(BF)

    gate, up, hidden = stages.run(rows_b, ahead, jobs[5], settle[5])
    held["down", layer] = build("down", layer)
    return x_rows, rows_a, query, keys, values, context, mid, rows_b, gate, up, hidden


def layer_backward(
    stages, layer, grad_out, grad_mlp, gains, where, kept, also, jobs, settle
):
    held = stages.held
    cosine, sine, q_place, q_start, k_place = where
    x_rows, rows_a, query, keys, values, context, mid, rows_b, gate, up, hidden = kept
    w_q, w_k, w_v, w_ot = held["attn", layer]
    w_gu, w_dt = held["gu", layer], held["down", layer]
    tok = rows_a.shape[0]
    held["rows_b"], held["hidden"], held["grad_mlp"] = rows_b, hidden, grad_mlp

    def feed_back(rows):
        grad_hidden = mm(rows, w_dt)
        sig = jax.nn.sigmoid(gate)
        grad_gate = (grad_hidden * up * sig * (1.0 + gate * (1.0 - sig))).astype(BF)
        grad_up = (grad_hidden * gate * sig).astype(BF)
        both = jnp.concatenate([grad_gate, grad_up], axis=1)
        return grad_gate, grad_up, mm_t(both, w_gu).astype(BF), also(hidden)

    grad_gate, grad_up, partial, extra = stages.run(grad_mlp, feed_back, jobs[0], settle[0])
    held["grad_gate"], held["grad_up"] = grad_gate, grad_up
    grad_b = stages.run(partial, sum_rows, jobs[1], settle[1])
    grad_mid, gain_b = norm_back(mid, gains[1], grad_b)
    grad_mid = grad_mid + grad_out
    grad_attn = stages.run(grad_mid.astype(BF), gather_rows, jobs[2], settle[2])

    def attention_back(rows):
        grad_context = mm(rows, w_ot).astype(BF)
        grad_context = grad_context.reshape(tok, -1, HEAD_SIZE).transpose(1, 0, 2)
        return attend_back(query, grad_context, keys, values, q_place, q_start, k_place)

    def keys_back(grads):
        kv = jnp.concatenate(grads, axis=1)
        kv = kv.reshape((-1, tok) + kv.shape[1:])
        return sum_others([kv[k] for k in range(kv.shape[0])], "grp").astype(BF)

    def queries_back(grad_q):
        grad_q = grad_q.transpose(1, 0, 2).astype(F32)
        grad_q = rotary_apply(grad_q, cosine, -sine).astype(BF).reshape(tok, -1)
        return grad_q, mm_t(grad_q, w_q)

    held["grad_q"], *grads = stages.run(grad_attn, attention_back, jobs[3])
    own_kv = stages.run(
        grads, keys_back, [("g_q", queries_back, ("grad_q",))] + jobs[4], settle[4]
    )
    grad_q, partial = held["g_q"]
    grad_k = own_kv[:, :HEAD_SIZE].astype(F32)
    grad_k = rotary_apply(grad_k[:, None, :], cosine, -sine).astype(BF)[:, 0]
    grad_v = own_kv[:, HEAD_SIZE:]
    partial = (partial + mm_t(grad_k, w_k) + mm_t(grad_v, w_v)).astype(BF)

    def attn_pair(g_q, g_k, g_v):
        half_q = g_q.shape[1] // 2

        def term(cut):
            right = jnp.concatenate([g_q[:, cut], g_k, g_v], axis=1)
            left = [mm_tl(rows_a, right), mm_tl(grad_attn, context[:, cut])]
            return jnp.concatenate(left, axis=1)

        return grad_pair(term(slice(0, half_q)), term(slice(half_q, None)))

    held["g_q"], held["g_k"], held["g_v"] = grad_q, grad_k, grad_v
    grad_a = stages.run(partial, sum_rows, jobs[5](attn_pair), settle[5])
    grad_in, gain_a = norm_back(x_rows, gains[0], grad_a)
    return grad_mid + grad_in, jnp.stack([gain_a, gain_b]), extra


def own_layer(first, second):
    core = lax.axis_index("pipe")
    keep = jnp.where(core == 0, first, second)
    return keep, hop(jnp.where(core == 0, second, first), "pipe", 1)


def body(
    block_input,
    cotangent,
    segments,
    norm_gains,
    w_query,
    key_matrix,
    value_matrix,
    w_output,
    w_gate,
    w_up,
    w_down,
):
    core = lax.axis_index("pipe")
    grp = lax.axis_index("grp")
    wd = lax.axis_size("wd")
    groups = lax.axis_size("grp")
    cores = lax.axis_size("pipe")
    tok = block_input.shape[1] * lax.axis_size(CUBE)

    stages = Stages()
    held = stages.held
    packed = pack_attention(w_query[0], key_matrix[0], value_matrix[0], w_output[0], cores)
    gains = spread_gains(norm_gains[0])
    packed, gains = lax.optimization_barrier((packed, gains))
    attn_cols = columns_out(to_blocks(packed, cores))
    held["gate_out"] = to_blocks(w_gate[0], cores)
    held["up_out"] = to_blocks(w_up[0], cores)
    held["down_out"] = to_blocks(w_down[0].T, cores)
    query_w, out_w = w_query.shape[2] // (wd * cores), w_output.shape[1] // (wd * cores)
    widths = (query_w, key_matrix.shape[2] // wd, out_w)

    def move(name):
        return (name, columns_out, (name + "_out",), "later")

    def rows_of(name, layer):
        return lax.all_gather(held[name][layer], "grp", axis=0, tiled=True)

    def put(*names):
        return put_together([[m] for n in names for m in (held[n], hop(held[n], "pipe", 1))])

    def build(kind, layer):
        if kind == "attn":
            return unpack_attention(held["own", "attn", layer], widths)
        if kind == "gu":
            return put(("own", "gate", layer), ("own", "up", layer))
        return put(("own", "down", layer))

    held["attn"] = attn_cols
    for layer in range(2):
        held["own", "attn", layer] = rows_of("attn", layer)

    def start(name):
        for layer in range(2):
            held["own", name, layer] = rows_of(name, layer)

    stages.then.update(gate=start, up=start, down=start)

    seg_row = lax.dynamic_index_in_dim(segments, core, 0, keepdims=False)
    starts = doc_starts(seg_row)
    rows_own = tok // lax.axis_size(CUBE)

    def in_row_order(values):
        values = relative(values, 0, CUBE)
        return jnp.concatenate(
            [values[j * rows_own : (j + 1) * rows_own] for j in ROW_ORDER], axis=0
        )

    local = in_row_order(jnp.arange(tok, dtype=jnp.int32))
    q_place = grp * tok + local
    q_start = in_row_order(lax.dynamic_slice_in_dim(starts, grp * tok, tok))
    cosine, sine = rope_tables(q_place - q_start)
    k_place = jnp.concatenate([(grp ^ k) * tok + local for k in range(groups)])
    where = (cosine, sine, q_place[:, None], q_start[:, None], k_place[None, :])

    rows = lax.dynamic_index_in_dim(block_input, core, 0, keepdims=False)
    grad = lax.dynamic_index_in_dim(cotangent, core, 0, keepdims=False)
    held["cotangent"] = grad
    kept = [None, None]
    outs = [None, None]
    kept[0] = layer_forward(
        stages,
        0,
        rows.astype(F32),
        gains[0],
        where,
        build,
        [
            [],
            [move("gate")],
            [move("up"), ("last", gather_rows, ("cotangent",))],
            [move("down")],
            [],
            [],
        ],
        [
            (),
            (("own", "attn", 1),),
            (("own", "gate", 0),),
            (("own", "up", 0),),
            (("own", "down", 0),),
            (),
        ],
    )

    def close(hidden, layer):
        return (kept[layer][6] + sum_rows(mm_t(hidden, held["down", layer]))).astype(BF)

    outs[0] = stages.run(
        kept[0][-1], lambda h: close(h, 0), [], (("own", "gate", 1),)
    )
    kept[1] = layer_forward(
        stages,
        1,
        outs[0].astype(F32),
        gains[1],
        where,
        build,
        [[]] * 6,
        [(("own", "up", 1),), (), (("own", "down", 1),), (), (), ()],
    )

    def grad_of(name, layer):
        sources = {
            "down": ("grad_mlp", "hidden"),
            "gate": ("rows_b", "grad_gate"),
            "up": ("rows_b", "grad_up"),
        }[name]
        return (("pair", name, layer), mlp_pair, sources)

    def group_sum(name, layer):
        return (("sum", name, layer), grad_group, (("pair", name, layer),), "later")

    def home(name, layer):
        return (("home", name, layer), grad_home, (("sum", name, layer),), "later")

    def attn_grad(layer):
        return lambda pair: (("pair", "attn", layer), pair, ("g_q", "g_k", "g_v"))

    def final(name, turned):
        def ready(first, second):
            return place(*own_layer(first, second), turned)

        return (("final", name), ready, (("home", name, 0), ("home", name, 1)))

    held["hidden"], held["grad_mlp"] = kept[1][-1], held["last"]
    hidden = stages.run(kept[1][-1], lambda h: h, [grad_of("down", 1)])

    grads_in = [None, None]
    gain_grads = [None, None]
    grad_in, gain_grads[1], outs[1] = layer_backward(
        stages,
        1,
        grad.astype(F32),
        held["last"],
        gains[1],
        where,
        kept[1][:-1] + (hidden,),
        lambda h: close(h, 1),
        (
            [],
            [group_sum("down", 1), grad_of("gate", 1)],
            [group_sum("gate", 1), grad_of("up", 1)],
            [group_sum("up", 1)],
            [],
            lambda pair: [attn_grad(1)(pair)],
        ),
        [(), (), (), (), (), (("sum", "gate", 1),)],
    )
    grads_in[1] = grad_in.astype(BF)
    grad_mlp = stages.run(grads_in[1], gather_rows, [group_sum("attn", 1)], (("sum", "up", 1),))
    grad_in, gain_grads[0], _ = layer_backward(
        stages,
        0,
        grads_in[1].astype(F32),
        grad_mlp,
        gains[0],
        where,
        kept[0],
        lambda h: (),
        (
            [grad_of("down", 0), home("down", 1), home("gate", 1)],
            [group_sum("down", 0), grad_of("gate", 0), home("up", 1)],
            [group_sum("gate", 0), grad_of("up", 0), home("attn", 1)],
            [group_sum("up", 0)],
            [home("down", 0)],
            lambda pair: [attn_grad(0)(pair)],
        ),
        [
            (),
            (("sum", "attn", 1), ("home", "down", 1), ("home", "gate", 1)),
            (("sum", "down", 0), ("home", "up", 1)),
            (),
            (("sum", "gate", 0), ("home", "attn", 1)),
            (("sum", "up", 0), ("home", "down", 0)),
        ],
    )
    grads_in[0] = grad_in.astype(BF)
    for key, job, names, *_ in (
        group_sum("attn", 0),
        home("gate", 0),
        final("down", True),
        final("gate", False),
        home("up", 0),
        final("up", False),
    ):
        held[key] = job(*[held[name] for name in names])
    keys = (("sum", "attn", 0),) + tuple(("final", name) for name in ("down", "gate", "up"))
    held.update(zip(keys, lax.optimization_barrier([held[key] for key in keys])))
    key, job, *_ = home("attn", 0)
    held[key] = job(held["sum", "attn", 0])

    def by_batch(pair):
        own, other = own_layer(pair[0], pair[1])
        both = jnp.where(core == 0, jnp.stack([own, other]), jnp.stack([other, own]))
        return both[None]

    layer_out = by_batch(outs)
    input_grad = by_batch(grads_in)

    grad_norm_gains = sum_gains(gain_grads)[None]

    def both(name):
        return own_layer(held["home", name, 0], held["home", name, 1])

    keep, got = both("attn")
    cuts = (0, widths[0], widths[0] + widths[1], widths[0] + 2 * widths[1], keep.shape[2])
    q_pair, k_pair, v_pair, o_pair = (
        (keep[..., lo:hi], got[..., lo:hi]) for lo, hi in zip(cuts[:-1], cuts[1:])
    )

    def small(pair):
        order = pair[0].transpose(1, 0, 2).astype(F32)
        return order.reshape(order.shape[0], -1)[None]

    grad_wq = place(*q_pair, False)[None]
    grad_wk = small(k_pair)
    grad_wv = small(v_pair)
    grad_wo = place(*o_pair, True)[None]
    grad_wg = held["final", "gate"][None]
    grad_wu = held["final", "up"][None]
    grad_wd = held["final", "down"][None]
    return (
        layer_out,
        input_grad,
        grad_norm_gains,
        grad_wq,
        grad_wk,
        grad_wv,
        grad_wo,
        grad_wg,
        grad_wu,
        grad_wd,
    )


def solution(mesh):
    sizes = dict(mesh.shape)
    wd = KV_HEADS // sizes["tensor"]
    fine = Mesh(
        mesh.devices.reshape(sizes["pipe"], sizes["dp"] // wd, wd, sizes["tensor"]),
        ("pipe", "grp", "wd", "tensor"),
    )
    dp = ("grp", "wd")
    tokens = P(None, dp + ("tensor",), None)
    outs = P("pipe", None, dp + ("tensor",), None)
    gains = P("pipe", None, dp + ("tensor",))
    tall = P("pipe", dp, "tensor")
    wide = P("pipe", "tensor", dp)
    weights = (tall, tall, tall, wide, tall, tall, wide)
    return jax.shard_map(
        body,
        mesh=fine,
        in_specs=(tokens, tokens, P(), gains) + weights,
        out_specs=(outs, outs, gains) + weights,
        check_vma=False,
    )
```
